32 devices in a mesh: seq: 16 (over z, y, core), ch: 2 (over x).
Axes of the slice: x: 2, y: 2, z: 4, core: 2. Of those that a mesh axis runs over, the one named last changes fastest.
Arguments:
- ids: int32 [2, 2048], P(None, 'seq'), may hold values from 0 to 15
- live: int32 [2], replicated, may hold values from 1024 to 2048
- embed: float32 [16, 256], replicated, may hold values from -6 to 6
- norm_gain: float32 [2, 2, 256], replicated, may hold values from 0.5 to 1.5
- in_weight: bfloat16 [2, 256, 3, 256], P(None, None, None, 'ch'), may hold values from -0.375 to 0.375
- short_kernel: float32 [2, 3, 3, 256], P(None, None, None, 'ch'), may hold values from -3 to 3
- filter_first: float32 [2, 33, 64], replicated, may hold values from -3 to 3
- filter_second: float32 [2, 64, 256], P(None, None, 'ch'), may hold values from -0.03125 to 0.03125
- skip_gain: float32 [2, 256], P(None, 'ch'), may hold values from -4 to 4
- out_weight: bfloat16 [2, 256, 256], P(None, 'ch'), may hold values from -0.375 to 0.375
- up_weight: bfloat16 [2, 256, 1024], P(None, None, 'ch'), may hold values from -0.375 to 0.375
- down_weight: bfloat16 [2, 1024, 256], P(None, 'ch'), may hold values from -0.375 to 0.375
- cotangent: float32 [2, 2048, 256], P(None, 'seq'), may hold values from -6 to 6
Outputs:
- block_out: float32 [2, 2048, 256], P(None, 'seq')
- grad_embed: float32 [16, 256], replicated
- grad_norm_gain: float32 [2, 2, 256], replicated
- grad_in_weight: float32 [2, 256, 3, 256], P(None, None, None, 'ch')
- grad_short_kernel: float32 [2, 3, 3, 256], P(None, None, None, 'ch')
- grad_filter_first: float32 [2, 33, 64], replicated
- grad_filter_second: float32 [2, 64, 256], P(None, None, 'ch')
- grad_skip_gain: float32 [2, 256], P(None, 'ch')
- grad_out_weight: float32 [2, 256, 256], P(None, 'ch')
- grad_up_weight: float32 [2, 256, 1024], P(None, None, 'ch')
- grad_down_weight: float32 [2, 1024, 256], P(None, 'ch')
The draws below stay inside these ranges and needn't reach their ends.
All inputs are finite; a program needn't handle non-finite values.
Results may differ from the reference program's by a relative error of at most 0.012.
Values sent between devices are 32-bit elements; how exact they have to be, the bound alone decides.
No kernel may reach another device: no remote copies, remote signals or barrier semaphores. Data moves between devices by JAX's collectives and lax.ppermute only.
A program may use at most 128 MiB of HBM per device.

```python
import math
import jax
import jax.numpy as jnp
from jax import lax

D = 256
FF = 1024
HID = 64
FEAT = 33
VOCAB = 16
SHORT = 3
LAYERS = 2
MICRO = 2
SEQ = 2048


def plant(drawn, key, smallest, top_value):
    longest = drawn.shape.index(max(drawn.shape))
    spots = []
    for shift in (0, 1):
        where = [jax.random.randint(jax.random.fold_in(key, axis), (), 0, length) for axis, length in enumerate(drawn.shape)]
        where[longest] = (where[longest] + shift) % drawn.shape[longest]
        spots.append(tuple(where))
    return drawn.at[spots[0]].set(smallest).at[spots[1]].set(top_value)


def steps_of(stream_key, dims, pieces, smallest, largest):
    def one(position, parts):
        draws = jax.random.uniform(jax.random.fold_in(jax.random.fold_in(stream_key, 6), position), (parts,), jnp.float32, smallest / len(pieces), largest / len(pieces))
        return jnp.repeat(jnp.exp(draws), dims[position] // parts).reshape((-1,) + (1,) * (len(dims) - position - 1))

    level = one(*pieces[0])
    for cut in pieces[1:]:
        level = level * one(*cut)
    return level


def scatter_about(stream_key, dims, scale, bound, cuts=(), kind=jnp.bfloat16):
    drawn = jax.random.normal(stream_key, dims, jnp.float32) * scale
    if len(cuts) > 0:
        drawn = steps_of(stream_key, dims, cuts, -0.22, 0.18) * drawn
    return jnp.clip(drawn, min=-bound, max=bound).astype(kind)


def setup_inputs(seed: int = 0) -> dict:
    streams_of = jax.random.split(jax.random.key(seed), 14)
    ids = plant(jax.random.randint(streams_of[0], (MICRO, SEQ), 0, VOCAB), jax.random.fold_in(streams_of[0], 1), 0, VOCAB - 1).astype(jnp.int32)
    live = jax.random.randint(streams_of[1], (MICRO,), SEQ // 2, SEQ + 1).astype(jnp.int32)
    embed = scatter_about(streams_of[2], (VOCAB, D), 1.0, 6.0, (), jnp.float32)
    norm_gain = jnp.clip(1.0 + 0.1 * jax.random.normal(streams_of[3], (LAYERS, 2, D), jnp.float32), 0.5, 1.5)
    in_weight = scatter_about(streams_of[4], (LAYERS, D, 3, D), D ** -0.5, 0.375, ((3, 2),))
    short_kernel = scatter_about(streams_of[5], (LAYERS, SHORT, 3, D), 0.5, 3.0, ((3, 2),), jnp.float32)
    filter_first = scatter_about(streams_of[6], (LAYERS, FEAT, HID), 4 ** -0.5, 3.0, (), jnp.float32)
    filter_second = scatter_about(streams_of[7], (LAYERS, HID, D), (16 * SEQ) ** -0.5, 0.03125, ((2, 2),), jnp.float32)
    skip_gain = scatter_about(streams_of[8], (LAYERS, D), 1.0, 4.0, ((1, 2),), jnp.float32)
    out_weight = scatter_about(streams_of[9], (LAYERS, D, D), D ** -0.5, 0.375, ((1, 2),))
    up_weight = scatter_about(streams_of[10], (LAYERS, D, FF), D ** -0.5, 0.375, ((2, 2),))
    down_weight = scatter_about(streams_of[11], (LAYERS, FF, D), (FF // 4) ** -0.5, 0.375, ((1, 2),))
    cotangent = scatter_about(streams_of[12], (MICRO, SEQ, D), 1.0, 6.0, ((1, 16),), jnp.float32)
    return dict(ids=ids, live=live, embed=embed, norm_gain=norm_gain, in_weight=in_weight, short_kernel=short_kernel, filter_first=filter_first, filter_second=filter_second, skip_gain=skip_gain, out_weight=out_weight, up_weight=up_weight, down_weight=down_weight, cotangent=cotangent)


precise = lax.Precision.HIGHEST
epsilon = 1e-05

@jax.custom_vjp
def low(v):
    return lax.optimization_barrier(v.astype(jnp.bfloat16)).astype(jnp.float32)

@jax.custom_vjp
def low_back(v):
    return v

def low_keep(v):
    return (low(v), None)

def low_pass(kept, grad):
    return (grad,)

def back_keep(v):
    return (v, None)

def back_low(kept, grad):
    return (low(grad),)
low.defvjp(low_keep, low_pass)
low_back.defvjp(back_keep, back_low)

def layer_norm(inputs, gain_vec):
    center = inputs - lax.optimization_barrier(jnp.mean(inputs, axis=-1, keepdims=True))
    spread = lax.optimization_barrier(jnp.mean(center * center, axis=-1, keepdims=True))
    return center * lax.rsqrt(spread + epsilon) * gain_vec

def position_features(length):
    places = jnp.arange(length, dtype=jnp.int32)
    band_ids = jnp.arange(1, (FEAT - 1) // 2 + 1, dtype=jnp.int32)
    turn_counts = places[:, None] * band_ids[None, :] % length
    angles = turn_counts.astype(jnp.float32) * (2.0 * math.pi / length)
    ramp_vals = places.astype(jnp.float32)[:, None] / length
    return jnp.concatenate([ramp_vals, jnp.cos(angles), jnp.sin(angles)], axis=1)

def decay_rates(channels):
    return 0.3 * 10.0 ** (channels.astype(jnp.float32) / (D - 1))

def decay_table(length, channels):
    ramp_vals = jnp.arange(length, dtype=jnp.int32).astype(jnp.float32)[:, None] / length
    return jnp.exp(-ramp_vals * decay_rates(channels)[None, :])

def short_conv(mixed_in, kernel):
    shift_one = jnp.pad(mixed_in, ((1, 0), (0, 0), (0, 0)))[:-1]
    shift_two = jnp.pad(mixed_in, ((2, 0), (0, 0), (0, 0)))[:-2]
    return kernel[0] * mixed_in + kernel[1] * shift_one + kernel[2] * shift_two

def long_conv(product, filt, skip_vec):
    length = product.shape[0]
    size_full = 2 * length
    spectrum = jnp.fft.rfft(product, n=size_full, axis=0) * jnp.fft.rfft(filt, n=size_full, axis=0)
    return jnp.fft.irfft(spectrum, n=size_full, axis=0)[:length] + skip_vec * product

def hyena_layer(stream, norm_gains, w_in, kernel, w_out, w_up, w_down, filt, skip_vec):
    normed = low(layer_norm(stream, norm_gains[0]))
    mixed_in = low_back(jnp.einsum('td,dgc->tgc', normed, w_in, precision=precise))
    gate_vals = short_conv(mixed_in, kernel)
    conv_out = long_conv(gate_vals[:, 2] * gate_vals[:, 1], filt, skip_vec)
    gated_out = low(conv_out * gate_vals[:, 0])
    mid_state = stream + low_back(jnp.dot(gated_out, w_out, precision=precise))
    normed_mid = low(layer_norm(mid_state, norm_gains[1]))
    pre_act = low_back(jnp.dot(normed_mid, w_up, precision=precise))
    hidden = low(jax.nn.gelu(pre_act))
    return mid_state + low_back(jnp.dot(hidden, w_down, precision=precise))

def forward(ids, live, embed, norm_gain, in_weight, short_kernel, filter_first, filter_second, skip_gain, out_weight, up_weight, down_weight):
    features = position_features(SEQ)
    decay = decay_table(SEQ, jnp.arange(D, dtype=jnp.int32))
    filters = [jnp.dot(jnp.sin(jnp.dot(features, filter_first[level_idx], precision=precise)), filter_second[level_idx], precision=precise) * decay for level_idx in range(LAYERS)]
    ramp_col = jnp.arange(SEQ, dtype=jnp.int32).astype(jnp.float32)[:, None] / SEQ
    penalty = sum((0.25 * SEQ * jnp.sum(ramp_col * filt * filt) for filt in filters))
    vocab_ids = jnp.arange(VOCAB, dtype=jnp.int32)
    places = jnp.arange(SEQ, dtype=jnp.int32)
    results = []
    for batch_idx in range(MICRO):
        keep_mask = (places < live[batch_idx]).astype(jnp.float32)
        onehot = (ids[batch_idx][:, None] == vocab_ids[None, :]).astype(jnp.float32)
        stream = jnp.dot(onehot, embed, precision=precise) * keep_mask[:, None]
        for level_idx in range(LAYERS):
            stream = hyena_layer(stream, norm_gain[level_idx], in_weight[level_idx], short_kernel[level_idx], out_weight[level_idx], up_weight[level_idx], down_weight[level_idx], filters[level_idx], skip_gain[level_idx])
        results.append(stream * keep_mask[:, None])
    return (jnp.stack(results), penalty)

def reference(ids, live, embed, norm_gain, in_weight, short_kernel, filter_first, filter_second, skip_gain, out_weight, up_weight, down_weight, cotangent):
    floats = tuple((member.astype(jnp.float32) for member in (embed, norm_gain, in_weight, short_kernel, filter_first, filter_second, skip_gain, out_weight, up_weight, down_weight)))

    def run_forward(*params):
        return forward(ids, live, *params)
    (block_out, penalty), pullback = jax.vjp(run_forward, *floats)
    grad_embed, grad_gain, grad_in, grad_kernel, grad_first, grad_second, grad_skip, grad_out, grad_up, grad_down = pullback((cotangent.astype(jnp.float32), jnp.ones_like(penalty)))
    return (block_out, grad_embed, grad_gain, grad_in, grad_kernel, grad_first, grad_second, grad_skip, grad_out, grad_up, grad_down)
```

```python
import functools
import math

import jax
import jax.numpy as jnp
import numpy as np
from jax import lax
from jax.experimental import pallas as pl
from jax.experimental.pallas import tpu as pltpu
from jax.sharding import PartitionSpec as P

D = 256
FEAT = 33


precise = lax.Precision.HIGHEST
epsilon = 1e-05


def passed_along(value, axis, steps):
    count = lax.axis_size(axis)
    leading, last = (max(0, -steps), min(count, count - steps))
    return lax.ppermute(value, axis, [(source, source + steps) for source in range(leading, last)])


def layer_norm(inputs, gain_vec):
    center = inputs - jnp.mean(inputs, axis=-1, keepdims=True)
    spread = jnp.mean(center * center, axis=-1, keepdims=True)
    return center * lax.rsqrt(spread + epsilon) * gain_vec


def position_features(length):
    places = jnp.arange(length, dtype=jnp.int32)
    band_ids = jnp.arange(1, (FEAT - 1) // 2 + 1, dtype=jnp.int32)
    turn_counts = places[:, None] * band_ids[None, :] % length
    angles = turn_counts.astype(jnp.float32) * (2.0 * math.pi / length)
    ramp_vals = places.astype(jnp.float32)[:, None] / length
    return jnp.concatenate([ramp_vals, jnp.cos(angles), jnp.sin(angles)], axis=1)


def decay_rates(channels):
    return 0.3 * 10.0 ** (channels.astype(jnp.float32) / (D - 1))


def dft_tables(blocks, block_len):
    doubled = 2 * blocks
    span_total = doubled * block_len
    frequency = jnp.arange(doubled, dtype=jnp.int32)
    places = jnp.arange(blocks, dtype=jnp.int32)
    inner_idx = jnp.arange(block_len, dtype=jnp.int32)
    outer_angle = (frequency[:, None] * places[None, :] % doubled).astype(jnp.float32) * (
        2.0 * math.pi / doubled
    )
    twist_angle = (frequency[:, None] * inner_idx[None, :] % span_total).astype(jnp.float32) * (
        2.0 * math.pi / span_total
    )
    inner_angle = (inner_idx[:, None] * inner_idx[None, :] % block_len).astype(jnp.float32) * (
        2.0 * math.pi / block_len
    )
    return (
        jnp.cos(outer_angle),
        jnp.sin(outer_angle),
        jnp.cos(twist_angle),
        jnp.sin(twist_angle),
        jnp.cos(inner_angle),
        jnp.sin(inner_angle),
    )


def along_block(values, table):
    return jnp.einsum("...kb,bj->...kj", values, table, precision=precise)


def to_spectrum(signal, tables):
    outer_cos, outer_sin, twist_cos, twist_sin, inner_cos, inner_sin = tables
    first_re = jnp.einsum("kp,...pb->...kb", outer_cos, signal, precision=precise)
    first_im = -jnp.einsum("kp,...pb->...kb", outer_sin, signal, precision=precise)
    turned_re = first_re * twist_cos + first_im * twist_sin
    turned_im = first_im * twist_cos - first_re * twist_sin
    spec_re = along_block(turned_re, inner_cos) + along_block(turned_im, inner_sin)
    spec_im = along_block(turned_im, inner_cos) - along_block(turned_re, inner_sin)
    return (spec_re, spec_im)


def from_spectrum(spec_re, spec_im, tables):
    outer_cos, outer_sin, twist_cos, twist_sin, inner_cos, inner_sin = tables
    back_re = along_block(spec_re, inner_cos) - along_block(spec_im, inner_sin)
    back_im = along_block(spec_re, inner_sin) + along_block(spec_im, inner_cos)
    turned_re = back_re * twist_cos - back_im * twist_sin
    turned_im = back_re * twist_sin + back_im * twist_cos
    scale_back = 1.0 / (outer_cos.shape[0] * inner_cos.shape[0])
    signal = jnp.einsum("kp,...kb->...pb", outer_cos, turned_re, precision=precise) - jnp.einsum(
        "kp,...kb->...pb", outer_sin, turned_im, precision=precise
    )
    return signal * scale_back


def causal_filter(received, filt_spec, skip_part, tables):
    item_count, chan_count, length = received.shape
    blocks = tables[0].shape[1]
    spec_re, spec_im = to_spectrum(
        received.reshape(item_count, chan_count, blocks, length // blocks), tables
    )
    prod_re = spec_re * filt_spec[0] - spec_im * filt_spec[1]
    prod_im = spec_re * filt_spec[1] + spec_im * filt_spec[0]
    result_sig = from_spectrum(prod_re, prod_im, tables).reshape(item_count, chan_count, length)
    return result_sig + skip_part[:, None] * received


def filter_backward(grad_cols, moved_in, filt_spec, skip_part, tables):
    item_count, chan_count, length = grad_cols.shape
    blocks = tables[0].shape[1]
    grad_re, grad_im = to_spectrum(
        grad_cols.reshape(item_count, chan_count, blocks, length // blocks), tables
    )
    input_re, input_im = to_spectrum(
        moved_in.reshape(item_count, chan_count, blocks, length // blocks), tables
    )
    back_re = grad_re * filt_spec[0] + grad_im * filt_spec[1]
    back_im = grad_im * filt_spec[0] - grad_re * filt_spec[1]
    grad_u_cols = (
        from_spectrum(back_re, back_im, tables).reshape(item_count, chan_count, length)
        + skip_part[:, None] * grad_cols
    )
    corr_re = grad_re * input_re + grad_im * input_im
    corr_im = grad_im * input_re - grad_re * input_im
    grad_filt = jnp.sum(from_spectrum(corr_re, corr_im, tables), axis=0).reshape(chan_count, length)
    grad_skip_part = jnp.sum(grad_cols * moved_in, axis=(0, 2))
    return (grad_u_cols, grad_filt, grad_skip_part)


def local_filter(first, second, features, select, group_idx, chan_local):
    hidden_pre = jnp.dot(features, first, precision=precise)
    hidden_act = jnp.sin(hidden_pre)
    chan_width = second.shape[1]
    second_part = jnp.dot(second, select, precision=precise)
    channel_ids = group_idx * chan_width + chan_local
    length = features.shape[0]
    ramp_vals = jnp.arange(length, dtype=jnp.int32).astype(jnp.float32) / length
    decay_part = jnp.exp(-decay_rates(channel_ids)[:, None] * ramp_vals[None, :])
    filt_cols = jnp.einsum("hc,th->ct", second_part, hidden_act, precision=precise) * decay_part
    return (filt_cols, hidden_pre, hidden_act, second_part, decay_part)


def filter_mlp_backward(grad_filt, features, filter_parts):
    hidden_pre, hidden_act, second_part, decay_part = filter_parts
    grad_shaped = grad_filt * decay_part
    grad_second_part = jnp.einsum("ct,th->hc", grad_shaped, hidden_act, precision=precise)
    grad_act = jnp.einsum("ct,hc->th", grad_shaped, second_part, precision=precise)
    grad_first = jnp.einsum(
        "tf,th->fh", features, grad_act * jnp.cos(hidden_pre), precision=precise
    )
    return (grad_first, grad_second_part)


def embed_lookup(ids, live, embed, seq_rank):
    tok_rows = ids.shape[1]
    places = seq_rank * tok_rows + jnp.arange(tok_rows, dtype=jnp.int32)
    keep_mask = (places[None, :] < live[:, None]).astype(jnp.float32)
    vocab_ids = jnp.arange(embed.shape[0], dtype=jnp.int32)
    onehot = (ids[:, :, None] == vocab_ids[None, None, :]).astype(jnp.float32) * keep_mask[
        :, :, None
    ]
    stream = jnp.einsum("mtv,vd->mtd", onehot, embed, precision=precise)
    return (stream, onehot, keep_mask)


def channel_total(partial_sum):
    return lax.psum(partial_sum, "ch")


def input_total(partial_sum):
    return lax.psum(partial_sum, "ch")


def layer_forward(stream, params, filt_spec, skip_part, tables):
    norm_gains, w_in, kernel, w_out, w_up, w_down = params
    normed = layer_norm(stream, norm_gains[0]).astype(jnp.bfloat16)
    mixed_in = jnp.einsum("mtd,dgc->mtgc", normed, w_in, preferred_element_type=jnp.float32)
    rim_rows = passed_along(mixed_in[:, -2:], "seq", 1)
    padded = jnp.concatenate([rim_rows, mixed_in], axis=1)
    micro_count, tok_rows = (mixed_in.shape[0], mixed_in.shape[1])
    chan_width = mixed_in.shape[3]
    gate_vals = (
        kernel[0] * mixed_in
        + kernel[1] * padded[:, 1 : tok_rows + 1]
        + kernel[2] * padded[:, 0:tok_rows]
    )
    product_in = gate_vals[:, :, 2] * gate_vals[:, :, 1]
    flat_rows = jnp.swapaxes(product_in, 1, 2).reshape(1, micro_count * chan_width, tok_rows)
    received = lax.all_to_all(flat_rows, "seq", split_axis=1, concat_axis=2, tiled=True)
    result_sig = causal_filter(received, filt_spec, skip_part, tables)
    conv_flat = lax.all_to_all(result_sig, "seq", split_axis=2, concat_axis=1, tiled=True)
    conv_out = jnp.swapaxes(conv_flat.reshape(micro_count, chan_width, tok_rows), 1, 2)
    gated_out = (conv_out * gate_vals[:, :, 0]).astype(jnp.bfloat16)
    mid_state = stream + channel_total(
        jnp.einsum("mtc,cd->mtd", gated_out, w_out, preferred_element_type=jnp.float32)
    )
    normed_mid = layer_norm(mid_state, norm_gains[1]).astype(jnp.bfloat16)
    pre_act = jnp.einsum("mtd,df->mtf", normed_mid, w_up, preferred_element_type=jnp.float32)
    hidden = jax.nn.gelu(pre_act).astype(jnp.bfloat16)
    new_stream = mid_state + channel_total(
        jnp.einsum("mtf,fd->mtd", hidden, w_down, preferred_element_type=jnp.float32)
    )
    kept_vals = (
        stream,
        normed,
        mixed_in,
        padded,
        gate_vals,
        received,
        conv_out,
        gated_out,
        mid_state,
        normed_mid,
        pre_act,
        hidden,
    )
    return (new_stream, kept_vals)


def layer_backward(grad_stream, kept_vals, params, filt_spec, skip_part, tables):
    norm_gains, w_in, kernel, w_out, w_up, w_down = params
    (
        stream,
        normed,
        mixed_in,
        padded,
        gate_vals,
        moved_in,
        conv_out,
        gated_out,
        mid_state,
        normed_mid,
        pre_act,
        hidden,
    ) = kept_vals
    micro_count, tok_rows = (mixed_in.shape[0], mixed_in.shape[1])
    chan_width = mixed_in.shape[3]
    grad_low = grad_stream.astype(jnp.bfloat16)
    grad_down = jnp.einsum("mtf,mtd->fd", hidden, grad_low, preferred_element_type=jnp.float32)
    grad_hidden = jnp.einsum("mtd,fd->mtf", grad_low, w_down, preferred_element_type=jnp.float32)
    _, gelu_back = jax.vjp(jax.nn.gelu, pre_act)
    grad_pre = gelu_back(grad_hidden)[0].astype(jnp.bfloat16)
    grad_up = jnp.einsum("mtd,mtf->df", normed_mid, grad_pre, preferred_element_type=jnp.float32)
    grad_normed_mid = input_total(
        jnp.einsum("mtf,df->mtd", grad_pre, w_up, preferred_element_type=jnp.float32)
    )
    _, norm_back_mid = jax.vjp(layer_norm, mid_state, norm_gains[1])
    grad_mid_norm, grad_gain_mid = norm_back_mid(grad_normed_mid)
    grad_mid = grad_stream + grad_mid_norm
    grad_mid_low = grad_mid.astype(jnp.bfloat16)
    grad_out = jnp.einsum(
        "mtc,mtd->cd", gated_out, grad_mid_low, preferred_element_type=jnp.float32
    )
    grad_gated = jnp.einsum("mtd,cd->mtc", grad_mid_low, w_out, preferred_element_type=jnp.float32)
    grad_conv = grad_gated * gate_vals[:, :, 0]
    grad_first_gate = grad_gated * conv_out
    grad_flat = jnp.swapaxes(grad_conv, 1, 2).reshape(1, micro_count * chan_width, tok_rows)
    grad_cols = lax.all_to_all(grad_flat, "seq", split_axis=1, concat_axis=2, tiled=True)
    grad_u_cols, grad_filt, grad_skip_part = filter_backward(
        grad_cols, moved_in, filt_spec, skip_part, tables
    )
    grad_back_flat = lax.all_to_all(grad_u_cols, "seq", split_axis=2, concat_axis=1, tiled=True)
    grad_product = jnp.swapaxes(grad_back_flat.reshape(micro_count, chan_width, tok_rows), 1, 2)
    grad_gates = jnp.stack(
        [grad_first_gate, grad_product * gate_vals[:, :, 2], grad_product * gate_vals[:, :, 1]],
        axis=2,
    )
    rim_back = passed_along(grad_gates[:, :2], "seq", -1)
    extended = jnp.concatenate([grad_gates, rim_back], axis=1)
    grad_mixed = (
        kernel[0] * grad_gates
        + kernel[1] * extended[:, 1 : tok_rows + 1]
        + kernel[2] * extended[:, 2 : tok_rows + 2]
    )
    grad_kernel = jnp.stack(
        [
            jnp.sum(grad_gates * mixed_in, axis=(0, 1)),
            jnp.sum(grad_gates * padded[:, 1 : tok_rows + 1], axis=(0, 1)),
            jnp.sum(grad_gates * padded[:, 0:tok_rows], axis=(0, 1)),
        ]
    )
    grad_mixed_low = grad_mixed.astype(jnp.bfloat16)
    grad_in = jnp.einsum(
        "mtd,mtgc->dgc", normed, grad_mixed_low, preferred_element_type=jnp.float32
    )
    grad_normed = input_total(
        jnp.einsum("mtgc,dgc->mtd", grad_mixed_low, w_in, preferred_element_type=jnp.float32)
    )
    _, norm_back_in = jax.vjp(layer_norm, stream, norm_gains[0])
    grad_stream_norm, grad_gain_in = norm_back_in(grad_normed)
    grad_before = grad_mid + grad_stream_norm
    layer_grads = (
        jnp.stack([grad_gain_in, grad_gain_mid]),
        grad_in,
        grad_kernel,
        grad_skip_part,
        grad_out,
        grad_up,
        grad_down,
    )
    return (grad_before, layer_grads, grad_filt)


def local(
    ids,
    live,
    embed,
    norm_gain,
    in_weight,
    short_kernel,
    filter_first,
    filter_second,
    skip_gain,
    out_weight,
    up_weight,
    down_weight,
    cotangent,
):
    seq_count = lax.axis_size("seq")
    seq_rank = lax.axis_index("seq")
    group_idx = lax.axis_index("ch")
    micro_count = ids.shape[0]
    tok_rows = ids.shape[1]
    length = tok_rows * seq_count
    chan_width = in_weight.shape[3]
    own_rows = micro_count * chan_width // seq_count
    layer_count = in_weight.shape[0]
    row_start = seq_rank * own_rows
    row_ids = row_start + jnp.arange(own_rows, dtype=jnp.int32)
    chan_local = row_ids % chan_width
    first_rows = (row_ids < chan_width).astype(jnp.float32)
    select = (jnp.arange(chan_width, dtype=jnp.int32)[:, None] == chan_local[None, :]).astype(
        jnp.float32
    )
    tables = dft_tables(seq_count, tok_rows)
    features = position_features(length)
    ramp_row = jnp.arange(length, dtype=jnp.int32).astype(jnp.float32) / length
    stream, onehot, keep_mask = embed_lookup(ids, live, embed, seq_rank)
    filters = []
    for level_idx in range(layer_count):
        filt_cols, hidden_pre, hidden_act, second_part, decay_part = local_filter(
            filter_first[level_idx],
            filter_second[level_idx],
            features,
            select,
            group_idx,
            chan_local,
        )
        filt_spec = to_spectrum(filt_cols.reshape(own_rows, seq_count, tok_rows), tables)
        skip_part = jnp.dot(skip_gain[level_idx], select, precision=precise)
        penalty_grad = 0.5 * length * ramp_row[None, :] * filt_cols * first_rows[:, None]
        params = (
            norm_gain[level_idx],
            in_weight[level_idx],
            short_kernel[level_idx],
            out_weight[level_idx],
            up_weight[level_idx],
            down_weight[level_idx],
        )
        filters.append(
            (
                params,
                filt_spec,
                skip_part,
                (hidden_pre, hidden_act, second_part, decay_part),
                penalty_grad,
            )
        )
    stored = []
    for level_idx in range(layer_count):
        params, filt_spec, skip_part, _, _ = filters[level_idx]
        layer_input = stream
        stream, kept_vals = layer_forward(stream, params, filt_spec, skip_part, tables)
        stored.append(layer_input)
    block_out = stream * keep_mask[:, :, None]
    grad_stream = cotangent * keep_mask[:, :, None]
    collected = [None] * layer_count
    first_grads = [None] * layer_count
    grad_embed = None
    for level_idx in reversed(range(layer_count)):
        params, filt_spec, skip_part, filter_parts, penalty_grad = filters[level_idx]
        _, kept_vals = layer_forward(stored[level_idx], params, filt_spec, skip_part, tables)
        grad_stream, layer_grads, grad_filt = layer_backward(
            grad_stream, kept_vals, params, filt_spec, skip_part, tables
        )
        grad_first, grad_second_part = filter_mlp_backward(
            grad_filt + penalty_grad, features, filter_parts
        )
        first_grads[level_idx] = grad_first
        grad_second = jnp.dot(grad_second_part, select.T, precision=precise)
        grad_skip = jnp.dot(layer_grads[3], select.T, precision=precise)
        gain_grad, in_grad, kernel_grad, _, out_grad, up_grad, down_grad = layer_grads
        if level_idx == 0:
            embed_part = jnp.einsum("mtv,mtd->vd", onehot, grad_stream, precision=precise)
            summed = lax.psum(
                (
                    gain_grad,
                    in_grad,
                    kernel_grad,
                    grad_second,
                    grad_skip,
                    out_grad,
                    up_grad,
                    down_grad,
                    embed_part,
                ),
                "seq",
            )
            collected[level_idx] = summed[:8]
            grad_embed = summed[8]
        else:
            collected[level_idx] = lax.psum(
                (
                    gain_grad,
                    in_grad,
                    kernel_grad,
                    grad_second,
                    grad_skip,
                    out_grad,
                    up_grad,
                    down_grad,
                ),
                "seq",
            )
    stacked = [
        jnp.stack([collected[level_idx][member] for level_idx in range(layer_count)])
        for member in range(8)
    ]
    filter_grads = lax.psum(jnp.stack(first_grads), ("seq", "ch"))
    return (
        block_out,
        grad_embed,
        stacked[0],
        stacked[1],
        stacked[2],
        filter_grads,
        stacked[3],
        stacked[4],
        stacked[5],
        stacked[6],
        stacked[7],
    )


HALO = 16
ROOT_HALF = math.sqrt(0.5)
GELU_A = math.sqrt(2.0 / math.pi)
GELU_B = 0.044715
BLOCKS = 8
BLOCK = 256
KINDS = 9
VMEM_LIMIT = 20 * 2**20
f32 = jnp.float32
bf16 = jnp.bfloat16


def run(body, outs, scalars, *arrays, scratch=()):
    vmem = pl.BlockSpec(memory_space=pltpu.VMEM)
    smem = pl.BlockSpec(memory_space=pltpu.SMEM)
    single = not isinstance(outs, (list, tuple))
    shapes = [outs] if single else list(outs)
    result = pl.pallas_call(
        body,
        out_shape=shapes,
        in_specs=[smem] + [vmem] * len(arrays),
        out_specs=[vmem] * len(shapes),
        scratch_shapes=list(scratch),
        compiler_params=pltpu.CompilerParams(vmem_limit_bytes=VMEM_LIMIT),
    )(scalars, *arrays)
    return result[0] if single else result


def arr(*shape, kind=f32):
    return jax.ShapeDtypeStruct(shape, kind)


def mm(a, b):
    return jnp.dot(a, b, preferred_element_type=f32)


def mm_nt(a, b):
    return lax.dot_general(a, b, (((1,), (1,)), ((), ())), preferred_element_type=f32)


def mm_tn(a, b):
    return lax.dot_general(a, b, (((0,), (0,)), ((), ())), preferred_element_type=f32)


def split(a):
    high = a.astype(bf16)
    return high, (a - high.astype(f32)).astype(bf16)


def mm3(a, b):
    a_high, a_low = split(a)
    b_high, b_low = split(b)
    return mm(a_high, b_high) + (mm(a_low, b_high) + mm(a_high, b_low))


def unit(rows):
    center = rows - jnp.mean(rows, axis=-1, keepdims=True)
    scale = lax.rsqrt(jnp.mean(center * center, axis=-1, keepdims=True) + epsilon)
    return center * scale, scale


def unit_back(grad, normal, scale):
    inner = jnp.mean(grad * normal, axis=-1, keepdims=True)
    return scale * (grad - jnp.mean(grad, axis=-1, keepdims=True) - normal * inner)


def at(start, size, unit_rows=16):
    return pl.ds(pl.multiple_of(start, unit_rows), size)


def dft_table():
    turns = np.outer(np.arange(BLOCK), np.arange(BLOCK)) % BLOCK
    angle = 2.0 * np.pi * turns / BLOCK
    return np.concatenate([np.cos(angle), np.sin(angle)], axis=1).astype(np.float32)


def twiddle_table():
    angle = 2.0 * np.pi * np.outer(np.arange(1, KINDS), np.arange(BLOCK)) / (2 * BLOCKS * BLOCK)
    pair = np.stack([np.cos(angle), np.sin(angle)], axis=1).astype(np.float32)
    return np.broadcast_to(pair[..., None], (KINDS - 1, 2, BLOCK, 128)).copy()


def feature_table(length):
    places = np.arange(length)
    turns = np.outer(places, np.arange(1, (FEAT - 1) // 2 + 1)) % length
    angle = 2.0 * np.pi * turns / length
    ramp = places[:, None] / length
    return np.concatenate([ramp, np.cos(angle), np.sin(angle)], axis=1).astype(np.float32)


def rate_table():
    return (0.3 * 10.0 ** (np.arange(D) / (D - 1))).astype(np.float32).reshape(2, 1, D // 2)


def four_real(a, b, c, d):
    s, m, t, n = a + c, a - c, b + d, b - d
    hn, ht = ROOT_HALF * n, ROOT_HALF * t
    return (s + t, s - t, (a + hn, -(ht + c)), (m, -n), (a - hn, c - ht))


def turn(k):
    angle = 2.0 * math.pi * k / (2 * BLOCKS)
    return math.cos(angle), math.sin(angle)


def put_pair(stage, kind, row, re, im):
    rows = re.shape[0]
    re, im = re.astype(bf16), im.astype(bf16)
    stage[kind, pl.ds(row, rows), 0:128] = re
    stage[kind, pl.ds(row, rows), 128:256] = im
    stage[kind, pl.ds(row + BLOCK, rows), 0:128] = im
    stage[kind, pl.ds(row + BLOCK, rows), 128:256] = -re


def put_pair_back(stage, kind, row, re, im):
    rows = re.shape[0]
    re, im = re.astype(bf16), im.astype(bf16)
    stage[kind, pl.ds(row, rows), 0:128] = re
    stage[kind, pl.ds(row, rows), 128:256] = im
    stage[kind, pl.ds(row + BLOCK, rows), 0:128] = -im
    stage[kind, pl.ds(row + BLOCK, rows), 128:256] = re


def all_kinds(dft, stage, out):
    def one(kind, carry):
        out[kind] = mm(dft[...], stage[kind])
        return carry

    lax.fori_loop(0, KINDS, one, 0)


def to_freq(load, dft, twiddle, stage, out):
    def chunk(step, carry):
        row = pl.multiple_of(step * 16, 16)
        u = [load(p, row) for p in range(BLOCKS)]
        e0, e4, e1, e2, e3 = four_real(u[0], u[2], u[4], u[6])
        o0, o4, o1, o2, o3 = four_real(u[1], u[3], u[5], u[7])

        def put(kind, re, im):
            c, s = twiddle[kind - 1, 0, pl.ds(row, 16), :], twiddle[kind - 1, 1, pl.ds(row, 16), :]
            put_pair(stage, kind, row, re * c + im * s, im * c - re * s)

        put_pair(stage, 0, row, e0 + o0, jnp.zeros_like(e0))
        last = e0 - o0
        c, s = twiddle[7, 0, pl.ds(row, 16), :], twiddle[7, 1, pl.ds(row, 16), :]
        put_pair(stage, 8, row, last * c, -(last * s))
        put(4, e4, -o4)
        for k, (er, ei), (orr, oi) in ((1, e1, o1), (2, e2, o2), (3, e3, o3)):
            c, s = turn(k)
            wr, wi = orr * c + oi * s, oi * c - orr * s
            put(k, er + wr, ei + wi)
            put(8 - k, er - wr, wi - ei)
        return carry

    lax.fori_loop(0, BLOCK // 16, chunk, 0)
    all_kinds(dft, stage, out)


def from_freq(dft, twiddle, stage, back, store):
    all_kinds(dft, stage, back)

    def chunk(step, carry):
        row = pl.multiple_of(step * 16, 16)

        def get(kind):
            re = back[kind, pl.ds(row, 16), 0:128]
            im = back[kind, pl.ds(row, 16), 128:256]
            c, s = twiddle[kind - 1, 0, pl.ds(row, 16), :], twiddle[kind - 1, 1, pl.ds(row, 16), :]
            return re * c - im * s, re * s + im * c

        first = 0.5 * back[0, pl.ds(row, 16), 0:128]
        last = 0.5 * get(8)[0]
        mid_re, mid_im = get(4)
        even, odd = {}, {}
        for k in (1, 2, 3):
            ar, ai = get(k)
            br, bi = get(8 - k)
            even[k] = (ar + br, ai - bi)
            c, s = turn(k)
            dr, di = ar - br, ai + bi
            odd[k] = (dr * c - di * s, dr * s + di * c)
        for shift, base, extra, part in (
            (0, first + last, mid_re, even),
            (1, first - last, -mid_im, odd),
        ):
            (r1, i1), (r2, i2), (r3, i3) = part[1], part[2], part[3]
            plus, minus = base + extra, base - extra
            diff, both = ROOT_HALF * (r1 - r3), ROOT_HALF * (i1 + i3)
            store(shift, row, plus + (r1 + r2 + r3))
            store(shift + 2, row, minus - i2 + (diff - both))
            store(shift + 4, row, plus - r2 - (i1 - i3))
            store(shift + 6, row, minus + i2 - (diff + both))
        return carry

    lax.fori_loop(0, BLOCK // 16, chunk, 0)


def times(first, second, stage, conj):
    def chunk(step, carry):
        row = pl.multiple_of(step * 16, 16)
        for kind in range(KINDS):
            fr = first[kind, pl.ds(row, 16), 0:128]
            fi = first[kind, pl.ds(row, 16), 128:256]
            ur = second[kind, pl.ds(row, 16), 0:128]
            ui = second[kind, pl.ds(row, 16), 128:256]
            if conj:
                put_pair_back(stage, kind, row, fr * ur + fi * ui, fr * ui - fi * ur)
            else:
                put_pair_back(stage, kind, row, fr * ur - fi * ui, fr * ui + fi * ur)
        return carry

    lax.fori_loop(0, BLOCK // 16, chunk, 0)


SPECTRUM = (KINDS, BLOCK, 256)


def stage_scratch():
    return pltpu.VMEM((KINDS, 2 * BLOCK, 256), bf16)


def spec_scratch():
    return pltpu.VMEM(SPECTRUM, f32)


PACK_SECOND = 48
PACK_SHORT = 176
PACK_SKIP = 194
PACK_ROWS = 200


def pack_kernel(s, embed, gain, in_own, second, short, skip, out):
    normal, _ = unit(embed[...])
    low = (normal * gain[0, 0:1, :]).astype(bf16)
    for g in range(3):
        out[16 * g : 16 * g + 16, :] = mm(low, in_own[0, g])
    for l in range(2):
        out[PACK_SECOND + 64 * l : PACK_SECOND + 64 * l + 64, :] = second[l]
        for k in range(3):
            row = PACK_SHORT + 9 * l + 3 * k
            out[row : row + 3, :] = short[l, k]
    out[PACK_SKIP : PACK_SKIP + 2, :] = skip[...]
    out[PACK_SKIP + 2 : PACK_ROWS, :] = jnp.zeros((PACK_ROWS - PACK_SKIP - 2, 128), f32)


def table_kernel(s, own, peer, embed, mine_out, other_out, conv_table, gate_table):
    first = s[0] == 0
    mine = jnp.where(first, own[...], peer[...])
    other = jnp.where(first, peer[...], own[...])
    mine_out[...] = mine
    other_out[...] = other

    def fill(table, lanes, parts):
        whole = jnp.concatenate(parts, axis=0)
        high, low = split(whole)
        table[0:48, lanes] = high
        table[48:96, lanes] = low
        table[96:128, lanes] = jnp.zeros((32, 128), bf16)

    def gate(pack, g):
        parts = []
        for k in range(3):
            row = PACK_SHORT + 3 * k + g
            parts.append(pack[16 * g : 16 * g + 16] * pack[row : row + 1])
        return parts

    fill(conv_table, slice(0, 128), gate(mine, 1))
    fill(conv_table, slice(128, 256), gate(mine, 2))
    fill(gate_table, slice(0, 128), gate(mine, 0))
    fill(gate_table, slice(128, 256), gate(other, 0))
    zero = jnp.zeros((16, 128), f32)
    fill(gate_table, slice(256, 384), [embed[:, 0:128], zero, zero])
    fill(gate_table, slice(384, 512), [embed[:, 128:256], zero, zero])


def onehot_kernel(s, ids, out, turned, work):
    live = s[2]
    count, width = ids.shape
    work[0:HALO, :] = jnp.zeros((HALO, 128), f32)
    work[HALO + count * width : 2 * HALO + count * width, :] = jnp.zeros((HALO, 128), f32)
    vocab = lax.broadcasted_iota(jnp.int32, (128, width), 0) % 16
    place = lax.broadcasted_iota(jnp.int32, (128, width), 1)
    for i in range(count):
        token = jnp.broadcast_to(ids[i : i + 1, :], (128, width))
        hit = (token == vocab) & (place + i * width < live)
        work[HALO + width * i : HALO + width * (i + 1), :] = jnp.where(hit, 1.0, 0.0).T
    lane = lax.broadcasted_iota(jnp.int32, (width, 128), 1) % 48 // 16
    used = lax.broadcasted_iota(jnp.int32, (width, 128), 1) < 96
    half = count // 2
    for i in range(count):
        row = HALO + width * i
        now = work[row : row + width, :]
        one = work[row - 1 : row - 1 + width, :]
        two = work[row - 2 : row - 2 + width, :]
        picked = jnp.where(lane == 0, now, jnp.where(lane == 1, one, two))
        picked = jnp.where(used, picked, 0.0)
        out[row : row + width, :] = picked.astype(bf16)
        turned[i // half, :, width * (i % half) : width * (i % half + 1)] = picked.T.astype(bf16)
    out[0:HALO, :] = jnp.zeros((HALO, 128), bf16)
    out[HALO + count * width : 2 * HALO + count * width, :] = jnp.zeros((HALO, 128), bf16)


def sine_kernel(s, feats, firsts, sine, cosine, turned):
    both = jnp.concatenate([firsts[0], firsts[1]], axis=1)
    count = feats.shape[0] // 256

    def chunk(i, carry):
        rows = at(256 * i, 256)
        angle = jnp.dot(feats[rows, :], both, precision=precise, preferred_element_type=f32)
        act = jnp.sin(angle)
        sine[rows, :] = act
        cosine[rows, :] = jnp.cos(angle)
        turned[:, at(256 * i, 256, 256)] = act.T.astype(bf16)
        return carry

    lax.fori_loop(0, count, chunk, 0)


def decay_of(rates, start, rows, length):
    place = (lax.broadcasted_iota(jnp.int32, (rows, 1), 0) + start).astype(f32) / length
    return jnp.exp(-place * rates), place


def filter_kernel(s, sine, mine, rates, dft, twiddle, filt0, filt1, freq0, freq1, stage, work):
    length = sine.shape[0]
    rate = rates[s[3]]
    zero = jnp.zeros((64, 128), f32)
    left = jnp.concatenate([mine[PACK_SECOND : PACK_SECOND + 64], zero], axis=0)
    right = jnp.concatenate([zero, mine[PACK_SECOND + 64 : PACK_SECOND + 128]], axis=0)
    weights = jnp.concatenate([left, right], axis=1)

    def chunk(i, carry):
        rows = at(256 * i, 256)
        decay, _ = decay_of(rate, 256 * i, 256, length)
        both = mm3(sine[rows, :], weights)
        filt0[rows, :] = both[:, 0:128] * decay
        filt1[rows, :] = both[:, 128:256] * decay
        return carry

    lax.fori_loop(0, length // 256, chunk, 0)
    for filt, freq in ((filt0, freq0), (filt1, freq1)):
        to_freq(lambda p, row: filt[pl.ds(BLOCK * p + row, 16), :] * (1.0 / length), dft, twiddle, stage, freq)


def causal(load, skip_row, freq_filt, dft, twiddle, spec, stage, work, line):
    to_freq(load, dft, twiddle, stage, spec)
    times(freq_filt, spec, stage, False)

    def store(p, row, value):
        line[pl.ds(HALO + BLOCK * p + row, 16), :] = value + skip_row * load(p, row)

    from_freq(dft, twiddle, stage, work, store)


def hand_out(s, line, keep, send):
    half = (line.shape[0] - 2 * HALO) // 2
    span = half + 2 * HALO
    k = s[0]
    line[0:HALO, :] = jnp.zeros((HALO, 128), f32)
    line[HALO + 2 * half :, :] = jnp.zeros((HALO, 128), f32)
    keep[...] = line[at(half * k, span), :]
    send[...] = line[at(half * (1 - k), span), :]


def conv_first_kernel(s, onehot, conv_table, mine, freq_filt, dft, twiddle, keep, send, spec, product, stage, work, line):
    def chunk(i, carry):
        rows = at(256 * i, 256)
        pair = mm(onehot[at(256 * i + HALO, 256), :], conv_table[...])
        product[rows, :] = pair[:, 0:128] * pair[:, 128:256]
        return carry

    lax.fori_loop(0, product.shape[0] // 256, chunk, 0)
    skip_row = mine[PACK_SKIP : PACK_SKIP + 1, :]
    causal(lambda p, row: product[pl.ds(BLOCK * p + row, 16), :], skip_row, freq_filt, dft, twiddle, spec, stage, work, line)
    hand_out(s, line, keep, send)


def join_rows(s, whole, kept, received):
    half = kept.shape[0]
    whole[at(half * s[0], half), :] = kept[...]
    whole[at(half * (1 - s[0]), half), :] = received[...]


def conv_second_kernel(s, kept, received, mine, freq_filt, dft, twiddle, keep, send, spec, product, stage, work, line):
    join_rows(s, product, kept, received)
    skip_row = mine[PACK_SKIP + 1 : PACK_SKIP + 2, :]
    causal(lambda p, row: product[pl.ds(BLOCK * p + row, 16), :], skip_row, freq_filt, dft, twiddle, spec, stage, work, line)
    hand_out(s, line, keep, send)


def gelu_parts(p):
    squared = p * p
    th = jnp.tanh(GELU_A * p * (1.0 + GELU_B * squared))
    half = 0.5 * (1.0 + th)
    slope = half + 0.5 * p * (1.0 - th * th) * (GELU_A + (3.0 * GELU_A * GELU_B) * squared)
    return p * half, slope


def gelu_only(p):
    return 0.5 * p * (1.0 + jnp.tanh(GELU_A * p * (1.0 + GELU_B * (p * p))))


CHUNK = 352


def forward_first_kernel(
    s, onehot, gate_table, conv_mine, conv_other, gain, w_out, w_up, w_down, w_in, mine, other,
    keep, send, mid_out, stream_out, gates, mixed,
):
    span = mid_out.shape[0]
    half = span - 2 * HALO
    k = s[0]
    taps = [
        jnp.concatenate([pack[PACK_SHORT + 9 + 3 * t + g : PACK_SHORT + 10 + 3 * t + g, :] for g in range(3) for pack in (mine, other)], axis=1)
        for t in range(3)
    ]

    def chunk(i, carry):
        rows = at(CHUNK * i, CHUNK)
        looked = mm(onehot[at(half * k + CHUNK * i, CHUNK), :], gate_table[...])
        conv = jnp.concatenate([conv_mine[rows, :], conv_other[rows, :]], axis=1)
        gated = (conv * looked[:, 0:256]).astype(bf16)
        mid = looked[:, 256:512] + mm(gated, w_out[...])
        mid_out[rows, :] = mid
        normal, _ = unit(mid)
        low = (normal * gain[0, 1:2, :]).astype(bf16)
        hidden = gelu_only(mm(low, w_up[...])).astype(bf16)
        stream = mid + mm(hidden, w_down[...])
        stream_out[rows, :] = stream
        normal, _ = unit(stream)
        low = (normal * gain[1, 0:1, :]).astype(bf16)
        mixed[rows, :] = mm(low, w_in[...])
        return carry

    lax.fori_loop(0, span // CHUNK, chunk, 0)
    gates[0:HALO, :] = jnp.zeros((HALO, 768), f32)
    step = 80
    for start in range(HALO, span, step):
        stop = start + step
        gates[start:stop, :] = (
            taps[0] * mixed[start:stop, :]
            + taps[1] * mixed[start - 1 : stop - 1, :]
            + taps[2] * mixed[start - 2 : stop - 2, :]
        )
    own = slice(HALO, HALO + half)
    keep[...] = gates[own, 256:384] * gates[own, 512:640]
    send[...] = gates[own, 384:512] * gates[own, 640:768]


def turn_back_kernel(
    s, conv_mine, conv_other, gates, stream, cot, gain, w_out, w_up, w_down,
    keep, send, grad_x0, grad_mid, block_out, hidden_out, low_out, normed_out, pre_out, gated_out, mid_low_out, gain_out,
    cot_rows, conv_grads,
):
    span = stream.shape[0]
    half = span - 2 * HALO
    k = s[0]
    live = s[2]
    cot_rows[0:HALO, :] = jnp.zeros((HALO, 256), f32)
    cot_rows[HALO : HALO + half, :] = cot[at(half * k, half), :]
    cot_rows[HALO + half :, :] = jnp.where(k == 0, cot[half : half + HALO, :], 0.0)
    gain_out[...] = jnp.zeros_like(gain_out)

    def chunk(i, carry):
        rows = at(CHUNK * i, CHUNK)
        local_row = lax.broadcasted_iota(jnp.int32, (CHUNK, 1), 0) + CHUNK * i
        keep_mask = (local_row + (half * k - HALO) < live).astype(f32)
        own_mask = ((local_row >= HALO) & (local_row < HALO + half)).astype(f32)
        x0 = gates[rows, 0:256]
        conv = jnp.concatenate([conv_mine[rows, :], conv_other[rows, :]], axis=1)
        gated = (conv * x0).astype(bf16)
        gated_out[rows, :] = gated
        mid = stream[rows, :] + mm(gated, w_out[...])
        normal, scale = unit(mid)
        gain_row = gain[1, 1:2, :]
        low = (normal * gain_row).astype(bf16)
        normed_out[rows, :] = low
        act, slope = gelu_parts(mm(low, w_up[...]))
        hidden = act.astype(bf16)
        hidden_out[rows, :] = hidden
        block_out[rows, :] = (mid + mm(hidden, w_down[...])) * keep_mask
        grad = cot_rows[rows, :] * keep_mask
        grad_low = grad.astype(bf16)
        low_out[rows, :] = grad_low
        grad_pre = (slope * mm_nt(grad_low, w_down[...])).astype(bf16)
        pre_out[rows, :] = grad_pre
        grad_normed = mm_nt(grad_pre, w_up[...])
        gain_out[0:1, :] += jnp.sum(grad_normed * normal * own_mask, axis=0, keepdims=True)
        mid_grad = grad + unit_back(grad_normed * gain_row, normal, scale)
        grad_mid[rows, :] = mid_grad
        mid_low = mid_grad.astype(bf16)
        mid_low_out[rows, :] = mid_low
        grad_gated = mm_nt(mid_low, w_out[...])
        conv_grads[rows, :] = grad_gated * x0
        grad_x0[rows, :] = grad_gated * conv
        return carry

    lax.fori_loop(0, span // CHUNK, chunk, 0)
    own = slice(HALO, HALO + half)
    keep[...] = conv_grads[own, 0:128]
    send[...] = conv_grads[own, 128:256]


def conv_back_kernel(s, kept, received, mine, freq_filt, dft, twiddle, keep, send, spec, grads, stage, work, line):
    join_rows(s, grads, kept, received)
    skip_row = mine[PACK_SKIP + 1 : PACK_SKIP + 2, :]
    load = lambda p, row: grads[pl.ds(BLOCK * p + row, 16), :]
    to_freq(load, dft, twiddle, stage, spec)
    times(freq_filt, spec, stage, True)

    def store(p, row, value):
        line[pl.ds(HALO + BLOCK * p + row, 16), :] = value + skip_row * load(p, row)

    from_freq(dft, twiddle, stage, work, store)
    hand_out(s, line, keep, send)


def conv_back_first_kernel(
    s, kept, received, mine, freq_filt, dft, twiddle, onehot, turned, conv_table, spec, grads, by_token, stage, work, line
):
    length = grads.shape[0]
    join_rows(s, grads, kept, received)
    skip_row = mine[PACK_SKIP : PACK_SKIP + 1, :]
    load = lambda p, row: grads[pl.ds(BLOCK * p + row, 16), :]
    to_freq(load, dft, twiddle, stage, spec)
    times(freq_filt, spec, stage, True)

    def store(p, row, value):
        line[pl.ds(BLOCK * p + row, 16), :] = value + skip_row * load(p, row)

    from_freq(dft, twiddle, stage, work, store)
    by_token[...] = jnp.zeros_like(by_token)
    width = turned.shape[2]
    for i in range(length // width):
        rows = slice(width * i, width * (i + 1))
        pair = mm(onehot[HALO + width * i : HALO + width * (i + 1), :], conv_table[...])
        back = line[rows, :]
        gate_grads = jnp.concatenate([back * pair[:, 128:256], back * pair[:, 0:128]], axis=1).astype(bf16)
        by_token[...] += mm(turned[i], gate_grads)[0:48, :]


def filter_back_kernel(
    level, s, spec_grad, spec_in, grads, product, filt, cosine, sine_turned, mine, rates, feats_turned, dft, twiddle,
    second_out, first_out, skip_out, stage, work, line, inner,
):
    length = filt.shape[0]
    times(spec_in, spec_grad, stage, True)

    def store(p, row, value):
        line[pl.ds(BLOCK * p + row, 16), :] = value

    from_freq(dft, twiddle, stage, work, store)
    rate = rates[s[3]]
    second = mine[PACK_SECOND + 64 * level : PACK_SECOND + 64 * level + 64, :].astype(bf16)
    weight = jnp.where(s[1] == 0, 0.5 * length, 0.0)
    skip_out[...] = jnp.zeros_like(skip_out)
    second_out[...] = jnp.zeros_like(second_out)
    first_out[...] = jnp.zeros_like(first_out)
    for i in range(length // 512):
        rows = slice(512 * i, 512 * (i + 1))
        decay, place = decay_of(rate, 512 * i, 512, length)
        shaped = ((line[rows, :] * (1.0 / length) + (weight * place) * filt[rows, :]) * decay).astype(bf16)
        skip_out[...] += jnp.sum((grads[rows, :] * product[rows, :]).reshape(64, 8, 128), axis=0)
        second_out[...] += mm(sine_turned[64 * level : 64 * level + 64, rows], shaped)
        inner = (mm_nt(shaped, second) * cosine[rows, 64 * level : 64 * level + 64]).astype(bf16)
        first_out[...] += mm(feats_turned[:, rows], inner)


def back_gates_kernel(
    s, prod_mine, prod_other, grad_x0, gates, mixed, grad_mid, stream, gain, mine, other, w_in,
    grad_stream, normed_out, mixed_low, short_out, gain_out, line,
):
    span = stream.shape[0]
    half = span - 2 * HALO
    taps = [
        jnp.concatenate([pack[PACK_SHORT + 9 + 3 * t + g : PACK_SHORT + 10 + 3 * t + g, :] for g in range(3) for pack in (mine, other)], axis=1)
        for t in range(3)
    ]
    step = 128
    for start in list(range(HALO, HALO + half, step)) + [HALO + half]:
        stop = start + (step if start < HALO + half else HALO)
        product = jnp.concatenate([prod_mine[start:stop, :], prod_other[start:stop, :]], axis=1)
        line[start:stop, 0:256] = grad_x0[start:stop, :]
        line[start:stop, 256:512] = product * gates[start:stop, 512:768]
        line[start:stop, 512:768] = product * gates[start:stop, 256:512]
    short_out[...] = jnp.zeros_like(short_out)
    gain_out[...] = jnp.zeros_like(gain_out)
    step = 64
    for start in range(HALO, HALO + half, step):
        stop = start + step
        values = mixed[start:stop, :]
        total = None
        for t in range(3):
            shifted = line[start + t : stop + t, :]
            part = taps[t] * shifted
            total = part if total is None else total + part
            short_out[t] += jnp.sum((shifted * values).reshape(step // 8, 8, 768), axis=0)
        mixed_low[start - HALO : stop - HALO, :] = total.astype(bf16)

    def chunk(i, carry):
        rows = at(256 * i, 256)
        wide = at(256 * i + HALO, 256)
        normal, scale = unit(stream[wide, :])
        gain_row = gain[1, 0:1, :]
        normed_out[rows, :] = (normal * gain_row).astype(bf16)
        grad_normed = mm_nt(mixed_low[rows, :], w_in[...])
        gain_out[0:1, :] += jnp.sum(grad_normed * normal, axis=0, keepdims=True)
        grad_stream[rows, :] = grad_mid[wide, :] + unit_back(grad_normed * gain_row, normal, scale)
        return carry

    lax.fori_loop(0, half // 256, chunk, 0)


def back_first_kernel(
    s, grad_stream, mid, onehot, turned, gate_table, conv_mine, conv_other, gain, w_out, w_up, w_down,
    keep, send, hidden_out, low_out, normed_out, pre_out, gated_out, mid_low_out, by_token, gain_out,
):
    half = grad_stream.shape[0]
    k = s[0]
    by_token[...] = jnp.zeros_like(by_token)
    gain_out[...] = jnp.zeros_like(gain_out)

    def chunk(i, carry):
        rows = at(256 * i, 256)
        wide = at(256 * i + HALO, 256)
        hot = onehot[at(half * k + 256 * i + HALO, 256), :]
        x0 = mm(hot, gate_table[:, 0:256])
        conv = jnp.concatenate([conv_mine[wide, :], conv_other[wide, :]], axis=1)
        gated_out[rows, :] = (conv * x0).astype(bf16)
        normal, scale = unit(mid[wide, :])
        gain_row = gain[0, 1:2, :]
        low = (normal * gain_row).astype(bf16)
        normed_out[rows, :] = low
        act, slope = gelu_parts(mm(low, w_up[...]))
        hidden_out[rows, :] = act.astype(bf16)
        grad = grad_stream[rows, :]
        grad_low = grad.astype(bf16)
        low_out[rows, :] = grad_low
        grad_pre = (slope * mm_nt(grad_low, w_down[...])).astype(bf16)
        pre_out[rows, :] = grad_pre
        grad_normed = mm_nt(grad_pre, w_up[...])
        gain_out[0:1, :] += jnp.sum(grad_normed * normal, axis=0, keepdims=True)
        mid_grad = grad + unit_back(grad_normed * gain_row, normal, scale)
        mid_low = mid_grad.astype(bf16)
        mid_low_out[rows, :] = mid_low
        grad_gated = mm_nt(mid_low, w_out[...])
        conv_grad = grad_gated * x0
        keep[rows, :] = conv_grad[:, 0:128]
        send[rows, :] = conv_grad[:, 128:256]
        flips = turned[k, :, at(256 * i, 256, 256)]
        rest = mid_grad - mid_low.astype(f32)
        gate_grads = jnp.concatenate([(grad_gated * conv).astype(bf16), mid_low, rest.astype(bf16)], axis=1)
        by_token[...] += mm(flips, gate_grads)[0:48, :]
        return carry

    lax.fori_loop(0, half // 256, chunk, 0)


R_OUT, R_UP, R_DOWN, R_IN = 128, 512, 512, 384


def send_weights_kernel(level, with_in, s, w_out, w_up, w_down, w_in, out):
    k = s[0]
    first = k == 0
    pick = lambda a, b: jnp.where(first, a.astype(f32), b.astype(f32))
    out[0:128, :] = pick(w_out[level, :, 0:128], w_out[level, :, 128:256])
    for j in range(2):
        lanes = slice(128 * j, 128 * j + 128)
        out[128 + 256 * j : 384 + 256 * j, :] = pick(
            w_up[level, :, 128 * j : 128 * j + 128], w_up[level, :, 256 + 128 * j : 384 + 128 * j]
        )
        out[640 + 256 * j : 896 + 256 * j, :] = pick(w_down[level, 0:256, lanes], w_down[level, 256:512, lanes])
    if with_in:
        for g in range(3):
            out[1152 + 128 * g : 1280 + 128 * g, :] = pick(w_in[level, g, 0:128, :], w_in[level, g, 128:256, :])


def join_weights_kernel(level, with_in, s, w_out, w_up, w_down, w_in, first_part, second_part, out_full, up_full, down_full, *in_full):
    k = s[0]
    first = k == 0
    low = lambda ref, a, b: ref[a:b, :].astype(bf16)
    pick = lambda a, b: jnp.where(first, a, b)
    mine_out = w_out[level]
    a, b = first_part[0:128, :], second_part[0:128, :]
    peer_out = jnp.concatenate([pick(a, b), pick(b, a)], axis=1).astype(bf16)
    out_full[0:128, :] = pick(mine_out.astype(f32), peer_out.astype(f32)).astype(bf16)
    out_full[128:256, :] = pick(peer_out.astype(f32), mine_out.astype(f32)).astype(bf16)
    up_a, up_b = w_up[level, :, 0:256].astype(f32), w_up[level, :, 256:512].astype(f32)
    up_full[:, 0:256] = pick(up_a, up_b).astype(bf16)
    up_full[:, 256:512] = pick(up_b, up_a).astype(bf16)
    down_a, down_b = w_down[level, 0:256, :].astype(f32), w_down[level, 256:512, :].astype(f32)
    down_full[0:256, :] = pick(down_a, down_b).astype(bf16)
    down_full[256:512, :] = pick(down_b, down_a).astype(bf16)
    for n, part in enumerate((first_part, second_part)):
        for j in range(2):
            up_full[:, 512 + 256 * n + 128 * j : 640 + 256 * n + 128 * j] = low(part, 128 + 256 * j, 384 + 256 * j)
            down_full[512 + 256 * n : 768 + 256 * n, 128 * j : 128 * j + 128] = low(part, 640 + 256 * j, 896 + 256 * j)
    if with_in:
        (full,) = in_full
        for g in range(3):
            own = w_in[level, g].astype(f32)
            a, b = first_part[1152 + 128 * g : 1280 + 128 * g, :], second_part[1152 + 128 * g : 1280 + 128 * g, :]
            peer = jnp.concatenate([pick(a, b), pick(b, a)], axis=0)
            full[:, 256 * g : 256 * g + 128] = pick(own, peer).astype(bf16)
            full[:, 256 * g + 128 : 256 * g + 256] = pick(peer, own).astype(bf16)


def put_wide_grads(s, keep, send, row, gated, mid_low, normed, grad_pre, hidden, grad_low):
    k = s[0]
    first = k == 0
    out = mm_tn(gated, mid_low)
    for m in range(2):
        a, b = out[128 * m : 128 * m + 128, 0:128], out[128 * m : 128 * m + 128, 128:256]
        half = m + k - 2 * m * k
        keep[half, row : row + 128, :] = jnp.where(first, a, b)
        send[half, row : row + 128, :] = jnp.where(first, b, a)
    for j in range(4):
        target = (keep, send)[j % 2]
        up = mm_tn(normed, grad_pre[:, 256 * j : 256 * j + 256])
        down = mm_tn(hidden[:, 256 * j : 256 * j + 256], grad_low)
        for n in range(2):
            lanes = slice(128 * n, 128 * n + 128)
            target[j // 2, row + 128 + 256 * n : row + 384 + 256 * n, :] = up[:, lanes]
            target[j // 2, row + 640 + 256 * n : row + 896 + 256 * n, :] = down[:, lanes]


def wide_grads_kernel(pad, s, gated, mid_low, normed, grad_pre, hidden, grad_low, keep, send):
    stop = gated.shape[0] - pad
    own = lambda ref: ref[pad:stop, :]
    put_wide_grads(s, keep, send, 0, own(gated), own(mid_low), own(normed), own(grad_pre), own(hidden), own(grad_low))


def wide_and_in_grads_kernel(s, gated, mid_low, normed, grad_pre, hidden, grad_low, normed_in, mixed_low, keep, send):
    k = s[0]
    first = k == 0
    put_wide_grads(
        s, keep, send, 0, gated[...], mid_low[...], normed[...], grad_pre[...], hidden[...], grad_low[...]
    )
    for g in range(3):
        both = mm_tn(normed_in[...], mixed_low[:, 256 * g : 256 * g + 256])
        for m in range(2):
            block = both[:, 128 * m : 128 * m + 128]
            half = m + k - 2 * m * k
            row = 1152 + 128 * g
            keep[half, row : row + 128, :] = jnp.where(first, block[0:128], block[128:256])
            send[half, row : row + 128, :] = jnp.where(first, block[128:256], block[0:128])


def add_kernel(s, kept, received, own_out, peer_out):
    own_out[...] = kept[0] + received[0]
    peer_out[...] = kept[1] + received[1]


def add_one_kernel(s, kept, received, out):
    out[...] = kept[...] + received[...]


def spread_grads_kernel(with_in, s, kept, received, out, up, down, *w_in):
    first = s[0] == 0
    a, b = kept, received
    pick = lambda x, y: jnp.where(first, x, y)

    def both(row, rows):
        x, y = a[row : row + rows, :], b[row : row + rows, :]
        return pick(x, y), pick(y, x)

    x, y = both(0, 128)
    out[:, 0:128] = x
    out[:, 128:256] = y
    for j in range(2):
        lanes = slice(128 * j, 128 * j + 128)
        x, y = both(128 + 256 * j, 256)
        up[:, 128 * j : 128 * j + 128] = x
        up[:, 256 + 128 * j : 384 + 128 * j] = y
        x, y = both(640 + 256 * j, 256)
        down[0:256, lanes] = x
        down[256:512, lanes] = y
    if with_in:
        for g in range(3):
            x, y = both(1152 + 128 * g, 128)
            w_in[0][g, 0:128, :] = x
            w_in[0][g, 128:256, :] = y


F_GAIN1, F_GAIN0, F_EMBED, F_FIRST, F_SKIPPAD, F_SHORT, F_TOKEN = 0, 8, 16, 32, 72, 80, 112
F_ROWS = 160
C_SECOND1, C_SECOND0, C_SKIP, C_TOKEN = 0, 64, 128, 136
C_ROWS = 232


def small_kernel(
    s, gain_mid1, gain_in1, gain_mid0, by_token0, by_token12, first1, first0, short1, second1, second0, skip1, skip0, flat, mine
):
    k = s[0]
    flat[...] = jnp.zeros_like(flat)
    flat[F_GAIN1 : F_GAIN1 + 8, :] = gain_mid1[...]
    flat[F_GAIN0 : F_GAIN0 + 8, :] = gain_mid0[...]
    flat[F_GAIN1 + 1 : F_GAIN1 + 2, :] = gain_in1[0:1, :]
    flat[F_EMBED : F_EMBED + 16, :] = by_token0[0:16, 256:512] + by_token0[0:16, 512:768]
    flat[F_FIRST : F_FIRST + 40, 0:64] = first0[...]
    flat[F_FIRST : F_FIRST + 40, 128:192] = first1[...]
    swap = lambda v: jnp.where(k == 0, v, jnp.concatenate([v[:, 128:256], v[:, 0:128]], axis=1))
    for t in range(3):
        total = jnp.sum(short1[t], axis=0, keepdims=True)
        for g in range(3):
            flat[F_SHORT + 3 * t + g : F_SHORT + 3 * t + g + 1, :] = swap(total[:, 256 * g : 256 * g + 256])
    flat[F_TOKEN : F_TOKEN + 48, :] = swap(by_token0[:, 0:256])
    mine[C_SECOND1 : C_SECOND1 + 64, :] = second1[...]
    mine[C_SECOND0 : C_SECOND0 + 64, :] = second0[...]
    mine[C_SKIP : C_SKIP + 8, :] = jnp.zeros((8, 128), f32)
    mine[C_SKIP : C_SKIP + 1, :] = jnp.sum(skip0[...], axis=0, keepdims=True)
    mine[C_SKIP + 1 : C_SKIP + 2, :] = jnp.sum(skip1[...], axis=0, keepdims=True)
    mine[C_TOKEN : C_TOKEN + 48, :] = by_token12[:, 0:128]
    mine[C_TOKEN + 48 : C_TOKEN + 96, :] = by_token12[:, 128:256]


def chip_kernel(s, flat, flat_in, mine, mine_in, out):
    first = s[0] == 0
    total = flat[...] + flat_in[...]
    out[0:F_ROWS, :] = total
    out[F_ROWS : F_ROWS + C_ROWS, 0:128] = jnp.where(first, mine[...], mine_in[...])
    out[F_ROWS : F_ROWS + C_ROWS, 128:256] = jnp.where(first, mine_in[...], mine[...])


def last_kernel(
    s, here, there, embed, gain, own, peer, w_own, w_first, w_second,
    embed_out, gain_out, in_out, short_out, first_out, second_out, skip_out,
):
    first = s[0] == 0
    pick = lambda x, y: jnp.where(first, x, y)

    def plain(row, rows):
        return here[row : row + rows, :] + there[row : row + rows, :]

    def halves(row, rows):
        left = here[row : row + rows, 0:128] + there[row : row + rows, 128:256]
        right = here[row : row + rows, 128:256] + there[row : row + rows, 0:128]
        return left, right

    gains1 = plain(F_GAIN1, 8)
    gains0 = plain(F_GAIN0, 8)
    gain_out[1, 0:1, :] = gains1[1:2, :]
    gain_out[1, 1:2, :] = gains1[0:1, :]
    gain_out[0, 1:2, :] = gains0[0:1, :]
    firsts = plain(F_FIRST, 40)
    first_out[0] = firsts[0:33, 0:64]
    first_out[1] = firsts[0:33, 128:192]
    short = halves(F_SHORT, 16)[0]
    for t in range(3):
        short_out[1, t] = short[3 * t : 3 * t + 3, :]
    mine_rows = lambda row, rows: halves(F_ROWS + row, rows)
    second_out[1] = mine_rows(C_SECOND1, 64)[0]
    second_out[0] = mine_rows(C_SECOND0, 64)[0]
    skip_out[...] = mine_rows(C_SKIP, 8)[0][0:2]
    tokens = [halves(F_TOKEN, 48), mine_rows(C_TOKEN, 48), mine_rows(C_TOKEN + 48, 48)]
    normal, scale = unit(embed[...])
    gain_row = gain[0, 0:1, :]
    low = (normal * gain_row).astype(bf16)
    grad_normed = jnp.zeros((16, 256), f32)
    for g in range(3):
        for h, pack in ((0, own), (1, peer)):
            grads = tokens[g][h]
            table = pack[16 * g : 16 * g + 16, :]
            summed = jnp.zeros((16, 128), f32)
            for t in range(3):
                row = PACK_SHORT + 3 * t + g
                part = grads[16 * t : 16 * t + 16, :]
                summed += pack[row : row + 1, :] * part
                if h == 0:
                    short_out[0, t, g : g + 1, :] = jnp.sum(table * part, axis=0, keepdims=True)
            if h == 0:
                in_out[g] = lax.dot_general(
                    low.astype(f32), summed, (((0,), (0,)), ((), ())), precision=precise, preferred_element_type=f32
                )
                weight = w_own[0, g].astype(f32)
            else:
                rows = slice(128 * g, 128 * g + 128)
                a, b = w_first[rows, :], w_second[rows, :]
                weight = jnp.concatenate([pick(a, b), pick(b, a)], axis=0)
            grad_normed += lax.dot_general(
                summed, weight, (((1,), (1,)), ((), ())), precision=precise, preferred_element_type=f32
            )
    gain_out[0, 0:1, :] = jnp.sum(grad_normed * normal, axis=0, keepdims=True)
    embed_out[...] = plain(F_EMBED, 16) + unit_back(grad_normed * gain_row, normal, scale)


def send_in_kernel(s, w_in, out):
    first = s[0] == 0
    for g in range(3):
        a, b = w_in[0, g, 0:128, :].astype(f32), w_in[0, g, 128:256, :].astype(f32)
        out[128 * g : 128 * g + 128, :] = jnp.where(first, a, b)


def block_send_kernel(s, block_out, mine, other):
    spot = s[4]
    mine[...] = block_out[at(HALO + 128 * spot, 128), :]
    near = spot + 1 - 2 * s[0]
    other[...] = block_out[at(HALO + 128 * near, 128), :]


def block_pick_kernel(s, mine, received, out):
    out[...] = jnp.where(s[5] == 1, mine[...], received[...])


def block_join_kernel(s, here, there, out):
    first = s[1] == 0
    out[0] = jnp.where(first, here[...], there[...])
    out[1] = jnp.where(first, there[...], here[...])


def chip_local(
    ids, live, embed, norm_gain, in_weight, short_kernel, filter_first, filter_second, skip_gain,
    out_weight, up_weight, down_weight, cotangent,
):
    count = lax.axis_size("seq")
    rank = lax.axis_index("seq")
    group = lax.axis_index("ch")
    width = ids.shape[1]
    length = width * count
    half = length // 2
    span = half + 2 * HALO
    core = rank % 2
    swaps = [(i, i ^ 1) for i in range(count)]
    across = lambda v: lax.ppermute(v, "ch", [(0, 1), (1, 0)])
    beside = lambda v: lax.ppermute(v, "seq", swaps)
    half_ranks = count // 2
    holder = (rank // half_ranks == core).astype(jnp.int32)
    s = jnp.stack([core, group, live[group], group ^ core, rank % half_ranks, holder]).astype(jnp.int32)
    dft = jnp.asarray(dft_table()).astype(bf16)
    twiddle = jnp.asarray(twiddle_table())
    feats = jnp.asarray(feature_table(length))
    feats_turned = jnp.asarray(np.pad(feature_table(length).T, ((0, 40 - FEAT), (0, 0)))).astype(bf16)
    rates = jnp.asarray(rate_table())

    in_own = jnp.swapaxes(in_weight, 1, 2)
    pack = run(pack_kernel, arr(PACK_ROWS, 128), s, embed, norm_gain, in_own, filter_second, short_kernel, skip_gain)
    pack_in = across(pack)
    own_ids = lax.dynamic_index_in_dim(ids, group, 0, True)
    all_ids = lax.all_to_all(jnp.broadcast_to(own_ids, (count, width)), "seq", split_axis=0, concat_axis=0, tiled=True)
    cot = lax.all_gather(lax.dynamic_index_in_dim(cotangent, group, 0, False), "seq", axis=0, tiled=True)

    sine, cosine, sine_turned = run(
        sine_kernel, [arr(length, 128), arr(length, 128), arr(128, length, kind=bf16)], s, feats, filter_first
    )
    weights = []
    for level, with_in in ((0, False), (1, True)):
        rows = 1536 if with_in else 1152
        part = run(
            functools.partial(send_weights_kernel, level, with_in), arr(rows, 128), s, out_weight, up_weight, down_weight, in_own
        )
        part_in = across(part)
        other_in = beside(part_in)
        shapes = [arr(256, 256, kind=bf16), arr(256, 1024, kind=bf16), arr(1024, 256, kind=bf16)]
        if with_in:
            shapes.append(arr(256, 768, kind=bf16))
        weights.append(
            run(
                functools.partial(join_weights_kernel, level, with_in), shapes, s, out_weight, up_weight, down_weight, in_own,
                part_in, other_in,
            )
        )
    (w_out0, w_up0, w_down0), (w_out1, w_up1, w_down1, w_in1) = weights
    first_in = across(run(send_in_kernel, arr(384, 128), s, in_own))
    first_in_other = beside(first_in)

    mine, other, conv_table, gate_table = run(
        table_kernel,
        [arr(PACK_ROWS, 128), arr(PACK_ROWS, 128), arr(128, 256, kind=bf16), arr(128, 512, kind=bf16)],
        s, pack, pack_in, embed,
    )
    filt0, filt1, freq0, freq1 = run(
        filter_kernel, [arr(length, 128), arr(length, 128), arr(*SPECTRUM), arr(*SPECTRUM)], s, sine, mine, rates, dft, twiddle,
        scratch=[stage_scratch(), spec_scratch()],
    )
    onehot, turned = run(
        onehot_kernel, [arr(length + 2 * HALO, 128, kind=bf16), arr(2, 128, half, kind=bf16)], s, all_ids,
        scratch=[pltpu.VMEM((length + 2 * HALO, 128), f32)],
    )
    line = pltpu.VMEM((length + 2 * HALO, 128), f32)
    conv_scratch = [stage_scratch(), spec_scratch(), line]

    conv_mine0, sent, spec0, product0 = run(
        conv_first_kernel, [arr(span, 128), arr(span, 128), arr(*SPECTRUM), arr(length, 128)],
        s, onehot, conv_table, mine, freq0, dft, twiddle, scratch=conv_scratch,
    )
    conv_other0 = beside(sent)
    kept, sent, mid0, stream1, gates1, mixed1 = run(
        forward_first_kernel,
        [arr(half, 128), arr(half, 128), arr(span, 256), arr(span, 256), arr(span, 768), arr(span, 768)],
        s, onehot, gate_table, conv_mine0, conv_other0, norm_gain, w_out0, w_up0, w_down0, w_in1, mine, other,
    )
    received = beside(sent)
    conv_mine1, sent, spec1, product1 = run(
        conv_second_kernel, [arr(span, 128), arr(span, 128), arr(*SPECTRUM), arr(length, 128)],
        s, kept, received, mine, freq1, dft, twiddle, scratch=conv_scratch,
    )
    conv_other1 = beside(sent)
    low = lambda *shape: arr(*shape, kind=bf16)
    (kept, sent, grad_x0, grad_mid1, block, hidden, grad_low, normed, grad_pre, gated, mid_low, gain_mid1) = run(
        turn_back_kernel,
        [
            arr(half, 128), arr(half, 128), arr(span, 256), arr(span, 256), arr(span, 256), low(span, 1024), low(span, 256),
            low(span, 256), low(span, 1024), low(span, 256), low(span, 256), arr(8, 256),
        ],
        s, conv_mine1, conv_other1, gates1, stream1, cot, norm_gain, w_out1, w_up1, w_down1,
        scratch=[pltpu.VMEM((span, 256), f32), pltpu.VMEM((span, 256), f32)],
    )
    received = beside(sent)
    grads_keep, grads_send = run(
        functools.partial(wide_grads_kernel, HALO), [arr(2, 1152, 128), arr(2, 1152, 128)],
        s, gated, mid_low, normed, grad_pre, hidden, grad_low,
    )
    block_mine, block_other = run(block_send_kernel, [arr(width, 256), arr(width, 256)], s, block)
    block_here = run(block_pick_kernel, arr(width, 256), s, block_mine, beside(block_other))
    block_out = run(block_join_kernel, arr(2, width, 256), s, block_here, across(block_here))

    prod_mine, sent, spec_grad1, grads1 = run(
        conv_back_kernel, [arr(span, 128), arr(span, 128), arr(*SPECTRUM), arr(length, 128)],
        s, kept, received, mine, freq1, dft, twiddle, scratch=conv_scratch,
    )
    prod_other = beside(sent)
    filter_shapes = [arr(64, 128), arr(40, 64), arr(8, 128)]
    filter_scratch = [stage_scratch(), spec_scratch(), pltpu.VMEM((length, 128), f32), pltpu.VMEM((8, 128), f32)]
    second1, first1, skip1 = run(
        functools.partial(filter_back_kernel, 1), filter_shapes, s, spec_grad1, spec1, grads1, product1, filt1, cosine,
        sine_turned, mine, rates, feats_turned, dft, twiddle, scratch=filter_scratch,
    )

    def reduce_wide(keep, send, with_in):
        rows = keep.shape[1]
        own, peer = run(add_kernel, [arr(rows, 128), arr(rows, 128)], s, keep, beside(send))
        total = run(add_one_kernel, arr(rows, 128), s, own, across(peer))
        shapes = [arr(128, 256), arr(256, 512), arr(512, 256)] + ([arr(3, 256, 128)] if with_in else [])
        return run(functools.partial(spread_grads_kernel, with_in), shapes, s, total, beside(total))

    grad_out1, grad_up1, grad_down1 = reduce_wide(grads_keep, grads_send, False)
    grad_stream1, normed_in, mixed_low, short1, gain_in1 = run(
        back_gates_kernel,
        [arr(half, 256), low(half, 256), low(half, 768), arr(3, 8, 768), arr(8, 256)],
        s, prod_mine, prod_other, grad_x0, gates1, mixed1, grad_mid1, stream1, norm_gain, mine, other, w_in1,
        scratch=[pltpu.VMEM((span, 768), f32)],
    )
    (kept, sent, hidden, grad_low, normed, grad_pre, gated, mid_low, by_token0, gain_mid0) = run(
        back_first_kernel,
        [
            arr(half, 128), arr(half, 128), low(half, 1024), low(half, 256), low(half, 256), low(half, 1024), low(half, 256),
            low(half, 256), arr(48, 768), arr(8, 256),
        ],
        s, grad_stream1, mid0, onehot, turned, gate_table, conv_mine0, conv_other0, norm_gain, w_out0, w_up0, w_down0,
    )
    received = beside(sent)
    grads_keep, grads_send = run(
        wide_and_in_grads_kernel, [arr(2, 1536, 128), arr(2, 1536, 128)],
        s, gated, mid_low, normed, grad_pre, hidden, grad_low, normed_in, mixed_low,
    )
    grad_out0, grad_up0, grad_down0, grad_in1 = reduce_wide(grads_keep, grads_send, True)
    spec_grad0, grads0, by_token12 = run(
        conv_back_first_kernel, [arr(*SPECTRUM), arr(length, 128), arr(48, 256)],
        s, kept, received, mine, freq0, dft, twiddle, onehot, turned, conv_table, scratch=conv_scratch,
    )
    second0, first0, skip0 = run(
        functools.partial(filter_back_kernel, 0), filter_shapes, s, spec_grad0, spec0, grads0, product0, filt0, cosine,
        sine_turned, mine, rates, feats_turned, dft, twiddle, scratch=filter_scratch,
    )
    flat, parts = run(
        small_kernel, [arr(F_ROWS, 256), arr(C_ROWS, 128)],
        s, gain_mid1, gain_in1, gain_mid0, by_token0, by_token12, first1, first0, short1, second1, second0, skip1, skip0,
    )
    here = run(chip_kernel, arr(F_ROWS + C_ROWS, 256), s, flat, beside(flat), parts, beside(parts))
    grad_embed, grad_gain, grad_in0, grad_short, grad_first, grad_second, grad_skip = run(
        last_kernel,
        [
            arr(16, 256), arr(2, 2, 256), arr(3, 256, 128), arr(2, 3, 3, 128), arr(2, FEAT, 64), arr(2, 64, 128), arr(2, 128),
        ],
        s, here, across(here), embed, norm_gain, pack, pack_in, in_own, first_in, first_in_other,
    )
    return (
        block_out,
        grad_embed,
        grad_gain,
        jnp.swapaxes(jnp.stack([grad_in0, grad_in1]), 1, 2),
        grad_short,
        grad_first,
        grad_second,
        grad_skip,
        jnp.stack([grad_out0, grad_out1]),
        jnp.stack([grad_up0, grad_up1]),
        jnp.stack([grad_down0, grad_down1]),
    )


def solution(mesh):
    in_specs = (
        P(None, "seq"),
        P(),
        P(),
        P(),
        P(None, None, None, "ch"),
        P(None, None, None, "ch"),
        P(),
        P(None, None, "ch"),
        P(None, "ch"),
        P(None, "ch", None),
        P(None, None, "ch"),
        P(None, "ch", None),
        P(None, "seq", None),
    )
    out_specs = (
        P(None, "seq", None),
        P(),
        P(),
        P(None, None, None, "ch"),
        P(None, None, None, "ch"),
        P(),
        P(None, None, "ch"),
        P(None, "ch"),
        P(None, "ch", None),
        P(None, None, "ch"),
        P(None, "ch", None),
    )

    def either(*args):
        length = args[0].shape[1] * lax.axis_size("seq")
        return (chip_local if length == BLOCKS * BLOCK else local)(*args)

    return jax.shard_map(either, mesh=mesh, in_specs=in_specs, out_specs=out_specs, check_vma=False)
```

```python
import functools
import math

import jax
import jax.numpy as jnp
import numpy as np
from jax import lax
from jax.experimental import pallas as pl
from jax.experimental.pallas import tpu as pltpu
from jax.sharding import PartitionSpec as P

D = 256
FEAT = 33


precise = lax.Precision.HIGHEST
epsilon = 1e-05


def passed_along(value, axis, steps):
    count = lax.axis_size(axis)
    leading, last = (max(0, -steps), min(count, count - steps))
    return lax.ppermute(value, axis, [(source, source + steps) for source in range(leading, last)])


def layer_norm(inputs, gain_vec):
    center = inputs - jnp.mean(inputs, axis=-1, keepdims=True)
    spread = jnp.mean(center * center, axis=-1, keepdims=True)
    return center * lax.rsqrt(spread + epsilon) * gain_vec


def position_features(length):
    places = jnp.arange(length, dtype=jnp.int32)
    band_ids = jnp.arange(1, (FEAT - 1) // 2 + 1, dtype=jnp.int32)
    turn_counts = places[:, None] * band_ids[None, :] % length
    angles = turn_counts.astype(jnp.float32) * (2.0 * math.pi / length)
    ramp_vals = places.astype(jnp.float32)[:, None] / length
    return jnp.concatenate([ramp_vals, jnp.cos(angles), jnp.sin(angles)], axis=1)


def decay_rates(channels):
    return 0.3 * 10.0 ** (channels.astype(jnp.float32) / (D - 1))


def dft_tables(blocks, block_len):
    doubled = 2 * blocks
    span_total = doubled * block_len
    frequency = jnp.arange(doubled, dtype=jnp.int32)
    places = jnp.arange(blocks, dtype=jnp.int32)
    inner_idx = jnp.arange(block_len, dtype=jnp.int32)
    outer_angle = (frequency[:, None] * places[None, :] % doubled).astype(jnp.float32) * (
        2.0 * math.pi / doubled
    )
    twist_angle = (frequency[:, None] * inner_idx[None, :] % span_total).astype(jnp.float32) * (
        2.0 * math.pi / span_total
    )
    inner_angle = (inner_idx[:, None] * inner_idx[None, :] % block_len).astype(jnp.float32) * (
        2.0 * math.pi / block_len
    )
    return (
        jnp.cos(outer_angle),
        jnp.sin(outer_angle),
        jnp.cos(twist_angle),
        jnp.sin(twist_angle),
        jnp.cos(inner_angle),
        jnp.sin(inner_angle),
    )


def along_block(values, table):
    return jnp.einsum("...kb,bj->...kj", values, table, precision=precise)


def to_spectrum(signal, tables):
    outer_cos, outer_sin, twist_cos, twist_sin, inner_cos, inner_sin = tables
    first_re = jnp.einsum("kp,...pb->...kb", outer_cos, signal, precision=precise)
    first_im = -jnp.einsum("kp,...pb->...kb", outer_sin, signal, precision=precise)
    turned_re = first_re * twist_cos + first_im * twist_sin
    turned_im = first_im * twist_cos - first_re * twist_sin
    spec_re = along_block(turned_re, inner_cos) + along_block(turned_im, inner_sin)
    spec_im = along_block(turned_im, inner_cos) - along_block(turned_re, inner_sin)
    return (spec_re, spec_im)


def from_spectrum(spec_re, spec_im, tables):
    outer_cos, outer_sin, twist_cos, twist_sin, inner_cos, inner_sin = tables
    back_re = along_block(spec_re, inner_cos) - along_block(spec_im, inner_sin)
    back_im = along_block(spec_re, inner_sin) + along_block(spec_im, inner_cos)
    turned_re = back_re * twist_cos - back_im * twist_sin
    turned_im = back_re * twist_sin + back_im * twist_cos
    scale_back = 1.0 / (outer_cos.shape[0] * inner_cos.shape[0])
    signal = jnp.einsum("kp,...kb->...pb", outer_cos, turned_re, precision=precise) - jnp.einsum(
        "kp,...kb->...pb", outer_sin, turned_im, precision=precise
    )
    return signal * scale_back


def causal_filter(received, filt_spec, skip_part, tables):
    item_count, chan_count, length = received.shape
    blocks = tables[0].shape[1]
    spec_re, spec_im = to_spectrum(
        received.reshape(item_count, chan_count, blocks, length // blocks), tables
    )
    prod_re = spec_re * filt_spec[0] - spec_im * filt_spec[1]
    prod_im = spec_re * filt_spec[1] + spec_im * filt_spec[0]
    result_sig = from_spectrum(prod_re, prod_im, tables).reshape(item_count, chan_count, length)
    return result_sig + skip_part[:, None] * received


def filter_backward(grad_cols, moved_in, filt_spec, skip_part, tables):
    item_count, chan_count, length = grad_cols.shape
    blocks = tables[0].shape[1]
    grad_re, grad_im = to_spectrum(
        grad_cols.reshape(item_count, chan_count, blocks, length // blocks), tables
    )
    input_re, input_im = to_spectrum(
        moved_in.reshape(item_count, chan_count, blocks, length // blocks), tables
    )
    back_re = grad_re * filt_spec[0] + grad_im * filt_spec[1]
    back_im = grad_im * filt_spec[0] - grad_re * filt_spec[1]
    grad_u_cols = (
        from_spectrum(back_re, back_im, tables).reshape(item_count, chan_count, length)
        + skip_part[:, None] * grad_cols
    )
    corr_re = grad_re * input_re + grad_im * input_im
    corr_im = grad_im * input_re - grad_re * input_im
    grad_filt = jnp.sum(from_spectrum(corr_re, corr_im, tables), axis=0).reshape(chan_count, length)
    grad_skip_part = jnp.sum(grad_cols * moved_in, axis=(0, 2))
    return (grad_u_cols, grad_filt, grad_skip_part)


def local_filter(first, second, features, select, group_idx, chan_local):
    hidden_pre = jnp.dot(features, first, precision=precise)
    hidden_act = jnp.sin(hidden_pre)
    chan_width = second.shape[1]
    second_part = jnp.dot(second, select, precision=precise)
    channel_ids = group_idx * chan_width + chan_local
    length = features.shape[0]
    ramp_vals = jnp.arange(length, dtype=jnp.int32).astype(jnp.float32) / length
    decay_part = jnp.exp(-decay_rates(channel_ids)[:, None] * ramp_vals[None, :])
    filt_cols = jnp.einsum("hc,th->ct", second_part, hidden_act, precision=precise) * decay_part
    return (filt_cols, hidden_pre, hidden_act, second_part, decay_part)


def filter_mlp_backward(grad_filt, features, filter_parts):
    hidden_pre, hidden_act, second_part, decay_part = filter_parts
    grad_shaped = grad_filt * decay_part
    grad_second_part = jnp.einsum("ct,th->hc", grad_shaped, hidden_act, precision=precise)
    grad_act = jnp.einsum("ct,hc->th", grad_shaped, second_part, precision=precise)
    grad_first = jnp.einsum(
        "tf,th->fh", features, grad_act * jnp.cos(hidden_pre), precision=precise
    )
    return (grad_first, grad_second_part)


def embed_lookup(ids, live, embed, seq_rank):
    tok_rows = ids.shape[1]
    places = seq_rank * tok_rows + jnp.arange(tok_rows, dtype=jnp.int32)
    keep_mask = (places[None, :] < live[:, None]).astype(jnp.float32)
    vocab_ids = jnp.arange(embed.shape[0], dtype=jnp.int32)
    onehot = (ids[:, :, None] == vocab_ids[None, None, :]).astype(jnp.float32) * keep_mask[
        :, :, None
    ]
    stream = jnp.einsum("mtv,vd->mtd", onehot, embed, precision=precise)
    return (stream, onehot, keep_mask)


def channel_total(partial_sum):
    return lax.psum(partial_sum, "ch")


def input_total(partial_sum):
    return lax.psum(partial_sum, "ch")


def layer_forward(stream, params, filt_spec, skip_part, tables):
    norm_gains, w_in, kernel, w_out, w_up, w_down = params
    normed = layer_norm(stream, norm_gains[0]).astype(jnp.bfloat16)
    mixed_in = jnp.einsum("mtd,dgc->mtgc", normed, w_in, preferred_element_type=jnp.float32)
    rim_rows = passed_along(mixed_in[:, -2:], "seq", 1)
    padded = jnp.concatenate([rim_rows, mixed_in], axis=1)
    micro_count, tok_rows = (mixed_in.shape[0], mixed_in.shape[1])
    chan_width = mixed_in.shape[3]
    gate_vals = (
        kernel[0] * mixed_in
        + kernel[1] * padded[:, 1 : tok_rows + 1]
        + kernel[2] * padded[:, 0:tok_rows]
    )
    product_in = gate_vals[:, :, 2] * gate_vals[:, :, 1]
    flat_rows = jnp.swapaxes(product_in, 1, 2).reshape(1, micro_count * chan_width, tok_rows)
    received = lax.all_to_all(flat_rows, "seq", split_axis=1, concat_axis=2, tiled=True)
    result_sig = causal_filter(received, filt_spec, skip_part, tables)
    conv_flat = lax.all_to_all(result_sig, "seq", split_axis=2, concat_axis=1, tiled=True)
    conv_out = jnp.swapaxes(conv_flat.reshape(micro_count, chan_width, tok_rows), 1, 2)
    gated_out = (conv_out * gate_vals[:, :, 0]).astype(jnp.bfloat16)
    mid_state = stream + channel_total(
        jnp.einsum("mtc,cd->mtd", gated_out, w_out, preferred_element_type=jnp.float32)
    )
    normed_mid = layer_norm(mid_state, norm_gains[1]).astype(jnp.bfloat16)
    pre_act = jnp.einsum("mtd,df->mtf", normed_mid, w_up, preferred_element_type=jnp.float32)
    hidden = jax.nn.gelu(pre_act).astype(jnp.bfloat16)
    new_stream = mid_state + channel_total(
        jnp.einsum("mtf,fd->mtd", hidden, w_down, preferred_element_type=jnp.float32)
    )
    kept_vals = (
        stream,
        normed,
        mixed_in,
        padded,
        gate_vals,
        received,
        conv_out,
        gated_out,
        mid_state,
        normed_mid,
        pre_act,
        hidden,
    )
    return (new_stream, kept_vals)


def layer_backward(grad_stream, kept_vals, params, filt_spec, skip_part, tables):
    norm_gains, w_in, kernel, w_out, w_up, w_down = params
    (
        stream,
        normed,
        mixed_in,
        padded,
        gate_vals,
        moved_in,
        conv_out,
        gated_out,
        mid_state,
        normed_mid,
        pre_act,
        hidden,
    ) = kept_vals
    micro_count, tok_rows = (mixed_in.shape[0], mixed_in.shape[1])
    chan_width = mixed_in.shape[3]
    grad_low = grad_stream.astype(jnp.bfloat16)
    grad_down = jnp.einsum("mtf,mtd->fd", hidden, grad_low, preferred_element_type=jnp.float32)
    grad_hidden = jnp.einsum("mtd,fd->mtf", grad_low, w_down, preferred_element_type=jnp.float32)
    _, gelu_back = jax.vjp(jax.nn.gelu, pre_act)
    grad_pre = gelu_back(grad_hidden)[0].astype(jnp.bfloat16)
    grad_up = jnp.einsum("mtd,mtf->df", normed_mid, grad_pre, preferred_element_type=jnp.float32)
    grad_normed_mid = input_total(
        jnp.einsum("mtf,df->mtd", grad_pre, w_up, preferred_element_type=jnp.float32)
    )
    _, norm_back_mid = jax.vjp(layer_norm, mid_state, norm_gains[1])
    grad_mid_norm, grad_gain_mid = norm_back_mid(grad_normed_mid)
    grad_mid = grad_stream + grad_mid_norm
    grad_mid_low = grad_mid.astype(jnp.bfloat16)
    grad_out = jnp.einsum(
        "mtc,mtd->cd", gated_out, grad_mid_low, preferred_element_type=jnp.float32
    )
    grad_gated = jnp.einsum("mtd,cd->mtc", grad_mid_low, w_out, preferred_element_type=jnp.float32)
    grad_conv = grad_gated * gate_vals[:, :, 0]
    grad_first_gate = grad_gated * conv_out
    grad_flat = jnp.swapaxes(grad_conv, 1, 2).reshape(1, micro_count * chan_width, tok_rows)
    grad_cols = lax.all_to_all(grad_flat, "seq", split_axis=1, concat_axis=2, tiled=True)
    grad_u_cols, grad_filt, grad_skip_part = filter_backward(
        grad_cols, moved_in, filt_spec, skip_part, tables
    )
    grad_back_flat = lax.all_to_all(grad_u_cols, "seq", split_axis=2, concat_axis=1, tiled=True)
    grad_product = jnp.swapaxes(grad_back_flat.reshape(micro_count, chan_width, tok_rows), 1, 2)
    grad_gates = jnp.stack(
        [grad_first_gate, grad_product * gate_vals[:, :, 2], grad_product * gate_vals[:, :, 1]],
        axis=2,
    )
    rim_back = passed_along(grad_gates[:, :2], "seq", -1)
    extended = jnp.concatenate([grad_gates, rim_back], axis=1)
    grad_mixed = (
        kernel[0] * grad_gates
        + kernel[1] * extended[:, 1 : tok_rows + 1]
        + kernel[2] * extended[:, 2 : tok_rows + 2]
    )
    grad_kernel = jnp.stack(
        [
            jnp.sum(grad_gates * mixed_in, axis=(0, 1)),
            jnp.sum(grad_gates * padded[:, 1 : tok_rows + 1], axis=(0, 1)),
            jnp.sum(grad_gates * padded[:, 0:tok_rows], axis=(0, 1)),
        ]
    )
    grad_mixed_low = grad_mixed.astype(jnp.bfloat16)
    grad_in = jnp.einsum(
        "mtd,mtgc->dgc", normed, grad_mixed_low, preferred_element_type=jnp.float32
    )
    grad_normed = input_total(
        jnp.einsum("mtgc,dgc->mtd", grad_mixed_low, w_in, preferred_element_type=jnp.float32)
    )
    _, norm_back_in = jax.vjp(layer_norm, stream, norm_gains[0])
    grad_stream_norm, grad_gain_in = norm_back_in(grad_normed)
    grad_before = grad_mid + grad_stream_norm
    layer_grads = (
        jnp.stack([grad_gain_in, grad_gain_mid]),
        grad_in,
        grad_kernel,
        grad_skip_part,
        grad_out,
        grad_up,
        grad_down,
    )
    return (grad_before, layer_grads, grad_filt)


def local(
    ids,
    live,
    embed,
    norm_gain,
    in_weight,
    short_kernel,
    filter_first,
    filter_second,
    skip_gain,
    out_weight,
    up_weight,
    down_weight,
    cotangent,
):
    seq_count = lax.axis_size("seq")
    seq_rank = lax.axis_index("seq")
    group_idx = lax.axis_index("ch")
    micro_count = ids.shape[0]
    tok_rows = ids.shape[1]
    length = tok_rows * seq_count
    chan_width = in_weight.shape[3]
    own_rows = micro_count * chan_width // seq_count
    layer_count = in_weight.shape[0]
    row_start = seq_rank * own_rows
    row_ids = row_start + jnp.arange(own_rows, dtype=jnp.int32)
    chan_local = row_ids % chan_width
    first_rows = (row_ids < chan_width).astype(jnp.float32)
    select = (jnp.arange(chan_width, dtype=jnp.int32)[:, None] == chan_local[None, :]).astype(
        jnp.float32
    )
    tables = dft_tables(seq_count, tok_rows)
    features = position_features(length)
    ramp_row = jnp.arange(length, dtype=jnp.int32).astype(jnp.float32) / length
    stream, onehot, keep_mask = embed_lookup(ids, live, embed, seq_rank)
    filters = []
    for level_idx in range(layer_count):
        filt_cols, hidden_pre, hidden_act, second_part, decay_part = local_filter(
            filter_first[level_idx],
            filter_second[level_idx],
            features,
            select,
            group_idx,
            chan_local,
        )
        filt_spec = to_spectrum(filt_cols.reshape(own_rows, seq_count, tok_rows), tables)
        skip_part = jnp.dot(skip_gain[level_idx], select, precision=precise)
        penalty_grad = 0.5 * length * ramp_row[None, :] * filt_cols * first_rows[:, None]
        params = (
            norm_gain[level_idx],
            in_weight[level_idx],
            short_kernel[level_idx],
            out_weight[level_idx],
            up_weight[level_idx],
            down_weight[level_idx],
        )
        filters.append(
            (
                params,
                filt_spec,
                skip_part,
                (hidden_pre, hidden_act, second_part, decay_part),
                penalty_grad,
            )
        )
    stored = []
    for level_idx in range(layer_count):
        params, filt_spec, skip_part, _, _ = filters[level_idx]
        layer_input = stream
        stream, kept_vals = layer_forward(stream, params, filt_spec, skip_part, tables)
        stored.append(layer_input)
    block_out = stream * keep_mask[:, :, None]
    grad_stream = cotangent * keep_mask[:, :, None]
    collected = [None] * layer_count
    first_grads = [None] * layer_count
    grad_embed = None
    for level_idx in reversed(range(layer_count)):
        params, filt_spec, skip_part, filter_parts, penalty_grad = filters[level_idx]
        _, kept_vals = layer_forward(stored[level_idx], params, filt_spec, skip_part, tables)
        grad_stream, layer_grads, grad_filt = layer_backward(
            grad_stream, kept_vals, params, filt_spec, skip_part, tables
        )
        grad_first, grad_second_part = filter_mlp_backward(
            grad_filt + penalty_grad, features, filter_parts
        )
        first_grads[level_idx] = grad_first
        grad_second = jnp.dot(grad_second_part, select.T, precision=precise)
        grad_skip = jnp.dot(layer_grads[3], select.T, precision=precise)
        gain_grad, in_grad, kernel_grad, _, out_grad, up_grad, down_grad = layer_grads
        if level_idx == 0:
            embed_part = jnp.einsum("mtv,mtd->vd", onehot, grad_stream, precision=precise)
            summed = lax.psum(
                (
                    gain_grad,
                    in_grad,
                    kernel_grad,
                    grad_second,
                    grad_skip,
                    out_grad,
                    up_grad,
                    down_grad,
                    embed_part,
                ),
                "seq",
            )
            collected[level_idx] = summed[:8]
            grad_embed = summed[8]
        else:
            collected[level_idx] = lax.psum(
                (
                    gain_grad,
                    in_grad,
                    kernel_grad,
                    grad_second,
                    grad_skip,
                    out_grad,
                    up_grad,
                    down_grad,
                ),
                "seq",
            )
    stacked = [
        jnp.stack([collected[level_idx][member] for level_idx in range(layer_count)])
        for member in range(8)
    ]
    filter_grads = lax.psum(jnp.stack(first_grads), ("seq", "ch"))
    return (
        block_out,
        grad_embed,
        stacked[0],
        stacked[1],
        stacked[2],
        filter_grads,
        stacked[3],
        stacked[4],
        stacked[5],
        stacked[6],
        stacked[7],
    )


HALO = 16
ROOT_HALF = math.sqrt(0.5)
GELU_A = math.sqrt(2.0 / math.pi)
GELU_B = 0.044715
BLOCKS = 8
BLOCK = 256
KINDS = 9
VMEM_LIMIT = 20 * 2**20
FLOPS = 10**10
f32 = jnp.float32
bf16 = jnp.bfloat16


class Numbers:
    def __init__(self, table):
        self.table = table

    def __getitem__(self, row):
        return self.table[row, 0]


CORE, GROUP, LIVE, WHICH, SPOT, HOLDER, BIT1, BIT2, BIT3 = range(9)
NUMBER_ROWS = 16


def number_table(count):
    rows = np.zeros((count, 2, NUMBER_ROWS, 128), np.int32)
    half = count // 2
    for rank in range(count):
        for group in range(2):
            core = rank % 2
            values = (core, group, 0, group ^ core, rank % half, int(rank // half == core), rank // 2 % 2, rank // 4 % 2, rank // 8 % 2)
            for row, value in enumerate(values):
                rows[rank, group, row] = value
    return rows


def numbers_kernel(s, live, out):
    out[...] = s.table[...]
    out[LIVE : LIVE + 1, :] = jnp.broadcast_to(jnp.where(s[GROUP] == 0, live[0:1, 0:1], live[0:1, 1:2]), (1, 128))


def run(body, outs, scalars, *arrays, scratch=(), after=(), hbm=()):
    vmem = pl.BlockSpec(memory_space=pltpu.VMEM)
    far = pl.BlockSpec(memory_space=pl.ANY)
    single = not isinstance(outs, (list, tuple))
    shapes = [outs] if single else list(outs)
    used, waits = 1 + len(arrays), len(after)

    def call(table, *refs):
        body(Numbers(table), *refs[: used - 1], *refs[used - 1 + waits :])

    inner = getattr(body, "func", body)
    result = pl.pallas_call(
        call,
        out_shape=shapes,
        in_specs=[vmem] + [far if i in hbm else vmem for i in range(len(arrays))] + [far] * waits,
        out_specs=[vmem] * len(shapes),
        scratch_shapes=list(scratch),
        compiler_params=pltpu.CompilerParams(vmem_limit_bytes=VMEM_LIMIT),
        cost_estimate=pl.CostEstimate(flops=FLOPS, bytes_accessed=1, transcendentals=0),
        name=inner.__name__,
    )(scalars, *arrays, *after)
    return result[0] if single else result


def arr(*shape, kind=f32):
    return jax.ShapeDtypeStruct(shape, kind)


def mm(a, b):
    return jnp.dot(a, b, preferred_element_type=f32)


def mm_nt(a, b):
    return lax.dot_general(a, b, (((1,), (1,)), ((), ())), preferred_element_type=f32)


def mm_tn(a, b):
    return lax.dot_general(a, b, (((0,), (0,)), ((), ())), preferred_element_type=f32)


def split(a):
    high = a.astype(bf16)
    return high, (a - high.astype(f32)).astype(bf16)


def mm3(a, b):
    a_high, a_low = split(a)
    b_high, b_low = split(b)
    return mm(a_high, b_high) + (mm(a_low, b_high) + mm(a_high, b_low))


def unit(rows):
    center = rows - jnp.mean(rows, axis=-1, keepdims=True)
    scale = lax.rsqrt(jnp.mean(center * center, axis=-1, keepdims=True) + epsilon)
    return center * scale, scale


def unit_back(grad, normal, scale):
    inner = jnp.mean(grad * normal, axis=-1, keepdims=True)
    return scale * (grad - jnp.mean(grad, axis=-1, keepdims=True) - normal * inner)


def at(start, size, unit_rows=16):
    return pl.ds(pl.multiple_of(start, unit_rows), size)


def dft_table():
    turns = np.outer(np.arange(BLOCK), np.arange(BLOCK)) % BLOCK
    angle = 2.0 * np.pi * turns / BLOCK
    return np.concatenate([np.cos(angle), np.sin(angle)], axis=1).astype(np.float32)


def twiddle_table():
    angle = 2.0 * np.pi * np.outer(np.arange(1, KINDS), np.arange(BLOCK)) / (2 * BLOCKS * BLOCK)
    pair = np.stack([np.cos(angle), np.sin(angle)], axis=1).astype(np.float32)
    return np.broadcast_to(pair[..., None], (KINDS - 1, 2, BLOCK, 128)).copy()


def feature_table(length):
    places = np.arange(length)
    turns = np.outer(places, np.arange(1, (FEAT - 1) // 2 + 1)) % length
    angle = 2.0 * np.pi * turns / length
    ramp = places[:, None] / length
    return np.concatenate([ramp, np.cos(angle), np.sin(angle)], axis=1).astype(np.float32)


def rate_table():
    return (0.3 * 10.0 ** (np.arange(D) / (D - 1))).astype(np.float32).reshape(2, 1, D // 2)


def four_real(a, b, c, d):
    s, m, t, n = a + c, a - c, b + d, b - d
    hn, ht = ROOT_HALF * n, ROOT_HALF * t
    return (s + t, s - t, (a + hn, -(ht + c)), (m, -n), (a - hn, c - ht))


def turn(k):
    angle = 2.0 * math.pi * k / (2 * BLOCKS)
    return math.cos(angle), math.sin(angle)


def put_pair(stage, kind, row, re, im):
    rows = re.shape[0]
    re, im = re.astype(bf16), im.astype(bf16)
    stage[kind, pl.ds(row, rows), 0:128] = re
    stage[kind, pl.ds(row, rows), 128:256] = im
    stage[kind, pl.ds(row + BLOCK, rows), 0:128] = im
    stage[kind, pl.ds(row + BLOCK, rows), 128:256] = -re


def put_pair_back(stage, kind, row, re, im):
    rows = re.shape[0]
    re, im = re.astype(bf16), im.astype(bf16)
    stage[kind, pl.ds(row, rows), 0:128] = re
    stage[kind, pl.ds(row, rows), 128:256] = im
    stage[kind, pl.ds(row + BLOCK, rows), 0:128] = -im
    stage[kind, pl.ds(row + BLOCK, rows), 128:256] = re


def all_kinds(dft, stage, out):
    def one(kind, carry):
        out[kind] = mm(dft[...], stage[kind])
        return carry

    lax.fori_loop(0, KINDS, one, 0)


def to_freq(load, dft, twiddle, stage, out):
    def chunk(step, carry):
        row = pl.multiple_of(step * 16, 16)
        u = [load(p, row) for p in range(BLOCKS)]
        e0, e4, e1, e2, e3 = four_real(u[0], u[2], u[4], u[6])
        o0, o4, o1, o2, o3 = four_real(u[1], u[3], u[5], u[7])

        def put(kind, re, im):
            c, s = twiddle[kind - 1, 0, pl.ds(row, 16), :], twiddle[kind - 1, 1, pl.ds(row, 16), :]
            put_pair(stage, kind, row, re * c + im * s, im * c - re * s)

        put_pair(stage, 0, row, e0 + o0, jnp.zeros_like(e0))
        last = e0 - o0
        c, s = twiddle[7, 0, pl.ds(row, 16), :], twiddle[7, 1, pl.ds(row, 16), :]
        put_pair(stage, 8, row, last * c, -(last * s))
        put(4, e4, -o4)
        for k, (er, ei), (orr, oi) in ((1, e1, o1), (2, e2, o2), (3, e3, o3)):
            c, s = turn(k)
            wr, wi = orr * c + oi * s, oi * c - orr * s
            put(k, er + wr, ei + wi)
            put(8 - k, er - wr, wi - ei)
        return carry

    lax.fori_loop(0, BLOCK // 16, chunk, 0)
    all_kinds(dft, stage, out)


def from_freq(dft, twiddle, stage, back, store):
    all_kinds(dft, stage, back)

    def chunk(step, carry):
        row = pl.multiple_of(step * 16, 16)

        def get(kind):
            re = back[kind, pl.ds(row, 16), 0:128]
            im = back[kind, pl.ds(row, 16), 128:256]
            c, s = twiddle[kind - 1, 0, pl.ds(row, 16), :], twiddle[kind - 1, 1, pl.ds(row, 16), :]
            return re * c - im * s, re * s + im * c

        first = 0.5 * back[0, pl.ds(row, 16), 0:128]
        last = 0.5 * get(8)[0]
        mid_re, mid_im = get(4)
        even, odd = {}, {}
        for k in (1, 2, 3):
            ar, ai = get(k)
            br, bi = get(8 - k)
            even[k] = (ar + br, ai - bi)
            c, s = turn(k)
            dr, di = ar - br, ai + bi
            odd[k] = (dr * c - di * s, dr * s + di * c)
        for shift, base, extra, part in (
            (0, first + last, mid_re, even),
            (1, first - last, -mid_im, odd),
        ):
            (r1, i1), (r2, i2), (r3, i3) = part[1], part[2], part[3]
            plus, minus = base + extra, base - extra
            diff, both = ROOT_HALF * (r1 - r3), ROOT_HALF * (i1 + i3)
            store(shift, row, plus + (r1 + r2 + r3))
            store(shift + 2, row, minus - i2 + (diff - both))
            store(shift + 4, row, plus - r2 - (i1 - i3))
            store(shift + 6, row, minus + i2 - (diff + both))
        return carry

    lax.fori_loop(0, BLOCK // 16, chunk, 0)


def times(first, second, stage, conj):
    def chunk(step, carry):
        row = pl.multiple_of(step * 16, 16)
        for kind in range(KINDS):
            fr = first[kind, pl.ds(row, 16), 0:128]
            fi = first[kind, pl.ds(row, 16), 128:256]
            ur = second[kind, pl.ds(row, 16), 0:128]
            ui = second[kind, pl.ds(row, 16), 128:256]
            if conj:
                put_pair_back(stage, kind, row, fr * ur + fi * ui, fr * ui - fi * ur)
            else:
                put_pair_back(stage, kind, row, fr * ur - fi * ui, fr * ui + fi * ur)
        return carry

    lax.fori_loop(0, BLOCK // 16, chunk, 0)


SPECTRUM = (KINDS, BLOCK, 256)


def stage_scratch():
    return pltpu.VMEM((KINDS, 2 * BLOCK, 256), bf16)


def spec_scratch():
    return pltpu.VMEM(SPECTRUM, f32)


PACK_SECOND = 48
PACK_SHORT = 176
PACK_SKIP = 194
PACK_ROWS = 200


def pack_kernel(s, embed, gain, in_own, second, short, skip, out):
    normal, _ = unit(embed[...])
    low = (normal * gain[0, 0:1, :]).astype(bf16)
    for g in range(3):
        out[16 * g : 16 * g + 16, :] = mm(low, in_own[0, g])
    for l in range(2):
        out[PACK_SECOND + 64 * l : PACK_SECOND + 64 * l + 64, :] = second[l]
        for k in range(3):
            row = PACK_SHORT + 9 * l + 3 * k
            out[row : row + 3, :] = short[l, k]
    out[PACK_SKIP : PACK_SKIP + 2, :] = skip[...]
    out[PACK_SKIP + 2 : PACK_ROWS, :] = jnp.zeros((PACK_ROWS - PACK_SKIP - 2, 128), f32)


def table_kernel(s, own, peer, embed, mine_out, other_out, conv_table, gate_table):
    first = s[CORE] == 0
    mine = jnp.where(first, own[...], peer[...])
    other = jnp.where(first, peer[...], own[...])
    mine_out[...] = mine
    other_out[...] = other

    def fill(table, lanes, parts):
        whole = jnp.concatenate(parts, axis=0)
        high, low = split(whole)
        table[0:48, lanes] = high
        table[48:96, lanes] = low
        table[96:128, lanes] = jnp.zeros((32, 128), bf16)

    def gate(pack, g):
        parts = []
        for k in range(3):
            row = PACK_SHORT + 3 * k + g
            parts.append(pack[16 * g : 16 * g + 16] * pack[row : row + 1])
        return parts

    fill(conv_table, slice(0, 128), gate(mine, 1))
    fill(conv_table, slice(128, 256), gate(mine, 2))
    fill(gate_table, slice(0, 128), gate(mine, 0))
    fill(gate_table, slice(128, 256), gate(other, 0))
    zero = jnp.zeros((16, 128), f32)
    fill(gate_table, slice(256, 384), [embed[:, 0:128], zero, zero])
    fill(gate_table, slice(384, 512), [embed[:, 128:256], zero, zero])


def onehot_kernel(s, ids, out, turned, work):
    live = s[LIVE]
    count, _, width = ids.shape
    work[0:HALO, :] = jnp.zeros((HALO, 128), f32)
    work[HALO + count * width : 2 * HALO + count * width, :] = jnp.zeros((HALO, 128), f32)
    vocab = lax.broadcasted_iota(jnp.int32, (128, width), 0) % 16
    place = lax.broadcasted_iota(jnp.int32, (128, width), 1)
    for i in range(count):
        token = jnp.broadcast_to(ids[i, 0:1, :], (128, width))
        hit = (token == vocab) & (place + i * width < live)
        work[HALO + width * i : HALO + width * (i + 1), :] = jnp.where(hit, 1.0, 0.0).T
    lane = lax.broadcasted_iota(jnp.int32, (width, 128), 1) % 48 // 16
    used = lax.broadcasted_iota(jnp.int32, (width, 128), 1) < 96
    half = count // 2
    for i in range(count):
        row = HALO + width * i
        now = work[row : row + width, :]
        one = work[row - 1 : row - 1 + width, :]
        two = work[row - 2 : row - 2 + width, :]
        picked = jnp.where(lane == 0, now, jnp.where(lane == 1, one, two))
        picked = jnp.where(used, picked, 0.0)
        out[row : row + width, :] = picked.astype(bf16)
        turned[i // half, :, width * (i % half) : width * (i % half + 1)] = picked.T.astype(bf16)
    out[0:HALO, :] = jnp.zeros((HALO, 128), bf16)
    out[HALO + count * width : 2 * HALO + count * width, :] = jnp.zeros((HALO, 128), bf16)


def sine_and_cosine(angle):
    turns = jnp.round(angle * (2.0 / math.pi))
    x = ((angle - turns * 1.5703125) - turns * 4.837512969970703125e-4) - turns * 7.549789948768648e-8
    z = x * x
    sin = ((-1.9515295891e-4 * z + 8.3321608736e-3) * z - 1.6666654611e-1) * z * x + x
    cos = ((2.443315711809948e-5 * z - 1.388731625493765e-3) * z + 4.166664568298827e-2) * z * z - 0.5 * z + 1.0
    quarter = turns.astype(jnp.int32) & 3
    odd = (quarter & 1) == 1
    first, second = jnp.where(odd, cos, sin), jnp.where(odd, sin, cos)
    first = jnp.where(quarter >= 2, -first, first)
    second = jnp.where((quarter == 1) | (quarter == 2), -second, second)
    return first, second


def sine_kernel(s, feats, firsts, sine, cosine, turned):
    both = jnp.concatenate([firsts[0], firsts[1]], axis=1)
    count = feats.shape[0] // 256

    def chunk(i, carry):
        rows = at(256 * i, 256)
        angle = jnp.dot(feats[rows, :], both, precision=precise, preferred_element_type=f32)
        act, cosine[rows, :] = sine_and_cosine(angle)
        sine[rows, :] = act
        turned[:, at(256 * i, 256, 256)] = act.T.astype(bf16)
        return carry

    lax.fori_loop(0, count, chunk, 0)


def decay_of(rates, start, rows, length):
    place = (lax.broadcasted_iota(jnp.int32, (rows, 1), 0) + start).astype(f32) / length
    return jnp.exp(-place * rates), place


def filter_kernel(s, sine, mine, rates, dft, twiddle, filt0, filt1, freq0, freq1, stage, work):
    length = sine.shape[0]
    rate = rates[s[WHICH]]
    zero = jnp.zeros((64, 128), f32)
    left = jnp.concatenate([mine[PACK_SECOND : PACK_SECOND + 64], zero], axis=0)
    right = jnp.concatenate([zero, mine[PACK_SECOND + 64 : PACK_SECOND + 128]], axis=0)
    weights = jnp.concatenate([left, right], axis=1)

    def chunk(i, carry):
        rows = at(256 * i, 256)
        decay, _ = decay_of(rate, 256 * i, 256, length)
        both = mm3(sine[rows, :], weights)
        filt0[rows, :] = both[:, 0:128] * decay
        filt1[rows, :] = both[:, 128:256] * decay
        return carry

    lax.fori_loop(0, length // 256, chunk, 0)
    for filt, freq in ((filt0, freq0), (filt1, freq1)):
        to_freq(lambda p, row: filt[pl.ds(BLOCK * p + row, 16), :] * (1.0 / length), dft, twiddle, stage, freq)


def causal(load, skip_row, freq_filt, dft, twiddle, spec, stage, work, line):
    to_freq(load, dft, twiddle, stage, spec)
    times(freq_filt, spec, stage, False)

    def store(p, row, value):
        line[pl.ds(HALO + BLOCK * p + row, 16), :] = value + skip_row * load(p, row)

    from_freq(dft, twiddle, stage, work, store)


def hand_out(s, line, keep, send):
    half = (line.shape[0] - 2 * HALO) // 2
    span = half + 2 * HALO
    k = s[CORE]
    line[0:HALO, :] = jnp.zeros((HALO, 128), f32)
    line[HALO + 2 * half :, :] = jnp.zeros((HALO, 128), f32)
    keep[...] = line[at(half * k, span), :]
    send[...] = line[at(half * (1 - k), span), :]


def conv_first_kernel(s, onehot, conv_table, mine, freq_filt, dft, twiddle, keep, send, spec, product, stage, work, line):
    def chunk(i, carry):
        rows = at(256 * i, 256)
        pair = mm(onehot[at(256 * i + HALO, 256), :], conv_table[...])
        product[rows, :] = pair[:, 0:128] * pair[:, 128:256]
        return carry

    lax.fori_loop(0, product.shape[0] // 256, chunk, 0)
    skip_row = mine[PACK_SKIP : PACK_SKIP + 1, :]
    causal(lambda p, row: product[pl.ds(BLOCK * p + row, 16), :], skip_row, freq_filt, dft, twiddle, spec, stage, work, line)
    hand_out(s, line, keep, send)


def join_rows(s, whole, kept, received):
    half = kept.shape[0]
    whole[at(half * s[CORE], half), :] = kept[...]
    whole[at(half * (1 - s[CORE]), half), :] = received[...]


def conv_second_kernel(s, kept, received, mine, freq_filt, dft, twiddle, keep, send, spec, product, stage, work, line):
    join_rows(s, product, kept, received)
    skip_row = mine[PACK_SKIP + 1 : PACK_SKIP + 2, :]
    causal(lambda p, row: product[pl.ds(BLOCK * p + row, 16), :], skip_row, freq_filt, dft, twiddle, spec, stage, work, line)
    hand_out(s, line, keep, send)


def gelu_parts(p):
    squared = p * p
    th = jnp.tanh(GELU_A * p * (1.0 + GELU_B * squared))
    half = 0.5 * (1.0 + th)
    slope = half + 0.5 * p * (1.0 - th * th) * (GELU_A + (3.0 * GELU_A * GELU_B) * squared)
    return p * half, slope


def gelu_only(p):
    return 0.5 * p * (1.0 + jnp.tanh(GELU_A * p * (1.0 + GELU_B * (p * p))))


CHUNK = 352


def forward_first_kernel(
    s, onehot, gate_table, conv_mine, conv_other, gain, w_out, w_up, w_down, w_in, mine, other,
    keep, send, mid_out, stream_out, gates, mixed,
):
    span = mid_out.shape[0]
    half = span - 2 * HALO
    k = s[CORE]
    taps = [
        jnp.concatenate([pack[PACK_SHORT + 9 + 3 * t + g : PACK_SHORT + 10 + 3 * t + g, :] for g in range(3) for pack in (mine, other)], axis=1)
        for t in range(3)
    ]

    def chunk(i, carry):
        rows = at(CHUNK * i, CHUNK)
        looked = mm(onehot[at(half * k + CHUNK * i, CHUNK), :], gate_table[...])
        conv = jnp.concatenate([conv_mine[rows, :], conv_other[rows, :]], axis=1)
        gated = (conv * looked[:, 0:256]).astype(bf16)
        mid = looked[:, 256:512] + mm(gated, w_out[...])
        mid_out[rows, :] = mid
        normal, _ = unit(mid)
        low = (normal * gain[0, 1:2, :]).astype(bf16)
        hidden = gelu_only(mm(low, w_up[...])).astype(bf16)
        stream = mid + mm(hidden, w_down[...])
        stream_out[rows, :] = stream
        normal, _ = unit(stream)
        low = (normal * gain[1, 0:1, :]).astype(bf16)
        mixed[rows, :] = mm(low, w_in[...])
        return carry

    lax.fori_loop(0, span // CHUNK, chunk, 0)
    gates[0:HALO, :] = jnp.zeros((HALO, 768), f32)
    step = 80
    for start in range(HALO, span, step):
        stop = start + step
        gates[start:stop, :] = (
            taps[0] * mixed[start:stop, :]
            + taps[1] * mixed[start - 1 : stop - 1, :]
            + taps[2] * mixed[start - 2 : stop - 2, :]
        )
    own = slice(HALO, HALO + half)
    keep[...] = gates[own, 256:384] * gates[own, 512:640]
    send[...] = gates[own, 384:512] * gates[own, 640:768]


def turn_back_kernel(
    s, conv_mine, conv_other, gates, stream, cot_near, cot_far, cot_rim, gain, w_out, w_up, w_down,
    keep, send, grad_x0, grad_mid, block_out, hidden_out, low_out, normed_out, pre_out, gated_out, mid_low_out, gain_out,
    cot_rows, conv_grads,
):
    span = stream.shape[0]
    half = span - 2 * HALO
    k = s[CORE]
    live = s[LIVE]
    cot_rows[0:HALO, :] = jnp.zeros((HALO, 256), f32)
    cot_rows[HALO : HALO + half, :] = jnp.where(s[HOLDER] == 1, cot_near[...], cot_far[...]).reshape(half, 256)
    cot_rows[HALO + half :, :] = jnp.where(k == 0, cot_rim[...], 0.0)
    gain_out[...] = jnp.zeros_like(gain_out)

    def chunk(i, carry):
        rows = at(CHUNK * i, CHUNK)
        local_row = lax.broadcasted_iota(jnp.int32, (CHUNK, 1), 0) + CHUNK * i
        keep_mask = (local_row + (half * k - HALO) < live).astype(f32)
        own_mask = ((local_row >= HALO) & (local_row < HALO + half)).astype(f32)
        x0 = gates[rows, 0:256]
        conv = jnp.concatenate([conv_mine[rows, :], conv_other[rows, :]], axis=1)
        gated = (conv * x0).astype(bf16)
        gated_out[rows, :] = gated
        mid = stream[rows, :] + mm(gated, w_out[...])
        normal, scale = unit(mid)
        gain_row = gain[1, 1:2, :]
        low = (normal * gain_row).astype(bf16)
        normed_out[rows, :] = low
        act, slope = gelu_parts(mm(low, w_up[...]))
        hidden = act.astype(bf16)
        hidden_out[rows, :] = hidden
        block_out[rows, :] = (mid + mm(hidden, w_down[...])) * keep_mask
        grad = cot_rows[rows, :] * keep_mask
        grad_low = grad.astype(bf16)
        low_out[rows, :] = grad_low
        grad_pre = (slope * mm_nt(grad_low, w_down[...])).astype(bf16)
        pre_out[rows, :] = grad_pre
        grad_normed = mm_nt(grad_pre, w_up[...])
        gain_out[0:1, :] += jnp.sum(grad_normed * normal * own_mask, axis=0, keepdims=True)
        mid_grad = grad + unit_back(grad_normed * gain_row, normal, scale)
        grad_mid[rows, :] = mid_grad
        mid_low = mid_grad.astype(bf16)
        mid_low_out[rows, :] = mid_low
        grad_gated = mm_nt(mid_low, w_out[...])
        conv_grads[rows, :] = grad_gated * x0
        grad_x0[rows, :] = grad_gated * conv
        return carry

    lax.fori_loop(0, span // CHUNK, chunk, 0)
    own = slice(HALO, HALO + half)
    keep[...] = conv_grads[own, 0:128]
    send[...] = conv_grads[own, 128:256]


def conv_back_kernel(s, kept, received, mine, freq_filt, dft, twiddle, keep, send, spec, grads, stage, work, line):
    join_rows(s, grads, kept, received)
    skip_row = mine[PACK_SKIP + 1 : PACK_SKIP + 2, :]
    load = lambda p, row: grads[pl.ds(BLOCK * p + row, 16), :]
    to_freq(load, dft, twiddle, stage, spec)
    times(freq_filt, spec, stage, True)

    def store(p, row, value):
        line[pl.ds(HALO + BLOCK * p + row, 16), :] = value + skip_row * load(p, row)

    from_freq(dft, twiddle, stage, work, store)
    hand_out(s, line, keep, send)


def grad_freq_kernel(s, kept, received, dft, twiddle, spec, grads, stage):
    join_rows(s, grads, kept, received)
    to_freq(lambda p, row: grads[pl.ds(BLOCK * p + row, 16), :], dft, twiddle, stage, spec)


def filter_back(
    level, s, spec_grad, spec_in, grads, product, filt, cosine, sine_turned, mine, rates, feats_turned, dft, twiddle,
    second_out, first_out, skip_out, stage, work, line,
):
    length = filt.shape[0]
    times(spec_in, spec_grad, stage, True)

    def store(p, row, value):
        line[pl.ds(BLOCK * p + row, 16), :] = value

    from_freq(dft, twiddle, stage, work, store)
    rate = rates[s[WHICH]]
    second = mine[PACK_SECOND + 64 * level : PACK_SECOND + 64 * level + 64, :].astype(bf16)
    weight = jnp.where(s[GROUP] == 0, 0.5 * length, 0.0)
    skip_out[...] = jnp.zeros_like(skip_out)
    second_out[...] = jnp.zeros_like(second_out)
    first_out[...] = jnp.zeros_like(first_out)
    for i in range(length // 512):
        rows = slice(512 * i, 512 * (i + 1))
        decay, place = decay_of(rate, 512 * i, 512, length)
        shaped = ((line[rows, :] * (1.0 / length) + (weight * place) * filt[rows, :]) * decay).astype(bf16)
        skip_out[...] += jnp.sum((grads[rows, :] * product[rows, :]).reshape(64, 8, 128), axis=0)
        second_out[...] += mm(sine_turned[64 * level : 64 * level + 64, rows], shaped)
        inner = (mm_nt(shaped, second) * cosine[rows, 64 * level : 64 * level + 64]).astype(bf16)
        first_out[...] += mm(feats_turned[:, rows], inner)


def filter_back_kernel(s, *refs):
    filter_back(1, s, *refs)


def token_back_kernel(
    s, spec_grad, spec_in, grads, product, filt, cosine, sine_turned, mine, rates, feats_turned, dft, twiddle,
    freq_filt, onehot, turned, conv_table, second_out, first_out, skip_out, by_token, stage, work, line,
):
    length = grads.shape[0]
    skip_row = mine[PACK_SKIP : PACK_SKIP + 1, :]
    times(freq_filt, spec_grad, stage, True)

    def store(p, row, value):
        line[pl.ds(BLOCK * p + row, 16), :] = value + skip_row * grads[pl.ds(BLOCK * p + row, 16), :]

    from_freq(dft, twiddle, stage, work, store)
    by_token[...] = jnp.zeros_like(by_token)
    width = turned.shape[2]
    for i in range(length // width):
        rows = slice(width * i, width * (i + 1))
        pair = mm(onehot[HALO + width * i : HALO + width * (i + 1), :], conv_table[...])
        back = line[rows, :]
        gate_grads = jnp.concatenate([back * pair[:, 128:256], back * pair[:, 0:128]], axis=1).astype(bf16)
        by_token[...] += mm(turned[i], gate_grads)[0:48, :]
    filter_back(
        0, s, spec_grad, spec_in, grads, product, filt, cosine, sine_turned, mine, rates, feats_turned, dft, twiddle,
        second_out, first_out, skip_out, stage, work, line,
    )


def back_gates_kernel(
    s, prod_mine, prod_other, grad_x0, gates, mixed, grad_mid, stream, gain, mine, other, w_in,
    grad_stream, normed_out, mixed_low, short_out, gain_out, line,
):
    span = stream.shape[0]
    half = span - 2 * HALO
    taps = [
        jnp.concatenate([pack[PACK_SHORT + 9 + 3 * t + g : PACK_SHORT + 10 + 3 * t + g, :] for g in range(3) for pack in (mine, other)], axis=1)
        for t in range(3)
    ]
    step = 128
    for start in list(range(HALO, HALO + half, step)) + [HALO + half]:
        stop = start + (step if start < HALO + half else HALO)
        product = jnp.concatenate([prod_mine[start:stop, :], prod_other[start:stop, :]], axis=1)
        line[start:stop, 0:256] = grad_x0[start:stop, :]
        line[start:stop, 256:512] = product * gates[start:stop, 512:768]
        line[start:stop, 512:768] = product * gates[start:stop, 256:512]
    short_out[...] = jnp.zeros_like(short_out)
    gain_out[...] = jnp.zeros_like(gain_out)
    step = 64
    for start in range(HALO, HALO + half, step):
        stop = start + step
        values = mixed[start:stop, :]
        total = None
        for t in range(3):
            shifted = line[start + t : stop + t, :]
            part = taps[t] * shifted
            total = part if total is None else total + part
            short_out[t] += jnp.sum((shifted * values).reshape(step // 8, 8, 768), axis=0)
        mixed_low[start - HALO : stop - HALO, :] = total.astype(bf16)

    def chunk(i, carry):
        rows = at(256 * i, 256)
        wide = at(256 * i + HALO, 256)
        normal, scale = unit(stream[wide, :])
        gain_row = gain[1, 0:1, :]
        normed_out[rows, :] = (normal * gain_row).astype(bf16)
        grad_normed = mm_nt(mixed_low[rows, :], w_in[...])
        gain_out[0:1, :] += jnp.sum(grad_normed * normal, axis=0, keepdims=True)
        grad_stream[rows, :] = grad_mid[wide, :] + unit_back(grad_normed * gain_row, normal, scale)
        return carry

    lax.fori_loop(0, half // 256, chunk, 0)


def back_first_kernel(
    s, grad_stream, mid, onehot, turned, gate_table, conv_mine, conv_other, gain, w_out, w_up, w_down,
    keep, send, hidden_out, low_out, normed_out, pre_out, gated_out, mid_low_out, by_token, gain_out,
):
    half = grad_stream.shape[0]
    k = s[CORE]
    by_token[...] = jnp.zeros_like(by_token)
    gain_out[...] = jnp.zeros_like(gain_out)

    def chunk(i, carry):
        rows = at(256 * i, 256)
        wide = at(256 * i + HALO, 256)
        hot = onehot[at(half * k + 256 * i + HALO, 256), :]
        x0 = mm(hot, gate_table[:, 0:256])
        conv = jnp.concatenate([conv_mine[wide, :], conv_other[wide, :]], axis=1)
        gated_out[rows, :] = (conv * x0).astype(bf16)
        normal, scale = unit(mid[wide, :])
        gain_row = gain[0, 1:2, :]
        low = (normal * gain_row).astype(bf16)
        normed_out[rows, :] = low
        act, slope = gelu_parts(mm(low, w_up[...]))
        hidden_out[rows, :] = act.astype(bf16)
        grad = grad_stream[rows, :]
        grad_low = grad.astype(bf16)
        low_out[rows, :] = grad_low
        grad_pre = (slope * mm_nt(grad_low, w_down[...])).astype(bf16)
        pre_out[rows, :] = grad_pre
        grad_normed = mm_nt(grad_pre, w_up[...])
        gain_out[0:1, :] += jnp.sum(grad_normed * normal, axis=0, keepdims=True)
        mid_grad = grad + unit_back(grad_normed * gain_row, normal, scale)
        mid_low = mid_grad.astype(bf16)
        mid_low_out[rows, :] = mid_low
        grad_gated = mm_nt(mid_low, w_out[...])
        conv_grad = grad_gated * x0
        keep[rows, :] = conv_grad[:, 0:128]
        send[rows, :] = conv_grad[:, 128:256]
        flips = turned[k, :, at(256 * i, 256, 256)]
        rest = mid_grad - mid_low.astype(f32)
        gate_grads = jnp.concatenate([(grad_gated * conv).astype(bf16), mid_low, rest.astype(bf16)], axis=1)
        by_token[...] += mm(flips, gate_grads)[0:48, :]
        return carry

    lax.fori_loop(0, half // 256, chunk, 0)


R_OUT, R_UP, R_DOWN, R_IN = 128, 512, 512, 384


def send_weights_kernel(s, w_out, w_up, w_down, w_in, part0, part1, raw_out, raw_up, raw_down, raw_in, done):
    copies = [
        pltpu.make_async_copy(far, near, done.at[i])
        for i, (far, near) in enumerate(((w_out, raw_out), (w_up, raw_up), (w_down, raw_down), (w_in, raw_in)))
    ]
    for copy in copies:
        copy.start()
    for copy in copies:
        copy.wait()
    first = s[CORE] == 0
    pick = lambda a, b: jnp.where(first, a.astype(f32), b.astype(f32))
    for level, out in ((0, part0), (1, part1)):
        out[0:128, :] = pick(raw_out[level, :, 0:128], raw_out[level, :, 128:256])
        for j in range(2):
            lanes = slice(128 * j, 128 * j + 128)
            out[128 + 256 * j : 384 + 256 * j, :] = pick(
                raw_up[level, :, 128 * j : 128 * j + 128], raw_up[level, :, 256 + 128 * j : 384 + 128 * j]
            )
            out[640 + 256 * j : 896 + 256 * j, :] = pick(raw_down[level, 0:256, lanes], raw_down[level, 256:512, lanes])
        for g in range(3):
            out[1152 + 128 * g : 1280 + 128 * g, :] = pick(raw_in[1 - level, g, 0:128, :], raw_in[1 - level, g, 128:256, :])


def ids_kernel(s, ids, out):
    row = jnp.where(s[GROUP] == 0, ids[0:1, :], ids[1:2, :])
    out[0] = jnp.broadcast_to(row, out.shape[1:])


def pick_kernel(s, values, out):
    out[0] = values[s[GROUP]]


def rim_kernel(s, near, far_rows, out):
    out[...] = jnp.where(s[HOLDER] == 1, near[0, 0:HALO, :], far_rows[0, 0:HALO, :])


def relay_kernel(s, value, out):
    out[...] = value[...]


def join_weights_kernel(level, s, w_out, w_up, w_down, w_in, first_part, second_part, out_full, up_full, down_full, *in_full):
    first = s[CORE] == 0
    low = lambda ref, a, b: ref[a:b, :].astype(bf16)
    pick = lambda a, b: jnp.where(first, a, b)
    mine_out = w_out[level]
    a, b = first_part[0:128, :], second_part[0:128, :]
    peer_out = jnp.concatenate([pick(a, b), pick(b, a)], axis=1)
    out_full[0:128, :] = pick(mine_out.astype(f32), peer_out).astype(bf16)
    out_full[128:256, :] = pick(peer_out, mine_out.astype(f32)).astype(bf16)
    up_a, up_b = w_up[level, :, 0:256].astype(f32), w_up[level, :, 256:512].astype(f32)
    up_full[:, 0:256] = pick(up_a, up_b).astype(bf16)
    up_full[:, 256:512] = pick(up_b, up_a).astype(bf16)
    down_a, down_b = w_down[level, 0:256, :].astype(f32), w_down[level, 256:512, :].astype(f32)
    down_full[0:256, :] = pick(down_a, down_b).astype(bf16)
    down_full[256:512, :] = pick(down_b, down_a).astype(bf16)
    for n, part in enumerate((first_part, second_part)):
        for j in range(2):
            up_full[:, 512 + 256 * n + 128 * j : 640 + 256 * n + 128 * j] = low(part, 128 + 256 * j, 384 + 256 * j)
            down_full[512 + 256 * n : 768 + 256 * n, 128 * j : 128 * j + 128] = low(part, 640 + 256 * j, 896 + 256 * j)
    if in_full:
        (full,) = in_full
        for g in range(3):
            own = w_in[1 - level, g].astype(f32)
            a, b = first_part[1152 + 128 * g : 1280 + 128 * g, :], second_part[1152 + 128 * g : 1280 + 128 * g, :]
            peer = jnp.concatenate([pick(a, b), pick(b, a)], axis=0)
            full[:, 256 * g : 256 * g + 128] = pick(own, peer).astype(bf16)
            full[:, 256 * g + 128 : 256 * g + 256] = pick(peer, own).astype(bf16)


def wide_grads_kernel(pad, s, gated, mid_low, normed, grad_pre, hidden, grad_low, keep, send):
    k = s[CORE]
    first = k == 0
    stop = gated.shape[0] - pad
    own = lambda ref: ref[pad:stop, :]
    out = mm_tn(own(gated), own(mid_low))
    for m in range(2):
        a, b = out[128 * m : 128 * m + 128, 0:128], out[128 * m : 128 * m + 128, 128:256]
        half = m + k - 2 * m * k
        keep[half, 0:128, :] = jnp.where(first, a, b)
        send[half, 0:128, :] = jnp.where(first, b, a)
    for j in range(4):
        target = (keep, send)[j % 2]
        up = mm_tn(own(normed), grad_pre[pad:stop, 256 * j : 256 * j + 256])
        down = mm_tn(hidden[pad:stop, 256 * j : 256 * j + 256], own(grad_low))
        for n in range(2):
            lanes = slice(128 * n, 128 * n + 128)
            target[j // 2, 128 + 256 * n : 384 + 256 * n, :] = up[:, lanes]
            target[j // 2, 640 + 256 * n : 896 + 256 * n, :] = down[:, lanes]


def in_grads_kernel(s, normed_in, mixed_low, keep, send):
    k = s[CORE]
    first = k == 0
    for g in range(3):
        both = mm_tn(normed_in[...], mixed_low[:, 256 * g : 256 * g + 256])
        for m in range(2):
            block = both[:, 128 * m : 128 * m + 128]
            half = m + k - 2 * m * k
            keep[half, 128 * g : 128 * g + 128, :] = jnp.where(first, block[0:128], block[128:256])
            send[half, 128 * g : 128 * g + 128, :] = jnp.where(first, block[128:256], block[0:128])


def add_kernel(s, kept, received, own_out, peer_out):
    own_out[...] = kept[0] + received[0]
    peer_out[...] = kept[1] + received[1]


def add_one_kernel(s, kept, received, out):
    out[...] = kept[...] + received[...]


def spread_wide_kernel(s, kept1, received1, kept0, received0, out, up, down):
    first = s[CORE] == 0
    pick = lambda x, y: jnp.where(first, x, y)
    for level, a, b in ((0, kept0, received0), (1, kept1, received1)):

        def both(row, rows):
            x, y = a[row : row + rows, :], b[row : row + rows, :]
            return pick(x, y), pick(y, x)

        x, y = both(0, 128)
        out[level, :, 0:128] = x
        out[level, :, 128:256] = y
        for j in range(2):
            lanes = slice(128 * j, 128 * j + 128)
            x, y = both(128 + 256 * j, 256)
            up[level, :, 128 * j : 128 * j + 128] = x
            up[level, :, 256 + 128 * j : 384 + 128 * j] = y
            x, y = both(640 + 256 * j, 256)
            down[level, 0:256, lanes] = x
            down[level, 256:512, lanes] = y


def spread_in_kernel(s, in_first, kept, received, out):
    first = s[CORE] == 0
    for g in range(3):
        x, y = kept[128 * g : 128 * g + 128, :], received[128 * g : 128 * g + 128, :]
        out[0, g] = in_first[g]
        out[1, g, 0:128, :] = jnp.where(first, x, y)
        out[1, g, 128:256, :] = jnp.where(first, y, x)


def pair_kernel(bit, s, own, received, out):
    spot = s[(CORE, BIT1, BIT2, BIT3)[bit]]
    size = own.shape[0]
    if bit == 0:
        for j in range(size):
            out[2 * j + spot] = own[j]
            out[2 * j + 1 - spot] = received[j]
    else:
        out[pl.ds(size * spot, size)] = own[...]
        out[pl.ds(size * (1 - spot), size)] = received[...]


E_GAIN1, E_GAIN0, E_EMBED, E_FIRST, E_SHORT, E_TOKEN, E_ROWS = 0, 8, 16, 32, 72, 88, 136
EM_SECOND, EM_SKIP, EM_ROWS = 0, 64, 72
L_TOKEN, L_SECOND, L_SKIP, L_ROWS = 0, 96, 160, 168
FIRST_ROWS = 40


def early_kernel(s, gain_mid1, gain_in1, gain_mid0, by_token0, first1, short1, second1, skip1, flat, mine):
    k = s[CORE]
    flat[...] = jnp.zeros_like(flat)
    flat[E_GAIN1 : E_GAIN1 + 8, :] = gain_mid1[...]
    flat[E_GAIN0 : E_GAIN0 + 8, :] = gain_mid0[...]
    flat[E_GAIN1 + 1 : E_GAIN1 + 2, :] = gain_in1[0:1, :]
    flat[E_EMBED : E_EMBED + 16, :] = by_token0[0:16, 256:512] + by_token0[0:16, 512:768]
    flat[E_FIRST : E_FIRST + FIRST_ROWS, 0:64] = first1[...]
    swap = lambda v: jnp.where(k == 0, v, jnp.concatenate([v[:, 128:256], v[:, 0:128]], axis=1))
    for t in range(3):
        total = jnp.sum(short1[t], axis=0, keepdims=True)
        for g in range(3):
            flat[E_SHORT + 3 * t + g : E_SHORT + 3 * t + g + 1, :] = swap(total[:, 256 * g : 256 * g + 256])
    flat[E_TOKEN : E_TOKEN + 48, :] = swap(by_token0[:, 0:256])
    mine[EM_SECOND : EM_SECOND + 64, :] = second1[...]
    mine[EM_SKIP : EM_SKIP + 8, :] = jnp.broadcast_to(jnp.sum(skip1[...], axis=0, keepdims=True), (8, 128))


def late_kernel(s, by_token12, second0, skip0, first0, mine, first_out):
    mine[L_TOKEN : L_TOKEN + 48, :] = by_token12[:, 0:128]
    mine[L_TOKEN + 48 : L_TOKEN + 96, :] = by_token12[:, 128:256]
    mine[L_SECOND : L_SECOND + 64, :] = second0[...]
    mine[L_SKIP : L_SKIP + 8, :] = jnp.broadcast_to(jnp.sum(skip0[...], axis=0, keepdims=True), (8, 128))
    first_out[:, 0:64] = first0[...]
    first_out[:, 64:128] = jnp.zeros((FIRST_ROWS, 64), f32)


def chip_kernel(s, flat, flat_in, mine, mine_in, out):
    first = s[CORE] == 0
    rows = flat.shape[0]
    total = flat[...] + flat_in[...]
    out[0:rows, 0 : total.shape[1]] = total
    if total.shape[1] == 128:
        out[0:rows, 128:256] = jnp.zeros((rows, 128), f32)
    out[rows:, 0:128] = jnp.where(first, mine[...], mine_in[...])
    out[rows:, 128:256] = jnp.where(first, mine_in[...], mine[...])


def last_kernel(
    s, early, early_in, late, late_in, embed, gain, own, peer, w_own, w_first, w_second,
    embed_out, gain_out, in_out, short_out, first_out, second_out, skip_out,
):
    pick = lambda x, y: jnp.where(s[CORE] == 0, x, y)

    def plain(pair, row, rows):
        return pair[0][row : row + rows, :] + pair[1][row : row + rows, :]

    def halves(pair, row, rows):
        here, there = pair
        left = here[row : row + rows, 0:128] + there[row : row + rows, 128:256]
        right = here[row : row + rows, 128:256] + there[row : row + rows, 0:128]
        return left, right

    early, late = (early, early_in), (late, late_in)
    gains1 = plain(early, E_GAIN1, 8)
    gains0 = plain(early, E_GAIN0, 8)
    gain_out[1, 0:1, :] = gains1[1:2, :]
    gain_out[1, 1:2, :] = gains1[0:1, :]
    gain_out[0, 1:2, :] = gains0[0:1, :]
    first_out[0] = plain(late, 0, FIRST_ROWS)[0:33, 0:64]
    first_out[1] = plain(early, E_FIRST, FIRST_ROWS)[0:33, 0:64]
    short = halves(early, E_SHORT, 16)[0]
    for t in range(3):
        short_out[1, t] = short[3 * t : 3 * t + 3, :]
    second_out[1] = halves(early, E_ROWS + EM_SECOND, 64)[0]
    second_out[0] = halves(late, FIRST_ROWS + L_SECOND, 64)[0]
    skip_out[0:1, :] = halves(late, FIRST_ROWS + L_SKIP, 8)[0][0:1]
    skip_out[1:2, :] = halves(early, E_ROWS + EM_SKIP, 8)[0][0:1]
    tokens = [
        halves(early, E_TOKEN, 48),
        halves(late, FIRST_ROWS + L_TOKEN, 48),
        halves(late, FIRST_ROWS + L_TOKEN + 48, 48),
    ]
    normal, scale = unit(embed[...])
    gain_row = gain[0, 0:1, :]
    low = (normal * gain_row).astype(bf16)
    grad_normed = jnp.zeros((16, 256), f32)
    for g in range(3):
        for h, pack in ((0, own), (1, peer)):
            grads = tokens[g][h]
            table = pack[16 * g : 16 * g + 16, :]
            summed = jnp.zeros((16, 128), f32)
            for t in range(3):
                row = PACK_SHORT + 3 * t + g
                part = grads[16 * t : 16 * t + 16, :]
                summed += pack[row : row + 1, :] * part
                if h == 0:
                    short_out[0, t, g : g + 1, :] = jnp.sum(table * part, axis=0, keepdims=True)
            high, rest = split(summed)
            if h == 0:
                in_out[g] = mm_tn(low, high) + mm_tn(low, rest)
                weight = w_own[0, g]
            else:
                rows = slice(1152 + 128 * g, 1280 + 128 * g)
                a, b = w_first[rows, :], w_second[rows, :]
                weight = jnp.concatenate([pick(a, b), pick(b, a)], axis=0).astype(bf16)
            grad_normed += mm_nt(high, weight) + mm_nt(rest, weight)
    gain_out[0, 0:1, :] = jnp.sum(grad_normed * normal, axis=0, keepdims=True)
    embed_out[...] = plain(early, E_EMBED, 16) + unit_back(grad_normed * gain_row, normal, scale)


def block_send_kernel(s, block_out, mine, other):
    spot = s[SPOT]
    mine[...] = block_out[at(HALO + 128 * spot, 128), :]
    near = spot + 1 - 2 * s[CORE]
    other[...] = block_out[at(HALO + 128 * near, 128), :]


def block_pick_kernel(s, mine, received, out):
    out[...] = jnp.where(s[HOLDER] == 1, mine[...], received[...])


def block_join_kernel(s, here, there, out):
    first = s[GROUP] == 0
    out[0] = jnp.where(first, here[...], there[...])
    out[1] = jnp.where(first, there[...], here[...])


def chip_local(
    ids, live, embed, norm_gain, in_weight, short_kernel, filter_first, filter_second, skip_gain,
    out_weight, up_weight, down_weight, cotangent,
):
    count = lax.axis_size("seq")
    rank = lax.axis_index("seq")
    group = lax.axis_index("ch")
    width = ids.shape[1]
    length = width * count
    half = length // 2
    span = half + 2 * HALO
    core = rank % 2
    across = lambda v: lax.ppermute(v, "ch", [(0, 1), (1, 0)])
    trade = lambda v, bit: lax.ppermute(v, "seq", [(i, i ^ bit) for i in range(count)])
    beside = lambda v: trade(v, 1)
    half_ranks = count // 2
    table = jnp.asarray(number_table(count))[rank, group]
    dft = jnp.asarray(dft_table()).astype(bf16)
    twiddle = jnp.asarray(twiddle_table())
    feats = jnp.asarray(feature_table(length))
    feats_turned = jnp.asarray(np.pad(feature_table(length).T, ((0, 40 - FEAT), (0, 0)))).astype(bf16)
    rates = jnp.asarray(rate_table())
    low = lambda *shape: arr(*shape, kind=bf16)
    line = pltpu.VMEM((length + 2 * HALO, 128), f32)
    conv_scratch = [stage_scratch(), spec_scratch(), line]

    s = run(numbers_kernel, arr(NUMBER_ROWS, 128, kind=jnp.int32), table, live.reshape(1, 2))
    row_shape = lambda rows: arr(rows, 8, width, kind=jnp.int32)
    own_ids = run(ids_kernel, row_shape(1), s, ids)
    in_own = jnp.swapaxes(in_weight, 1, 2)
    pack = run(pack_kernel, arr(PACK_ROWS, 128), s, embed, norm_gain, in_own, filter_second, short_kernel, skip_gain, after=(own_ids,))
    pack_in = across(pack)
    parts = run(
        send_weights_kernel, [arr(1536, 128), arr(1536, 128)], s, out_weight, up_weight, down_weight, in_own, hbm=(0, 1, 2, 3),
        scratch=[
            pltpu.VMEM(w.shape, w.dtype) for w in (out_weight, up_weight, down_weight, in_own)
        ] + [pltpu.SemaphoreType.DMA((4,))], after=(pack,),
    )
    parts_in = [across(parts[0])]
    all_ids = run(functools.partial(pair_kernel, 1), row_shape(2), s, own_ids, trade(own_ids, 2), after=(parts[0],))
    parts_in.append(across(parts[1]))
    all_ids = run(functools.partial(pair_kernel, 2), row_shape(4), s, all_ids, trade(all_ids, 4))
    sine, cosine, sine_turned = run(
        sine_kernel, [arr(length, 128), arr(length, 128), low(128, length)], s, feats, filter_first, after=(all_ids,)
    )
    all_ids = run(functools.partial(pair_kernel, 3), row_shape(8), s, all_ids, trade(all_ids, 8), after=(sine,))
    all_ids = run(functools.partial(pair_kernel, 0), row_shape(16), s, all_ids, beside(all_ids))

    cot = run(pick_kernel, arr(1, width, 256), s, cotangent, after=(sine,))
    cot = run(functools.partial(pair_kernel, 1), arr(2, width, 256), s, cot, trade(cot, 2), after=(all_ids,))
    cot = run(functools.partial(pair_kernel, 2), arr(4, width, 256), s, cot, trade(cot, 4))
    cot = run(functools.partial(pair_kernel, 0), arr(8, width, 256), s, cot, beside(cot))
    cot_far = lax.ppermute(cot, "seq", [(i, i ^ 8) for i in range(count) if i % 2 == i // half_ranks])

    onehot, turned = run(
        onehot_kernel, [low(length + 2 * HALO, 128), low(2, 128, half)], s, all_ids,
        scratch=[pltpu.VMEM((length + 2 * HALO, 128), f32)],
    )
    mine, other, conv_table, gate_table = run(
        table_kernel, [arr(PACK_ROWS, 128), arr(PACK_ROWS, 128), low(128, 256), low(128, 512)], s, pack, pack_in, embed,
    )
    filt0, filt1, freq0, freq1 = run(
        filter_kernel, [arr(length, 128), arr(length, 128), arr(*SPECTRUM), arr(*SPECTRUM)], s, sine, mine, rates, dft, twiddle,
        scratch=[stage_scratch(), spec_scratch()],
    )
    first_part = run(relay_kernel, arr(1536, 128), s, parts_in[0], after=(freq1,))
    first_beside = beside(first_part)
    conv_mine0, sent, spec0, product0 = run(
        conv_first_kernel, [arr(span, 128), arr(span, 128), arr(*SPECTRUM), arr(length, 128)],
        s, onehot, conv_table, mine, freq0, dft, twiddle, scratch=conv_scratch, after=(first_part,),
    )
    conv_other0 = beside(sent)
    w_out0, w_up0, w_down0, w_in1 = run(
        functools.partial(join_weights_kernel, 0), [low(256, 256), low(256, 1024), low(1024, 256), low(256, 768)],
        s, out_weight, up_weight, down_weight, in_own, first_part, first_beside, after=(sent,),
    )
    kept, sent, mid0, stream1, gates1, mixed1 = run(
        forward_first_kernel,
        [arr(half, 128), arr(half, 128), arr(span, 256), arr(span, 256), arr(span, 768), arr(span, 768)],
        s, onehot, gate_table, conv_mine0, conv_other0, norm_gain, w_out0, w_up0, w_down0, w_in1, mine, other,
    )
    received = beside(sent)
    second_part = run(relay_kernel, arr(1536, 128), s, parts_in[1], after=(sent,))
    second_beside = beside(second_part)
    conv_mine1, sent, spec1, product1 = run(
        conv_second_kernel, [arr(span, 128), arr(span, 128), arr(*SPECTRUM), arr(length, 128)],
        s, kept, received, mine, freq1, dft, twiddle, scratch=conv_scratch, after=(second_part,),
    )
    conv_other1 = beside(sent)
    w_out1, w_up1, w_down1 = run(
        functools.partial(join_weights_kernel, 1), [low(256, 256), low(256, 1024), low(1024, 256)],
        s, out_weight, up_weight, down_weight, in_own, second_part, second_beside, after=(sent,),
    )
    cot_rim = beside(run(rim_kernel, arr(HALO, 256), s, cot, cot_far, after=(sent,)))
    (kept, sent, grad_x0, grad_mid1, block, hidden, grad_low, normed, grad_pre, gated, mid_low, gain_mid1) = run(
        turn_back_kernel,
        [
            arr(half, 128), arr(half, 128), arr(span, 256), arr(span, 256), arr(span, 256), low(span, 1024), low(span, 256),
            low(span, 256), low(span, 1024), low(span, 256), low(span, 256), arr(8, 256),
        ],
        s, conv_mine1, conv_other1, gates1, stream1, cot, cot_far, cot_rim, norm_gain, w_out1, w_up1, w_down1,
        scratch=[pltpu.VMEM((span, 256), f32), pltpu.VMEM((span, 256), f32)],
    )
    received = beside(sent)
    grads_keep1, grads_send1 = run(
        functools.partial(wide_grads_kernel, HALO), [arr(2, 1152, 128), arr(2, 1152, 128)],
        s, gated, mid_low, normed, grad_pre, hidden, grad_low,
    )
    block_mine, block_other = run(block_send_kernel, [arr(width, 256), arr(width, 256)], s, block)
    grads_in1 = beside(grads_send1)
    block_beside = beside(block_other)

    prod_mine, sent, spec_grad1, grads1 = run(
        conv_back_kernel, [arr(span, 128), arr(span, 128), arr(*SPECTRUM), arr(length, 128)],
        s, kept, received, mine, freq1, dft, twiddle, scratch=conv_scratch, after=(grads_send1, block_mine),
    )
    prod_other = beside(sent)
    own1, peer1 = run(add_kernel, [arr(1152, 128), arr(1152, 128)], s, grads_keep1, grads_in1, after=(sent,))
    across1 = across(peer1)
    filter_shapes = [arr(64, 128), arr(40, 64), arr(8, 128)]
    filter_scratch = [stage_scratch(), spec_scratch(), pltpu.VMEM((length, 128), f32)]
    second1, first1, skip1 = run(
        filter_back_kernel, filter_shapes, s, spec_grad1, spec1, grads1, product1, filt1, cosine,
        sine_turned, mine, rates, feats_turned, dft, twiddle, scratch=filter_scratch, after=(peer1,),
    )
    grad_stream1, normed_in, mixed_low, short1, gain_in1 = run(
        back_gates_kernel,
        [arr(half, 256), low(half, 256), low(half, 768), arr(3, 8, 768), arr(8, 256)],
        s, prod_mine, prod_other, grad_x0, gates1, mixed1, grad_mid1, stream1, norm_gain, mine, other, w_in1,
        scratch=[pltpu.VMEM((span, 768), f32)], after=(skip1,),
    )
    in_keep, in_send = run(in_grads_kernel, [arr(2, 384, 128), arr(2, 384, 128)], s, normed_in, mixed_low)
    in_beside = beside(in_send)
    block_here = run(block_pick_kernel, arr(width, 256), s, block_mine, block_beside, after=(in_send,))
    block_across = across(block_here)
    (kept, sent, hidden, grad_low, normed, grad_pre, gated, mid_low, by_token0, gain_mid0) = run(
        back_first_kernel,
        [
            arr(half, 128), arr(half, 128), low(half, 1024), low(half, 256), low(half, 256), low(half, 1024), low(half, 256),
            low(half, 256), arr(48, 768), arr(8, 256),
        ],
        s, grad_stream1, mid0, onehot, turned, gate_table, conv_mine0, conv_other0, norm_gain, w_out0, w_up0, w_down0,
        after=(in_send, block_here),
    )
    received = beside(sent)
    block_out = run(block_join_kernel, arr(2, width, 256), s, block_here, block_across, after=(sent,))
    grads_keep0, grads_send0 = run(
        functools.partial(wide_grads_kernel, 0), [arr(2, 1152, 128), arr(2, 1152, 128)],
        s, gated, mid_low, normed, grad_pre, hidden, grad_low, after=(block_out,),
    )
    grads_in0 = beside(grads_send0)
    in_own1, in_peer1 = run(add_kernel, [arr(384, 128), arr(384, 128)], s, in_keep, in_beside, after=(grads_send0,))
    in_across = across(in_peer1)
    early_flat, early_mine = run(
        early_kernel, [arr(E_ROWS, 256), arr(EM_ROWS, 128)],
        s, gain_mid1, gain_in1, gain_mid0, by_token0, first1, short1, second1, skip1, after=(in_peer1,),
    )
    early_flat_in, early_mine_in = beside(early_flat), beside(early_mine)
    spec_grad0, grads0 = run(
        grad_freq_kernel, [arr(*SPECTRUM), arr(length, 128)], s, kept, received, dft, twiddle, scratch=[stage_scratch()],
        after=(grads_send0, in_peer1, early_flat),
    )
    own0, peer0 = run(add_kernel, [arr(1152, 128), arr(1152, 128)], s, grads_keep0, grads_in0, after=(spec_grad0,))
    across0 = across(peer0)
    early = run(chip_kernel, arr(E_ROWS + EM_ROWS, 256), s, early_flat, early_flat_in, early_mine, early_mine_in, after=(peer0,))
    early_in = across(early)
    total1 = run(add_one_kernel, arr(1152, 128), s, own1, across1, after=(peer0,))
    in_total = run(add_one_kernel, arr(384, 128), s, in_own1, in_across, after=(peer0,))
    total1_beside, in_total_beside = beside(total1), beside(in_total)
    second0, first0, skip0, by_token12 = run(
        token_back_kernel, filter_shapes + [arr(48, 256)], s, spec_grad0, spec0, grads0, product0, filt0, cosine,
        sine_turned, mine, rates, feats_turned, dft, twiddle, freq0, onehot, turned, conv_table, scratch=filter_scratch,
        after=(peer0, early, total1, in_total),
    )
    late_mine, late_first = run(late_kernel, [arr(L_ROWS, 128), arr(FIRST_ROWS, 128)], s, by_token12, second0, skip0, first0, after=(early_in,))
    late = run(chip_kernel, arr(FIRST_ROWS + L_ROWS, 256), s, late_first, beside(late_first), late_mine, beside(late_mine))
    late_in = across(late)
    total0 = run(add_one_kernel, arr(1152, 128), s, own0, across0, after=(late,))
    total0_beside = beside(total0)
    grad_out, grad_up, grad_down = run(
        spread_wide_kernel, [arr(2, 128, 256), arr(2, 256, 512), arr(2, 512, 256)],
        s, total1, total1_beside, total0, total0_beside,
    )
    grad_embed, grad_gain, grad_in0, grad_short, grad_first, grad_second, grad_skip = run(
        last_kernel,
        [
            arr(16, 256), arr(2, 2, 256), arr(3, 256, 128), arr(2, 3, 3, 128), arr(2, FEAT, 64), arr(2, 64, 128), arr(2, 128),
        ],
        s, early, early_in, late, late_in, embed, norm_gain, pack, pack_in, in_own, second_part, second_beside,
    )
    grad_in = run(spread_in_kernel, arr(2, 3, 256, 128), s, grad_in0, in_total, in_total_beside)
    return (
        block_out,
        grad_embed,
        grad_gain,
        jnp.swapaxes(grad_in, 1, 2),
        grad_short,
        grad_first,
        grad_second,
        grad_skip,
        grad_out,
        grad_up,
        grad_down,
    )


def solution(mesh):
    in_specs = (
        P(None, "seq"),
        P(),
        P(),
        P(),
        P(None, None, None, "ch"),
        P(None, None, None, "ch"),
        P(),
        P(None, None, "ch"),
        P(None, "ch"),
        P(None, "ch", None),
        P(None, None, "ch"),
        P(None, "ch", None),
        P(None, "seq", None),
    )
    out_specs = (
        P(None, "seq", None),
        P(),
        P(),
        P(None, None, None, "ch"),
        P(None, None, None, "ch"),
        P(),
        P(None, None, "ch"),
        P(None, "ch"),
        P(None, "ch", None),
        P(None, None, "ch"),
        P(None, "ch", None),
    )

    def either(*args):
        length = args[0].shape[1] * lax.axis_size("seq")
        near = length == BLOCKS * BLOCK and lax.axis_size("seq") == 16
        return (chip_local if near else local)(*args)

    return jax.shard_map(either, mesh=mesh, in_specs=in_specs, out_specs=out_specs, check_vma=False)
```

```python
import functools
import math

import jax
import jax.numpy as jnp
import numpy as np
from jax import lax
from jax.experimental import pallas as pl
from jax.experimental.pallas import tpu as pltpu
from jax.sharding import PartitionSpec as P

D = 256
FEAT = 33


precise = lax.Precision.HIGHEST
epsilon = 1e-05


def passed_along(value, axis, steps):
    count = lax.axis_size(axis)
    leading, last = (max(0, -steps), min(count, count - steps))
    return lax.ppermute(value, axis, [(source, source + steps) for source in range(leading, last)])


def layer_norm(inputs, gain_vec):
    center = inputs - jnp.mean(inputs, axis=-1, keepdims=True)
    spread = jnp.mean(center * center, axis=-1, keepdims=True)
    return center * lax.rsqrt(spread + epsilon) * gain_vec


def position_features(length):
    places = jnp.arange(length, dtype=jnp.int32)
    band_ids = jnp.arange(1, (FEAT - 1) // 2 + 1, dtype=jnp.int32)
    turn_counts = places[:, None] * band_ids[None, :] % length
    angles = turn_counts.astype(jnp.float32) * (2.0 * math.pi / length)
    ramp_vals = places.astype(jnp.float32)[:, None] / length
    return jnp.concatenate([ramp_vals, jnp.cos(angles), jnp.sin(angles)], axis=1)


def decay_rates(channels):
    return 0.3 * 10.0 ** (channels.astype(jnp.float32) / (D - 1))


def dft_tables(blocks, block_len):
    doubled = 2 * blocks
    span_total = doubled * block_len
    frequency = jnp.arange(doubled, dtype=jnp.int32)
    places = jnp.arange(blocks, dtype=jnp.int32)
    inner_idx = jnp.arange(block_len, dtype=jnp.int32)
    outer_angle = (frequency[:, None] * places[None, :] % doubled).astype(jnp.float32) * (
        2.0 * math.pi / doubled
    )
    twist_angle = (frequency[:, None] * inner_idx[None, :] % span_total).astype(jnp.float32) * (
        2.0 * math.pi / span_total
    )
    inner_angle = (inner_idx[:, None] * inner_idx[None, :] % block_len).astype(jnp.float32) * (
        2.0 * math.pi / block_len
    )
    return (
        jnp.cos(outer_angle),
        jnp.sin(outer_angle),
        jnp.cos(twist_angle),
        jnp.sin(twist_angle),
        jnp.cos(inner_angle),
        jnp.sin(inner_angle),
    )


def along_block(values, table):
    return jnp.einsum("...kb,bj->...kj", values, table, precision=precise)


def to_spectrum(signal, tables):
    outer_cos, outer_sin, twist_cos, twist_sin, inner_cos, inner_sin = tables
    first_re = jnp.einsum("kp,...pb->...kb", outer_cos, signal, precision=precise)
    first_im = -jnp.einsum("kp,...pb->...kb", outer_sin, signal, precision=precise)
    turned_re = first_re * twist_cos + first_im * twist_sin
    turned_im = first_im * twist_cos - first_re * twist_sin
    spec_re = along_block(turned_re, inner_cos) + along_block(turned_im, inner_sin)
    spec_im = along_block(turned_im, inner_cos) - along_block(turned_re, inner_sin)
    return (spec_re, spec_im)


def from_spectrum(spec_re, spec_im, tables):
    outer_cos, outer_sin, twist_cos, twist_sin, inner_cos, inner_sin = tables
    back_re = along_block(spec_re, inner_cos) - along_block(spec_im, inner_sin)
    back_im = along_block(spec_re, inner_sin) + along_block(spec_im, inner_cos)
    turned_re = back_re * twist_cos - back_im * twist_sin
    turned_im = back_re * twist_sin + back_im * twist_cos
    scale_back = 1.0 / (outer_cos.shape[0] * inner_cos.shape[0])
    signal = jnp.einsum("kp,...kb->...pb", outer_cos, turned_re, precision=precise) - jnp.einsum(
        "kp,...kb->...pb", outer_sin, turned_im, precision=precise
    )
    return signal * scale_back


def causal_filter(received, filt_spec, skip_part, tables):
    item_count, chan_count, length = received.shape
    blocks = tables[0].shape[1]
    spec_re, spec_im = to_spectrum(
        received.reshape(item_count, chan_count, blocks, length // blocks), tables
    )
    prod_re = spec_re * filt_spec[0] - spec_im * filt_spec[1]
    prod_im = spec_re * filt_spec[1] + spec_im * filt_spec[0]
    result_sig = from_spectrum(prod_re, prod_im, tables).reshape(item_count, chan_count, length)
    return result_sig + skip_part[:, None] * received


def filter_backward(grad_cols, moved_in, filt_spec, skip_part, tables):
    item_count, chan_count, length = grad_cols.shape
    blocks = tables[0].shape[1]
    grad_re, grad_im = to_spectrum(
        grad_cols.reshape(item_count, chan_count, blocks, length // blocks), tables
    )
    input_re, input_im = to_spectrum(
        moved_in.reshape(item_count, chan_count, blocks, length // blocks), tables
    )
    back_re = grad_re * filt_spec[0] + grad_im * filt_spec[1]
    back_im = grad_im * filt_spec[0] - grad_re * filt_spec[1]
    grad_u_cols = (
        from_spectrum(back_re, back_im, tables).reshape(item_count, chan_count, length)
        + skip_part[:, None] * grad_cols
    )
    corr_re = grad_re * input_re + grad_im * input_im
    corr_im = grad_im * input_re - grad_re * input_im
    grad_filt = jnp.sum(from_spectrum(corr_re, corr_im, tables), axis=0).reshape(chan_count, length)
    grad_skip_part = jnp.sum(grad_cols * moved_in, axis=(0, 2))
    return (grad_u_cols, grad_filt, grad_skip_part)


def local_filter(first, second, features, select, group_idx, chan_local):
    hidden_pre = jnp.dot(features, first, precision=precise)
    hidden_act = jnp.sin(hidden_pre)
    chan_width = second.shape[1]
    second_part = jnp.dot(second, select, precision=precise)
    channel_ids = group_idx * chan_width + chan_local
    length = features.shape[0]
    ramp_vals = jnp.arange(length, dtype=jnp.int32).astype(jnp.float32) / length
    decay_part = jnp.exp(-decay_rates(channel_ids)[:, None] * ramp_vals[None, :])
    filt_cols = jnp.einsum("hc,th->ct", second_part, hidden_act, precision=precise) * decay_part
    return (filt_cols, hidden_pre, hidden_act, second_part, decay_part)


def filter_mlp_backward(grad_filt, features, filter_parts):
    hidden_pre, hidden_act, second_part, decay_part = filter_parts
    grad_shaped = grad_filt * decay_part
    grad_second_part = jnp.einsum("ct,th->hc", grad_shaped, hidden_act, precision=precise)
    grad_act = jnp.einsum("ct,hc->th", grad_shaped, second_part, precision=precise)
    grad_first = jnp.einsum(
        "tf,th->fh", features, grad_act * jnp.cos(hidden_pre), precision=precise
    )
    return (grad_first, grad_second_part)


def embed_lookup(ids, live, embed, seq_rank):
    tok_rows = ids.shape[1]
    places = seq_rank * tok_rows + jnp.arange(tok_rows, dtype=jnp.int32)
    keep_mask = (places[None, :] < live[:, None]).astype(jnp.float32)
    vocab_ids = jnp.arange(embed.shape[0], dtype=jnp.int32)
    onehot = (ids[:, :, None] == vocab_ids[None, None, :]).astype(jnp.float32) * keep_mask[
        :, :, None
    ]
    stream = jnp.einsum("mtv,vd->mtd", onehot, embed, precision=precise)
    return (stream, onehot, keep_mask)


def channel_total(partial_sum):
    return lax.psum(partial_sum, "ch")


def input_total(partial_sum):
    return lax.psum(partial_sum, "ch")


def layer_forward(stream, params, filt_spec, skip_part, tables):
    norm_gains, w_in, kernel, w_out, w_up, w_down = params
    normed = layer_norm(stream, norm_gains[0]).astype(jnp.bfloat16)
    mixed_in = jnp.einsum("mtd,dgc->mtgc", normed, w_in, preferred_element_type=jnp.float32)
    rim_rows = passed_along(mixed_in[:, -2:], "seq", 1)
    padded = jnp.concatenate([rim_rows, mixed_in], axis=1)
    micro_count, tok_rows = (mixed_in.shape[0], mixed_in.shape[1])
    chan_width = mixed_in.shape[3]
    gate_vals = (
        kernel[0] * mixed_in
        + kernel[1] * padded[:, 1 : tok_rows + 1]
        + kernel[2] * padded[:, 0:tok_rows]
    )
    product_in = gate_vals[:, :, 2] * gate_vals[:, :, 1]
    flat_rows = jnp.swapaxes(product_in, 1, 2).reshape(1, micro_count * chan_width, tok_rows)
    received = lax.all_to_all(flat_rows, "seq", split_axis=1, concat_axis=2, tiled=True)
    result_sig = causal_filter(received, filt_spec, skip_part, tables)
    conv_flat = lax.all_to_all(result_sig, "seq", split_axis=2, concat_axis=1, tiled=True)
    conv_out = jnp.swapaxes(conv_flat.reshape(micro_count, chan_width, tok_rows), 1, 2)
    gated_out = (conv_out * gate_vals[:, :, 0]).astype(jnp.bfloat16)
    mid_state = stream + channel_total(
        jnp.einsum("mtc,cd->mtd", gated_out, w_out, preferred_element_type=jnp.float32)
    )
    normed_mid = layer_norm(mid_state, norm_gains[1]).astype(jnp.bfloat16)
    pre_act = jnp.einsum("mtd,df->mtf", normed_mid, w_up, preferred_element_type=jnp.float32)
    hidden = jax.nn.gelu(pre_act).astype(jnp.bfloat16)
    new_stream = mid_state + channel_total(
        jnp.einsum("mtf,fd->mtd", hidden, w_down, preferred_element_type=jnp.float32)
    )
    kept_vals = (
        stream,
        normed,
        mixed_in,
        padded,
        gate_vals,
        received,
        conv_out,
        gated_out,
        mid_state,
        normed_mid,
        pre_act,
        hidden,
    )
    return (new_stream, kept_vals)


def layer_backward(grad_stream, kept_vals, params, filt_spec, skip_part, tables):
    norm_gains, w_in, kernel, w_out, w_up, w_down = params
    (
        stream,
        normed,
        mixed_in,
        padded,
        gate_vals,
        moved_in,
        conv_out,
        gated_out,
        mid_state,
        normed_mid,
        pre_act,
        hidden,
    ) = kept_vals
    micro_count, tok_rows = (mixed_in.shape[0], mixed_in.shape[1])
    chan_width = mixed_in.shape[3]
    grad_low = grad_stream.astype(jnp.bfloat16)
    grad_down = jnp.einsum("mtf,mtd->fd", hidden, grad_low, preferred_element_type=jnp.float32)
    grad_hidden = jnp.einsum("mtd,fd->mtf", grad_low, w_down, preferred_element_type=jnp.float32)
    _, gelu_back = jax.vjp(jax.nn.gelu, pre_act)
    grad_pre = gelu_back(grad_hidden)[0].astype(jnp.bfloat16)
    grad_up = jnp.einsum("mtd,mtf->df", normed_mid, grad_pre, preferred_element_type=jnp.float32)
    grad_normed_mid = input_total(
        jnp.einsum("mtf,df->mtd", grad_pre, w_up, preferred_element_type=jnp.float32)
    )
    _, norm_back_mid = jax.vjp(layer_norm, mid_state, norm_gains[1])
    grad_mid_norm, grad_gain_mid = norm_back_mid(grad_normed_mid)
    grad_mid = grad_stream + grad_mid_norm
    grad_mid_low = grad_mid.astype(jnp.bfloat16)
    grad_out = jnp.einsum(
        "mtc,mtd->cd", gated_out, grad_mid_low, preferred_element_type=jnp.float32
    )
    grad_gated = jnp.einsum("mtd,cd->mtc", grad_mid_low, w_out, preferred_element_type=jnp.float32)
    grad_conv = grad_gated * gate_vals[:, :, 0]
    grad_first_gate = grad_gated * conv_out
    grad_flat = jnp.swapaxes(grad_conv, 1, 2).reshape(1, micro_count * chan_width, tok_rows)
    grad_cols = lax.all_to_all(grad_flat, "seq", split_axis=1, concat_axis=2, tiled=True)
    grad_u_cols, grad_filt, grad_skip_part = filter_backward(
        grad_cols, moved_in, filt_spec, skip_part, tables
    )
    grad_back_flat = lax.all_to_all(grad_u_cols, "seq", split_axis=2, concat_axis=1, tiled=True)
    grad_product = jnp.swapaxes(grad_back_flat.reshape(micro_count, chan_width, tok_rows), 1, 2)
    grad_gates = jnp.stack(
        [grad_first_gate, grad_product * gate_vals[:, :, 2], grad_product * gate_vals[:, :, 1]],
        axis=2,
    )
    rim_back = passed_along(grad_gates[:, :2], "seq", -1)
    extended = jnp.concatenate([grad_gates, rim_back], axis=1)
    grad_mixed = (
        kernel[0] * grad_gates
        + kernel[1] * extended[:, 1 : tok_rows + 1]
        + kernel[2] * extended[:, 2 : tok_rows + 2]
    )
    grad_kernel = jnp.stack(
        [
            jnp.sum(grad_gates * mixed_in, axis=(0, 1)),
            jnp.sum(grad_gates * padded[:, 1 : tok_rows + 1], axis=(0, 1)),
            jnp.sum(grad_gates * padded[:, 0:tok_rows], axis=(0, 1)),
        ]
    )
    grad_mixed_low = grad_mixed.astype(jnp.bfloat16)
    grad_in = jnp.einsum(
        "mtd,mtgc->dgc", normed, grad_mixed_low, preferred_element_type=jnp.float32
    )
    grad_normed = input_total(
        jnp.einsum("mtgc,dgc->mtd", grad_mixed_low, w_in, preferred_element_type=jnp.float32)
    )
    _, norm_back_in = jax.vjp(layer_norm, stream, norm_gains[0])
    grad_stream_norm, grad_gain_in = norm_back_in(grad_normed)
    grad_before = grad_mid + grad_stream_norm
    layer_grads = (
        jnp.stack([grad_gain_in, grad_gain_mid]),
        grad_in,
        grad_kernel,
        grad_skip_part,
        grad_out,
        grad_up,
        grad_down,
    )
    return (grad_before, layer_grads, grad_filt)


def local(
    ids,
    live,
    embed,
    norm_gain,
    in_weight,
    short_kernel,
    filter_first,
    filter_second,
    skip_gain,
    out_weight,
    up_weight,
    down_weight,
    cotangent,
):
    seq_count = lax.axis_size("seq")
    seq_rank = lax.axis_index("seq")
    group_idx = lax.axis_index("ch")
    micro_count = ids.shape[0]
    tok_rows = ids.shape[1]
    length = tok_rows * seq_count
    chan_width = in_weight.shape[3]
    own_rows = micro_count * chan_width // seq_count
    layer_count = in_weight.shape[0]
    row_start = seq_rank * own_rows
    row_ids = row_start + jnp.arange(own_rows, dtype=jnp.int32)
    chan_local = row_ids % chan_width
    first_rows = (row_ids < chan_width).astype(jnp.float32)
    select = (jnp.arange(chan_width, dtype=jnp.int32)[:, None] == chan_local[None, :]).astype(
        jnp.float32
    )
    tables = dft_tables(seq_count, tok_rows)
    features = position_features(length)
    ramp_row = jnp.arange(length, dtype=jnp.int32).astype(jnp.float32) / length
    stream, onehot, keep_mask = embed_lookup(ids, live, embed, seq_rank)
    filters = []
    for level_idx in range(layer_count):
        filt_cols, hidden_pre, hidden_act, second_part, decay_part = local_filter(
            filter_first[level_idx],
            filter_second[level_idx],
            features,
            select,
            group_idx,
            chan_local,
        )
        filt_spec = to_spectrum(filt_cols.reshape(own_rows, seq_count, tok_rows), tables)
        skip_part = jnp.dot(skip_gain[level_idx], select, precision=precise)
        penalty_grad = 0.5 * length * ramp_row[None, :] * filt_cols * first_rows[:, None]
        params = (
            norm_gain[level_idx],
            in_weight[level_idx],
            short_kernel[level_idx],
            out_weight[level_idx],
            up_weight[level_idx],
            down_weight[level_idx],
        )
        filters.append(
            (
                params,
                filt_spec,
                skip_part,
                (hidden_pre, hidden_act, second_part, decay_part),
                penalty_grad,
            )
        )
    stored = []
    for level_idx in range(layer_count):
        params, filt_spec, skip_part, _, _ = filters[level_idx]
        layer_input = stream
        stream, kept_vals = layer_forward(stream, params, filt_spec, skip_part, tables)
        stored.append(layer_input)
    block_out = stream * keep_mask[:, :, None]
    grad_stream = cotangent * keep_mask[:, :, None]
    collected = [None] * layer_count
    first_grads = [None] * layer_count
    grad_embed = None
    for level_idx in reversed(range(layer_count)):
        params, filt_spec, skip_part, filter_parts, penalty_grad = filters[level_idx]
        _, kept_vals = layer_forward(stored[level_idx], params, filt_spec, skip_part, tables)
        grad_stream, layer_grads, grad_filt = layer_backward(
            grad_stream, kept_vals, params, filt_spec, skip_part, tables
        )
        grad_first, grad_second_part = filter_mlp_backward(
            grad_filt + penalty_grad, features, filter_parts
        )
        first_grads[level_idx] = grad_first
        grad_second = jnp.dot(grad_second_part, select.T, precision=precise)
        grad_skip = jnp.dot(layer_grads[3], select.T, precision=precise)
        gain_grad, in_grad, kernel_grad, _, out_grad, up_grad, down_grad = layer_grads
        if level_idx == 0:
            embed_part = jnp.einsum("mtv,mtd->vd", onehot, grad_stream, precision=precise)
            summed = lax.psum(
                (
                    gain_grad,
                    in_grad,
                    kernel_grad,
                    grad_second,
                    grad_skip,
                    out_grad,
                    up_grad,
                    down_grad,
                    embed_part,
                ),
                "seq",
            )
            collected[level_idx] = summed[:8]
            grad_embed = summed[8]
        else:
            collected[level_idx] = lax.psum(
                (
                    gain_grad,
                    in_grad,
                    kernel_grad,
                    grad_second,
                    grad_skip,
                    out_grad,
                    up_grad,
                    down_grad,
                ),
                "seq",
            )
    stacked = [
        jnp.stack([collected[level_idx][member] for level_idx in range(layer_count)])
        for member in range(8)
    ]
    filter_grads = lax.psum(jnp.stack(first_grads), ("seq", "ch"))
    return (
        block_out,
        grad_embed,
        stacked[0],
        stacked[1],
        stacked[2],
        filter_grads,
        stacked[3],
        stacked[4],
        stacked[5],
        stacked[6],
        stacked[7],
    )


HALO = 16
ROOT_HALF = math.sqrt(0.5)
GELU_A = math.sqrt(2.0 / math.pi)
GELU_B = 0.044715
BLOCKS = 8
BLOCK = 256
KINDS = 9
VMEM_LIMIT = 8 * 2**20
VMEM_LIMITS = dict(turn_back_kernel=20 * 2**20, back_first_kernel=16 * 2**20)
FLOPS, FEW_FLOPS, MANY_FLOPS = 10**10, 10**8, 10**12
f32 = jnp.float32
bf16 = jnp.bfloat16


class Numbers:
    def __init__(self, table):
        self.table = table

    def __getitem__(self, row):
        return self.table[row, 0]


CORE, GROUP, LIVE, WHICH, SPOT, HOLDER, BIT1, BIT2, BIT3 = range(9)
NUMBER_ROWS = 16


def bring(pairs, done):
    copies = [pltpu.make_async_copy(far, near, done.at[i]) for i, (far, near) in enumerate(pairs)]
    for copy in copies:
        copy.start()
    for copy in copies:
        copy.wait()


def numbers_kernel(*refs):
    far, (table, own_ids, cot, pack), near, done = refs[:9], refs[9:13], refs[13:21], refs[21]
    far_live, far_ids, far_cot, far_embed, far_gain, far_in, far_second, far_short, far_skip = far
    live, ids, embed, gain, in_own, second, short, skip = near
    rank, group = lax.axis_index("seq"), lax.axis_index("ch")
    bring(
        (
            (far_live, live), (far_ids, ids), (far_cot.at[group], cot.at[0]), (far_embed, embed), (far_gain, gain),
            (far_in.at[0], in_own), (far_second, second), (far_short, short), (far_skip, skip),
        ),
        done,
    )
    fill_pack(embed, gain, in_own, second, short, skip, pack)
    core, half = rank % 2, lax.axis_size("seq") // 2
    first = group == 0
    holder = jnp.where(rank // half == core, 1, 0)
    values = (core, group, None, group + core - 2 * group * core, rank % half, holder, rank // 2 % 2, rank // 4 % 2, rank // 8 % 2)
    for row, value in enumerate(values):
        if row != LIVE:
            table[row : row + 1, :] = jnp.full((1, 128), value, jnp.int32)
    chosen = jnp.where(first, live[0:1, 0:1], live[0:1, 1:2])
    table[LIVE : LIVE + 1, :] = jnp.broadcast_to(chosen, (1, 128))
    own_ids[0] = jnp.broadcast_to(jnp.where(first, ids[0:1, :], ids[1:2, :]), own_ids.shape[1:])


def in_hbm(value):
    return pltpu.with_memory_space_constraint(value, pltpu.HBM)


def start(body, outs, *arrays, scratch):
    vmem, far = pl.BlockSpec(memory_space=pltpu.VMEM), pl.BlockSpec(memory_space=pltpu.HBM)
    return pl.pallas_call(
        body, out_shape=outs, in_specs=[far] * len(arrays), out_specs=[vmem] * len(outs), name=body.__name__,
        scratch_shapes=list(scratch),
        cost_estimate=pl.CostEstimate(flops=MANY_FLOPS, bytes_accessed=1, transcendentals=0),
        compiler_params=pltpu.CompilerParams(vmem_limit_bytes=VMEM_LIMIT),
    )(*(in_hbm(v) for v in arrays))


def run(body, outs, scalars, *arrays, scratch=(), after=(), hbm=(), flops=FLOPS, hbm_outs=(), aliases=(), token=False):
    vmem = pl.BlockSpec(memory_space=pltpu.VMEM)
    far, wait = pl.BlockSpec(memory_space=pltpu.HBM), pl.BlockSpec(memory_space=pl.ANY)
    single = not isinstance(outs, (list, tuple))
    shapes = [outs] if single else list(outs)
    count = len(shapes)
    shapes += [arr(8, 128)] * token
    used, waits = 1 + len(arrays), len(after)

    def call(table, *refs):
        given, rest = refs[: used - 1], refs[used - 1 + waits :]
        body(Numbers(table), *given, *rest[:count], *rest[count + token :])
        if token:
            rest[count][...] = jnp.zeros((8, 128), f32)

    inner = getattr(body, "func", body)
    result = pl.pallas_call(
        call,
        out_shape=shapes,
        in_specs=[vmem] + [far if i in hbm else vmem for i in range(len(arrays))] + [wait] * waits,
        out_specs=[far if i in hbm_outs else vmem for i in range(len(shapes))],
        input_output_aliases={1 + a: b for a, b in aliases},
        scratch_shapes=list(scratch),
        compiler_params=pltpu.CompilerParams(vmem_limit_bytes=VMEM_LIMITS.get(inner.__name__, VMEM_LIMIT)),
        cost_estimate=pl.CostEstimate(flops=flops, bytes_accessed=1, transcendentals=0),
        name=inner.__name__,
    )(scalars, *(in_hbm(v) if i in hbm else v for i, v in enumerate(arrays)), *after)
    return result[0] if len(shapes) == 1 else result


def arr(*shape, kind=f32):
    return jax.ShapeDtypeStruct(shape, kind)


def mm(a, b):
    return jnp.dot(a, b, preferred_element_type=f32)


def mm_nt(a, b):
    return lax.dot_general(a, b, (((1,), (1,)), ((), ())), preferred_element_type=f32)


def mm_tn(a, b):
    return lax.dot_general(a, b, (((0,), (0,)), ((), ())), preferred_element_type=f32)


def split(a):
    high = a.astype(bf16)
    return high, (a - high.astype(f32)).astype(bf16)


def mm3(a, b):
    a_high, a_low = split(a)
    b_high, b_low = split(b)
    return mm(a_high, b_high) + (mm(a_low, b_high) + mm(a_high, b_low))


def unit(rows):
    center = rows - jnp.mean(rows, axis=-1, keepdims=True)
    scale = lax.rsqrt(jnp.mean(center * center, axis=-1, keepdims=True) + epsilon)
    return center * scale, scale


def unit_back(grad, normal, scale):
    inner = jnp.mean(grad * normal, axis=-1, keepdims=True)
    return scale * (grad - jnp.mean(grad, axis=-1, keepdims=True) - normal * inner)


def every(count, step):
    for i in range(count):
        step(i, 0)


def at(start, size, unit_rows=16):
    return pl.ds(start if isinstance(start, int) else pl.multiple_of(start, unit_rows), size)


def dft_table():
    turns = np.outer(np.arange(BLOCK), np.arange(BLOCK)) % BLOCK
    angle = 2.0 * np.pi * turns / BLOCK
    return np.concatenate([np.cos(angle), np.sin(angle)], axis=1).astype(np.float32)


def twiddle_table():
    angle = 2.0 * np.pi * np.outer(np.arange(1, KINDS), np.arange(BLOCK)) / (2 * BLOCKS * BLOCK)
    pair = np.stack([np.cos(angle), np.sin(angle)], axis=1).astype(np.float32)
    return np.broadcast_to(pair[..., None], (KINDS - 1, 2, BLOCK, 128)).copy()


def feature_table(length):
    places = np.arange(length)
    turns = np.outer(places, np.arange(1, (FEAT - 1) // 2 + 1)) % length
    angle = 2.0 * np.pi * turns / length
    ramp = places[:, None] / length
    return np.concatenate([ramp, np.cos(angle), np.sin(angle)], axis=1).astype(np.float32)


def rate_table():
    return (0.3 * 10.0 ** (np.arange(D) / (D - 1))).astype(np.float32).reshape(2, 1, D // 2)


def four_real(a, b, c, d):
    s, m, t, n = a + c, a - c, b + d, b - d
    hn, ht = ROOT_HALF * n, ROOT_HALF * t
    return (s + t, s - t, (a + hn, -(ht + c)), (m, -n), (a - hn, c - ht))


def turn(k):
    angle = 2.0 * math.pi * k / (2 * BLOCKS)
    return math.cos(angle), math.sin(angle)


def put_pair(stage, kind, row, re, im):
    rows = re.shape[0]
    re, im = re.astype(bf16), im.astype(bf16)
    stage[kind, pl.ds(row, rows), 0:128] = re
    stage[kind, pl.ds(row, rows), 128:256] = im
    stage[kind, pl.ds(row + BLOCK, rows), 0:128] = im
    stage[kind, pl.ds(row + BLOCK, rows), 128:256] = -re


def put_pair_back(stage, kind, row, re, im):
    rows = re.shape[0]
    re, im = re.astype(bf16), im.astype(bf16)
    stage[kind, pl.ds(row, rows), 0:128] = re
    stage[kind, pl.ds(row, rows), 128:256] = im
    stage[kind, pl.ds(row + BLOCK, rows), 0:128] = -im
    stage[kind, pl.ds(row + BLOCK, rows), 128:256] = re


def all_kinds(dft, stage, out):
    table = dft[...]
    for kind in range(KINDS):
        out[kind] = mm(table, stage[kind])


def to_freq(load, dft, twiddle, stage, out):
    def chunk(step, carry):
        row = pl.multiple_of(step * 16, 16)
        u = [load(p, row) for p in range(BLOCKS)]
        e0, e4, e1, e2, e3 = four_real(u[0], u[2], u[4], u[6])
        o0, o4, o1, o2, o3 = four_real(u[1], u[3], u[5], u[7])

        def put(kind, re, im):
            c, s = twiddle[kind - 1, 0, pl.ds(row, 16), :], twiddle[kind - 1, 1, pl.ds(row, 16), :]
            put_pair(stage, kind, row, re * c + im * s, im * c - re * s)

        put_pair(stage, 0, row, e0 + o0, jnp.zeros_like(e0))
        last = e0 - o0
        c, s = twiddle[7, 0, pl.ds(row, 16), :], twiddle[7, 1, pl.ds(row, 16), :]
        put_pair(stage, 8, row, last * c, -(last * s))
        put(4, e4, -o4)
        for k, (er, ei), (orr, oi) in ((1, e1, o1), (2, e2, o2), (3, e3, o3)):
            c, s = turn(k)
            wr, wi = orr * c + oi * s, oi * c - orr * s
            put(k, er + wr, ei + wi)
            put(8 - k, er - wr, wi - ei)
        return carry

    lax.fori_loop(0, BLOCK // 16, chunk, 0)
    all_kinds(dft, stage, out)


def from_freq(dft, twiddle, stage, back, store):
    all_kinds(dft, stage, back)

    def chunk(step, carry):
        row = pl.multiple_of(step * 16, 16)

        def get(kind):
            re = back[kind, pl.ds(row, 16), 0:128]
            im = back[kind, pl.ds(row, 16), 128:256]
            c, s = twiddle[kind - 1, 0, pl.ds(row, 16), :], twiddle[kind - 1, 1, pl.ds(row, 16), :]
            return re * c - im * s, re * s + im * c

        first = 0.5 * back[0, pl.ds(row, 16), 0:128]
        last = 0.5 * get(8)[0]
        mid_re, mid_im = get(4)
        even, odd = {}, {}
        for k in (1, 2, 3):
            ar, ai = get(k)
            br, bi = get(8 - k)
            even[k] = (ar + br, ai - bi)
            c, s = turn(k)
            dr, di = ar - br, ai + bi
            odd[k] = (dr * c - di * s, dr * s + di * c)
        for shift, base, extra, part in (
            (0, first + last, mid_re, even),
            (1, first - last, -mid_im, odd),
        ):
            (r1, i1), (r2, i2), (r3, i3) = part[1], part[2], part[3]
            plus, minus = base + extra, base - extra
            diff, both = ROOT_HALF * (r1 - r3), ROOT_HALF * (i1 + i3)
            store(shift, row, plus + (r1 + r2 + r3))
            store(shift + 2, row, minus - i2 + (diff - both))
            store(shift + 4, row, plus - r2 - (i1 - i3))
            store(shift + 6, row, minus + i2 - (diff + both))
        return carry

    lax.fori_loop(0, BLOCK // 16, chunk, 0)


def times(first, second, stage, conj):
    def chunk(step, carry):
        row = pl.multiple_of(step * 16, 16)
        for kind in range(KINDS):
            fr = first[kind, pl.ds(row, 16), 0:128]
            fi = first[kind, pl.ds(row, 16), 128:256]
            ur = second[kind, pl.ds(row, 16), 0:128]
            ui = second[kind, pl.ds(row, 16), 128:256]
            if conj:
                put_pair_back(stage, kind, row, fr * ur + fi * ui, fr * ui - fi * ur)
            else:
                put_pair_back(stage, kind, row, fr * ur - fi * ui, fr * ui + fi * ur)
        return carry

    lax.fori_loop(0, BLOCK // 16, chunk, 0)


SPECTRUM = (KINDS, BLOCK, 256)


def stage_scratch():
    return pltpu.VMEM((KINDS, 2 * BLOCK, 256), bf16)


def spec_scratch():
    return pltpu.VMEM(SPECTRUM, f32)


PACK_SECOND = 48
PACK_SHORT = 176
PACK_SKIP = 194
PACK_ROWS = 200


def fill_pack(embed, gain, in_own, second, short, skip, out):
    normal, _ = unit(embed[...])
    low = (normal * gain[0, 0:1, :]).astype(bf16)
    for g in range(3):
        out[16 * g : 16 * g + 16, :] = mm(low, in_own[g])
    for l in range(2):
        out[PACK_SECOND + 64 * l : PACK_SECOND + 64 * l + 64, :] = second[l]
        for k in range(3):
            for g in range(3):
                row = PACK_SHORT + 9 * l + 3 * k + g
                out[row : row + 1, :] = short[k, g, l : l + 1, :]
    out[PACK_SKIP : PACK_SKIP + 2, :] = skip[...]
    out[PACK_SKIP + 2 : PACK_ROWS, :] = jnp.zeros((PACK_ROWS - PACK_SKIP - 2, 128), f32)


def table_kernel(s, own, peer, embed, mine_out, other_out, conv_table, gate_table):
    first = s[CORE] == 0
    mine = jnp.where(first, own[...], peer[...])
    other = jnp.where(first, peer[...], own[...])
    mine_out[...] = mine
    other_out[...] = other

    def fill(table, lanes, parts):
        whole = jnp.concatenate(parts, axis=0)
        high, low = split(whole)
        table[0:48, lanes] = high
        table[48:96, lanes] = low
        table[96:128, lanes] = jnp.zeros((32, 128), bf16)

    def gate(pack, g):
        parts = []
        for k in range(3):
            row = PACK_SHORT + 3 * k + g
            parts.append(pack[16 * g : 16 * g + 16] * pack[row : row + 1])
        return parts

    fill(conv_table, slice(0, 128), gate(mine, 1))
    fill(conv_table, slice(128, 256), gate(mine, 2))
    fill(gate_table, slice(0, 128), gate(mine, 0))
    fill(gate_table, slice(128, 256), gate(other, 0))
    zero = jnp.zeros((16, 128), f32)
    fill(gate_table, slice(256, 384), [embed[:, 0:128], zero, zero])
    fill(gate_table, slice(384, 512), [embed[:, 128:256], zero, zero])


def onehot_kernel(s, ids, out, turned, work):
    live = s[LIVE]
    count, _, width = ids.shape
    work[0:HALO, :] = jnp.zeros((HALO, 128), f32)
    work[HALO + count * width : 2 * HALO + count * width, :] = jnp.zeros((HALO, 128), f32)
    vocab = lax.broadcasted_iota(jnp.int32, (128, width), 0) % 16
    place = lax.broadcasted_iota(jnp.int32, (128, width), 1)
    for i in range(count):
        token = jnp.broadcast_to(ids[i, 0:1, :], (128, width))
        hit = (token == vocab) & (place + i * width < live)
        work[HALO + width * i : HALO + width * (i + 1), :] = jnp.where(hit, 1.0, 0.0).T
    lane = lax.broadcasted_iota(jnp.int32, (width, 128), 1) % 48 // 16
    used = lax.broadcasted_iota(jnp.int32, (width, 128), 1) < 96
    half = count // 2
    for i in range(count):
        row = HALO + width * i
        now = work[row : row + width, :]
        one = work[row - 1 : row - 1 + width, :]
        two = work[row - 2 : row - 2 + width, :]
        picked = jnp.where(lane == 0, now, jnp.where(lane == 1, one, two))
        picked = jnp.where(used, picked, 0.0)
        out[row : row + width, :] = picked.astype(bf16)
        turned[i // half, :, width * (i % half) : width * (i % half + 1)] = picked.T.astype(bf16)
    out[0:HALO, :] = jnp.zeros((HALO, 128), bf16)
    out[HALO + count * width : 2 * HALO + count * width, :] = jnp.zeros((HALO, 128), bf16)


def sine_and_cosine(angle):
    turns = jnp.round(angle * (2.0 / math.pi))
    x = ((angle - turns * 1.5703125) - turns * 4.837512969970703125e-4) - turns * 7.549789948768648e-8
    z = x * x
    sin = ((-1.9515295891e-4 * z + 8.3321608736e-3) * z - 1.6666654611e-1) * z * x + x
    cos = ((2.443315711809948e-5 * z - 1.388731625493765e-3) * z + 4.166664568298827e-2) * z * z - 0.5 * z + 1.0
    quarter = turns.astype(jnp.int32) & 3
    odd = (quarter & 1) == 1
    first, second = jnp.where(odd, cos, sin), jnp.where(odd, sin, cos)
    first = jnp.where(quarter >= 2, -first, first)
    second = jnp.where((quarter == 1) | (quarter == 2), -second, second)
    return first, second


def sine_kernel(s, feats, firsts, sine, cosine, turned):
    both = jnp.concatenate([firsts[:, 0, :], firsts[:, 1, :]], axis=1)
    count = feats.shape[0] // 512

    def chunk(i, carry):
        rows = at(512 * i, 512)
        angle = jnp.dot(feats[rows, :], both, precision=precise, preferred_element_type=f32)
        act, cosine[rows, :] = sine_and_cosine(angle)
        sine[rows, :] = act
        turned[:, at(512 * i, 512, 256)] = act.T.astype(bf16)
        return carry

    every(count, chunk)


def decay_of(rates, start, rows, length):
    place = (lax.broadcasted_iota(jnp.int32, (rows, 1), 0) + start).astype(f32) / length
    return jnp.exp(-place * rates), place


def filter_kernel(s, sine, mine, rates, dft, twiddle, filt0, filt1, freq0, freq1, stage, work):
    length = sine.shape[0]
    rate = rates[s[WHICH]]
    zero = jnp.zeros((64, 128), f32)
    left = jnp.concatenate([mine[PACK_SECOND : PACK_SECOND + 64], zero], axis=0)
    right = jnp.concatenate([zero, mine[PACK_SECOND + 64 : PACK_SECOND + 128]], axis=0)
    weights = jnp.concatenate([left, right], axis=1)

    def chunk(i, carry):
        rows = at(512 * i, 512)
        decay, _ = decay_of(rate, 512 * i, 512, length)
        both = mm3(sine[rows, :], weights)
        filt0[rows, :] = both[:, 0:128] * decay
        filt1[rows, :] = both[:, 128:256] * decay
        return carry

    every(length // 512, chunk)
    for filt, freq in ((filt0, freq0), (filt1, freq1)):
        to_freq(lambda p, row: filt[pl.ds(BLOCK * p + row, 16), :] * (1.0 / length), dft, twiddle, stage, freq)


def causal(load, skip_row, freq_filt, dft, twiddle, spec, stage, work, line):
    to_freq(load, dft, twiddle, stage, spec)
    times(freq_filt, spec, stage, False)

    def store(p, row, value):
        line[pl.ds(HALO + BLOCK * p + row, 16), :] = value + skip_row * load(p, row)

    from_freq(dft, twiddle, stage, work, store)


def hand_out(s, line, keep, send):
    half = (line.shape[0] - 2 * HALO) // 2
    span = half + 2 * HALO
    k = s[CORE]
    line[0:HALO, :] = jnp.zeros((HALO, 128), f32)
    line[HALO + 2 * half :, :] = jnp.zeros((HALO, 128), f32)
    keep[...] = line[at(half * k, span), :]
    send[...] = line[at(half * (1 - k), span), :]


def conv_first_kernel(s, onehot, conv_table, mine, freq_filt, dft, twiddle, keep, send, spec, product, stage, work, line):
    def chunk(i, carry):
        rows = at(512 * i, 512)
        pair = mm(onehot[at(512 * i + HALO, 512), :], conv_table[...])
        product[rows, :] = pair[:, 0:128] * pair[:, 128:256]
        return carry

    every(product.shape[0] // 512, chunk)
    skip_row = mine[PACK_SKIP : PACK_SKIP + 1, :]
    causal(lambda p, row: product[pl.ds(BLOCK * p + row, 16), :], skip_row, freq_filt, dft, twiddle, spec, stage, work, line)
    hand_out(s, line, keep, send)


def join_rows(s, whole, kept, received):
    half = kept.shape[0]
    whole[at(half * s[CORE], half), :] = kept[...]
    whole[at(half * (1 - s[CORE]), half), :] = received[...]


def conv_second_kernel(s, kept, received, mine, freq_filt, dft, twiddle, keep, send, spec, product, stage, work, line):
    join_rows(s, product, kept, received)
    skip_row = mine[PACK_SKIP + 1 : PACK_SKIP + 2, :]
    causal(lambda p, row: product[pl.ds(BLOCK * p + row, 16), :], skip_row, freq_filt, dft, twiddle, spec, stage, work, line)
    hand_out(s, line, keep, send)


def gelu_parts(p):
    squared = p * p
    th = jnp.tanh(GELU_A * p * (1.0 + GELU_B * squared))
    half = 0.5 * (1.0 + th)
    slope = half + 0.5 * p * (1.0 - th * th) * (GELU_A + (3.0 * GELU_A * GELU_B) * squared)
    return p * half, slope


def gelu_only(p):
    return 0.5 * p * (1.0 + jnp.tanh(GELU_A * p * (1.0 + GELU_B * (p * p))))


def forward_first_kernel(
    s, onehot, gate_table, conv_mine, conv_other, gain, w_out, w_up, w_down, w_in, mine, other,
    keep, send, mid_out, stream_out, gates, mixed,
):
    span = mid_out.shape[0]
    half = span - 2 * HALO
    k = s[CORE]
    taps = [
        jnp.concatenate([pack[PACK_SHORT + 9 + 3 * t + g : PACK_SHORT + 10 + 3 * t + g, :] for g in range(3) for pack in (mine, other)], axis=1)
        for t in range(3)
    ]

    def chunk(i, carry):
        rows = at(span * i, span)
        looked = mm(onehot[at(half * k + span * i, span), :], gate_table[...])
        conv = jnp.concatenate([conv_mine[rows, :], conv_other[rows, :]], axis=1)
        gated = (conv * looked[:, 0:256]).astype(bf16)
        mid = looked[:, 256:512] + mm(gated, w_out[...])
        mid_out[rows, :] = mid
        normal, _ = unit(mid)
        low = (normal * gain[0, 1:2, :]).astype(bf16)
        hidden = gelu_only(mm(low, w_up[...])).astype(bf16)
        stream = mid + mm(hidden, w_down[...])
        stream_out[rows, :] = stream
        normal, _ = unit(stream)
        low = (normal * gain[1, 0:1, :]).astype(bf16)
        mixed[rows, :] = mm(low, w_in[...])
        return carry

    every(1, chunk)
    gates[0:HALO, :] = jnp.zeros((HALO, 768), f32)
    step = 80
    for start in range(HALO, span, step):
        stop = start + step
        gates[start:stop, :] = (
            taps[0] * mixed[start:stop, :]
            + taps[1] * mixed[start - 1 : stop - 1, :]
            + taps[2] * mixed[start - 2 : stop - 2, :]
        )
    own = slice(HALO, HALO + half)
    keep[...] = gates[own, 256:384] * gates[own, 512:640]
    send[...] = gates[own, 384:512] * gates[own, 640:768]


def turn_back_kernel(
    s, conv_mine, conv_other, gates, stream, cot, cot_rim, gain, w_out, w_up, w_down,
    keep, send, grad_x0, grad_mid, block_out, hidden_out, low_out, normed_out, pre_out, gated_out, mid_low_out, gain_out,
    cot_rows, conv_grads,
):
    span = stream.shape[0]
    half = span - 2 * HALO
    k = s[CORE]
    live = s[LIVE]
    cot_rows[0:HALO, :] = jnp.zeros((HALO, 256), f32)
    cot_rows[HALO : HALO + half, :] = cot[...].reshape(half, 256)
    cot_rows[HALO + half :, :] = jnp.where(k == 0, cot_rim[...], 0.0)
    gain_out[...] = jnp.zeros_like(gain_out)

    def chunk(i, carry):
        rows = at(span * i, span)
        local_row = lax.broadcasted_iota(jnp.int32, (span, 1), 0) + span * i
        keep_mask = (local_row + (half * k - HALO) < live).astype(f32)
        own_mask = ((local_row >= HALO) & (local_row < HALO + half)).astype(f32)
        x0 = gates[rows, 0:256]
        conv = jnp.concatenate([conv_mine[rows, :], conv_other[rows, :]], axis=1)
        gated = (conv * x0).astype(bf16)
        gated_out[rows, :] = gated
        mid = stream[rows, :] + mm(gated, w_out[...])
        normal, scale = unit(mid)
        gain_row = gain[1, 1:2, :]
        low = (normal * gain_row).astype(bf16)
        normed_out[rows, :] = low
        act, slope = gelu_parts(mm(low, w_up[...]))
        hidden = act.astype(bf16)
        hidden_out[rows, :] = hidden
        block_out[rows, :] = (mid + mm(hidden, w_down[...])) * keep_mask
        grad = cot_rows[rows, :] * keep_mask
        grad_low = grad.astype(bf16)
        low_out[rows, :] = grad_low
        grad_pre = (slope * mm_nt(grad_low, w_down[...])).astype(bf16)
        pre_out[rows, :] = grad_pre
        grad_normed = mm_nt(grad_pre, w_up[...])
        gain_out[0:1, :] += jnp.sum(grad_normed * normal * own_mask, axis=0, keepdims=True)
        mid_grad = grad + unit_back(grad_normed * gain_row, normal, scale)
        grad_mid[rows, :] = mid_grad
        mid_low = mid_grad.astype(bf16)
        mid_low_out[rows, :] = mid_low
        grad_gated = mm_nt(mid_low, w_out[...])
        conv_grads[rows, :] = grad_gated * x0
        grad_x0[rows, :] = grad_gated * conv
        return carry

    every(1, chunk)
    own = slice(HALO, HALO + half)
    keep[...] = conv_grads[own, 0:128]
    send[...] = conv_grads[own, 128:256]


def conv_back_kernel(s, kept, received, mine, freq_filt, dft, twiddle, keep, send, spec, grads, stage, work, line):
    join_rows(s, grads, kept, received)
    skip_row = mine[PACK_SKIP + 1 : PACK_SKIP + 2, :]
    load = lambda p, row: grads[pl.ds(BLOCK * p + row, 16), :]
    to_freq(load, dft, twiddle, stage, spec)
    times(freq_filt, spec, stage, True)

    def store(p, row, value):
        line[pl.ds(HALO + BLOCK * p + row, 16), :] = value + skip_row * load(p, row)

    from_freq(dft, twiddle, stage, work, store)
    hand_out(s, line, keep, send)


def grad_freq_kernel(s, kept, received, dft, twiddle, spec, grads, stage):
    join_rows(s, grads, kept, received)
    to_freq(lambda p, row: grads[pl.ds(BLOCK * p + row, 16), :], dft, twiddle, stage, spec)


def filter_back(
    level, s, spec_grad, spec_in, grads, product, filt, cosine, sine_turned, mine, rates, feats_turned, dft, twiddle,
    second_out, first_out, skip_out, stage, work, line,
):
    length = filt.shape[0]
    times(spec_in, spec_grad, stage, True)

    def store(p, row, value):
        line[pl.ds(BLOCK * p + row, 16), :] = value

    from_freq(dft, twiddle, stage, work, store)
    rate = rates[s[WHICH]]
    second = mine[PACK_SECOND + 64 * level : PACK_SECOND + 64 * level + 64, :].astype(bf16)
    weight = jnp.where(s[GROUP] == 0, 0.5 * length, 0.0)
    skip_out[...] = jnp.zeros_like(skip_out)
    second_out[...] = jnp.zeros_like(second_out)
    first_out[...] = jnp.zeros_like(first_out)
    for i in range(length // 512):
        rows = slice(512 * i, 512 * (i + 1))
        decay, place = decay_of(rate, 512 * i, 512, length)
        shaped = ((line[rows, :] * (1.0 / length) + (weight * place) * filt[rows, :]) * decay).astype(bf16)
        skip_out[...] += jnp.sum((grads[rows, :] * product[rows, :]).reshape(64, 8, 128), axis=0)
        second_out[...] += mm(sine_turned[64 * level : 64 * level + 64, rows], shaped)
        inner = (mm_nt(shaped, second) * cosine[rows, 64 * level : 64 * level + 64]).astype(bf16)
        first_out[...] += mm(feats_turned[:, rows], inner)


def filter_back_kernel(s, *refs):
    filter_back(1, s, *refs)


def token_back_kernel(
    s, spec_grad, spec_in, grads, product, filt, cosine, sine_turned, mine, rates, feats_turned, dft, twiddle,
    freq_filt, onehot, turned, conv_table, second_out, first_out, skip_out, by_token, stage, work, line,
):
    length = grads.shape[0]
    skip_row = mine[PACK_SKIP : PACK_SKIP + 1, :]
    times(freq_filt, spec_grad, stage, True)

    def store(p, row, value):
        line[pl.ds(BLOCK * p + row, 16), :] = value + skip_row * grads[pl.ds(BLOCK * p + row, 16), :]

    from_freq(dft, twiddle, stage, work, store)
    by_token[...] = jnp.zeros_like(by_token)
    width = turned.shape[2]
    for i in range(length // width):
        rows = slice(width * i, width * (i + 1))
        pair = mm(onehot[HALO + width * i : HALO + width * (i + 1), :], conv_table[...])
        back = line[rows, :]
        gate_grads = jnp.concatenate([back * pair[:, 128:256], back * pair[:, 0:128]], axis=1).astype(bf16)
        by_token[...] += mm(turned[i], gate_grads)[0:48, :]
    filter_back(
        0, s, spec_grad, spec_in, grads, product, filt, cosine, sine_turned, mine, rates, feats_turned, dft, twiddle,
        second_out, first_out, skip_out, stage, work, line,
    )


def back_gates_kernel(
    s, prod_mine, prod_other, grad_x0, gates, mixed, grad_mid, stream, gain, mine, other, w_in,
    grad_stream, normed_out, mixed_low, short_out, gain_out, line,
):
    span = stream.shape[0]
    half = span - 2 * HALO
    taps = [
        jnp.concatenate([pack[PACK_SHORT + 9 + 3 * t + g : PACK_SHORT + 10 + 3 * t + g, :] for g in range(3) for pack in (mine, other)], axis=1)
        for t in range(3)
    ]
    step = 128
    for start in list(range(HALO, HALO + half, step)) + [HALO + half]:
        stop = start + (step if start < HALO + half else HALO)
        product = jnp.concatenate([prod_mine[start:stop, :], prod_other[start:stop, :]], axis=1)
        line[start:stop, 0:256] = grad_x0[start:stop, :]
        line[start:stop, 256:512] = product * gates[start:stop, 512:768]
        line[start:stop, 512:768] = product * gates[start:stop, 256:512]
    short_out[...] = jnp.zeros_like(short_out)
    gain_out[...] = jnp.zeros_like(gain_out)
    step = 64
    for start in range(HALO, HALO + half, step):
        stop = start + step
        values = mixed[start:stop, :]
        total = None
        for t in range(3):
            shifted = line[start + t : stop + t, :]
            part = taps[t] * shifted
            total = part if total is None else total + part
            short_out[t] += jnp.sum((shifted * values).reshape(step // 8, 8, 768), axis=0)
        mixed_low[start - HALO : stop - HALO, :] = total.astype(bf16)

    def chunk(i, carry):
        rows = at(512 * i, 512)
        wide = at(512 * i + HALO, 512)
        normal, scale = unit(stream[wide, :])
        gain_row = gain[1, 0:1, :]
        normed_out[rows, :] = (normal * gain_row).astype(bf16)
        grad_normed = mm_nt(mixed_low[rows, :], w_in[...])
        gain_out[0:1, :] += jnp.sum(grad_normed * normal, axis=0, keepdims=True)
        grad_stream[rows, :] = grad_mid[wide, :] + unit_back(grad_normed * gain_row, normal, scale)
        return carry

    every(half // 512, chunk)


def back_first_kernel(
    s, grad_stream, mid, onehot, turned, gate_table, conv_mine, conv_other, gain, w_out, w_up, w_down,
    keep, send, hidden_out, low_out, normed_out, pre_out, gated_out, mid_low_out, by_token, gain_out,
):
    half = grad_stream.shape[0]
    k = s[CORE]
    by_token[...] = jnp.zeros_like(by_token)
    gain_out[...] = jnp.zeros_like(gain_out)

    def chunk(i, carry):
        rows = at(half * i, half)
        wide = at(half * i + HALO, half)
        hot = onehot[at(half * k + half * i + HALO, half), :]
        x0 = mm(hot, gate_table[:, 0:256])
        conv = jnp.concatenate([conv_mine[wide, :], conv_other[wide, :]], axis=1)
        gated_out[rows, :] = (conv * x0).astype(bf16)
        normal, scale = unit(mid[wide, :])
        gain_row = gain[0, 1:2, :]
        low = (normal * gain_row).astype(bf16)
        normed_out[rows, :] = low
        act, slope = gelu_parts(mm(low, w_up[...]))
        hidden_out[rows, :] = act.astype(bf16)
        grad = grad_stream[rows, :]
        grad_low = grad.astype(bf16)
        low_out[rows, :] = grad_low
        grad_pre = (slope * mm_nt(grad_low, w_down[...])).astype(bf16)
        pre_out[rows, :] = grad_pre
        grad_normed = mm_nt(grad_pre, w_up[...])
        gain_out[0:1, :] += jnp.sum(grad_normed * normal, axis=0, keepdims=True)
        mid_grad = grad + unit_back(grad_normed * gain_row, normal, scale)
        mid_low = mid_grad.astype(bf16)
        mid_low_out[rows, :] = mid_low
        grad_gated = mm_nt(mid_low, w_out[...])
        conv_grad = grad_gated * x0
        keep[rows, :] = conv_grad[:, 0:128]
        send[rows, :] = conv_grad[:, 128:256]
        flips = turned[k, :, at(half * i, half, 256)]
        rest = mid_grad - mid_low.astype(f32)
        gate_grads = jnp.concatenate([(grad_gated * conv).astype(bf16), mid_low, rest.astype(bf16)], axis=1)
        by_token[...] += mm(flips, gate_grads)[0:48, :]
        return carry

    every(1, chunk)


R_OUT, R_UP, R_DOWN, R_IN = 128, 512, 512, 384


def send_weights_kernel(level, with_in, s, w_out, w_up, w_down, w_in, out, raw_out, raw_up, raw_down, raw_in, done):
    bring(((w_out.at[level], raw_out), (w_up.at[level], raw_up), (w_down.at[level], raw_down), (w_in.at[with_in], raw_in)), done)
    first = s[CORE] == 0
    pick = lambda a, b: jnp.where(first, a.astype(f32), b.astype(f32))
    out[0:128, :] = pick(raw_out[:, 0:128], raw_out[:, 128:256])
    for j in range(2):
        lanes = slice(128 * j, 128 * j + 128)
        out[128 + 256 * j : 384 + 256 * j, :] = pick(
            raw_up[:, 128 * j : 128 * j + 128], raw_up[:, 256 + 128 * j : 384 + 128 * j]
        )
        out[640 + 256 * j : 896 + 256 * j, :] = pick(raw_down[0:256, lanes], raw_down[256:512, lanes])
    for g in range(3):
        out[1152 + 128 * g : 1280 + 128 * g, :] = pick(raw_in[g, 0:128, :], raw_in[g, 128:256, :])


def cot_split_kernel(s, blocks, keep, send, rim):
    k = s[CORE]
    few = keep.shape[0]
    keep[...] = blocks[pl.ds(few * k, few)]
    send[...] = blocks[pl.ds(few * (1 - k), few)]
    rim[...] = blocks[few, 0:HALO, :]


def relay_kernel(s, value, out):
    out[...] = value[...]


def join_weights_kernel(level, s, w_out, w_up, w_down, w_in, first_part, second_part, out_full, up_full, down_full, *in_full):
    first = s[CORE] == 0
    low = lambda ref, a, b: ref[a:b, :].astype(bf16)
    pick = lambda a, b: jnp.where(first, a, b)
    mine_out = w_out[level]
    a, b = first_part[0:128, :], second_part[0:128, :]
    peer_out = jnp.concatenate([pick(a, b), pick(b, a)], axis=1)
    out_full[0:128, :] = pick(mine_out.astype(f32), peer_out).astype(bf16)
    out_full[128:256, :] = pick(peer_out, mine_out.astype(f32)).astype(bf16)
    up_a, up_b = w_up[level, :, 0:256].astype(f32), w_up[level, :, 256:512].astype(f32)
    up_full[:, 0:256] = pick(up_a, up_b).astype(bf16)
    up_full[:, 256:512] = pick(up_b, up_a).astype(bf16)
    down_a, down_b = w_down[level, 0:256, :].astype(f32), w_down[level, 256:512, :].astype(f32)
    down_full[0:256, :] = pick(down_a, down_b).astype(bf16)
    down_full[256:512, :] = pick(down_b, down_a).astype(bf16)
    for n, part in enumerate((first_part, second_part)):
        for j in range(2):
            up_full[:, 512 + 256 * n + 128 * j : 640 + 256 * n + 128 * j] = low(part, 128 + 256 * j, 384 + 256 * j)
            down_full[512 + 256 * n : 768 + 256 * n, 128 * j : 128 * j + 128] = low(part, 640 + 256 * j, 896 + 256 * j)
    if in_full:
        (full,) = in_full
        for g in range(3):
            own = w_in[1 - level, g].astype(f32)
            a, b = first_part[1152 + 128 * g : 1280 + 128 * g, :], second_part[1152 + 128 * g : 1280 + 128 * g, :]
            peer = jnp.concatenate([pick(a, b), pick(b, a)], axis=0)
            full[:, 256 * g : 256 * g + 128] = pick(own, peer).astype(bf16)
            full[:, 256 * g + 128 : 256 * g + 256] = pick(peer, own).astype(bf16)


def wide_grads_kernel(pad, s, gated, mid_low, normed, grad_pre, hidden, grad_low, keep, send):
    k = s[CORE]
    first = k == 0
    stop = gated.shape[0] - pad
    own = lambda ref: ref[pad:stop, :]
    out = mm_tn(own(gated), own(mid_low))
    for m in range(2):
        a, b = out[128 * m : 128 * m + 128, 0:128], out[128 * m : 128 * m + 128, 128:256]
        half = m + k - 2 * m * k
        keep[half, 0:128, :] = jnp.where(first, a, b)
        send[half, 0:128, :] = jnp.where(first, b, a)
    for j in range(4):
        target = (keep, send)[j % 2]
        up = mm_tn(own(normed), grad_pre[pad:stop, 256 * j : 256 * j + 256])
        down = mm_tn(hidden[pad:stop, 256 * j : 256 * j + 256], own(grad_low))
        for n in range(2):
            lanes = slice(128 * n, 128 * n + 128)
            target[j // 2, 128 + 256 * n : 384 + 256 * n, :] = up[:, lanes]
            target[j // 2, 640 + 256 * n : 896 + 256 * n, :] = down[:, lanes]


def in_grads_kernel(s, normed_in, mixed_low, keep, send):
    k = s[CORE]
    first = k == 0
    for g in range(3):
        both = mm_tn(normed_in[...], mixed_low[:, 256 * g : 256 * g + 256])
        for m in range(2):
            block = both[:, 128 * m : 128 * m + 128]
            half = m + k - 2 * m * k
            keep[half, 128 * g : 128 * g + 128, :] = jnp.where(first, block[0:128], block[128:256])
            send[half, 128 * g : 128 * g + 128, :] = jnp.where(first, block[128:256], block[0:128])


def add_kernel(s, kept, received, own_out, peer_out):
    own_out[...] = kept[0] + received[0]
    peer_out[...] = kept[1] + received[1]


def add_one_kernel(s, kept, received, out):
    out[...] = kept[...] + received[...]


def spread_wide_kernel(level, s, a, b, *refs):
    outs, (out, up, down), done = refs[-7:-4], refs[-4:-1], refs[-1]
    first = s[CORE] == 0
    pick = lambda x, y: jnp.where(first, x, y)

    def both(row, rows):
        x, y = a[row : row + rows, :], b[row : row + rows, :]
        return pick(x, y), pick(y, x)

    x, y = both(0, 128)
    out[:, 0:128] = x
    out[:, 128:256] = y
    for j in range(2):
        lanes = slice(128 * j, 128 * j + 128)
        x, y = both(128 + 256 * j, 256)
        up[:, 128 * j : 128 * j + 128] = x
        up[:, 256 + 128 * j : 384 + 128 * j] = y
        x, y = both(640 + 256 * j, 256)
        down[0:256, lanes] = x
        down[256:512, lanes] = y
    bring(zip((out, up, down), (whole.at[level] for whole in outs)), done)


def spread_in_kernel(s, kept, received, whole, near, done):
    first = s[CORE] == 0
    for g in range(3):
        x, y = kept[128 * g : 128 * g + 128, :], received[128 * g : 128 * g + 128, :]
        near[g, 0:128, :] = jnp.where(first, x, y)
        near[g, 128:256, :] = jnp.where(first, y, x)
    bring(((near, whole.at[1]),), done)


def pair_kernel(bit, s, own, received, out):
    spot = s[(CORE, BIT1, BIT2, BIT3)[bit]]
    for j in range(own.shape[0]):
        out[2 * j + spot] = own[j]
        out[2 * j + 1 - spot] = received[j]


E_GAIN1, E_GAIN0, E_EMBED, E_FIRST, E_SHORT, E_TOKEN, E_ROWS = 0, 8, 16, 32, 72, 88, 136
EM_SECOND, EM_SKIP, EM_ROWS = 0, 64, 72
L_TOKEN, L_SECOND, L_SKIP, L_ROWS = 0, 96, 160, 168
FIRST_ROWS = 40


def early_kernel(s, gain_mid1, gain_in1, gain_mid0, by_token0, first1, short1, second1, skip1, flat, mine):
    k = s[CORE]
    flat[...] = jnp.zeros_like(flat)
    flat[E_GAIN1 : E_GAIN1 + 8, :] = gain_mid1[...]
    flat[E_GAIN0 : E_GAIN0 + 8, :] = gain_mid0[...]
    flat[E_GAIN1 + 1 : E_GAIN1 + 2, :] = gain_in1[0:1, :]
    flat[E_EMBED : E_EMBED + 16, :] = by_token0[0:16, 256:512] + by_token0[0:16, 512:768]
    flat[E_FIRST : E_FIRST + FIRST_ROWS, 0:64] = first1[...]
    swap = lambda v: jnp.where(k == 0, v, jnp.concatenate([v[:, 128:256], v[:, 0:128]], axis=1))
    for t in range(3):
        total = jnp.sum(short1[t], axis=0, keepdims=True)
        for g in range(3):
            flat[E_SHORT + 3 * t + g : E_SHORT + 3 * t + g + 1, :] = swap(total[:, 256 * g : 256 * g + 256])
    flat[E_TOKEN : E_TOKEN + 48, :] = swap(by_token0[:, 0:256])
    mine[EM_SECOND : EM_SECOND + 64, :] = second1[...]
    mine[EM_SKIP : EM_SKIP + 8, :] = jnp.broadcast_to(jnp.sum(skip1[...], axis=0, keepdims=True), (8, 128))


def late_kernel(s, by_token12, second0, skip0, first0, mine, first_out):
    mine[L_TOKEN : L_TOKEN + 48, :] = by_token12[:, 0:128]
    mine[L_TOKEN + 48 : L_TOKEN + 96, :] = by_token12[:, 128:256]
    mine[L_SECOND : L_SECOND + 64, :] = second0[...]
    mine[L_SKIP : L_SKIP + 8, :] = jnp.broadcast_to(jnp.sum(skip0[...], axis=0, keepdims=True), (8, 128))
    first_out[:, 0:64] = first0[...]
    first_out[:, 64:128] = jnp.zeros((FIRST_ROWS, 64), f32)


def chip_kernel(s, flat, flat_in, mine, mine_in, out):
    first = s[CORE] == 0
    rows = flat.shape[0]
    total = flat[...] + flat_in[...]
    out[0:rows, 0 : total.shape[1]] = total
    if total.shape[1] == 128:
        out[0:rows, 128:256] = jnp.zeros((rows, 128), f32)
    out[rows:, 0:128] = jnp.where(first, mine[...], mine_in[...])
    out[rows:, 128:256] = jnp.where(first, mine_in[...], mine[...])


def last_kernel(
    s, early, early_in, late, late_in, embed, gain, own, peer, w_own, w_first, w_second, in_given,
    embed_out, gain_out, in_whole, short_out, first_out, second_out, skip_out, in_out, done,
):
    pick = lambda x, y: jnp.where(s[CORE] == 0, x, y)

    def plain(pair, row, rows):
        return pair[0][row : row + rows, :] + pair[1][row : row + rows, :]

    def halves(pair, row, rows):
        here, there = pair
        left = here[row : row + rows, 0:128] + there[row : row + rows, 128:256]
        right = here[row : row + rows, 128:256] + there[row : row + rows, 0:128]
        return left, right

    early, late = (early, early_in), (late, late_in)
    gains1 = plain(early, E_GAIN1, 8)
    gains0 = plain(early, E_GAIN0, 8)
    gain_out[1, 0:1, :] = gains1[1:2, :]
    gain_out[1, 1:2, :] = gains1[0:1, :]
    gain_out[0, 1:2, :] = gains0[0:1, :]
    first_out[:, 0, :] = plain(late, 0, FIRST_ROWS)[0:33, 0:64]
    first_out[:, 1, :] = plain(early, E_FIRST, FIRST_ROWS)[0:33, 0:64]
    short = halves(early, E_SHORT, 16)[0]
    for t in range(3):
        for g in range(3):
            short_out[t, g, 1:2, :] = short[3 * t + g : 3 * t + g + 1, :]
    second_out[1] = halves(early, E_ROWS + EM_SECOND, 64)[0]
    second_out[0] = halves(late, FIRST_ROWS + L_SECOND, 64)[0]
    skip_out[0:1, :] = halves(late, FIRST_ROWS + L_SKIP, 8)[0][0:1]
    skip_out[1:2, :] = halves(early, E_ROWS + EM_SKIP, 8)[0][0:1]
    tokens = [
        halves(early, E_TOKEN, 48),
        halves(late, FIRST_ROWS + L_TOKEN, 48),
        halves(late, FIRST_ROWS + L_TOKEN + 48, 48),
    ]
    normal, scale = unit(embed[...])
    gain_row = gain[0, 0:1, :]
    low = (normal * gain_row).astype(bf16)
    grad_normed = jnp.zeros((16, 256), f32)
    for g in range(3):
        for h, pack in ((0, own), (1, peer)):
            grads = tokens[g][h]
            table = pack[16 * g : 16 * g + 16, :]
            summed = jnp.zeros((16, 128), f32)
            for t in range(3):
                row = PACK_SHORT + 3 * t + g
                part = grads[16 * t : 16 * t + 16, :]
                summed += pack[row : row + 1, :] * part
                if h == 0:
                    short_out[t, g, 0:1, :] = jnp.sum(table * part, axis=0, keepdims=True)
            high, rest = split(summed)
            if h == 0:
                in_out[g] = mm_tn(low, high) + mm_tn(low, rest)
                weight = w_own[0, g]
            else:
                rows = slice(1152 + 128 * g, 1280 + 128 * g)
                a, b = w_first[rows, :], w_second[rows, :]
                weight = jnp.concatenate([pick(a, b), pick(b, a)], axis=0).astype(bf16)
            grad_normed += mm_nt(high, weight) + mm_nt(rest, weight)
    copy = pltpu.make_async_copy(in_out, in_whole.at[0], done.at[0])
    copy.start()
    gain_out[0, 0:1, :] = jnp.sum(grad_normed * normal, axis=0, keepdims=True)
    embed_out[...] = plain(early, E_EMBED, 16) + unit_back(grad_normed * gain_row, normal, scale)
    copy.wait()


def block_send_kernel(s, block_out, mine, other):
    spot = s[SPOT]
    mine[...] = block_out[at(HALO + 128 * spot, 128), :]
    near = spot + 1 - 2 * s[CORE]
    other[...] = block_out[at(HALO + 128 * near, 128), :]


def block_pick_kernel(s, mine, received, out):
    out[...] = jnp.where(s[HOLDER] == 1, mine[...], received[...])


def block_join_kernel(s, here, there, out):
    first = s[GROUP] == 0
    out[0] = jnp.where(first, here[...], there[...])
    out[1] = jnp.where(first, there[...], here[...])


def chip_local(
    ids, live, embed, norm_gain, in_weight, short_kernel, filter_first, filter_second, skip_gain,
    out_weight, up_weight, down_weight, cotangent,
):
    count = lax.axis_size("seq")
    rank = lax.axis_index("seq")
    group = lax.axis_index("ch")
    width = ids.shape[1]
    length = width * count
    half = length // 2
    span = half + 2 * HALO
    core = rank % 2
    across = lambda v: lax.ppermute(v, "ch", [(0, 1), (1, 0)])
    trade = lambda v, bit: lax.ppermute(v, "seq", [(i, i ^ bit) for i in range(count)])
    beside = lambda v: trade(v, 1)
    dft = jnp.asarray(dft_table()).astype(bf16)
    twiddle = jnp.asarray(twiddle_table())
    feats = jnp.asarray(feature_table(length))
    feats_turned = jnp.asarray(np.pad(feature_table(length).T, ((0, 40 - FEAT), (0, 0)))).astype(bf16)
    rates = jnp.asarray(rate_table())
    low = lambda *shape: arr(*shape, kind=bf16)
    line = pltpu.VMEM((length + 2 * HALO, 128), f32)
    conv_scratch = [stage_scratch(), spec_scratch(), line]
    pair = lambda bit, v, w, **kw: run(
        functools.partial(pair_kernel, bit), jax.ShapeDtypeStruct((2 * v.shape[0],) + v.shape[1:], v.dtype), s, v, w, **kw
    )

    row_shape = lambda rows: arr(rows, 8, width, kind=jnp.int32)
    in_own = jnp.swapaxes(in_weight, 1, 2)
    packed = (embed, norm_gain, in_own, filter_second, jnp.transpose(short_kernel, (1, 2, 0, 3)), skip_gain)
    held = [(1, 2), ids.shape, embed.shape, norm_gain.shape, in_own.shape[1:], filter_second.shape, packed[4].shape, skip_gain.shape]
    kinds = [jnp.int32, jnp.int32, f32, f32, bf16, f32, f32, f32]
    s, ids1, cot1, pack = start(
        numbers_kernel,
        [arr(NUMBER_ROWS, 128, kind=jnp.int32), row_shape(1), arr(1, width, 256), arr(PACK_ROWS, 128)],
        live.reshape(1, 2), ids, cotangent, *packed,
        scratch=[pltpu.VMEM(shape, kind) for shape, kind in zip(held, kinds)] + [pltpu.SemaphoreType.DMA((9,))],
    )
    pack_in = across(pack)
    wide = (out_weight, up_weight, down_weight, in_own)
    send_weights = lambda level, with_in, after: run(
        functools.partial(send_weights_kernel, level, with_in), arr(1536, 128), s, *wide, hbm=range(4), after=after,
        scratch=[pltpu.VMEM(v.shape[1:], v.dtype) for v in wide] + [pltpu.SemaphoreType.DMA((4,))],
    )
    part0 = send_weights(0, 1, (pack,))
    part0_in = across(part0)
    ids2 = pair(3, ids1, trade(ids1, 8), after=(part0,))
    sine, cosine, sine_turned = run(
        sine_kernel, [arr(length, 128), arr(length, 128), low(128, length)], s, feats, jnp.transpose(filter_first, (1, 0, 2)),
        after=(ids2,),
    )
    cot2 = pair(3, cot1, trade(cot1, 8), after=(sine,))
    ids4 = pair(2, ids2, trade(ids2, 4), after=(cot2,))
    part1 = send_weights(1, 0, (ids4,))
    part1_in = across(part1)
    mine, other, conv_table, gate_table = run(
        table_kernel, [arr(PACK_ROWS, 128), arr(PACK_ROWS, 128), low(128, 256), low(128, 512)], s, pack, pack_in, embed,
        after=(part1,),
    )
    filt0, filt1, freq0, freq1 = run(
        filter_kernel, [arr(length, 128), arr(length, 128), arr(*SPECTRUM), arr(*SPECTRUM)], s, sine, mine, rates, dft, twiddle,
        scratch=[stage_scratch(), spec_scratch()],
    )
    ids8 = pair(1, ids4, trade(ids4, 2), after=(filt0,))
    cot4 = pair(2, cot2, trade(cot2, 4), after=(ids8,))
    all_ids = pair(0, ids8, beside(ids8), after=(cot4,))
    onehot, turned = run(
        onehot_kernel, [low(length + 2 * HALO, 128), low(2, 128, half)], s, all_ids,
        scratch=[pltpu.VMEM((length + 2 * HALO, 128), f32)],
    )
    first_part = run(relay_kernel, arr(1536, 128), s, part0_in, after=(freq1,))
    first_beside = beside(first_part)
    conv_mine0, sent, spec0, product0 = run(
        conv_first_kernel, [arr(span, 128), arr(span, 128), arr(*SPECTRUM), arr(length, 128)],
        s, onehot, conv_table, mine, freq0, dft, twiddle, scratch=conv_scratch, after=(first_part,),
    )
    conv_other0 = beside(sent)
    w_out0, w_up0, w_down0, w_in1 = run(
        functools.partial(join_weights_kernel, 0), [low(256, 256), low(256, 1024), low(1024, 256), low(256, 768)],
        s, out_weight, up_weight, down_weight, in_own, first_part, first_beside, after=(sent,),
    )
    kept, sent, mid0, stream1, gates1, mixed1 = run(
        forward_first_kernel,
        [arr(half, 128), arr(half, 128), arr(span, 256), arr(span, 256), arr(span, 768), arr(span, 768)],
        s, onehot, gate_table, conv_mine0, conv_other0, norm_gain, w_out0, w_up0, w_down0, w_in1, mine, other,
    )
    received = beside(sent)
    cot8 = pair(1, cot4, trade(cot4, 2), after=(sent,))
    cot_keep, cot_send, cot_rim = run(
        cot_split_kernel, [arr(4, width, 256), arr(4, width, 256), arr(HALO, 256)], s, cot8
    )
    second_part = run(relay_kernel, arr(1536, 128), s, part1_in, after=(sent,))
    second_beside = beside(second_part)
    conv_mine1, sent, spec1, product1 = run(
        conv_second_kernel, [arr(span, 128), arr(span, 128), arr(*SPECTRUM), arr(length, 128)],
        s, kept, received, mine, freq1, dft, twiddle, scratch=conv_scratch, after=(second_part,),
    )
    conv_other1 = beside(sent)
    w_out1, w_up1, w_down1 = run(
        functools.partial(join_weights_kernel, 1), [low(256, 256), low(256, 1024), low(1024, 256)],
        s, out_weight, up_weight, down_weight, in_own, second_part, second_beside, after=(sent,),
    )
    cot = pair(0, cot_keep, beside(cot_send))
    (kept, sent, grad_x0, grad_mid1, block, hidden, grad_low, normed, grad_pre, gated, mid_low, gain_mid1) = run(
        turn_back_kernel,
        [
            arr(half, 128), arr(half, 128), arr(span, 256), arr(span, 256), arr(span, 256), low(span, 1024), low(span, 256),
            low(span, 256), low(span, 1024), low(span, 256), low(span, 256), arr(8, 256),
        ],
        s, conv_mine1, conv_other1, gates1, stream1, cot, cot_rim, norm_gain, w_out1, w_up1, w_down1,
        scratch=[pltpu.VMEM((span, 256), f32), pltpu.VMEM((span, 256), f32)],
    )
    received = beside(sent)
    grads_keep1, grads_send1 = run(
        functools.partial(wide_grads_kernel, HALO), [arr(2, 1152, 128), arr(2, 1152, 128)],
        s, gated, mid_low, normed, grad_pre, hidden, grad_low,
    )
    block_mine, block_other = run(block_send_kernel, [arr(width, 256), arr(width, 256)], s, block)
    grads_in1 = beside(grads_send1)
    block_beside = beside(block_other)

    prod_mine, sent, spec_grad1, grads1 = run(
        conv_back_kernel, [arr(span, 128), arr(span, 128), arr(*SPECTRUM), arr(length, 128)],
        s, kept, received, mine, freq1, dft, twiddle, scratch=conv_scratch, after=(grads_send1, block_mine),
    )
    prod_other = beside(sent)
    own1, peer1 = run(add_kernel, [arr(1152, 128), arr(1152, 128)], s, grads_keep1, grads_in1, after=(sent,))
    across1 = across(peer1)
    filter_shapes = [arr(64, 128), arr(40, 64), arr(8, 128)]
    filter_scratch = [stage_scratch(), spec_scratch(), pltpu.VMEM((length, 128), f32)]
    second1, first1, skip1 = run(
        filter_back_kernel, filter_shapes, s, spec_grad1, spec1, grads1, product1, filt1, cosine,
        sine_turned, mine, rates, feats_turned, dft, twiddle, scratch=filter_scratch, after=(peer1,),
    )
    grad_stream1, normed_in, mixed_low, short1, gain_in1 = run(
        back_gates_kernel,
        [arr(half, 256), low(half, 256), low(half, 768), arr(3, 8, 768), arr(8, 256)],
        s, prod_mine, prod_other, grad_x0, gates1, mixed1, grad_mid1, stream1, norm_gain, mine, other, w_in1,
        scratch=[pltpu.VMEM((span, 768), f32)], after=(skip1,),
    )
    in_keep, in_send = run(in_grads_kernel, [arr(2, 384, 128), arr(2, 384, 128)], s, normed_in, mixed_low)
    in_beside = beside(in_send)
    block_here = run(block_pick_kernel, arr(width, 256), s, block_mine, block_beside, after=(in_send,))
    block_across = across(block_here)
    in_own1, in_peer1 = run(add_kernel, [arr(384, 128), arr(384, 128)], s, in_keep, in_beside, after=(block_here,))
    in_across = across(in_peer1)
    (kept, sent, hidden, grad_low, normed, grad_pre, gated, mid_low, by_token0, gain_mid0) = run(
        back_first_kernel,
        [
            arr(half, 128), arr(half, 128), low(half, 1024), low(half, 256), low(half, 256), low(half, 1024), low(half, 256),
            low(half, 256), arr(48, 768), arr(8, 256),
        ],
        s, grad_stream1, mid0, onehot, turned, gate_table, conv_mine0, conv_other0, norm_gain, w_out0, w_up0, w_down0,
        after=(in_peer1,),
    )
    received = beside(sent)
    early_flat, early_mine = run(
        early_kernel, [arr(E_ROWS, 256), arr(EM_ROWS, 128)],
        s, gain_mid1, gain_in1, gain_mid0, by_token0, first1, short1, second1, skip1,
    )
    early_flat_in, early_mine_in = beside(early_flat), beside(early_mine)
    grads_keep0, grads_send0 = run(
        functools.partial(wide_grads_kernel, 0), [arr(2, 1152, 128), arr(2, 1152, 128)],
        s, gated, mid_low, normed, grad_pre, hidden, grad_low, after=(early_flat,),
    )
    grads_in0 = beside(grads_send0)
    early = run(
        chip_kernel, arr(E_ROWS + EM_ROWS, 256),
        s, early_flat, early_flat_in, early_mine, early_mine_in, after=(grads_send0,),
    )
    early_in = across(early)
    spec_grad0, grads0 = run(
        grad_freq_kernel, [arr(*SPECTRUM), arr(length, 128)], s, kept, received, dft, twiddle, scratch=[stage_scratch()],
        after=(early,),
    )
    own0, peer0 = run(add_kernel, [arr(1152, 128), arr(1152, 128)], s, grads_keep0, grads_in0, after=(spec_grad0,))
    across0 = across(peer0)
    total1 = run(add_one_kernel, arr(1152, 128), s, own1, across1, after=(peer0,))
    total1_beside = beside(total1)
    second0, first0, skip0, by_token12 = run(
        token_back_kernel, filter_shapes + [arr(48, 256)], s, spec_grad0, spec0, grads0, product0, filt0, cosine,
        sine_turned, mine, rates, feats_turned, dft, twiddle, freq0, onehot, turned, conv_table, scratch=filter_scratch,
        after=(peer0, early, total1),
    )
    wide_shapes = [arr(2, 128, 256), arr(2, 256, 512), arr(2, 512, 256)]
    wide_scratch = [pltpu.VMEM(v.shape[1:], f32) for v in wide_shapes] + [pltpu.SemaphoreType.DMA((3,))]
    late_mine, late_first = run(
        late_kernel, [arr(L_ROWS, 128), arr(FIRST_ROWS, 128)], s, by_token12, second0, skip0, first0, flops=FEW_FLOPS
    )
    late_mine_in, late_first_in = beside(late_mine), beside(late_first)
    in_total = run(add_one_kernel, arr(384, 128), s, in_own1, in_across, after=(late_mine,), flops=FEW_FLOPS)
    block_out, joined = run(block_join_kernel, arr(2, width, 256), s, block_here, block_across, after=(late_mine,), flops=FEW_FLOPS, token=True)
    late = run(
        chip_kernel, arr(FIRST_ROWS + L_ROWS, 256), s, late_first, late_first_in, late_mine, late_mine_in, flops=FEW_FLOPS,
        after=(joined, in_total, early_in),
    )
    late_in = across(late)
    in_total_beside = beside(in_total)
    *wide_buffers, wide_spread = run(
        functools.partial(spread_wide_kernel, 1), wide_shapes, s, total1, total1_beside, hbm_outs=(0, 1, 2), flops=FEW_FLOPS,
        scratch=wide_scratch, after=(late,), token=True,
    )
    in_buffer, in_spread = run(
        spread_in_kernel, arr(2, 3, 256, 128), s, in_total, in_total_beside, hbm_outs=(0,), flops=FEW_FLOPS, token=True,
        scratch=[pltpu.VMEM((3, 256, 128), f32), pltpu.SemaphoreType.DMA((1,))],
    )
    total0 = run(add_one_kernel, arr(1152, 128), s, own0, across0, after=(late_in, wide_spread, in_spread))
    total0_beside = beside(total0)
    grad_embed, grad_gain, grad_in, grad_short, grad_first, grad_second, grad_skip = run(
        last_kernel,
        [
            arr(16, 256), arr(2, 2, 256), arr(2, 3, 256, 128), arr(3, 3, 2, 128), arr(FEAT, 2, 64), arr(2, 64, 128), arr(2, 128),
        ],
        s, early, early_in, late, late_in, embed, norm_gain, pack, pack_in, in_own, second_part, second_beside, in_buffer,
        hbm=(11,), hbm_outs=(2,), aliases=((11, 2),), flops=FEW_FLOPS, after=(total0,),
        scratch=[pltpu.VMEM((3, 256, 128), f32), pltpu.SemaphoreType.DMA((1,))],
    )
    grad_out, grad_up, grad_down = run(
        functools.partial(spread_wide_kernel, 0), wide_shapes, s, total0, total0_beside, *wide_buffers,
        hbm=(2, 3, 4), hbm_outs=(0, 1, 2), aliases=((2, 0), (3, 1), (4, 2)), flops=FEW_FLOPS, scratch=wide_scratch,
    )
    return (
        block_out,
        grad_embed,
        grad_gain,
        jnp.swapaxes(grad_in, 1, 2),
        jnp.transpose(grad_short, (2, 0, 1, 3)),
        jnp.transpose(grad_first, (1, 0, 2)),
        grad_second,
        grad_skip,
        grad_out,
        grad_up,
        grad_down,
    )


def solution(mesh):
    in_specs = (
        P(None, "seq"),
        P(),
        P(),
        P(),
        P(None, None, None, "ch"),
        P(None, None, None, "ch"),
        P(),
        P(None, None, "ch"),
        P(None, "ch"),
        P(None, "ch", None),
        P(None, None, "ch"),
        P(None, "ch", None),
        P(None, "seq", None),
    )
    out_specs = (
        P(None, "seq", None),
        P(),
        P(),
        P(None, None, None, "ch"),
        P(None, None, None, "ch"),
        P(),
        P(None, None, "ch"),
        P(None, "ch"),
        P(None, "ch", None),
        P(None, None, "ch"),
        P(None, "ch", None),
    )

    def either(*args):
        length = args[0].shape[1] * lax.axis_size("seq")
        near = length == BLOCKS * BLOCK and lax.axis_size("seq") == 16
        return (chip_local if near else local)(*args)

    return jax.shard_map(either, mesh=mesh, in_specs=in_specs, out_specs=out_specs, check_vma=False)
```

```python
import collections
import functools
import math

import jax
import jax.numpy as jnp
import ml_dtypes
import numpy as np
from jax import lax
from jax.experimental import pallas as pl
from jax.experimental.pallas import tpu as pltpu
from jax.sharding import PartitionSpec as P

D = 256
FEAT = 33


precise = lax.Precision.HIGHEST
epsilon = 1e-05


def passed_along(value, axis, steps):
    count = lax.axis_size(axis)
    leading, last = (max(0, -steps), min(count, count - steps))
    return lax.ppermute(value, axis, [(source, source + steps) for source in range(leading, last)])


def layer_norm(inputs, gain_vec):
    center = inputs - jnp.mean(inputs, axis=-1, keepdims=True)
    spread = jnp.mean(center * center, axis=-1, keepdims=True)
    return center * lax.rsqrt(spread + epsilon) * gain_vec


def position_features(length):
    places = jnp.arange(length, dtype=jnp.int32)
    band_ids = jnp.arange(1, (FEAT - 1) // 2 + 1, dtype=jnp.int32)
    turn_counts = places[:, None] * band_ids[None, :] % length
    angles = turn_counts.astype(jnp.float32) * (2.0 * math.pi / length)
    ramp_vals = places.astype(jnp.float32)[:, None] / length
    return jnp.concatenate([ramp_vals, jnp.cos(angles), jnp.sin(angles)], axis=1)


def decay_rates(channels):
    return 0.3 * 10.0 ** (channels.astype(jnp.float32) / (D - 1))


def dft_tables(blocks, block_len):
    doubled = 2 * blocks
    span_total = doubled * block_len
    frequency = jnp.arange(doubled, dtype=jnp.int32)
    places = jnp.arange(blocks, dtype=jnp.int32)
    inner_idx = jnp.arange(block_len, dtype=jnp.int32)
    outer_angle = (frequency[:, None] * places[None, :] % doubled).astype(jnp.float32) * (
        2.0 * math.pi / doubled
    )
    twist_angle = (frequency[:, None] * inner_idx[None, :] % span_total).astype(jnp.float32) * (
        2.0 * math.pi / span_total
    )
    inner_angle = (inner_idx[:, None] * inner_idx[None, :] % block_len).astype(jnp.float32) * (
        2.0 * math.pi / block_len
    )
    return (
        jnp.cos(outer_angle),
        jnp.sin(outer_angle),
        jnp.cos(twist_angle),
        jnp.sin(twist_angle),
        jnp.cos(inner_angle),
        jnp.sin(inner_angle),
    )


def along_block(values, table):
    return jnp.einsum("...kb,bj->...kj", values, table, precision=precise)


def to_spectrum(signal, tables):
    outer_cos, outer_sin, twist_cos, twist_sin, inner_cos, inner_sin = tables
    first_re = jnp.einsum("kp,...pb->...kb", outer_cos, signal, precision=precise)
    first_im = -jnp.einsum("kp,...pb->...kb", outer_sin, signal, precision=precise)
    turned_re = first_re * twist_cos + first_im * twist_sin
    turned_im = first_im * twist_cos - first_re * twist_sin
    spec_re = along_block(turned_re, inner_cos) + along_block(turned_im, inner_sin)
    spec_im = along_block(turned_im, inner_cos) - along_block(turned_re, inner_sin)
    return (spec_re, spec_im)


def from_spectrum(spec_re, spec_im, tables):
    outer_cos, outer_sin, twist_cos, twist_sin, inner_cos, inner_sin = tables
    back_re = along_block(spec_re, inner_cos) - along_block(spec_im, inner_sin)
    back_im = along_block(spec_re, inner_sin) + along_block(spec_im, inner_cos)
    turned_re = back_re * twist_cos - back_im * twist_sin
    turned_im = back_re * twist_sin + back_im * twist_cos
    scale_back = 1.0 / (outer_cos.shape[0] * inner_cos.shape[0])
    signal = jnp.einsum("kp,...kb->...pb", outer_cos, turned_re, precision=precise) - jnp.einsum(
        "kp,...kb->...pb", outer_sin, turned_im, precision=precise
    )
    return signal * scale_back


def causal_filter(received, filt_spec, skip_part, tables):
    item_count, chan_count, length = received.shape
    blocks = tables[0].shape[1]
    spec_re, spec_im = to_spectrum(
        received.reshape(item_count, chan_count, blocks, length // blocks), tables
    )
    prod_re = spec_re * filt_spec[0] - spec_im * filt_spec[1]
    prod_im = spec_re * filt_spec[1] + spec_im * filt_spec[0]
    result_sig = from_spectrum(prod_re, prod_im, tables).reshape(item_count, chan_count, length)
    return result_sig + skip_part[:, None] * received


def filter_backward(grad_cols, moved_in, filt_spec, skip_part, tables):
    item_count, chan_count, length = grad_cols.shape
    blocks = tables[0].shape[1]
    grad_re, grad_im = to_spectrum(
        grad_cols.reshape(item_count, chan_count, blocks, length // blocks), tables
    )
    input_re, input_im = to_spectrum(
        moved_in.reshape(item_count, chan_count, blocks, length // blocks), tables
    )
    back_re = grad_re * filt_spec[0] + grad_im * filt_spec[1]
    back_im = grad_im * filt_spec[0] - grad_re * filt_spec[1]
    grad_u_cols = (
        from_spectrum(back_re, back_im, tables).reshape(item_count, chan_count, length)
        + skip_part[:, None] * grad_cols
    )
    corr_re = grad_re * input_re + grad_im * input_im
    corr_im = grad_im * input_re - grad_re * input_im
    grad_filt = jnp.sum(from_spectrum(corr_re, corr_im, tables), axis=0).reshape(chan_count, length)
    grad_skip_part = jnp.sum(grad_cols * moved_in, axis=(0, 2))
    return (grad_u_cols, grad_filt, grad_skip_part)


def local_filter(first, second, features, select, group_idx, chan_local):
    hidden_pre = jnp.dot(features, first, precision=precise)
    hidden_act = jnp.sin(hidden_pre)
    chan_width = second.shape[1]
    second_part = jnp.dot(second, select, precision=precise)
    channel_ids = group_idx * chan_width + chan_local
    length = features.shape[0]
    ramp_vals = jnp.arange(length, dtype=jnp.int32).astype(jnp.float32) / length
    decay_part = jnp.exp(-decay_rates(channel_ids)[:, None] * ramp_vals[None, :])
    filt_cols = jnp.einsum("hc,th->ct", second_part, hidden_act, precision=precise) * decay_part
    return (filt_cols, hidden_pre, hidden_act, second_part, decay_part)


def filter_mlp_backward(grad_filt, features, filter_parts):
    hidden_pre, hidden_act, second_part, decay_part = filter_parts
    grad_shaped = grad_filt * decay_part
    grad_second_part = jnp.einsum("ct,th->hc", grad_shaped, hidden_act, precision=precise)
    grad_act = jnp.einsum("ct,hc->th", grad_shaped, second_part, precision=precise)
    grad_first = jnp.einsum(
        "tf,th->fh", features, grad_act * jnp.cos(hidden_pre), precision=precise
    )
    return (grad_first, grad_second_part)


def embed_lookup(ids, live, embed, seq_rank):
    tok_rows = ids.shape[1]
    places = seq_rank * tok_rows + jnp.arange(tok_rows, dtype=jnp.int32)
    keep_mask = (places[None, :] < live[:, None]).astype(jnp.float32)
    vocab_ids = jnp.arange(embed.shape[0], dtype=jnp.int32)
    onehot = (ids[:, :, None] == vocab_ids[None, None, :]).astype(jnp.float32) * keep_mask[
        :, :, None
    ]
    stream = jnp.einsum("mtv,vd->mtd", onehot, embed, precision=precise)
    return (stream, onehot, keep_mask)


def channel_total(partial_sum):
    return lax.psum(partial_sum, "ch")


def input_total(partial_sum):
    return lax.psum(partial_sum, "ch")


def layer_forward(stream, params, filt_spec, skip_part, tables):
    norm_gains, w_in, kernel, w_out, w_up, w_down = params
    normed = layer_norm(stream, norm_gains[0]).astype(jnp.bfloat16)
    mixed_in = jnp.einsum("mtd,dgc->mtgc", normed, w_in, preferred_element_type=jnp.float32)
    rim_rows = passed_along(mixed_in[:, -2:], "seq", 1)
    padded = jnp.concatenate([rim_rows, mixed_in], axis=1)
    micro_count, tok_rows = (mixed_in.shape[0], mixed_in.shape[1])
    chan_width = mixed_in.shape[3]
    gate_vals = (
        kernel[0] * mixed_in
        + kernel[1] * padded[:, 1 : tok_rows + 1]
        + kernel[2] * padded[:, 0:tok_rows]
    )
    product_in = gate_vals[:, :, 2] * gate_vals[:, :, 1]
    flat_rows = jnp.swapaxes(product_in, 1, 2).reshape(1, micro_count * chan_width, tok_rows)
    received = lax.all_to_all(flat_rows, "seq", split_axis=1, concat_axis=2, tiled=True)
    result_sig = causal_filter(received, filt_spec, skip_part, tables)
    conv_flat = lax.all_to_all(result_sig, "seq", split_axis=2, concat_axis=1, tiled=True)
    conv_out = jnp.swapaxes(conv_flat.reshape(micro_count, chan_width, tok_rows), 1, 2)
    gated_out = (conv_out * gate_vals[:, :, 0]).astype(jnp.bfloat16)
    mid_state = stream + channel_total(
        jnp.einsum("mtc,cd->mtd", gated_out, w_out, preferred_element_type=jnp.float32)
    )
    normed_mid = layer_norm(mid_state, norm_gains[1]).astype(jnp.bfloat16)
    pre_act = jnp.einsum("mtd,df->mtf", normed_mid, w_up, preferred_element_type=jnp.float32)
    hidden = jax.nn.gelu(pre_act).astype(jnp.bfloat16)
    new_stream = mid_state + channel_total(
        jnp.einsum("mtf,fd->mtd", hidden, w_down, preferred_element_type=jnp.float32)
    )
    kept_vals = (
        stream,
        normed,
        mixed_in,
        padded,
        gate_vals,
        received,
        conv_out,
        gated_out,
        mid_state,
        normed_mid,
        pre_act,
        hidden,
    )
    return (new_stream, kept_vals)


def layer_backward(grad_stream, kept_vals, params, filt_spec, skip_part, tables):
    norm_gains, w_in, kernel, w_out, w_up, w_down = params
    (
        stream,
        normed,
        mixed_in,
        padded,
        gate_vals,
        moved_in,
        conv_out,
        gated_out,
        mid_state,
        normed_mid,
        pre_act,
        hidden,
    ) = kept_vals
    micro_count, tok_rows = (mixed_in.shape[0], mixed_in.shape[1])
    chan_width = mixed_in.shape[3]
    grad_low = grad_stream.astype(jnp.bfloat16)
    grad_down = jnp.einsum("mtf,mtd->fd", hidden, grad_low, preferred_element_type=jnp.float32)
    grad_hidden = jnp.einsum("mtd,fd->mtf", grad_low, w_down, preferred_element_type=jnp.float32)
    _, gelu_back = jax.vjp(jax.nn.gelu, pre_act)
    grad_pre = gelu_back(grad_hidden)[0].astype(jnp.bfloat16)
    grad_up = jnp.einsum("mtd,mtf->df", normed_mid, grad_pre, preferred_element_type=jnp.float32)
    grad_normed_mid = input_total(
        jnp.einsum("mtf,df->mtd", grad_pre, w_up, preferred_element_type=jnp.float32)
    )
    _, norm_back_mid = jax.vjp(layer_norm, mid_state, norm_gains[1])
    grad_mid_norm, grad_gain_mid = norm_back_mid(grad_normed_mid)
    grad_mid = grad_stream + grad_mid_norm
    grad_mid_low = grad_mid.astype(jnp.bfloat16)
    grad_out = jnp.einsum(
        "mtc,mtd->cd", gated_out, grad_mid_low, preferred_element_type=jnp.float32
    )
    grad_gated = jnp.einsum("mtd,cd->mtc", grad_mid_low, w_out, preferred_element_type=jnp.float32)
    grad_conv = grad_gated * gate_vals[:, :, 0]
    grad_first_gate = grad_gated * conv_out
    grad_flat = jnp.swapaxes(grad_conv, 1, 2).reshape(1, micro_count * chan_width, tok_rows)
    grad_cols = lax.all_to_all(grad_flat, "seq", split_axis=1, concat_axis=2, tiled=True)
    grad_u_cols, grad_filt, grad_skip_part = filter_backward(
        grad_cols, moved_in, filt_spec, skip_part, tables
    )
    grad_back_flat = lax.all_to_all(grad_u_cols, "seq", split_axis=2, concat_axis=1, tiled=True)
    grad_product = jnp.swapaxes(grad_back_flat.reshape(micro_count, chan_width, tok_rows), 1, 2)
    grad_gates = jnp.stack(
        [grad_first_gate, grad_product * gate_vals[:, :, 2], grad_product * gate_vals[:, :, 1]],
        axis=2,
    )
    rim_back = passed_along(grad_gates[:, :2], "seq", -1)
    extended = jnp.concatenate([grad_gates, rim_back], axis=1)
    grad_mixed = (
        kernel[0] * grad_gates
        + kernel[1] * extended[:, 1 : tok_rows + 1]
        + kernel[2] * extended[:, 2 : tok_rows + 2]
    )
    grad_kernel = jnp.stack(
        [
            jnp.sum(grad_gates * mixed_in, axis=(0, 1)),
            jnp.sum(grad_gates * padded[:, 1 : tok_rows + 1], axis=(0, 1)),
            jnp.sum(grad_gates * padded[:, 0:tok_rows], axis=(0, 1)),
        ]
    )
    grad_mixed_low = grad_mixed.astype(jnp.bfloat16)
    grad_in = jnp.einsum(
        "mtd,mtgc->dgc", normed, grad_mixed_low, preferred_element_type=jnp.float32
    )
    grad_normed = input_total(
        jnp.einsum("mtgc,dgc->mtd", grad_mixed_low, w_in, preferred_element_type=jnp.float32)
    )
    _, norm_back_in = jax.vjp(layer_norm, stream, norm_gains[0])
    grad_stream_norm, grad_gain_in = norm_back_in(grad_normed)
    grad_before = grad_mid + grad_stream_norm
    layer_grads = (
        jnp.stack([grad_gain_in, grad_gain_mid]),
        grad_in,
        grad_kernel,
        grad_skip_part,
        grad_out,
        grad_up,
        grad_down,
    )
    return (grad_before, layer_grads, grad_filt)


def local(
    ids,
    live,
    embed,
    norm_gain,
    in_weight,
    short_kernel,
    filter_first,
    filter_second,
    skip_gain,
    out_weight,
    up_weight,
    down_weight,
    cotangent,
):
    seq_count = lax.axis_size("seq")
    seq_rank = lax.axis_index("seq")
    group_idx = lax.axis_index("ch")
    micro_count = ids.shape[0]
    tok_rows = ids.shape[1]
    length = tok_rows * seq_count
    chan_width = in_weight.shape[3]
    own_rows = micro_count * chan_width // seq_count
    layer_count = in_weight.shape[0]
    row_start = seq_rank * own_rows
    row_ids = row_start + jnp.arange(own_rows, dtype=jnp.int32)
    chan_local = row_ids % chan_width
    first_rows = (row_ids < chan_width).astype(jnp.float32)
    select = (jnp.arange(chan_width, dtype=jnp.int32)[:, None] == chan_local[None, :]).astype(
        jnp.float32
    )
    tables = dft_tables(seq_count, tok_rows)
    features = position_features(length)
    ramp_row = jnp.arange(length, dtype=jnp.int32).astype(jnp.float32) / length
    stream, onehot, keep_mask = embed_lookup(ids, live, embed, seq_rank)
    filters = []
    for level_idx in range(layer_count):
        filt_cols, hidden_pre, hidden_act, second_part, decay_part = local_filter(
            filter_first[level_idx],
            filter_second[level_idx],
            features,
            select,
            group_idx,
            chan_local,
        )
        filt_spec = to_spectrum(filt_cols.reshape(own_rows, seq_count, tok_rows), tables)
        skip_part = jnp.dot(skip_gain[level_idx], select, precision=precise)
        penalty_grad = 0.5 * length * ramp_row[None, :] * filt_cols * first_rows[:, None]
        params = (
            norm_gain[level_idx],
            in_weight[level_idx],
            short_kernel[level_idx],
            out_weight[level_idx],
            up_weight[level_idx],
            down_weight[level_idx],
        )
        filters.append(
            (
                params,
                filt_spec,
                skip_part,
                (hidden_pre, hidden_act, second_part, decay_part),
                penalty_grad,
            )
        )
    stored = []
    for level_idx in range(layer_count):
        params, filt_spec, skip_part, _, _ = filters[level_idx]
        layer_input = stream
        stream, kept_vals = layer_forward(stream, params, filt_spec, skip_part, tables)
        stored.append(layer_input)
    block_out = stream * keep_mask[:, :, None]
    grad_stream = cotangent * keep_mask[:, :, None]
    collected = [None] * layer_count
    first_grads = [None] * layer_count
    grad_embed = None
    for level_idx in reversed(range(layer_count)):
        params, filt_spec, skip_part, filter_parts, penalty_grad = filters[level_idx]
        _, kept_vals = layer_forward(stored[level_idx], params, filt_spec, skip_part, tables)
        grad_stream, layer_grads, grad_filt = layer_backward(
            grad_stream, kept_vals, params, filt_spec, skip_part, tables
        )
        grad_first, grad_second_part = filter_mlp_backward(
            grad_filt + penalty_grad, features, filter_parts
        )
        first_grads[level_idx] = grad_first
        grad_second = jnp.dot(grad_second_part, select.T, precision=precise)
        grad_skip = jnp.dot(layer_grads[3], select.T, precision=precise)
        gain_grad, in_grad, kernel_grad, _, out_grad, up_grad, down_grad = layer_grads
        if level_idx == 0:
            embed_part = jnp.einsum("mtv,mtd->vd", onehot, grad_stream, precision=precise)
            summed = lax.psum(
                (
                    gain_grad,
                    in_grad,
                    kernel_grad,
                    grad_second,
                    grad_skip,
                    out_grad,
                    up_grad,
                    down_grad,
                    embed_part,
                ),
                "seq",
            )
            collected[level_idx] = summed[:8]
            grad_embed = summed[8]
        else:
            collected[level_idx] = lax.psum(
                (
                    gain_grad,
                    in_grad,
                    kernel_grad,
                    grad_second,
                    grad_skip,
                    out_grad,
                    up_grad,
                    down_grad,
                ),
                "seq",
            )
    stacked = [
        jnp.stack([collected[level_idx][member] for level_idx in range(layer_count)])
        for member in range(8)
    ]
    filter_grads = lax.psum(jnp.stack(first_grads), ("seq", "ch"))
    return (
        block_out,
        grad_embed,
        stacked[0],
        stacked[1],
        stacked[2],
        filter_grads,
        stacked[3],
        stacked[4],
        stacked[5],
        stacked[6],
        stacked[7],
    )


HALO = 16
FEAT_ROWS = 40
ROOT_HALF = math.sqrt(0.5)
GELU_A = math.sqrt(2.0 / math.pi)
GELU_B = 0.044715
BLOCKS = 8
BLOCK = 256
KINDS = 9
VMEM_LIMIT = 8 * 2**20
VMEM_LIMITS = dict(turn_back_kernel=20 * 2**20, back_first_kernel=16 * 2**20)
FLOPS, FEW_FLOPS, MANY_FLOPS = 10**10, 10**8, 10**12
FLOPS_OF = dict(conv_first1=100000000, pair5=10000000000, grad_freq1=30000000000, last1=1000000000, conv_second1=3000000000, join_weights2=100000000)
CALLS = collections.Counter()
f32 = jnp.float32
bf16 = jnp.bfloat16


class Numbers:
    def __init__(self, table):
        self.table = table

    def __getitem__(self, row):
        return self.table[row, 0]


CORE, GROUP, LIVE, WHICH, SPOT, HOLDER, BIT1, BIT2, BIT3 = range(9)
NUMBER_ROWS = 16


def bring(pairs, done):
    copies = [pltpu.make_async_copy(far, near, done.at[i]) for i, (far, near) in enumerate(pairs)]
    for copy in copies:
        copy.start()
    for copy in copies:
        copy.wait()


def numbers_kernel(*refs):
    far, (table, own_ids, cot, pack, part), near, done = refs[:13], refs[13:18], refs[18:30], refs[30]
    far_live, far_ids, far_cot, far_embed, far_gain, far_in, far_second, far_short, far_skip, far_out, far_up, far_down, far_in1 = far
    live, ids, embed, gain, in_own, second, short, skip, raw_out, raw_up, raw_down, in1 = near
    rank, group = lax.axis_index("seq"), lax.axis_index("ch")
    bring(
        (
            (far_live, live), (far_ids, ids), (far_cot.at[group], cot.at[0]), (far_embed, embed), (far_gain, gain),
            (far_in.at[0], in_own), (far_second, second), (far_short, short), (far_skip, skip), (far_out.at[0], raw_out),
            (far_up.at[0], raw_up), (far_down.at[0], raw_down), (far_in1.at[1], in1),
        ),
        done,
    )
    fill_pack(embed, gain, in_own, second, short, skip, pack)
    core, half = rank % 2, lax.axis_size("seq") // 2
    first = group == 0
    holder = jnp.where(rank // half == core, 1, 0)
    values = (core, group, None, group + core - 2 * group * core, rank % half, holder, rank // 2 % 2, rank // 4 % 2, rank // 8 % 2)
    for row, value in enumerate(values):
        if row != LIVE:
            table[row : row + 1, :] = jnp.full((1, 128), value, jnp.int32)
    chosen = jnp.where(first, live[0:1, 0:1], live[0:1, 1:2])
    table[LIVE : LIVE + 1, :] = jnp.broadcast_to(chosen, (1, 128))
    own_ids[0] = jnp.broadcast_to(jnp.where(first, ids[0:1, :], ids[1:2, :]), own_ids.shape[1:])
    s = Numbers(table)
    fill_part(s, raw_out, raw_up, raw_down, part)
    fill_in_part(s, in1, part.at[1152:1536])


def in_hbm(value):
    return pltpu.with_memory_space_constraint(value, pltpu.HBM)


def start(body, outs, *arrays, scratch):
    vmem, far = pl.BlockSpec(memory_space=pltpu.VMEM), pl.BlockSpec(memory_space=pltpu.HBM)
    return pl.pallas_call(
        body, out_shape=outs, in_specs=[far] * len(arrays), out_specs=[vmem] * len(outs), name=body.__name__,
        scratch_shapes=list(scratch),
        cost_estimate=pl.CostEstimate(flops=MANY_FLOPS, bytes_accessed=1, transcendentals=0),
        compiler_params=pltpu.CompilerParams(vmem_limit_bytes=VMEM_LIMIT),
    )(*(in_hbm(v) for v in arrays))


def run(body, outs, scalars, *arrays, scratch=(), after=(), hbm=(), flops=None, hbm_outs=(), aliases=(), token=False):
    vmem = pl.BlockSpec(memory_space=pltpu.VMEM)
    far, wait = pl.BlockSpec(memory_space=pltpu.HBM), pl.BlockSpec(memory_space=pl.ANY)
    single = not isinstance(outs, (list, tuple))
    shapes = [outs] if single else list(outs)
    count = len(shapes)
    shapes += [arr(8, 128)] * token
    used, waits = 1 + len(arrays), len(after)

    def call(table, *refs):
        given, rest = refs[: used - 1], refs[used - 1 + waits :]
        body(Numbers(table), *given, *rest[:count], *rest[count + token :])
        if token:
            rest[count][...] = jnp.zeros((8, 128), f32)

    inner = getattr(body, "func", body)
    CALLS[inner.__name__] += 1
    flops = flops or FLOPS_OF.get(f"{inner.__name__[:-7]}{CALLS[inner.__name__]}", FLOPS)
    result = pl.pallas_call(
        call,
        out_shape=shapes,
        in_specs=[vmem] + [far if i in hbm else vmem for i in range(len(arrays))] + [wait] * waits,
        out_specs=[far if i in hbm_outs else vmem for i in range(len(shapes))],
        input_output_aliases={1 + a: b for a, b in aliases},
        scratch_shapes=list(scratch),
        compiler_params=pltpu.CompilerParams(vmem_limit_bytes=VMEM_LIMITS.get(inner.__name__, VMEM_LIMIT)),
        cost_estimate=pl.CostEstimate(flops=flops, bytes_accessed=1, transcendentals=0),
        name=inner.__name__,
    )(scalars, *(in_hbm(v) if i in hbm else v for i, v in enumerate(arrays)), *after)
    return result[0] if len(shapes) == 1 else result


def arr(*shape, kind=f32):
    return jax.ShapeDtypeStruct(shape, kind)


def mm(a, b):
    return jnp.dot(a, b, preferred_element_type=f32)


def mm_nt(a, b):
    return lax.dot_general(a, b, (((1,), (1,)), ((), ())), preferred_element_type=f32)


def mm_tn(a, b):
    return lax.dot_general(a, b, (((0,), (0,)), ((), ())), preferred_element_type=f32)


def split(a):
    high = a.astype(bf16)
    return high, (a - high.astype(f32)).astype(bf16)


def unit(rows):
    center = rows - jnp.mean(rows, axis=-1, keepdims=True)
    scale = lax.rsqrt(jnp.mean(center * center, axis=-1, keepdims=True) + epsilon)
    return center * scale, scale


def unit_back(grad, normal, scale):
    inner = jnp.mean(grad * normal, axis=-1, keepdims=True)
    return scale * (grad - jnp.mean(grad, axis=-1, keepdims=True) - normal * inner)


def every(count, step):
    for i in range(count):
        step(i, 0)


def at(start, size, unit_rows=16):
    return pl.ds(start if isinstance(start, int) else pl.multiple_of(start, unit_rows), size)


def dft_table():
    turns = np.outer(np.arange(BLOCK), np.arange(BLOCK)) % BLOCK
    angle = 2.0 * np.pi * turns / BLOCK
    return np.concatenate([np.cos(angle), np.sin(angle)], axis=1).astype(np.float32)


def twiddle_table():
    angle = 2.0 * np.pi * np.outer(np.arange(1, KINDS), np.arange(BLOCK)) / (2 * BLOCKS * BLOCK)
    pair = np.stack([np.cos(angle), np.sin(angle)], axis=1).astype(np.float32)
    return np.broadcast_to(pair[..., None], (KINDS - 1, 2, BLOCK, 128)).copy()


def feature_table(length):
    places = np.arange(length)
    turns = np.outer(places, np.arange(1, (FEAT - 1) // 2 + 1)) % length
    angle = 2.0 * np.pi * turns / length
    ramp = places[:, None] / length
    return np.concatenate([ramp, np.cos(angle), np.sin(angle)], axis=1).astype(np.float32)


def thirds(values):
    low = lambda v: v.astype(ml_dtypes.bfloat16).astype(np.float32)
    first = low(values)
    second = low(values - first)
    return first, second, low(values - first - second)


def feature_parts(length):
    first, second, third = thirds(np.pad(feature_table(length), ((0, 0), (0, FEAT_ROWS - FEAT))))
    return np.pad(np.concatenate([first, first, second, second, first, third], axis=1), ((0, 0), (0, 256 - 6 * FEAT_ROWS)))


def rate_table():
    return (0.3 * 10.0 ** (np.arange(D) / (D - 1))).astype(np.float32).reshape(2, 1, D // 2)


def four_real(a, b, c, d):
    s, m, t, n = a + c, a - c, b + d, b - d
    hn, ht = ROOT_HALF * n, ROOT_HALF * t
    return (s + t, s - t, (a + hn, -(ht + c)), (m, -n), (a - hn, c - ht))


def turn(k):
    angle = 2.0 * math.pi * k / (2 * BLOCKS)
    return math.cos(angle), math.sin(angle)


def put_pair(stage, kind, row, re, im):
    rows = re.shape[0]
    re, im = re.astype(bf16), im.astype(bf16)
    stage[kind, pl.ds(row, rows), 0:128] = re
    stage[kind, pl.ds(row, rows), 128:256] = im
    stage[kind, pl.ds(row + BLOCK, rows), 0:128] = im
    stage[kind, pl.ds(row + BLOCK, rows), 128:256] = -re


def put_pair_back(stage, kind, row, re, im):
    rows = re.shape[0]
    re, im = re.astype(bf16), im.astype(bf16)
    stage[kind, pl.ds(row, rows), 0:128] = re
    stage[kind, pl.ds(row, rows), 128:256] = im
    stage[kind, pl.ds(row + BLOCK, rows), 0:128] = -im
    stage[kind, pl.ds(row + BLOCK, rows), 128:256] = re


def all_kinds(dft, stage, out):
    table = dft[...]
    for kind in range(KINDS):
        out[kind] = mm(table, stage[kind])


def to_freq(load, dft, twiddle, stage, out):
    def chunk(step, carry):
        row = step * 16
        u = [load(p, row) for p in range(BLOCKS)]
        e0, e4, e1, e2, e3 = four_real(u[0], u[2], u[4], u[6])
        o0, o4, o1, o2, o3 = four_real(u[1], u[3], u[5], u[7])

        def put(kind, re, im):
            c, s = twiddle[kind - 1, 0, pl.ds(row, 16), :], twiddle[kind - 1, 1, pl.ds(row, 16), :]
            put_pair(stage, kind, row, re * c + im * s, im * c - re * s)

        put_pair(stage, 0, row, e0 + o0, jnp.zeros_like(e0))
        last = e0 - o0
        c, s = twiddle[7, 0, pl.ds(row, 16), :], twiddle[7, 1, pl.ds(row, 16), :]
        put_pair(stage, 8, row, last * c, -(last * s))
        put(4, e4, -o4)
        for k, (er, ei), (orr, oi) in ((1, e1, o1), (2, e2, o2), (3, e3, o3)):
            c, s = turn(k)
            wr, wi = orr * c + oi * s, oi * c - orr * s
            put(k, er + wr, ei + wi)
            put(8 - k, er - wr, wi - ei)
        return carry

    every(BLOCK // 16, chunk)
    all_kinds(dft, stage, out)


def from_freq(dft, twiddle, stage, back, store):
    all_kinds(dft, stage, back)

    def chunk(step, carry):
        row = step * 16

        def get(kind):
            re = back[kind, pl.ds(row, 16), 0:128]
            im = back[kind, pl.ds(row, 16), 128:256]
            c, s = twiddle[kind - 1, 0, pl.ds(row, 16), :], twiddle[kind - 1, 1, pl.ds(row, 16), :]
            return re * c - im * s, re * s + im * c

        first = 0.5 * back[0, pl.ds(row, 16), 0:128]
        last = 0.5 * get(8)[0]
        mid_re, mid_im = get(4)
        even, odd = {}, {}
        for k in (1, 2, 3):
            ar, ai = get(k)
            br, bi = get(8 - k)
            even[k] = (ar + br, ai - bi)
            c, s = turn(k)
            dr, di = ar - br, ai + bi
            odd[k] = (dr * c - di * s, dr * s + di * c)
        for shift, base, extra, part in (
            (0, first + last, mid_re, even),
            (1, first - last, -mid_im, odd),
        ):
            (r1, i1), (r2, i2), (r3, i3) = part[1], part[2], part[3]
            plus, minus = base + extra, base - extra
            diff, both = ROOT_HALF * (r1 - r3), ROOT_HALF * (i1 + i3)
            store(shift, row, plus + (r1 + r2 + r3))
            store(shift + 2, row, minus - i2 + (diff - both))
            store(shift + 4, row, plus - r2 - (i1 - i3))
            store(shift + 6, row, minus + i2 - (diff + both))
        return carry

    every(BLOCK // 16, chunk)


def times(first, second, stage, conj):
    def chunk(step, carry):
        row = step * 16
        for kind in range(KINDS):
            fr = first[kind, pl.ds(row, 16), 0:128]
            fi = first[kind, pl.ds(row, 16), 128:256]
            ur = second[kind, pl.ds(row, 16), 0:128]
            ui = second[kind, pl.ds(row, 16), 128:256]
            if conj:
                put_pair_back(stage, kind, row, fr * ur + fi * ui, fr * ui - fi * ur)
            else:
                put_pair_back(stage, kind, row, fr * ur - fi * ui, fr * ui + fi * ur)
        return carry

    every(BLOCK // 16, chunk)


SPECTRUM = (KINDS, BLOCK, 256)


def stage_scratch():
    return pltpu.VMEM((KINDS, 2 * BLOCK, 256), bf16)


def spec_scratch():
    return pltpu.VMEM(SPECTRUM, f32)


PACK_SECOND = 48
PACK_SHORT = 176
PACK_SKIP = 194
PACK_ROWS = 200


def fill_pack(embed, gain, in_own, second, short, skip, out):
    normal, _ = unit(embed[...])
    low = (normal * gain[0, 0:1, :]).astype(bf16)
    for g in range(3):
        out[16 * g : 16 * g + 16, :] = mm(low, in_own[g])
    for l in range(2):
        out[PACK_SECOND + 64 * l : PACK_SECOND + 64 * l + 64, :] = second[l]
        for k in range(3):
            for g in range(3):
                row = PACK_SHORT + 9 * l + 3 * k + g
                out[row : row + 1, :] = short[k, g, l : l + 1, :]
    out[PACK_SKIP : PACK_SKIP + 2, :] = skip[...]
    out[PACK_SKIP + 2 : PACK_ROWS, :] = jnp.zeros((PACK_ROWS - PACK_SKIP - 2, 128), f32)


def table_kernel(s, own, peer, embed, mine_out, other_out, conv_table, gate_table):
    first = s[CORE] == 0
    mine = jnp.where(first, own[...], peer[...])
    other = jnp.where(first, peer[...], own[...])
    mine_out[...] = mine
    other_out[...] = other

    def fill(table, lanes, parts):
        whole = jnp.concatenate(parts, axis=0)
        high, low = split(whole)
        table[0:48, lanes] = high
        table[48:96, lanes] = low
        table[96:128, lanes] = jnp.zeros((32, 128), bf16)

    def gate(pack, g):
        parts = []
        for k in range(3):
            row = PACK_SHORT + 3 * k + g
            parts.append(pack[16 * g : 16 * g + 16] * pack[row : row + 1])
        return parts

    fill(conv_table, slice(0, 128), gate(mine, 1))
    fill(conv_table, slice(128, 256), gate(mine, 2))
    fill(gate_table, slice(0, 128), gate(mine, 0))
    fill(gate_table, slice(128, 256), gate(other, 0))
    zero = jnp.zeros((16, 128), f32)
    fill(gate_table, slice(256, 384), [embed[:, 0:128], zero, zero])
    fill(gate_table, slice(384, 512), [embed[:, 128:256], zero, zero])


def onehot_kernel(s, ids, out, turned, work):
    live = s[LIVE]
    count, _, width = ids.shape
    work[0:HALO, :] = jnp.zeros((HALO, 128), f32)
    work[HALO + count * width : 2 * HALO + count * width, :] = jnp.zeros((HALO, 128), f32)
    vocab = lax.broadcasted_iota(jnp.int32, (128, width), 0) % 16
    place = lax.broadcasted_iota(jnp.int32, (128, width), 1)
    for i in range(count):
        token = jnp.broadcast_to(ids[i, 0:1, :], (128, width))
        hit = (token == vocab) & (place + i * width < live)
        work[HALO + width * i : HALO + width * (i + 1), :] = jnp.where(hit, 1.0, 0.0).T
    lane = lax.broadcasted_iota(jnp.int32, (width, 128), 1) % 48 // 16
    used = lax.broadcasted_iota(jnp.int32, (width, 128), 1) < 96
    half = count // 2
    for i in range(count):
        row = HALO + width * i
        now = work[row : row + width, :]
        one = work[row - 1 : row - 1 + width, :]
        two = work[row - 2 : row - 2 + width, :]
        picked = jnp.where(lane == 0, now, jnp.where(lane == 1, one, two))
        picked = jnp.where(used, picked, 0.0)
        out[row : row + width, :] = picked.astype(bf16)
        turned[i // half, :, width * (i % half) : width * (i % half + 1)] = picked.T.astype(bf16)
    out[0:HALO, :] = jnp.zeros((HALO, 128), bf16)
    out[HALO + count * width : 2 * HALO + count * width, :] = jnp.zeros((HALO, 128), bf16)


def sine_and_cosine(angle):
    turns = jnp.round(angle * (2.0 / math.pi))
    x = ((angle - turns * 1.5703125) - turns * 4.837512969970703125e-4) - turns * 7.549789948768648e-8
    z = x * x
    sin = ((-1.9515295891e-4 * z + 8.3321608736e-3) * z - 1.6666654611e-1) * z * x + x
    cos = ((2.443315711809948e-5 * z - 1.388731625493765e-3) * z + 4.166664568298827e-2) * z * z - 0.5 * z + 1.0
    quarter = turns.astype(jnp.int32) & 3
    odd = (quarter & 1) == 1
    first, second = jnp.where(odd, cos, sin), jnp.where(odd, sin, cos)
    first = jnp.where(quarter >= 2, -first, first)
    second = jnp.where((quarter == 1) | (quarter == 2), -second, second)
    return first, second


def sine_kernel(s, feats, firsts, sine, cosine, turned, padded):
    padded[...] = jnp.zeros_like(padded)
    for l in range(2):
        padded[0:FEAT, 64 * l : 64 * l + 64] = firsts[:, l, :]
    both = padded[...]
    cut = lambda v: v.astype(bf16).astype(f32)
    first = cut(both)
    second = cut(both - first)
    third = both - first - second
    fill = jnp.zeros((256 - 6 * FEAT_ROWS, 128), f32)
    weights = jnp.concatenate([first, second, first, second, third, first, fill], axis=0).astype(bf16)
    count = feats.shape[0] // 512

    def chunk(i, carry):
        rows = at(512 * i, 512)
        act, cosine[rows, :] = sine_and_cosine(mm(feats[rows, :], weights))
        sine[rows, 0:128], sine[rows, 128:256] = split(act)
        turned[:, at(512 * i, 512, 256)] = act.T.astype(bf16)
        return carry

    every(count, chunk)


def decay_of(rates, start, rows, length):
    place = (lax.broadcasted_iota(jnp.int32, (rows, 1), 0) + start).astype(f32) / length
    return jnp.exp(-place * rates), place


def filter_kernel(level, s, sine, mine, rates, dft, twiddle, filt, freq, stage):
    length = sine.shape[0]
    rate = rates[s[WHICH]]
    zero = jnp.zeros((64, 128), f32)
    second = mine[PACK_SECOND + 64 * level : PACK_SECOND + 64 * level + 64]
    high, low = split(jnp.concatenate([zero, second] if level else [second, zero], axis=0))
    twice = jnp.concatenate([high, high], axis=0)

    def chunk(i, carry):
        rows = at(512 * i, 512)
        decay, _ = decay_of(rate, 512 * i, 512, length)
        filt[rows, :] = (mm(sine[rows, :], twice) + mm(sine[rows, 0:128], low)) * decay
        return carry

    every(length // 512, chunk)
    to_freq(lambda p, row: filt[pl.ds(BLOCK * p + row, 16), :] * (1.0 / length), dft, twiddle, stage, freq)


def causal(load, skip_row, freq_filt, dft, twiddle, spec, stage, work, line):
    to_freq(load, dft, twiddle, stage, spec)
    times(freq_filt, spec, stage, False)

    def store(p, row, value):
        line[pl.ds(HALO + BLOCK * p + row, 16), :] = value + skip_row * load(p, row)

    from_freq(dft, twiddle, stage, work, store)


def hand_out(s, line, keep, send):
    half = (line.shape[0] - 2 * HALO) // 2
    span = half + 2 * HALO
    k = s[CORE]
    line[0:HALO, :] = jnp.zeros((HALO, 128), f32)
    line[HALO + 2 * half :, :] = jnp.zeros((HALO, 128), f32)
    keep[...] = line[at(half * k, span), :]
    send[...] = line[at(half * (1 - k), span), :]


def conv_first_kernel(s, onehot, conv_table, mine, freq_filt, dft, twiddle, keep, send, spec, product, stage, work, line):
    def chunk(i, carry):
        rows = at(512 * i, 512)
        pair = mm(onehot[at(512 * i + HALO, 512), :], conv_table[...])
        product[rows, :] = pair[:, 0:128] * pair[:, 128:256]
        return carry

    every(product.shape[0] // 512, chunk)
    skip_row = mine[PACK_SKIP : PACK_SKIP + 1, :]
    causal(lambda p, row: product[pl.ds(BLOCK * p + row, 16), :], skip_row, freq_filt, dft, twiddle, spec, stage, work, line)
    hand_out(s, line, keep, send)


def join_rows(s, whole, kept, received):
    half = kept.shape[0]
    whole[at(half * s[CORE], half), :] = kept[...]
    whole[at(half * (1 - s[CORE]), half), :] = received[...]


def conv_second_kernel(s, kept, received, mine, freq_filt, dft, twiddle, keep, send, spec, product, stage, work, line):
    join_rows(s, product, kept, received)
    skip_row = mine[PACK_SKIP + 1 : PACK_SKIP + 2, :]
    causal(lambda p, row: product[pl.ds(BLOCK * p + row, 16), :], skip_row, freq_filt, dft, twiddle, spec, stage, work, line)
    hand_out(s, line, keep, send)


def gelu_parts(p):
    squared = p * p
    th = jnp.tanh(GELU_A * p * (1.0 + GELU_B * squared))
    half = 0.5 * (1.0 + th)
    slope = half + 0.5 * p * (1.0 - th * th) * (GELU_A + (3.0 * GELU_A * GELU_B) * squared)
    return p * half, slope


def gelu_only(p):
    return 0.5 * p * (1.0 + jnp.tanh(GELU_A * p * (1.0 + GELU_B * (p * p))))


def forward_first_kernel(
    s, onehot, gate_table, conv_mine, conv_other, gain, w_out, w_up, w_down, w_in, mine, other,
    keep, send, mid_out, stream_out, gates, mixed,
):
    span = mid_out.shape[0]
    half = span - 2 * HALO
    k = s[CORE]
    taps = [
        jnp.concatenate([pack[PACK_SHORT + 9 + 3 * t + g : PACK_SHORT + 10 + 3 * t + g, :] for g in range(3) for pack in (mine, other)], axis=1)
        for t in range(3)
    ]

    def chunk(i, carry):
        rows = at(span * i, span)
        looked = mm(onehot[at(half * k + span * i, span), :], gate_table[...])
        conv = jnp.concatenate([conv_mine[rows, :], conv_other[rows, :]], axis=1)
        gated = (conv * looked[:, 0:256]).astype(bf16)
        mid = looked[:, 256:512] + mm(gated, w_out[...])
        mid_out[rows, :] = mid
        normal, _ = unit(mid)
        low = (normal * gain[0, 1:2, :]).astype(bf16)
        hidden = gelu_only(mm(low, w_up[...])).astype(bf16)
        stream = mid + mm(hidden, w_down[...])
        stream_out[rows, :] = stream
        normal, _ = unit(stream)
        low = (normal * gain[1, 0:1, :]).astype(bf16)
        mixed[rows, :] = mm(low, w_in[...])
        return carry

    every(1, chunk)
    gates[0:HALO, :] = jnp.zeros((HALO, 768), f32)
    step = 80
    for start in range(HALO, span, step):
        stop = start + step
        gates[start:stop, :] = (
            taps[0] * mixed[start:stop, :]
            + taps[1] * mixed[start - 1 : stop - 1, :]
            + taps[2] * mixed[start - 2 : stop - 2, :]
        )
    own = slice(HALO, HALO + half)
    keep[...] = gates[own, 256:384] * gates[own, 512:640]
    send[...] = gates[own, 384:512] * gates[own, 640:768]


def turn_back_kernel(
    s, conv_mine, conv_other, gates, stream, cot, cot_rim, gain, w_out, w_up, w_down,
    keep, send, grad_x0, grad_mid, block_out, hidden_out, low_out, normed_out, pre_out, gated_out, mid_low_out, gain_out,
    cot_rows, conv_grads,
):
    span = stream.shape[0]
    half = span - 2 * HALO
    k = s[CORE]
    live = s[LIVE]
    cot_rows[0:HALO, :] = jnp.zeros((HALO, 256), f32)
    cot_rows[HALO : HALO + half, :] = cot[...]
    cot_rows[HALO + half :, :] = jnp.where(k == 0, cot_rim[...], 0.0)
    gain_out[...] = jnp.zeros_like(gain_out)

    def chunk(i, carry):
        rows = at(span * i, span)
        local_row = lax.broadcasted_iota(jnp.int32, (span, 1), 0) + span * i
        keep_mask = (local_row + (half * k - HALO) < live).astype(f32)
        own_mask = ((local_row >= HALO) & (local_row < HALO + half)).astype(f32)
        x0 = gates[rows, 0:256]
        conv = jnp.concatenate([conv_mine[rows, :], conv_other[rows, :]], axis=1)
        gated = (conv * x0).astype(bf16)
        gated_out[rows, :] = gated
        mid = stream[rows, :] + mm(gated, w_out[...])
        normal, scale = unit(mid)
        gain_row = gain[1, 1:2, :]
        low = (normal * gain_row).astype(bf16)
        normed_out[rows, :] = low
        act, slope = gelu_parts(mm(low, w_up[...]))
        hidden = act.astype(bf16)
        hidden_out[rows, :] = hidden
        block_out[rows, :] = (mid + mm(hidden, w_down[...])) * keep_mask
        grad = cot_rows[rows, :] * keep_mask
        grad_low = grad.astype(bf16)
        low_out[rows, :] = grad_low
        grad_pre = (slope * mm_nt(grad_low, w_down[...])).astype(bf16)
        pre_out[rows, :] = grad_pre
        grad_normed = mm_nt(grad_pre, w_up[...])
        gain_out[0:1, :] += jnp.sum(grad_normed * normal * own_mask, axis=0, keepdims=True)
        mid_grad = grad + unit_back(grad_normed * gain_row, normal, scale)
        grad_mid[rows, :] = mid_grad
        mid_low = mid_grad.astype(bf16)
        mid_low_out[rows, :] = mid_low
        grad_gated = mm_nt(mid_low, w_out[...])
        conv_grads[rows, :] = grad_gated * x0
        grad_x0[rows, :] = grad_gated * conv
        return carry

    every(1, chunk)
    own = slice(HALO, HALO + half)
    keep[...] = conv_grads[own, 0:128]
    send[...] = conv_grads[own, 128:256]


def conv_back_kernel(s, kept, received, mine, freq_filt, dft, twiddle, keep, send, spec, grads, stage, work, line):
    join_rows(s, grads, kept, received)
    skip_row = mine[PACK_SKIP + 1 : PACK_SKIP + 2, :]
    load = lambda p, row: grads[pl.ds(BLOCK * p + row, 16), :]
    to_freq(load, dft, twiddle, stage, spec)
    times(freq_filt, spec, stage, True)

    def store(p, row, value):
        line[pl.ds(HALO + BLOCK * p + row, 16), :] = value + skip_row * load(p, row)

    from_freq(dft, twiddle, stage, work, store)
    hand_out(s, line, keep, send)


def grad_freq_kernel(s, kept, received, dft, twiddle, spec, grads, stage):
    join_rows(s, grads, kept, received)
    to_freq(lambda p, row: grads[pl.ds(BLOCK * p + row, 16), :], dft, twiddle, stage, spec)


def filter_back(
    level, s, spec_grad, spec_in, grads, product, filt, cosine, sine_turned, mine, rates, feats_turned, dft, twiddle,
    second_out, first_out, skip_out, stage, work, line,
):
    length = filt.shape[0]
    times(spec_in, spec_grad, stage, True)

    def store(p, row, value):
        line[pl.ds(BLOCK * p + row, 16), :] = value

    from_freq(dft, twiddle, stage, work, store)
    rate = rates[s[WHICH]]
    second = mine[PACK_SECOND + 64 * level : PACK_SECOND + 64 * level + 64, :].astype(bf16)
    weight = jnp.where(s[GROUP] == 0, 0.5 * length, 0.0)
    skip_out[...] = jnp.zeros_like(skip_out)
    second_out[...] = jnp.zeros_like(second_out)
    first_out[...] = jnp.zeros_like(first_out)
    for i in range(length // 512):
        rows = slice(512 * i, 512 * (i + 1))
        decay, place = decay_of(rate, 512 * i, 512, length)
        shaped = ((line[rows, :] * (1.0 / length) + (weight * place) * filt[rows, :]) * decay).astype(bf16)
        skip_out[...] += jnp.sum((grads[rows, :] * product[rows, :]).reshape(64, 8, 128), axis=0)
        second_out[...] += mm(sine_turned[64 * level : 64 * level + 64, rows], shaped)
        inner = (mm_nt(shaped, second) * cosine[rows, 64 * level : 64 * level + 64]).astype(bf16)
        first_out[...] += mm(feats_turned[:, rows], inner)


def filter_back_kernel(s, *refs):
    filter_back(1, s, *refs)


def token_back_kernel(
    s, spec_grad, spec_in, grads, product, filt, cosine, sine_turned, mine, rates, feats_turned, dft, twiddle,
    freq_filt, onehot, turned, conv_table, second_out, first_out, skip_out, by_token, stage, work, line,
):
    length = grads.shape[0]
    skip_row = mine[PACK_SKIP : PACK_SKIP + 1, :]
    times(freq_filt, spec_grad, stage, True)

    def store(p, row, value):
        line[pl.ds(BLOCK * p + row, 16), :] = value + skip_row * grads[pl.ds(BLOCK * p + row, 16), :]

    from_freq(dft, twiddle, stage, work, store)
    by_token[...] = jnp.zeros_like(by_token)
    width = turned.shape[2]
    for i in range(length // width):
        rows = slice(width * i, width * (i + 1))
        pair = mm(onehot[HALO + width * i : HALO + width * (i + 1), :], conv_table[...])
        back = line[rows, :]
        gate_grads = jnp.concatenate([back * pair[:, 128:256], back * pair[:, 0:128]], axis=1).astype(bf16)
        by_token[...] += mm(turned[i], gate_grads)[0:48, :]
    filter_back(
        0, s, spec_grad, spec_in, grads, product, filt, cosine, sine_turned, mine, rates, feats_turned, dft, twiddle,
        second_out, first_out, skip_out, stage, work, line,
    )


def back_gates_kernel(
    s, prod_mine, prod_other, grad_x0, gates, mixed, grad_mid, stream, gain, mine, other, w_in,
    grad_stream, normed_out, mixed_low, short_out, gain_out, line,
):
    span = stream.shape[0]
    half = span - 2 * HALO
    taps = [
        jnp.concatenate([pack[PACK_SHORT + 9 + 3 * t + g : PACK_SHORT + 10 + 3 * t + g, :] for g in range(3) for pack in (mine, other)], axis=1)
        for t in range(3)
    ]
    step = 128
    for start in list(range(HALO, HALO + half, step)) + [HALO + half]:
        stop = start + (step if start < HALO + half else HALO)
        for lanes, prod in ((slice(0, 128), prod_mine), (slice(128, 256), prod_other)):
            first, second = slice(256 + lanes.start, 256 + lanes.stop), slice(512 + lanes.start, 512 + lanes.stop)
            product = prod[start:stop, :]
            line[start:stop, lanes] = product * gates[start:stop, second]
            line[start:stop, first] = product * gates[start:stop, first]
    short_out[...] = jnp.zeros_like(short_out)
    gain_out[...] = jnp.zeros_like(gain_out)
    for start in range(HALO, HALO + half, step):
        stop = start + step
        for g in range(3):
            lanes = slice(256 * g, 256 * g + 256)
            values = mixed[start:stop, lanes]
            total = None
            for t in range(3):
                shifted = grad_x0[start + t : stop + t, :] if g == 0 else line[start + t : stop + t, 256 * g - 256 : 256 * g]
                part = taps[t][:, lanes] * shifted
                total = part if total is None else total + part
                short_out[t, :, lanes] += jnp.sum((shifted * values).reshape(step // 8, 8, 256), axis=0)
            mixed_low[start - HALO : stop - HALO, lanes] = total.astype(bf16)

    def chunk(i, carry):
        rows = at(512 * i, 512)
        wide = at(512 * i + HALO, 512)
        normal, scale = unit(stream[wide, :])
        gain_row = gain[1, 0:1, :]
        normed_out[rows, :] = (normal * gain_row).astype(bf16)
        grad_normed = mm_nt(mixed_low[rows, :], w_in[...])
        gain_out[0:1, :] += jnp.sum(grad_normed * normal, axis=0, keepdims=True)
        grad_stream[rows, :] = grad_mid[wide, :] + unit_back(grad_normed * gain_row, normal, scale)
        return carry

    every(half // 512, chunk)


def back_first_kernel(
    s, grad_stream, mid, onehot, turned, gate_table, conv_mine, conv_other, gain, w_out, w_up, w_down,
    keep, send, hidden_out, low_out, normed_out, pre_out, gated_out, mid_low_out, by_token, gain_out,
):
    half = grad_stream.shape[0]
    k = s[CORE]
    by_token[...] = jnp.zeros_like(by_token)
    gain_out[...] = jnp.zeros_like(gain_out)

    def chunk(i, carry):
        rows = at(half * i, half)
        wide = at(half * i + HALO, half)
        hot = onehot[at(half * k + half * i + HALO, half), :]
        x0 = mm(hot, gate_table[:, 0:256])
        conv = jnp.concatenate([conv_mine[wide, :], conv_other[wide, :]], axis=1)
        gated_out[rows, :] = (conv * x0).astype(bf16)
        normal, scale = unit(mid[wide, :])
        gain_row = gain[0, 1:2, :]
        low = (normal * gain_row).astype(bf16)
        normed_out[rows, :] = low
        act, slope = gelu_parts(mm(low, w_up[...]))
        hidden_out[rows, :] = act.astype(bf16)
        grad = grad_stream[rows, :]
        grad_low = grad.astype(bf16)
        low_out[rows, :] = grad_low
        grad_pre = (slope * mm_nt(grad_low, w_down[...])).astype(bf16)
        pre_out[rows, :] = grad_pre
        grad_normed = mm_nt(grad_pre, w_up[...])
        gain_out[0:1, :] += jnp.sum(grad_normed * normal, axis=0, keepdims=True)
        mid_grad = grad + unit_back(grad_normed * gain_row, normal, scale)
        mid_low = mid_grad.astype(bf16)
        mid_low_out[rows, :] = mid_low
        grad_gated = mm_nt(mid_low, w_out[...])
        conv_grad = grad_gated * x0
        keep[rows, :] = conv_grad[:, 0:128]
        send[rows, :] = conv_grad[:, 128:256]
        flips = turned[k, :, at(half * i, half, 256)]
        rest = mid_grad - mid_low.astype(f32)
        gate_grads = jnp.concatenate([(grad_gated * conv).astype(bf16), mid_low, rest.astype(bf16)], axis=1)
        by_token[...] += mm(flips, gate_grads)[0:48, :]
        return carry

    every(1, chunk)


R_OUT, R_UP, R_DOWN, R_IN = 128, 512, 512, 384


def fill_part(s, raw_out, raw_up, raw_down, out):
    first = s[CORE] == 0
    pick = lambda a, b: jnp.where(first, a.astype(f32), b.astype(f32))
    out[0:128, :] = pick(raw_out[:, 0:128], raw_out[:, 128:256])
    for j in range(2):
        lanes = slice(128 * j, 128 * j + 128)
        out[128 + 256 * j : 384 + 256 * j, :] = pick(
            raw_up[:, 128 * j : 128 * j + 128], raw_up[:, 256 + 128 * j : 384 + 128 * j]
        )
        out[640 + 256 * j : 896 + 256 * j, :] = pick(raw_down[0:256, lanes], raw_down[256:512, lanes])


def fill_in_part(s, raw_in, out):
    first = s[CORE] == 0
    for g in range(3):
        a, b = raw_in[g, 0:128, :].astype(f32), raw_in[g, 128:256, :].astype(f32)
        out[128 * g : 128 * g + 128, :] = jnp.where(first, a, b)


def send_weights_kernel(s, w_out, w_up, w_down, out, raw_out, raw_up, raw_down, done):
    bring(((w_out.at[1], raw_out), (w_up.at[1], raw_up), (w_down.at[1], raw_down)), done)
    fill_part(s, raw_out, raw_up, raw_down, out)


def cot_split_kernel(s, blocks, keep, send):
    k = s[CORE]
    few = keep.shape[0]
    keep[...] = blocks[pl.ds(few * k, few)]
    send[...] = blocks[pl.ds(few * (1 - k), few)]


def cot_half_kernel(s, own, received, blocks, out):
    spot, width = s[CORE], own.shape[1]
    for j in range(own.shape[0]):
        out[pl.ds(width * (2 * j + spot), width), :] = own[j]
        out[pl.ds(width * (2 * j + 1 - spot), width), :] = received[j]
    out[2 * own.shape[0] * width :, :] = blocks[own.shape[0], 0:HALO, :]


def cot_whole_kernel(s, own, received, out, rim):
    spot = s[BIT1]
    rows = own.shape[0] - HALO
    two = rows // 2
    for j in range(2):
        out[pl.ds(two * (2 * j + spot), two), :] = own[two * j : two * j + two, :]
        out[pl.ds(two * (2 * j + 1 - spot), two), :] = received[two * j : two * j + two, :]
    rim[...] = jnp.where(spot == 0, own[rows:, :], received[rows:, :])


def relay_kernel(s, value, out):
    out[...] = value[...]


def join_weights_kernel(level, s, w_out, w_up, w_down, w_in, first_part, second_part, out_full, up_full, down_full, *in_full):
    first = s[CORE] == 0
    low = lambda ref, a, b: ref[a:b, :].astype(bf16)
    pick = lambda a, b: jnp.where(first, a, b)
    mine_out = w_out[level]
    a, b = first_part[0:128, :], second_part[0:128, :]
    peer_out = jnp.concatenate([pick(a, b), pick(b, a)], axis=1)
    out_full[0:128, :] = pick(mine_out.astype(f32), peer_out).astype(bf16)
    out_full[128:256, :] = pick(peer_out, mine_out.astype(f32)).astype(bf16)
    up_a, up_b = w_up[level, :, 0:256].astype(f32), w_up[level, :, 256:512].astype(f32)
    up_full[:, 0:256] = pick(up_a, up_b).astype(bf16)
    up_full[:, 256:512] = pick(up_b, up_a).astype(bf16)
    down_a, down_b = w_down[level, 0:256, :].astype(f32), w_down[level, 256:512, :].astype(f32)
    down_full[0:256, :] = pick(down_a, down_b).astype(bf16)
    down_full[256:512, :] = pick(down_b, down_a).astype(bf16)
    for n, part in enumerate((first_part, second_part)):
        for j in range(2):
            up_full[:, 512 + 256 * n + 128 * j : 640 + 256 * n + 128 * j] = low(part, 128 + 256 * j, 384 + 256 * j)
            down_full[512 + 256 * n : 768 + 256 * n, 128 * j : 128 * j + 128] = low(part, 640 + 256 * j, 896 + 256 * j)
    if in_full:
        (full,) = in_full
        for g in range(3):
            own = w_in[1 - level, g].astype(f32)
            a, b = first_part[1152 + 128 * g : 1280 + 128 * g, :], second_part[1152 + 128 * g : 1280 + 128 * g, :]
            peer = jnp.concatenate([pick(a, b), pick(b, a)], axis=0)
            full[:, 256 * g : 256 * g + 128] = pick(own, peer).astype(bf16)
            full[:, 256 * g + 128 : 256 * g + 256] = pick(peer, own).astype(bf16)


def wide_grads_kernel(pad, s, gated, mid_low, normed, grad_pre, hidden, grad_low, keep, send):
    k = s[CORE]
    first = k == 0
    stop = gated.shape[0] - pad
    own = lambda ref: ref[pad:stop, :]
    out = mm_tn(own(gated), own(mid_low))
    for m in range(2):
        a, b = out[128 * m : 128 * m + 128, 0:128], out[128 * m : 128 * m + 128, 128:256]
        half = m + k - 2 * m * k
        keep[half, 0:128, :] = jnp.where(first, a, b)
        send[half, 0:128, :] = jnp.where(first, b, a)
    for j in range(4):
        target = (keep, send)[j % 2]
        up = mm_tn(own(normed), grad_pre[pad:stop, 256 * j : 256 * j + 256])
        down = mm_tn(hidden[pad:stop, 256 * j : 256 * j + 256], own(grad_low))
        for n in range(2):
            lanes = slice(128 * n, 128 * n + 128)
            target[j // 2, 128 + 256 * n : 384 + 256 * n, :] = up[:, lanes]
            target[j // 2, 640 + 256 * n : 896 + 256 * n, :] = down[:, lanes]


def in_grads_kernel(s, normed_in, mixed_low, keep, send):
    k = s[CORE]
    first = k == 0
    for g in range(3):
        both = mm_tn(normed_in[...], mixed_low[:, 256 * g : 256 * g + 256])
        for m in range(2):
            block = both[:, 128 * m : 128 * m + 128]
            half = m + k - 2 * m * k
            keep[half, 128 * g : 128 * g + 128, :] = jnp.where(first, block[0:128], block[128:256])
            send[half, 128 * g : 128 * g + 128, :] = jnp.where(first, block[128:256], block[0:128])


def add_kernel(s, kept, received, own_out, peer_out):
    own_out[...] = kept[0] + received[0]
    peer_out[...] = kept[1] + received[1]


def add_half_kernel(s, kept, received, w_in, own_out, peer_out):
    rows = own_out.shape[0]
    part = at(rows * s[BIT1], rows, 8)
    own_out[...] = kept[0, part, :] + received[0, part, :]
    peer_out[0:rows, :] = kept[1, part, :] + received[1, part, :]
    fill_in_part(s, w_in.at[0], peer_out.at[rows : rows + 384])


def take_half_kernel(s, own, received, out, in_out):
    rows = own.shape[0]
    out[...] = own[...] + received[0:rows, :]
    in_out[...] = received[rows:, :]


def add_one_kernel(s, kept, received, out):
    out[...] = kept[...] + received[...]


def spread_wide_kernel(level, s, *refs):
    if level:
        outs, (a, b, out, up, down), done = refs[-9:-6], refs[-6:-1], refs[-1]
        rows = refs[0].shape[0]
        for whole, near, far in ((a, refs[0], refs[1]), (b, refs[2], refs[3])):
            whole[at(rows * s[BIT1], rows, 8), :] = near[...]
            whole[at(rows * (1 - s[BIT1]), rows, 8), :] = far[...]
    else:
        outs, (out, up, down), done = refs[-7:-4], refs[-4:-1], refs[-1]
        a, b = refs[:2]
    first = s[CORE] == 0
    pick = lambda x, y: jnp.where(first, x, y)

    def both(row, rows):
        x, y = a[row : row + rows, :], b[row : row + rows, :]
        return pick(x, y), pick(y, x)

    x, y = both(0, 128)
    out[:, 0:128] = x
    out[:, 128:256] = y
    for j in range(2):
        lanes = slice(128 * j, 128 * j + 128)
        x, y = both(128 + 256 * j, 256)
        up[:, 128 * j : 128 * j + 128] = x
        up[:, 256 + 128 * j : 384 + 128 * j] = y
        x, y = both(640 + 256 * j, 256)
        down[0:256, lanes] = x
        down[256:512, lanes] = y
    bring(zip((out, up, down), (whole.at[level] for whole in outs)), done)


def spread_in_kernel(s, kept, received, whole, near, done):
    first = s[CORE] == 0
    for g in range(3):
        x, y = kept[128 * g : 128 * g + 128, :], received[128 * g : 128 * g + 128, :]
        near[g, 0:128, :] = jnp.where(first, x, y)
        near[g, 128:256, :] = jnp.where(first, y, x)
    bring(((near, whole.at[1]),), done)


def pair_kernel(bit, s, own, received, out):
    spot = s[(CORE, BIT1, BIT2, BIT3)[bit]]
    for j in range(own.shape[0]):
        out[2 * j + spot] = own[j]
        out[2 * j + 1 - spot] = received[j]


E_GAIN, E_EMBED, E_FIRST, E_SHORT, E_TOKEN, E_ROWS = 0, 8, 24, 40, 56, 104
EM_SECOND, EM_SKIP, EM_ROWS = 0, 64, 72
L_TOKEN, L_SECOND, L_SKIP, L_ROWS = 0, 96, 160, 168
FIRST_ROWS = 16


def fold_first(values):
    last = jnp.concatenate([values[32:40], jnp.zeros((8, 64), f32)], axis=0)
    return jnp.concatenate([values[0:16], values[16:32], last, jnp.zeros((16, 64), f32)], axis=1)


def unfold_first(values):
    return jnp.concatenate([values[:, 0:64], values[:, 64:128], values[0:8, 128:192]], axis=0)[0:FEAT]


def early_kernel(s, gain_mid1, gain_in1, gain_mid0, by_token0, first1, short1, second1, skip1, flat, mine):
    k = s[CORE]
    flat[...] = jnp.zeros_like(flat)
    for row, values in enumerate((gain_mid1, gain_in1, gain_mid0)):
        flat[E_GAIN + row : E_GAIN + row + 1, :] = values[0:1, :]
    flat[E_EMBED : E_EMBED + 16, :] = by_token0[0:16, 256:512] + by_token0[0:16, 512:768]
    flat[E_FIRST : E_FIRST + FIRST_ROWS, :] = fold_first(first1[...])
    swap = lambda v: jnp.where(k == 0, v, jnp.concatenate([v[:, 128:256], v[:, 0:128]], axis=1))
    for t in range(3):
        total = jnp.sum(short1[t], axis=0, keepdims=True)
        for g in range(3):
            flat[E_SHORT + 3 * t + g : E_SHORT + 3 * t + g + 1, :] = swap(total[:, 256 * g : 256 * g + 256])
    flat[E_TOKEN : E_TOKEN + 48, :] = swap(by_token0[:, 0:256])
    mine[EM_SECOND : EM_SECOND + 64, :] = second1[...]
    mine[EM_SKIP : EM_SKIP + 8, :] = jnp.broadcast_to(jnp.sum(skip1[...], axis=0, keepdims=True), (8, 128))


def late_kernel(s, by_token12, second0, skip0, first0, mine, first_out):
    mine[L_TOKEN : L_TOKEN + 48, :] = by_token12[:, 0:128]
    mine[L_TOKEN + 48 : L_TOKEN + 96, :] = by_token12[:, 128:256]
    mine[L_SECOND : L_SECOND + 64, :] = second0[...]
    mine[L_SKIP : L_SKIP + 8, :] = jnp.broadcast_to(jnp.sum(skip0[...], axis=0, keepdims=True), (8, 128))
    first_out[...] = fold_first(first0[...])


def chip_kernel(s, flat, flat_in, mine, mine_in, out):
    first = s[CORE] == 0
    rows = flat.shape[0]
    total = flat[...] + flat_in[...]
    out[0:rows, :] = total
    out[rows:, 0:128] = jnp.where(first, mine[...], mine_in[...])
    out[rows:, 128:256] = jnp.where(first, mine_in[...], mine[...])


def last_kernel(
    s, early, early_in, late, late_in, embed, gain, own, peer, w_own, w_first, w_second, in_given,
    embed_out, gain_out, in_whole, short_out, first_out, second_out, skip_out, in_out, done,
):
    pick = lambda x, y: jnp.where(s[CORE] == 0, x, y)

    def plain(pair, row, rows):
        return pair[0][row : row + rows, :] + pair[1][row : row + rows, :]

    def halves(pair, row, rows):
        here, there = pair
        left = here[row : row + rows, 0:128] + there[row : row + rows, 128:256]
        right = here[row : row + rows, 128:256] + there[row : row + rows, 0:128]
        return left, right

    early, late = (early, early_in), (late, late_in)
    gains = plain(early, E_GAIN, 8)
    gain_out[1, 0:1, :] = gains[1:2, :]
    gain_out[1, 1:2, :] = gains[0:1, :]
    gain_out[0, 1:2, :] = gains[2:3, :]
    first_out[:, 0, :] = unfold_first(plain(late, 0, FIRST_ROWS))
    first_out[:, 1, :] = unfold_first(plain(early, E_FIRST, FIRST_ROWS))
    short = halves(early, E_SHORT, 16)[0]
    for t in range(3):
        for g in range(3):
            short_out[t, g, 1:2, :] = short[3 * t + g : 3 * t + g + 1, :]
    second_out[1] = halves(early, E_ROWS + EM_SECOND, 64)[0]
    second_out[0] = halves(late, FIRST_ROWS + L_SECOND, 64)[0]
    skip_out[0:1, :] = halves(late, FIRST_ROWS + L_SKIP, 8)[0][0:1]
    skip_out[1:2, :] = halves(early, E_ROWS + EM_SKIP, 8)[0][0:1]
    tokens = [
        halves(early, E_TOKEN, 48),
        halves(late, FIRST_ROWS + L_TOKEN, 48),
        halves(late, FIRST_ROWS + L_TOKEN + 48, 48),
    ]
    normal, scale = unit(embed[...])
    gain_row = gain[0, 0:1, :]
    low = (normal * gain_row).astype(bf16)
    grad_normed = jnp.zeros((16, 256), f32)
    for g in range(3):
        for h, pack in ((0, own), (1, peer)):
            grads = tokens[g][h]
            table = pack[16 * g : 16 * g + 16, :]
            summed = jnp.zeros((16, 128), f32)
            for t in range(3):
                row = PACK_SHORT + 3 * t + g
                part = grads[16 * t : 16 * t + 16, :]
                summed += pack[row : row + 1, :] * part
                if h == 0:
                    short_out[t, g, 0:1, :] = jnp.sum(table * part, axis=0, keepdims=True)
            high, rest = split(summed)
            if h == 0:
                in_out[g] = mm_tn(low, high) + mm_tn(low, rest)
                weight = w_own[0, g]
            else:
                rows = slice(128 * g, 128 * g + 128)
                a, b = w_first[rows, :], w_second[rows, :]
                weight = jnp.concatenate([pick(a, b), pick(b, a)], axis=0).astype(bf16)
            grad_normed += mm_nt(high, weight) + mm_nt(rest, weight)
    copy = pltpu.make_async_copy(in_out, in_whole.at[0], done.at[0])
    copy.start()
    gain_out[0, 0:1, :] = jnp.sum(grad_normed * normal, axis=0, keepdims=True)
    embed_out[...] = plain(early, E_EMBED, 16) + unit_back(grad_normed * gain_row, normal, scale)
    copy.wait()


def block_send_kernel(s, block_out, mine, other):
    spot = s[SPOT]
    mine[...] = block_out[at(HALO + 128 * spot, 128), :]
    near = spot + 1 - 2 * s[CORE]
    other[...] = block_out[at(HALO + 128 * near, 128), :]


def block_pick_kernel(s, mine, received, out):
    out[...] = jnp.where(s[HOLDER] == 1, mine[...], received[...])


def block_join_kernel(s, here, there, out):
    first = s[GROUP] == 0
    out[0] = jnp.where(first, here[...], there[...])
    out[1] = jnp.where(first, there[...], here[...])


def chip_local(
    ids, live, embed, norm_gain, in_weight, short_kernel, filter_first, filter_second, skip_gain,
    out_weight, up_weight, down_weight, cotangent,
):
    CALLS.clear()
    count = lax.axis_size("seq")
    rank = lax.axis_index("seq")
    group = lax.axis_index("ch")
    width = ids.shape[1]
    length = width * count
    half = length // 2
    span = half + 2 * HALO
    core = rank % 2
    across = lambda v: lax.ppermute(v, "ch", [(0, 1), (1, 0)])
    trade = lambda v, bit: lax.ppermute(v, "seq", [(i, i ^ bit) for i in range(count)])
    beside = lambda v: trade(v, 1)
    dft = jnp.asarray(dft_table()).astype(bf16)
    twiddle = jnp.asarray(twiddle_table())
    feats = jnp.asarray(feature_parts(length)).astype(bf16)
    feats_turned = jnp.asarray(np.pad(feature_table(length).T, ((0, FEAT_ROWS - FEAT), (0, 0)))).astype(bf16)
    rates = jnp.asarray(rate_table())
    low = lambda *shape: arr(*shape, kind=bf16)
    line = pltpu.VMEM((length + 2 * HALO, 128), f32)
    conv_scratch = [stage_scratch(), spec_scratch(), line]
    pair = lambda bit, v, w, **kw: run(
        functools.partial(pair_kernel, bit), jax.ShapeDtypeStruct((2 * v.shape[0],) + v.shape[1:], v.dtype), s, v, w, **kw
    )

    row_shape = lambda rows: arr(rows, 8, width, kind=jnp.int32)
    in_own = jnp.swapaxes(in_weight, 1, 2)
    packed = (embed, norm_gain, in_own, filter_second, jnp.transpose(short_kernel, (1, 2, 0, 3)), skip_gain)
    wide = (out_weight, up_weight, down_weight)
    held = [(1, 2), ids.shape, embed.shape, norm_gain.shape, in_own.shape[1:], filter_second.shape, packed[4].shape, skip_gain.shape]
    held += [v.shape[1:] for v in wide] + [in_own.shape[1:]]
    kinds = [jnp.int32, jnp.int32, f32, f32, bf16, f32, f32, f32] + [bf16] * 4
    s, ids1, cot1, pack, part0 = start(
        numbers_kernel,
        [arr(NUMBER_ROWS, 128, kind=jnp.int32), row_shape(1), arr(1, width, 256), arr(PACK_ROWS, 128), arr(1536, 128)],
        live.reshape(1, 2), ids, cotangent, *packed, *wide, in_own,
        scratch=[pltpu.VMEM(shape, kind) for shape, kind in zip(held, kinds)] + [pltpu.SemaphoreType.DMA((13,))],
    )
    pack_in = across(pack)
    part0_in = across(part0)
    ids2 = pair(3, ids1, trade(ids1, 8))
    sine, cosine, sine_turned = run(
        sine_kernel, [low(length, 256), arr(length, 128), low(128, length)], s, feats, jnp.transpose(filter_first, (1, 0, 2)),
        after=(ids2,), scratch=[pltpu.VMEM((FEAT_ROWS, 128), f32)],
    )
    cot2 = pair(3, cot1, trade(cot1, 8), after=(sine,))
    ids4 = pair(2, ids2, trade(ids2, 4), after=(cot2,))
    part1 = run(
        send_weights_kernel, arr(1152, 128), s, *wide, hbm=range(3), after=(ids4,),
        scratch=[pltpu.VMEM(v.shape[1:], v.dtype) for v in wide] + [pltpu.SemaphoreType.DMA((3,))],
    )
    part1_in = across(part1)
    mine, other, conv_table, gate_table = run(
        table_kernel, [arr(PACK_ROWS, 128), arr(PACK_ROWS, 128), low(128, 256), low(128, 512)], s, pack, pack_in, embed,
        after=(part1,),
    )
    make_filter = lambda level, after: run(
        functools.partial(filter_kernel, level), [arr(length, 128), arr(*SPECTRUM)], s, sine, mine, rates, dft, twiddle,
        scratch=[stage_scratch()], after=after,
    )
    filt0, freq0 = make_filter(0, ())
    ids8 = pair(1, ids4, trade(ids4, 2), after=(filt0,))
    cot4 = pair(2, cot2, trade(cot2, 4), after=(ids8,))
    cot_keep, cot_send = run(cot_split_kernel, [arr(2, width, 256), arr(2, width, 256)], s, cot4)
    all_ids = pair(0, ids8, beside(ids8), after=(cot_send,))
    onehot, turned = run(
        onehot_kernel, [low(length + 2 * HALO, 128), low(2, 128, half)], s, all_ids,
        scratch=[pltpu.VMEM((length + 2 * HALO, 128), f32)],
    )
    conv_mine0, sent, spec0, product0 = run(
        conv_first_kernel, [arr(span, 128), arr(span, 128), arr(*SPECTRUM), arr(length, 128)],
        s, onehot, conv_table, mine, freq0, dft, twiddle, scratch=conv_scratch,
    )
    conv_other0 = beside(sent)
    first_part = run(relay_kernel, arr(1536, 128), s, part0_in, after=(sent,))
    first_beside = beside(first_part)
    filt1, freq1 = make_filter(1, (first_part,))
    cot_half = run(cot_half_kernel, arr(4 * width + HALO, 256), s, cot_keep, beside(cot_send), cot4, after=(freq1,))
    cot_half_in = trade(cot_half, 2)
    w_out0, w_up0, w_down0, w_in1 = run(
        functools.partial(join_weights_kernel, 0), [low(256, 256), low(256, 1024), low(1024, 256), low(256, 768)],
        s, out_weight, up_weight, down_weight, in_own, first_part, first_beside, after=(cot_half,),
    )
    kept, sent, mid0, stream1, gates1, mixed1 = run(
        forward_first_kernel,
        [arr(half, 128), arr(half, 128), arr(span, 256), arr(span, 256), arr(span, 768), arr(span, 768)],
        s, onehot, gate_table, conv_mine0, conv_other0, norm_gain, w_out0, w_up0, w_down0, w_in1, mine, other,
    )
    received = beside(sent)
    second_part = run(relay_kernel, arr(1152, 128), s, part1_in, after=(sent,))
    second_beside = beside(second_part)
    conv_mine1, sent, spec1, product1 = run(
        conv_second_kernel, [arr(span, 128), arr(span, 128), arr(*SPECTRUM), arr(length, 128)],
        s, kept, received, mine, freq1, dft, twiddle, scratch=conv_scratch, after=(second_part,),
    )
    conv_other1 = beside(sent)
    cot, cot_rim = run(cot_whole_kernel, [arr(half, 256), arr(HALO, 256)], s, cot_half, cot_half_in, after=(sent,))
    w_out1, w_up1, w_down1 = run(
        functools.partial(join_weights_kernel, 1), [low(256, 256), low(256, 1024), low(1024, 256)],
        s, out_weight, up_weight, down_weight, in_own, second_part, second_beside, after=(cot_rim,),
    )
    (kept, sent, grad_x0, grad_mid1, block, hidden, grad_low, normed, grad_pre, gated, mid_low, gain_mid1) = run(
        turn_back_kernel,
        [
            arr(half, 128), arr(half, 128), arr(span, 256), arr(span, 256), arr(span, 256), low(span, 1024), low(span, 256),
            low(span, 256), low(span, 1024), low(span, 256), low(span, 256), arr(8, 256),
        ],
        s, conv_mine1, conv_other1, gates1, stream1, cot, cot_rim, norm_gain, w_out1, w_up1, w_down1,
        scratch=[pltpu.VMEM((span, 256), f32), pltpu.VMEM((span, 256), f32)],
    )
    received = beside(sent)
    grads_keep1, grads_send1 = run(
        functools.partial(wide_grads_kernel, HALO), [arr(2, 1152, 128), arr(2, 1152, 128)],
        s, gated, mid_low, normed, grad_pre, hidden, grad_low,
    )
    block_mine, block_other = run(block_send_kernel, [arr(width, 256), arr(width, 256)], s, block)
    grads_in1 = beside(grads_send1)
    block_beside = beside(block_other)

    prod_mine, sent, spec_grad1, grads1 = run(
        conv_back_kernel, [arr(span, 128), arr(span, 128), arr(*SPECTRUM), arr(length, 128)],
        s, kept, received, mine, freq1, dft, twiddle, scratch=conv_scratch, after=(grads_send1, block_mine),
    )
    prod_other = beside(sent)
    own1, peer1 = run(add_half_kernel, [arr(576, 128), arr(960, 128)], s, grads_keep1, grads_in1, in_own, after=(sent,))
    across1 = across(peer1)
    filter_shapes = [arr(64, 128), arr(40, 64), arr(8, 128)]
    filter_scratch = [stage_scratch(), spec_scratch(), pltpu.VMEM((length, 128), f32)]
    second1, first1, skip1 = run(
        filter_back_kernel, filter_shapes, s, spec_grad1, spec1, grads1, product1, filt1, cosine,
        sine_turned, mine, rates, feats_turned, dft, twiddle, scratch=filter_scratch, after=(peer1,),
    )
    grad_stream1, normed_in, mixed_low, short1, gain_in1 = run(
        back_gates_kernel,
        [arr(half, 256), low(half, 256), low(half, 768), arr(3, 8, 768), arr(8, 256)],
        s, prod_mine, prod_other, grad_x0, gates1, mixed1, grad_mid1, stream1, norm_gain, mine, other, w_in1,
        scratch=[pltpu.VMEM((span, 512), f32)], after=(skip1,),
    )
    in_keep, in_send = run(in_grads_kernel, [arr(2, 384, 128), arr(2, 384, 128)], s, normed_in, mixed_low)
    in_beside = beside(in_send)
    block_here = run(block_pick_kernel, arr(width, 256), s, block_mine, block_beside, after=(in_send,))
    block_across = across(block_here)
    in_own1, in_peer1 = run(add_kernel, [arr(384, 128), arr(384, 128)], s, in_keep, in_beside, after=(block_here,))
    in_across = across(in_peer1)
    total1, in0_first = run(take_half_kernel, [arr(576, 128), arr(384, 128)], s, own1, across1, after=(block_here,))
    total1_y, in0_second = trade(total1, 2), beside(in0_first)
    (kept, sent, hidden, grad_low, normed, grad_pre, gated, mid_low, by_token0, gain_mid0) = run(
        back_first_kernel,
        [
            arr(half, 128), arr(half, 128), low(half, 1024), low(half, 256), low(half, 256), low(half, 1024), low(half, 256),
            low(half, 256), arr(48, 768), arr(8, 256),
        ],
        s, grad_stream1, mid0, onehot, turned, gate_table, conv_mine0, conv_other0, norm_gain, w_out0, w_up0, w_down0,
        after=(in_peer1,),
    )
    received = beside(sent)
    early_flat, early_mine = run(
        early_kernel, [arr(E_ROWS, 256), arr(EM_ROWS, 128)],
        s, gain_mid1, gain_in1, gain_mid0, by_token0, first1, short1, second1, skip1,
    )
    early_flat_in, early_mine_in = beside(early_flat), beside(early_mine)
    grads_keep0, grads_send0 = run(
        functools.partial(wide_grads_kernel, 0), [arr(2, 1152, 128), arr(2, 1152, 128)],
        s, gated, mid_low, normed, grad_pre, hidden, grad_low, after=(early_flat,),
    )
    grads_in0 = beside(grads_send0)
    early = run(
        chip_kernel, arr(E_ROWS + EM_ROWS, 256),
        s, early_flat, early_flat_in, early_mine, early_mine_in, after=(grads_send0,),
    )
    early_in = across(early)
    spec_grad0, grads0 = run(
        grad_freq_kernel, [arr(*SPECTRUM), arr(length, 128)], s, kept, received, dft, twiddle, scratch=[stage_scratch()],
        after=(early,),
    )
    own0, peer0 = run(add_kernel, [arr(1152, 128), arr(1152, 128)], s, grads_keep0, grads_in0, after=(spec_grad0,))
    across0 = across(peer0)
    second0, first0, skip0, by_token12 = run(
        token_back_kernel, filter_shapes + [arr(48, 256)], s, spec_grad0, spec0, grads0, product0, filt0, cosine,
        sine_turned, mine, rates, feats_turned, dft, twiddle, freq0, onehot, turned, conv_table, scratch=filter_scratch,
        after=(peer0, early, total1),
    )
    wide_shapes = [arr(2, 128, 256), arr(2, 256, 512), arr(2, 512, 256)]
    wide_scratch = [pltpu.VMEM(v.shape[1:], f32) for v in wide_shapes] + [pltpu.SemaphoreType.DMA((3,))]
    late_mine, late_first = run(
        late_kernel, [arr(L_ROWS, 128), arr(FIRST_ROWS, 256)], s, by_token12, second0, skip0, first0, flops=FEW_FLOPS
    )
    late_mine_in, late_first_in = beside(late_mine), beside(late_first)
    in_total = run(add_one_kernel, arr(384, 128), s, in_own1, in_across, after=(late_mine,), flops=FEW_FLOPS)
    block_out, joined = run(block_join_kernel, arr(2, width, 256), s, block_here, block_across, after=(late_mine,), flops=FEW_FLOPS, token=True)
    late = run(
        chip_kernel, arr(FIRST_ROWS + L_ROWS, 256), s, late_first, late_first_in, late_mine, late_mine_in, flops=FEW_FLOPS,
        after=(joined, in_total, early_in),
    )
    late_in = across(late)
    near1_y = run(relay_kernel, arr(576, 128), s, total1_y, after=(late,), flops=FEW_FLOPS)
    quarters1 = (total1, near1_y, beside(total1), beside(near1_y))
    in_total_beside = beside(in_total)
    *wide_buffers, wide_spread = run(
        functools.partial(spread_wide_kernel, 1), wide_shapes, s, *quarters1, hbm_outs=(0, 1, 2), flops=FEW_FLOPS,
        scratch=[pltpu.VMEM((1152, 128), f32)] * 2 + wide_scratch, after=(late,), token=True,
    )
    in_buffer, in_spread = run(
        spread_in_kernel, arr(2, 3, 256, 128), s, in_total, in_total_beside, hbm_outs=(0,), flops=FEW_FLOPS, token=True,
        scratch=[pltpu.VMEM((3, 256, 128), f32), pltpu.SemaphoreType.DMA((1,))],
    )
    total0 = run(add_one_kernel, arr(1152, 128), s, own0, across0, after=(late_in, wide_spread, in_spread))
    total0_beside = beside(total0)
    grad_embed, grad_gain, grad_in, grad_short, grad_first, grad_second, grad_skip = run(
        last_kernel,
        [
            arr(16, 256), arr(2, 2, 256), arr(2, 3, 256, 128), arr(3, 3, 2, 128), arr(FEAT, 2, 64), arr(2, 64, 128), arr(2, 128),
        ],
        s, early, early_in, late, late_in, embed, norm_gain, pack, pack_in, in_own, in0_first, in0_second, in_buffer,
        hbm=(11,), hbm_outs=(2,), aliases=((11, 2),), flops=FEW_FLOPS, after=(total0,),
        scratch=[pltpu.VMEM((3, 256, 128), f32), pltpu.SemaphoreType.DMA((1,))],
    )
    grad_out, grad_up, grad_down = run(
        functools.partial(spread_wide_kernel, 0), wide_shapes, s, total0, total0_beside, *wide_buffers,
        hbm=(2, 3, 4), hbm_outs=(0, 1, 2), aliases=((2, 0), (3, 1), (4, 2)), flops=FEW_FLOPS, scratch=wide_scratch,
    )
    return (
        block_out,
        grad_embed,
        grad_gain,
        jnp.swapaxes(grad_in, 1, 2),
        jnp.transpose(grad_short, (2, 0, 1, 3)),
        jnp.transpose(grad_first, (1, 0, 2)),
        grad_second,
        grad_skip,
        grad_out,
        grad_up,
        grad_down,
    )


def solution(mesh):
    in_specs = (
        P(None, "seq"),
        P(),
        P(),
        P(),
        P(None, None, None, "ch"),
        P(None, None, None, "ch"),
        P(),
        P(None, None, "ch"),
        P(None, "ch"),
        P(None, "ch", None),
        P(None, None, "ch"),
        P(None, "ch", None),
        P(None, "seq", None),
    )
    out_specs = (
        P(None, "seq", None),
        P(),
        P(),
        P(None, None, None, "ch"),
        P(None, None, None, "ch"),
        P(),
        P(None, None, "ch"),
        P(None, "ch"),
        P(None, "ch", None),
        P(None, None, "ch"),
        P(None, "ch", None),
    )

    def either(*args):
        length = args[0].shape[1] * lax.axis_size("seq")
        near = length == BLOCKS * BLOCK and lax.axis_size("seq") == 16
        return (chip_local if near else local)(*args)

    return jax.shard_map(either, mesh=mesh, in_specs=in_specs, out_specs=out_specs, check_vma=False)
```

```python
import collections
import functools
import math

import jax
import jax.numpy as jnp
import ml_dtypes
import numpy as np
from jax import lax
from jax.experimental import pallas as pl
from jax.experimental.pallas import tpu as pltpu
from jax.sharding import PartitionSpec as P

D = 256
FEAT = 33


precise = lax.Precision.HIGHEST
epsilon = 1e-05


def passed_along(value, axis, steps):
    count = lax.axis_size(axis)
    leading, last = (max(0, -steps), min(count, count - steps))
    return lax.ppermute(value, axis, [(source, source + steps) for source in range(leading, last)])


def layer_norm(inputs, gain_vec):
    center = inputs - jnp.mean(inputs, axis=-1, keepdims=True)
    spread = jnp.mean(center * center, axis=-1, keepdims=True)
    return center * lax.rsqrt(spread + epsilon) * gain_vec


def position_features(length):
    places = jnp.arange(length, dtype=jnp.int32)
    band_ids = jnp.arange(1, (FEAT - 1) // 2 + 1, dtype=jnp.int32)
    turn_counts = places[:, None] * band_ids[None, :] % length
    angles = turn_counts.astype(jnp.float32) * (2.0 * math.pi / length)
    ramp_vals = places.astype(jnp.float32)[:, None] / length
    return jnp.concatenate([ramp_vals, jnp.cos(angles), jnp.sin(angles)], axis=1)


def decay_rates(channels):
    return 0.3 * 10.0 ** (channels.astype(jnp.float32) / (D - 1))


def dft_tables(blocks, block_len):
    doubled = 2 * blocks
    span_total = doubled * block_len
    frequency = jnp.arange(doubled, dtype=jnp.int32)
    places = jnp.arange(blocks, dtype=jnp.int32)
    inner_idx = jnp.arange(block_len, dtype=jnp.int32)
    outer_angle = (frequency[:, None] * places[None, :] % doubled).astype(jnp.float32) * (
        2.0 * math.pi / doubled
    )
    twist_angle = (frequency[:, None] * inner_idx[None, :] % span_total).astype(jnp.float32) * (
        2.0 * math.pi / span_total
    )
    inner_angle = (inner_idx[:, None] * inner_idx[None, :] % block_len).astype(jnp.float32) * (
        2.0 * math.pi / block_len
    )
    return (
        jnp.cos(outer_angle),
        jnp.sin(outer_angle),
        jnp.cos(twist_angle),
        jnp.sin(twist_angle),
        jnp.cos(inner_angle),
        jnp.sin(inner_angle),
    )


def along_block(values, table):
    return jnp.einsum("...kb,bj->...kj", values, table, precision=precise)


def to_spectrum(signal, tables):
    outer_cos, outer_sin, twist_cos, twist_sin, inner_cos, inner_sin = tables
    first_re = jnp.einsum("kp,...pb->...kb", outer_cos, signal, precision=precise)
    first_im = -jnp.einsum("kp,...pb->...kb", outer_sin, signal, precision=precise)
    turned_re = first_re * twist_cos + first_im * twist_sin
    turned_im = first_im * twist_cos - first_re * twist_sin
    spec_re = along_block(turned_re, inner_cos) + along_block(turned_im, inner_sin)
    spec_im = along_block(turned_im, inner_cos) - along_block(turned_re, inner_sin)
    return (spec_re, spec_im)


def from_spectrum(spec_re, spec_im, tables):
    outer_cos, outer_sin, twist_cos, twist_sin, inner_cos, inner_sin = tables
    back_re = along_block(spec_re, inner_cos) - along_block(spec_im, inner_sin)
    back_im = along_block(spec_re, inner_sin) + along_block(spec_im, inner_cos)
    turned_re = back_re * twist_cos - back_im * twist_sin
    turned_im = back_re * twist_sin + back_im * twist_cos
    scale_back = 1.0 / (outer_cos.shape[0] * inner_cos.shape[0])
    signal = jnp.einsum("kp,...kb->...pb", outer_cos, turned_re, precision=precise) - jnp.einsum(
        "kp,...kb->...pb", outer_sin, turned_im, precision=precise
    )
    return signal * scale_back


def causal_filter(received, filt_spec, skip_part, tables):
    item_count, chan_count, length = received.shape
    blocks = tables[0].shape[1]
    spec_re, spec_im = to_spectrum(
        received.reshape(item_count, chan_count, blocks, length // blocks), tables
    )
    prod_re = spec_re * filt_spec[0] - spec_im * filt_spec[1]
    prod_im = spec_re * filt_spec[1] + spec_im * filt_spec[0]
    result_sig = from_spectrum(prod_re, prod_im, tables).reshape(item_count, chan_count, length)
    return result_sig + skip_part[:, None] * received


def filter_backward(grad_cols, moved_in, filt_spec, skip_part, tables):
    item_count, chan_count, length = grad_cols.shape
    blocks = tables[0].shape[1]
    grad_re, grad_im = to_spectrum(
        grad_cols.reshape(item_count, chan_count, blocks, length // blocks), tables
    )
    input_re, input_im = to_spectrum(
        moved_in.reshape(item_count, chan_count, blocks, length // blocks), tables
    )
    back_re = grad_re * filt_spec[0] + grad_im * filt_spec[1]
    back_im = grad_im * filt_spec[0] - grad_re * filt_spec[1]
    grad_u_cols = (
        from_spectrum(back_re, back_im, tables).reshape(item_count, chan_count, length)
        + skip_part[:, None] * grad_cols
    )
    corr_re = grad_re * input_re + grad_im * input_im
    corr_im = grad_im * input_re - grad_re * input_im
    grad_filt = jnp.sum(from_spectrum(corr_re, corr_im, tables), axis=0).reshape(chan_count, length)
    grad_skip_part = jnp.sum(grad_cols * moved_in, axis=(0, 2))
    return (grad_u_cols, grad_filt, grad_skip_part)


def local_filter(first, second, features, select, group_idx, chan_local):
    hidden_pre = jnp.dot(features, first, precision=precise)
    hidden_act = jnp.sin(hidden_pre)
    chan_width = second.shape[1]
    second_part = jnp.dot(second, select, precision=precise)
    channel_ids = group_idx * chan_width + chan_local
    length = features.shape[0]
    ramp_vals = jnp.arange(length, dtype=jnp.int32).astype(jnp.float32) / length
    decay_part = jnp.exp(-decay_rates(channel_ids)[:, None] * ramp_vals[None, :])
    filt_cols = jnp.einsum("hc,th->ct", second_part, hidden_act, precision=precise) * decay_part
    return (filt_cols, hidden_pre, hidden_act, second_part, decay_part)


def filter_mlp_backward(grad_filt, features, filter_parts):
    hidden_pre, hidden_act, second_part, decay_part = filter_parts
    grad_shaped = grad_filt * decay_part
    grad_second_part = jnp.einsum("ct,th->hc", grad_shaped, hidden_act, precision=precise)
    grad_act = jnp.einsum("ct,hc->th", grad_shaped, second_part, precision=precise)
    grad_first = jnp.einsum(
        "tf,th->fh", features, grad_act * jnp.cos(hidden_pre), precision=precise
    )
    return (grad_first, grad_second_part)


def embed_lookup(ids, live, embed, seq_rank):
    tok_rows = ids.shape[1]
    places = seq_rank * tok_rows + jnp.arange(tok_rows, dtype=jnp.int32)
    keep_mask = (places[None, :] < live[:, None]).astype(jnp.float32)
    vocab_ids = jnp.arange(embed.shape[0], dtype=jnp.int32)
    onehot = (ids[:, :, None] == vocab_ids[None, None, :]).astype(jnp.float32) * keep_mask[
        :, :, None
    ]
    stream = jnp.einsum("mtv,vd->mtd", onehot, embed, precision=precise)
    return (stream, onehot, keep_mask)


def channel_total(partial_sum):
    return lax.psum(partial_sum, "ch")


def input_total(partial_sum):
    return lax.psum(partial_sum, "ch")


def layer_forward(stream, params, filt_spec, skip_part, tables):
    norm_gains, w_in, kernel, w_out, w_up, w_down = params
    normed = layer_norm(stream, norm_gains[0]).astype(jnp.bfloat16)
    mixed_in = jnp.einsum("mtd,dgc->mtgc", normed, w_in, preferred_element_type=jnp.float32)
    rim_rows = passed_along(mixed_in[:, -2:], "seq", 1)
    padded = jnp.concatenate([rim_rows, mixed_in], axis=1)
    micro_count, tok_rows = (mixed_in.shape[0], mixed_in.shape[1])
    chan_width = mixed_in.shape[3]
    gate_vals = (
        kernel[0] * mixed_in
        + kernel[1] * padded[:, 1 : tok_rows + 1]
        + kernel[2] * padded[:, 0:tok_rows]
    )
    product_in = gate_vals[:, :, 2] * gate_vals[:, :, 1]
    flat_rows = jnp.swapaxes(product_in, 1, 2).reshape(1, micro_count * chan_width, tok_rows)
    received = lax.all_to_all(flat_rows, "seq", split_axis=1, concat_axis=2, tiled=True)
    result_sig = causal_filter(received, filt_spec, skip_part, tables)
    conv_flat = lax.all_to_all(result_sig, "seq", split_axis=2, concat_axis=1, tiled=True)
    conv_out = jnp.swapaxes(conv_flat.reshape(micro_count, chan_width, tok_rows), 1, 2)
    gated_out = (conv_out * gate_vals[:, :, 0]).astype(jnp.bfloat16)
    mid_state = stream + channel_total(
        jnp.einsum("mtc,cd->mtd", gated_out, w_out, preferred_element_type=jnp.float32)
    )
    normed_mid = layer_norm(mid_state, norm_gains[1]).astype(jnp.bfloat16)
    pre_act = jnp.einsum("mtd,df->mtf", normed_mid, w_up, preferred_element_type=jnp.float32)
    hidden = jax.nn.gelu(pre_act).astype(jnp.bfloat16)
    new_stream = mid_state + channel_total(
        jnp.einsum("mtf,fd->mtd", hidden, w_down, preferred_element_type=jnp.float32)
    )
    kept_vals = (
        stream,
        normed,
        mixed_in,
        padded,
        gate_vals,
        received,
        conv_out,
        gated_out,
        mid_state,
        normed_mid,
        pre_act,
        hidden,
    )
    return (new_stream, kept_vals)


def layer_backward(grad_stream, kept_vals, params, filt_spec, skip_part, tables):
    norm_gains, w_in, kernel, w_out, w_up, w_down = params
    (
        stream,
        normed,
        mixed_in,
        padded,
        gate_vals,
        moved_in,
        conv_out,
        gated_out,
        mid_state,
        normed_mid,
        pre_act,
        hidden,
    ) = kept_vals
    micro_count, tok_rows = (mixed_in.shape[0], mixed_in.shape[1])
    chan_width = mixed_in.shape[3]
    grad_low = grad_stream.astype(jnp.bfloat16)
    grad_down = jnp.einsum("mtf,mtd->fd", hidden, grad_low, preferred_element_type=jnp.float32)
    grad_hidden = jnp.einsum("mtd,fd->mtf", grad_low, w_down, preferred_element_type=jnp.float32)
    _, gelu_back = jax.vjp(jax.nn.gelu, pre_act)
    grad_pre = gelu_back(grad_hidden)[0].astype(jnp.bfloat16)
    grad_up = jnp.einsum("mtd,mtf->df", normed_mid, grad_pre, preferred_element_type=jnp.float32)
    grad_normed_mid = input_total(
        jnp.einsum("mtf,df->mtd", grad_pre, w_up, preferred_element_type=jnp.float32)
    )
    _, norm_back_mid = jax.vjp(layer_norm, mid_state, norm_gains[1])
    grad_mid_norm, grad_gain_mid = norm_back_mid(grad_normed_mid)
    grad_mid = grad_stream + grad_mid_norm
    grad_mid_low = grad_mid.astype(jnp.bfloat16)
    grad_out = jnp.einsum(
        "mtc,mtd->cd", gated_out, grad_mid_low, preferred_element_type=jnp.float32
    )
    grad_gated = jnp.einsum("mtd,cd->mtc", grad_mid_low, w_out, preferred_element_type=jnp.float32)
    grad_conv = grad_gated * gate_vals[:, :, 0]
    grad_first_gate = grad_gated * conv_out
    grad_flat = jnp.swapaxes(grad_conv, 1, 2).reshape(1, micro_count * chan_width, tok_rows)
    grad_cols = lax.all_to_all(grad_flat, "seq", split_axis=1, concat_axis=2, tiled=True)
    grad_u_cols, grad_filt, grad_skip_part = filter_backward(
        grad_cols, moved_in, filt_spec, skip_part, tables
    )
    grad_back_flat = lax.all_to_all(grad_u_cols, "seq", split_axis=2, concat_axis=1, tiled=True)
    grad_product = jnp.swapaxes(grad_back_flat.reshape(micro_count, chan_width, tok_rows), 1, 2)
    grad_gates = jnp.stack(
        [grad_first_gate, grad_product * gate_vals[:, :, 2], grad_product * gate_vals[:, :, 1]],
        axis=2,
    )
    rim_back = passed_along(grad_gates[:, :2], "seq", -1)
    extended = jnp.concatenate([grad_gates, rim_back], axis=1)
    grad_mixed = (
        kernel[0] * grad_gates
        + kernel[1] * extended[:, 1 : tok_rows + 1]
        + kernel[2] * extended[:, 2 : tok_rows + 2]
    )
    grad_kernel = jnp.stack(
        [
            jnp.sum(grad_gates * mixed_in, axis=(0, 1)),
            jnp.sum(grad_gates * padded[:, 1 : tok_rows + 1], axis=(0, 1)),
            jnp.sum(grad_gates * padded[:, 0:tok_rows], axis=(0, 1)),
        ]
    )
    grad_mixed_low = grad_mixed.astype(jnp.bfloat16)
    grad_in = jnp.einsum(
        "mtd,mtgc->dgc", normed, grad_mixed_low, preferred_element_type=jnp.float32
    )
    grad_normed = input_total(
        jnp.einsum("mtgc,dgc->mtd", grad_mixed_low, w_in, preferred_element_type=jnp.float32)
    )
    _, norm_back_in = jax.vjp(layer_norm, stream, norm_gains[0])
    grad_stream_norm, grad_gain_in = norm_back_in(grad_normed)
    grad_before = grad_mid + grad_stream_norm
    layer_grads = (
        jnp.stack([grad_gain_in, grad_gain_mid]),
        grad_in,
        grad_kernel,
        grad_skip_part,
        grad_out,
        grad_up,
        grad_down,
    )
    return (grad_before, layer_grads, grad_filt)


def local(
    ids,
    live,
    embed,
    norm_gain,
    in_weight,
    short_kernel,
    filter_first,
    filter_second,
    skip_gain,
    out_weight,
    up_weight,
    down_weight,
    cotangent,
):
    seq_count = lax.axis_size("seq")
    seq_rank = lax.axis_index("seq")
    group_idx = lax.axis_index("ch")
    micro_count = ids.shape[0]
    tok_rows = ids.shape[1]
    length = tok_rows * seq_count
    chan_width = in_weight.shape[3]
    own_rows = micro_count * chan_width // seq_count
    layer_count = in_weight.shape[0]
    row_start = seq_rank * own_rows
    row_ids = row_start + jnp.arange(own_rows, dtype=jnp.int32)
    chan_local = row_ids % chan_width
    first_rows = (row_ids < chan_width).astype(jnp.float32)
    select = (jnp.arange(chan_width, dtype=jnp.int32)[:, None] == chan_local[None, :]).astype(
        jnp.float32
    )
    tables = dft_tables(seq_count, tok_rows)
    features = position_features(length)
    ramp_row = jnp.arange(length, dtype=jnp.int32).astype(jnp.float32) / length
    stream, onehot, keep_mask = embed_lookup(ids, live, embed, seq_rank)
    filters = []
    for level_idx in range(layer_count):
        filt_cols, hidden_pre, hidden_act, second_part, decay_part = local_filter(
            filter_first[level_idx],
            filter_second[level_idx],
            features,
            select,
            group_idx,
            chan_local,
        )
        filt_spec = to_spectrum(filt_cols.reshape(own_rows, seq_count, tok_rows), tables)
        skip_part = jnp.dot(skip_gain[level_idx], select, precision=precise)
        penalty_grad = 0.5 * length * ramp_row[None, :] * filt_cols * first_rows[:, None]
        params = (
            norm_gain[level_idx],
            in_weight[level_idx],
            short_kernel[level_idx],
            out_weight[level_idx],
            up_weight[level_idx],
            down_weight[level_idx],
        )
        filters.append(
            (
                params,
                filt_spec,
                skip_part,
                (hidden_pre, hidden_act, second_part, decay_part),
                penalty_grad,
            )
        )
    stored = []
    for level_idx in range(layer_count):
        params, filt_spec, skip_part, _, _ = filters[level_idx]
        layer_input = stream
        stream, kept_vals = layer_forward(stream, params, filt_spec, skip_part, tables)
        stored.append(layer_input)
    block_out = stream * keep_mask[:, :, None]
    grad_stream = cotangent * keep_mask[:, :, None]
    collected = [None] * layer_count
    first_grads = [None] * layer_count
    grad_embed = None
    for level_idx in reversed(range(layer_count)):
        params, filt_spec, skip_part, filter_parts, penalty_grad = filters[level_idx]
        _, kept_vals = layer_forward(stored[level_idx], params, filt_spec, skip_part, tables)
        grad_stream, layer_grads, grad_filt = layer_backward(
            grad_stream, kept_vals, params, filt_spec, skip_part, tables
        )
        grad_first, grad_second_part = filter_mlp_backward(
            grad_filt + penalty_grad, features, filter_parts
        )
        first_grads[level_idx] = grad_first
        grad_second = jnp.dot(grad_second_part, select.T, precision=precise)
        grad_skip = jnp.dot(layer_grads[3], select.T, precision=precise)
        gain_grad, in_grad, kernel_grad, _, out_grad, up_grad, down_grad = layer_grads
        if level_idx == 0:
            embed_part = jnp.einsum("mtv,mtd->vd", onehot, grad_stream, precision=precise)
            summed = lax.psum(
                (
                    gain_grad,
                    in_grad,
                    kernel_grad,
                    grad_second,
                    grad_skip,
                    out_grad,
                    up_grad,
                    down_grad,
                    embed_part,
                ),
                "seq",
            )
            collected[level_idx] = summed[:8]
            grad_embed = summed[8]
        else:
            collected[level_idx] = lax.psum(
                (
                    gain_grad,
                    in_grad,
                    kernel_grad,
                    grad_second,
                    grad_skip,
                    out_grad,
                    up_grad,
                    down_grad,
                ),
                "seq",
            )
    stacked = [
        jnp.stack([collected[level_idx][member] for level_idx in range(layer_count)])
        for member in range(8)
    ]
    filter_grads = lax.psum(jnp.stack(first_grads), ("seq", "ch"))
    return (
        block_out,
        grad_embed,
        stacked[0],
        stacked[1],
        stacked[2],
        filter_grads,
        stacked[3],
        stacked[4],
        stacked[5],
        stacked[6],
        stacked[7],
    )


HALO = 16
FEAT_ROWS = 40
ROOT_HALF = math.sqrt(0.5)
GELU_A = math.sqrt(2.0 / math.pi)
GELU_B = 0.044715
BLOCKS = 8
BLOCK = 256
KINDS = 9
VMEM_LIMIT = 8 * 2**20
VMEM_LIMITS = dict(turn_back_kernel=20 * 2**20, back_first_kernel=16 * 2**20)
FLOPS, FEW_FLOPS, MANY_FLOPS = 10**10, 10**8, 10**12
FLOPS_OF = dict(conv_first1=100000000, pair5=10000000000, grad_freq1=30000000000, last1=1000000000, conv_second1=3000000000, join_weights2=100000000)
CALLS = collections.Counter()
f32 = jnp.float32
bf16 = jnp.bfloat16


class Numbers:
    def __init__(self, table):
        self.table = table

    def __getitem__(self, row):
        return self.table[row, 0]


CORE, GROUP, LIVE, WHICH, SPOT, HOLDER, BIT1, BIT2, BIT3 = range(9)
NUMBER_ROWS = 16


def bring(pairs, done):
    copies = [pltpu.make_async_copy(far, near, done.at[i]) for i, (far, near) in enumerate(pairs)]
    for copy in copies:
        copy.start()
    for copy in copies:
        copy.wait()


def numbers_kernel(*refs):
    far, (table, own_ids, cot, pack, part), near, done = refs[:13], refs[13:18], refs[18:30], refs[30]
    far_live, far_ids, far_cot, far_embed, far_gain, far_in, far_second, far_short, far_skip, far_out, far_up, far_down, far_in1 = far
    live, ids, embed, gain, in_own, second, short, skip, raw_out, raw_up, raw_down, in1 = near
    rank, group = lax.axis_index("seq"), lax.axis_index("ch")
    bring(
        (
            (far_live, live), (far_ids, ids), (far_cot.at[group], cot.at[0]), (far_embed, embed), (far_gain, gain),
            (far_in.at[0], in_own), (far_second, second), (far_short, short), (far_skip, skip), (far_out.at[0], raw_out),
            (far_up.at[0], raw_up), (far_down.at[0], raw_down), (far_in1.at[1], in1),
        ),
        done,
    )
    fill_pack(embed, gain, in_own, second, short, skip, pack)
    core, half = rank % 2, lax.axis_size("seq") // 2
    first = group == 0
    holder = jnp.where(rank // half == core, 1, 0)
    values = (core, group, None, group + core - 2 * group * core, rank % half, holder, rank // 2 % 2, rank // 4 % 2, rank // 8 % 2)
    for row, value in enumerate(values):
        if row != LIVE:
            table[row : row + 1, :] = jnp.full((1, 128), value, jnp.int32)
    chosen = jnp.where(first, live[0:1, 0:1], live[0:1, 1:2])
    table[LIVE : LIVE + 1, :] = jnp.broadcast_to(chosen, (1, 128))
    own_ids[0] = jnp.broadcast_to(jnp.where(first, ids[0:1, :], ids[1:2, :]), own_ids.shape[1:])
    s = Numbers(table)
    fill_part(s, raw_out, raw_up, raw_down, part)
    fill_in_part(s, in1, part.at[1152:1536])


def in_hbm(value):
    return pltpu.with_memory_space_constraint(value, pltpu.HBM)


def start(body, outs, *arrays, scratch):
    vmem, far = pl.BlockSpec(memory_space=pltpu.VMEM), pl.BlockSpec(memory_space=pltpu.HBM)
    return pl.pallas_call(
        body, out_shape=outs, in_specs=[far] * len(arrays), out_specs=[vmem] * len(outs), name=body.__name__,
        scratch_shapes=list(scratch),
        cost_estimate=pl.CostEstimate(flops=MANY_FLOPS, bytes_accessed=1, transcendentals=0),
        compiler_params=pltpu.CompilerParams(vmem_limit_bytes=VMEM_LIMIT),
    )(*(in_hbm(v) for v in arrays))


def run(body, outs, scalars, *arrays, scratch=(), after=(), hbm=(), flops=None, hbm_outs=(), aliases=(), token=False):
    vmem = pl.BlockSpec(memory_space=pltpu.VMEM)
    far, wait = pl.BlockSpec(memory_space=pltpu.HBM), pl.BlockSpec(memory_space=pl.ANY)
    single = not isinstance(outs, (list, tuple))
    shapes = [outs] if single else list(outs)
    count = len(shapes)
    shapes += [arr(8, 128)] * token
    used, waits = 1 + len(arrays), len(after)

    def call(table, *refs):
        given, rest = refs[: used - 1], refs[used - 1 + waits :]
        body(Numbers(table), *given, *rest[:count], *rest[count + token :])
        if token:
            rest[count][...] = jnp.zeros((8, 128), f32)

    inner = getattr(body, "func", body)
    CALLS[inner.__name__] += 1
    flops = flops or FLOPS_OF.get(f"{inner.__name__[:-7]}{CALLS[inner.__name__]}", FLOPS)
    result = pl.pallas_call(
        call,
        out_shape=shapes,
        in_specs=[vmem] + [far if i in hbm else vmem for i in range(len(arrays))] + [wait] * waits,
        out_specs=[far if i in hbm_outs else vmem for i in range(len(shapes))],
        input_output_aliases={1 + a: b for a, b in aliases},
        scratch_shapes=list(scratch),
        compiler_params=pltpu.CompilerParams(vmem_limit_bytes=VMEM_LIMITS.get(inner.__name__, VMEM_LIMIT)),
        cost_estimate=pl.CostEstimate(flops=flops, bytes_accessed=1, transcendentals=0),
        name=inner.__name__,
    )(scalars, *(in_hbm(v) if i in hbm else v for i, v in enumerate(arrays)), *after)
    return result[0] if len(shapes) == 1 else result


def arr(*shape, kind=f32):
    return jax.ShapeDtypeStruct(shape, kind)


def mm(a, b):
    return jnp.dot(a, b, preferred_element_type=f32)


def mm_nt(a, b):
    return lax.dot_general(a, b, (((1,), (1,)), ((), ())), preferred_element_type=f32)


def mm_tn(a, b):
    return lax.dot_general(a, b, (((0,), (0,)), ((), ())), preferred_element_type=f32)


def split(a):
    high = a.astype(bf16)
    return high, (a - high.astype(f32)).astype(bf16)


def unit(rows):
    center = rows - jnp.mean(rows, axis=-1, keepdims=True)
    scale = lax.rsqrt(jnp.mean(center * center, axis=-1, keepdims=True) + epsilon)
    return center * scale, scale


def unit_back(grad, normal, scale):
    inner = jnp.mean(grad * normal, axis=-1, keepdims=True)
    return scale * (grad - jnp.mean(grad, axis=-1, keepdims=True) - normal * inner)


def every(count, step):
    for i in range(count):
        step(i, 0)


def at(start, size, unit_rows=16):
    return pl.ds(start if isinstance(start, int) else pl.multiple_of(start, unit_rows), size)


def dft_table():
    turns = np.outer(np.arange(BLOCK), np.arange(BLOCK)) % BLOCK
    angle = 2.0 * np.pi * turns / BLOCK
    return np.concatenate([np.cos(angle), np.sin(angle)], axis=1).astype(np.float32)


def twiddle_table():
    angle = 2.0 * np.pi * np.outer(np.arange(BLOCK), np.arange(1, KINDS)) / (2 * BLOCKS * BLOCK)
    return np.concatenate([np.cos(angle), np.sin(angle)], axis=1).astype(np.float32)


def twiddle_kernel(s, narrow, out):
    for kind in range(KINDS - 1):
        for part in range(2):
            column = (KINDS - 1) * part + kind
            out[kind, part] = jnp.broadcast_to(narrow[:, column : column + 1], (BLOCK, 128))


def feature_table(length):
    places = np.arange(length)
    turns = np.outer(places, np.arange(1, (FEAT - 1) // 2 + 1)) % length
    angle = 2.0 * np.pi * turns / length
    ramp = places[:, None] / length
    return np.concatenate([ramp, np.cos(angle), np.sin(angle)], axis=1).astype(np.float32)


def thirds(values):
    low = lambda v: v.astype(ml_dtypes.bfloat16).astype(np.float32)
    first = low(values)
    second = low(values - first)
    return first, second, low(values - first - second)


def feature_parts(length):
    first, second, third = thirds(np.pad(feature_table(length), ((0, 0), (0, FEAT_ROWS - FEAT))))
    return np.pad(np.concatenate([first, first, second, second, first, third], axis=1), ((0, 0), (0, 256 - 6 * FEAT_ROWS)))


def rate_table():
    return (0.3 * 10.0 ** (np.arange(D) / (D - 1))).astype(np.float32).reshape(2, 1, D // 2)


def four_real(a, b, c, d):
    s, m, t, n = a + c, a - c, b + d, b - d
    hn, ht = ROOT_HALF * n, ROOT_HALF * t
    return (s + t, s - t, (a + hn, -(ht + c)), (m, -n), (a - hn, c - ht))


def turn(k):
    angle = 2.0 * math.pi * k / (2 * BLOCKS)
    return math.cos(angle), math.sin(angle)


def put_pair(stage, kind, row, re, im):
    rows = re.shape[0]
    re, im = re.astype(bf16), im.astype(bf16)
    stage[kind, pl.ds(row, rows), 0:128] = re
    stage[kind, pl.ds(row, rows), 128:256] = im
    stage[kind, pl.ds(row + BLOCK, rows), 0:128] = im
    stage[kind, pl.ds(row + BLOCK, rows), 128:256] = -re


def put_pair_back(stage, kind, row, re, im):
    rows = re.shape[0]
    re, im = re.astype(bf16), im.astype(bf16)
    stage[kind, pl.ds(row, rows), 0:128] = re
    stage[kind, pl.ds(row, rows), 128:256] = im
    stage[kind, pl.ds(row + BLOCK, rows), 0:128] = -im
    stage[kind, pl.ds(row + BLOCK, rows), 128:256] = re


def all_kinds(dft, stage, out):
    table = dft[...]
    for kind in range(KINDS):
        out[kind] = mm(table, stage[kind])


def to_freq(load, dft, twiddle, stage, out):
    def chunk(step, carry):
        row = step * 16
        u = [load(p, row) for p in range(BLOCKS)]
        e0, e4, e1, e2, e3 = four_real(u[0], u[2], u[4], u[6])
        o0, o4, o1, o2, o3 = four_real(u[1], u[3], u[5], u[7])

        def put(kind, re, im):
            c, s = twiddle[kind - 1, 0, pl.ds(row, 16), :], twiddle[kind - 1, 1, pl.ds(row, 16), :]
            put_pair(stage, kind, row, re * c + im * s, im * c - re * s)

        put_pair(stage, 0, row, e0 + o0, jnp.zeros_like(e0))
        last = e0 - o0
        c, s = twiddle[7, 0, pl.ds(row, 16), :], twiddle[7, 1, pl.ds(row, 16), :]
        put_pair(stage, 8, row, last * c, -(last * s))
        put(4, e4, -o4)
        for k, (er, ei), (orr, oi) in ((1, e1, o1), (2, e2, o2), (3, e3, o3)):
            c, s = turn(k)
            wr, wi = orr * c + oi * s, oi * c - orr * s
            put(k, er + wr, ei + wi)
            put(8 - k, er - wr, wi - ei)
        return carry

    every(BLOCK // 16, chunk)
    all_kinds(dft, stage, out)


def from_freq(dft, twiddle, stage, back, store):
    all_kinds(dft, stage, back)

    def chunk(step, carry):
        row = step * 16

        def get(kind):
            re = back[kind, pl.ds(row, 16), 0:128]
            im = back[kind, pl.ds(row, 16), 128:256]
            c, s = twiddle[kind - 1, 0, pl.ds(row, 16), :], twiddle[kind - 1, 1, pl.ds(row, 16), :]
            return re * c - im * s, re * s + im * c

        first = 0.5 * back[0, pl.ds(row, 16), 0:128]
        last = 0.5 * get(8)[0]
        mid_re, mid_im = get(4)
        even, odd = {}, {}
        for k in (1, 2, 3):
            ar, ai = get(k)
            br, bi = get(8 - k)
            even[k] = (ar + br, ai - bi)
            c, s = turn(k)
            dr, di = ar - br, ai + bi
            odd[k] = (dr * c - di * s, dr * s + di * c)
        for shift, base, extra, part in (
            (0, first + last, mid_re, even),
            (1, first - last, -mid_im, odd),
        ):
            (r1, i1), (r2, i2), (r3, i3) = part[1], part[2], part[3]
            plus, minus = base + extra, base - extra
            diff, both = ROOT_HALF * (r1 - r3), ROOT_HALF * (i1 + i3)
            store(shift, row, plus + (r1 + r2 + r3))
            store(shift + 2, row, minus - i2 + (diff - both))
            store(shift + 4, row, plus - r2 - (i1 - i3))
            store(shift + 6, row, minus + i2 - (diff + both))
        return carry

    every(BLOCK // 16, chunk)


def times(first, second, stage, conj):
    def chunk(step, carry):
        row = step * 16
        for kind in range(KINDS):
            fr = first[kind, pl.ds(row, 16), 0:128]
            fi = first[kind, pl.ds(row, 16), 128:256]
            ur = second[kind, pl.ds(row, 16), 0:128]
            ui = second[kind, pl.ds(row, 16), 128:256]
            if conj:
                put_pair_back(stage, kind, row, fr * ur + fi * ui, fr * ui - fi * ur)
            else:
                put_pair_back(stage, kind, row, fr * ur - fi * ui, fr * ui + fi * ur)
        return carry

    every(BLOCK // 16, chunk)


SPECTRUM = (KINDS, BLOCK, 256)


def stage_scratch():
    return pltpu.VMEM((KINDS, 2 * BLOCK, 256), bf16)


def spec_scratch():
    return pltpu.VMEM(SPECTRUM, f32)


PACK_SECOND = 48
PACK_SHORT = 176
PACK_SKIP = 194
PACK_ROWS = 200


def fill_pack(embed, gain, in_own, second, short, skip, out):
    normal, _ = unit(embed[...])
    low = (normal * gain[0, 0:1, :]).astype(bf16)
    for g in range(3):
        out[16 * g : 16 * g + 16, :] = mm(low, in_own[g])
    for l in range(2):
        out[PACK_SECOND + 64 * l : PACK_SECOND + 64 * l + 64, :] = second[l]
        for k in range(3):
            for g in range(3):
                row = PACK_SHORT + 9 * l + 3 * k + g
                out[row : row + 1, :] = short[k, g, l : l + 1, :]
    out[PACK_SKIP : PACK_SKIP + 2, :] = skip[...]
    out[PACK_SKIP + 2 : PACK_ROWS, :] = jnp.zeros((PACK_ROWS - PACK_SKIP - 2, 128), f32)


def table_kernel(s, own, peer, embed, mine_out, other_out, conv_table, gate_table):
    first = s[CORE] == 0
    mine = jnp.where(first, own[...], peer[...])
    other = jnp.where(first, peer[...], own[...])
    mine_out[...] = mine
    other_out[...] = other

    def fill(table, lanes, parts):
        whole = jnp.concatenate(parts, axis=0)
        high, low = split(whole)
        table[0:48, lanes] = high
        table[48:96, lanes] = low
        table[96:128, lanes] = jnp.zeros((32, 128), bf16)

    def gate(pack, g):
        parts = []
        for k in range(3):
            row = PACK_SHORT + 3 * k + g
            parts.append(pack[16 * g : 16 * g + 16] * pack[row : row + 1])
        return parts

    fill(conv_table, slice(0, 128), gate(mine, 1))
    fill(conv_table, slice(128, 256), gate(mine, 2))
    fill(gate_table, slice(0, 128), gate(mine, 0))
    fill(gate_table, slice(128, 256), gate(other, 0))
    zero = jnp.zeros((16, 128), f32)
    fill(gate_table, slice(256, 384), [embed[:, 0:128], zero, zero])
    fill(gate_table, slice(384, 512), [embed[:, 128:256], zero, zero])


def onehot_kernel(s, ids, out, turned, work):
    live = s[LIVE]
    count, _, width = ids.shape
    work[0:HALO, :] = jnp.zeros((HALO, 128), f32)
    work[HALO + count * width : 2 * HALO + count * width, :] = jnp.zeros((HALO, 128), f32)
    vocab = lax.broadcasted_iota(jnp.int32, (128, width), 0) % 16
    place = lax.broadcasted_iota(jnp.int32, (128, width), 1)
    for i in range(count):
        token = jnp.broadcast_to(ids[i, 0:1, :], (128, width))
        hit = (token == vocab) & (place + i * width < live)
        work[HALO + width * i : HALO + width * (i + 1), :] = jnp.where(hit, 1.0, 0.0).T
    lane = lax.broadcasted_iota(jnp.int32, (width, 128), 1) % 48 // 16
    used = lax.broadcasted_iota(jnp.int32, (width, 128), 1) < 96
    half = count // 2
    for i in range(count):
        row = HALO + width * i
        now = work[row : row + width, :]
        one = work[row - 1 : row - 1 + width, :]
        two = work[row - 2 : row - 2 + width, :]
        picked = jnp.where(lane == 0, now, jnp.where(lane == 1, one, two))
        picked = jnp.where(used, picked, 0.0)
        out[row : row + width, :] = picked.astype(bf16)
        turned[i // half, :, width * (i % half) : width * (i % half + 1)] = picked.T.astype(bf16)
    out[0:HALO, :] = jnp.zeros((HALO, 128), bf16)
    out[HALO + count * width : 2 * HALO + count * width, :] = jnp.zeros((HALO, 128), bf16)


def sine_and_cosine(angle):
    turns = jnp.round(angle * (2.0 / math.pi))
    x = ((angle - turns * 1.5703125) - turns * 4.837512969970703125e-4) - turns * 7.549789948768648e-8
    z = x * x
    sin = ((-1.9515295891e-4 * z + 8.3321608736e-3) * z - 1.6666654611e-1) * z * x + x
    cos = ((2.443315711809948e-5 * z - 1.388731625493765e-3) * z + 4.166664568298827e-2) * z * z - 0.5 * z + 1.0
    quarter = turns.astype(jnp.int32) & 3
    odd = (quarter & 1) == 1
    first, second = jnp.where(odd, cos, sin), jnp.where(odd, sin, cos)
    first = jnp.where(quarter >= 2, -first, first)
    second = jnp.where((quarter == 1) | (quarter == 2), -second, second)
    return first, second


def sine_kernel(s, feats, firsts, sine, cosine, turned, padded):
    padded[...] = jnp.zeros_like(padded)
    for l in range(2):
        padded[0:FEAT, 64 * l : 64 * l + 64] = firsts[:, l, :]
    both = padded[...]
    cut = lambda v: v.astype(bf16).astype(f32)
    first = cut(both)
    second = cut(both - first)
    third = both - first - second
    fill = jnp.zeros((256 - 6 * FEAT_ROWS, 128), f32)
    weights = jnp.concatenate([first, second, first, second, third, first, fill], axis=0).astype(bf16)
    count = feats.shape[0] // 512

    def chunk(i, carry):
        rows = at(512 * i, 512)
        act, cosine[rows, :] = sine_and_cosine(mm(feats[rows, :], weights))
        sine[rows, 0:128], sine[rows, 128:256] = split(act)
        turned[:, at(512 * i, 512, 256)] = act.T.astype(bf16)
        return carry

    every(count, chunk)


def decay_of(rates, start, rows, length):
    place = (lax.broadcasted_iota(jnp.int32, (rows, 1), 0) + start).astype(f32) / length
    return jnp.exp(-place * rates), place


def filter_kernel(level, s, sine, mine, rates, dft, twiddle, filt, freq, stage):
    length = sine.shape[0]
    rate = rates[s[WHICH]]
    zero = jnp.zeros((64, 128), f32)
    second = mine[PACK_SECOND + 64 * level : PACK_SECOND + 64 * level + 64]
    high, low = split(jnp.concatenate([zero, second] if level else [second, zero], axis=0))
    twice = jnp.concatenate([high, high], axis=0)

    def chunk(i, carry):
        rows = at(512 * i, 512)
        decay, _ = decay_of(rate, 512 * i, 512, length)
        filt[rows, :] = (mm(sine[rows, :], twice) + mm(sine[rows, 0:128], low)) * decay
        return carry

    every(length // 512, chunk)
    to_freq(lambda p, row: filt[pl.ds(BLOCK * p + row, 16), :] * (1.0 / length), dft, twiddle, stage, freq)


def causal(load, skip_row, freq_filt, dft, twiddle, spec, stage, work, line):
    to_freq(load, dft, twiddle, stage, spec)
    times(freq_filt, spec, stage, False)

    def store(p, row, value):
        line[pl.ds(HALO + BLOCK * p + row, 16), :] = value + skip_row * load(p, row)

    from_freq(dft, twiddle, stage, work, store)


def hand_out(s, line, keep, send):
    half = (line.shape[0] - 2 * HALO) // 2
    span = half + 2 * HALO
    k = s[CORE]
    line[0:HALO, :] = jnp.zeros((HALO, 128), f32)
    line[HALO + 2 * half :, :] = jnp.zeros((HALO, 128), f32)
    keep[...] = line[at(half * k, span), :]
    send[...] = line[at(half * (1 - k), span), :]


def conv_first_kernel(s, onehot, conv_table, mine, freq_filt, dft, twiddle, keep, send, spec, product, stage, work, line):
    def chunk(i, carry):
        rows = at(512 * i, 512)
        pair = mm(onehot[at(512 * i + HALO, 512), :], conv_table[...])
        product[rows, :] = pair[:, 0:128] * pair[:, 128:256]
        return carry

    every(product.shape[0] // 512, chunk)
    skip_row = mine[PACK_SKIP : PACK_SKIP + 1, :]
    causal(lambda p, row: product[pl.ds(BLOCK * p + row, 16), :], skip_row, freq_filt, dft, twiddle, spec, stage, work, line)
    hand_out(s, line, keep, send)


def join_rows(s, whole, kept, received):
    half = kept.shape[0]
    whole[at(half * s[CORE], half), :] = kept[...]
    whole[at(half * (1 - s[CORE]), half), :] = received[...]


def conv_second_kernel(s, kept, received, mine, freq_filt, dft, twiddle, keep, send, spec, product, stage, work, line):
    join_rows(s, product, kept, received)
    skip_row = mine[PACK_SKIP + 1 : PACK_SKIP + 2, :]
    causal(lambda p, row: product[pl.ds(BLOCK * p + row, 16), :], skip_row, freq_filt, dft, twiddle, spec, stage, work, line)
    hand_out(s, line, keep, send)


def gelu_parts(p):
    squared = p * p
    th = jnp.tanh(GELU_A * p * (1.0 + GELU_B * squared))
    half = 0.5 * (1.0 + th)
    slope = half + 0.5 * p * (1.0 - th * th) * (GELU_A + (3.0 * GELU_A * GELU_B) * squared)
    return p * half, slope


def gelu_only(p):
    return 0.5 * p * (1.0 + jnp.tanh(GELU_A * p * (1.0 + GELU_B * (p * p))))


def forward_first_kernel(
    s, onehot, gate_table, conv_mine, conv_other, gain, w_out, w_up, w_down, w_in, mine, other,
    keep, send, mid_out, stream_out, gates, mixed,
):
    span = mid_out.shape[0]
    half = span - 2 * HALO
    k = s[CORE]
    taps = [
        jnp.concatenate([pack[PACK_SHORT + 9 + 3 * t + g : PACK_SHORT + 10 + 3 * t + g, :] for g in range(3) for pack in (mine, other)], axis=1)
        for t in range(3)
    ]

    def chunk(i, carry):
        rows = at(span * i, span)
        looked = mm(onehot[at(half * k + span * i, span), :], gate_table[...])
        conv = jnp.concatenate([conv_mine[rows, :], conv_other[rows, :]], axis=1)
        gated = (conv * looked[:, 0:256]).astype(bf16)
        mid = looked[:, 256:512] + mm(gated, w_out[...])
        mid_out[rows, :] = mid
        normal, _ = unit(mid)
        low = (normal * gain[0, 1:2, :]).astype(bf16)
        hidden = gelu_only(mm(low, w_up[...])).astype(bf16)
        stream = mid + mm(hidden, w_down[...])
        stream_out[rows, :] = stream
        normal, _ = unit(stream)
        low = (normal * gain[1, 0:1, :]).astype(bf16)
        mixed[rows, :] = mm(low, w_in[...])
        return carry

    every(1, chunk)
    gates[0:HALO, :] = jnp.zeros((HALO, 768), f32)
    step = 80
    for start in range(HALO, span, step):
        stop = start + step
        gates[start:stop, :] = (
            taps[0] * mixed[start:stop, :]
            + taps[1] * mixed[start - 1 : stop - 1, :]
            + taps[2] * mixed[start - 2 : stop - 2, :]
        )
    own = slice(HALO, HALO + half)
    keep[...] = gates[own, 256:384] * gates[own, 512:640]
    send[...] = gates[own, 384:512] * gates[own, 640:768]


def turn_back_kernel(
    s, conv_mine, conv_other, gates, stream, cot, cot_rim, gain, w_out, w_up, w_down,
    keep, send, grad_x0, grad_mid, block_out, hidden_out, low_out, normed_out, pre_out, gated_out, mid_low_out, gain_out,
    cot_rows, conv_grads,
):
    span = stream.shape[0]
    half = span - 2 * HALO
    k = s[CORE]
    live = s[LIVE]
    cot_rows[0:HALO, :] = jnp.zeros((HALO, 256), f32)
    cot_rows[HALO : HALO + half, :] = cot[...]
    cot_rows[HALO + half :, :] = jnp.where(k == 0, cot_rim[...], 0.0)
    gain_out[...] = jnp.zeros_like(gain_out)

    def chunk(i, carry):
        rows = at(span * i, span)
        local_row = lax.broadcasted_iota(jnp.int32, (span, 1), 0) + span * i
        keep_mask = (local_row + (half * k - HALO) < live).astype(f32)
        own_mask = ((local_row >= HALO) & (local_row < HALO + half)).astype(f32)
        x0 = gates[rows, 0:256]
        conv = jnp.concatenate([conv_mine[rows, :], conv_other[rows, :]], axis=1)
        gated = (conv * x0).astype(bf16)
        gated_out[rows, :] = gated
        mid = stream[rows, :] + mm(gated, w_out[...])
        normal, scale = unit(mid)
        gain_row = gain[1, 1:2, :]
        low = (normal * gain_row).astype(bf16)
        normed_out[rows, :] = low
        act, slope = gelu_parts(mm(low, w_up[...]))
        hidden = act.astype(bf16)
        hidden_out[rows, :] = hidden
        block_out[rows, :] = (mid + mm(hidden, w_down[...])) * keep_mask
        grad = cot_rows[rows, :] * keep_mask
        grad_low = grad.astype(bf16)
        low_out[rows, :] = grad_low
        grad_pre = (slope * mm_nt(grad_low, w_down[...])).astype(bf16)
        pre_out[rows, :] = grad_pre
        grad_normed = mm_nt(grad_pre, w_up[...])
        gain_out[0:1, :] += jnp.sum(grad_normed * normal * own_mask, axis=0, keepdims=True)
        mid_grad = grad + unit_back(grad_normed * gain_row, normal, scale)
        grad_mid[rows, :] = mid_grad
        mid_low = mid_grad.astype(bf16)
        mid_low_out[rows, :] = mid_low
        grad_gated = mm_nt(mid_low, w_out[...])
        conv_grads[rows, :] = grad_gated * x0
        grad_x0[rows, :] = grad_gated * conv
        return carry

    every(1, chunk)
    own = slice(HALO, HALO + half)
    keep[...] = conv_grads[own, 0:128]
    send[...] = conv_grads[own, 128:256]


def conv_back_kernel(s, kept, received, mine, freq_filt, dft, twiddle, keep, send, spec, grads, stage, work, line):
    join_rows(s, grads, kept, received)
    skip_row = mine[PACK_SKIP + 1 : PACK_SKIP + 2, :]
    load = lambda p, row: grads[pl.ds(BLOCK * p + row, 16), :]
    to_freq(load, dft, twiddle, stage, spec)
    times(freq_filt, spec, stage, True)

    def store(p, row, value):
        line[pl.ds(HALO + BLOCK * p + row, 16), :] = value + skip_row * load(p, row)

    from_freq(dft, twiddle, stage, work, store)
    hand_out(s, line, keep, send)


def grad_freq_kernel(s, kept, received, dft, twiddle, spec, grads, stage):
    join_rows(s, grads, kept, received)
    to_freq(lambda p, row: grads[pl.ds(BLOCK * p + row, 16), :], dft, twiddle, stage, spec)


def filter_back(
    level, s, spec_grad, spec_in, grads, product, filt, cosine, sine_turned, mine, rates, feats_turned, dft, twiddle,
    second_out, first_out, skip_out, stage, work, line,
):
    length = filt.shape[0]
    times(spec_in, spec_grad, stage, True)

    def store(p, row, value):
        line[pl.ds(BLOCK * p + row, 16), :] = value

    from_freq(dft, twiddle, stage, work, store)
    rate = rates[s[WHICH]]
    second = mine[PACK_SECOND + 64 * level : PACK_SECOND + 64 * level + 64, :].astype(bf16)
    weight = jnp.where(s[GROUP] == 0, 0.5 * length, 0.0)
    skip_out[...] = jnp.zeros_like(skip_out)
    second_out[...] = jnp.zeros_like(second_out)
    first_out[...] = jnp.zeros_like(first_out)
    for i in range(length // 512):
        rows = slice(512 * i, 512 * (i + 1))
        decay, place = decay_of(rate, 512 * i, 512, length)
        shaped = ((line[rows, :] * (1.0 / length) + (weight * place) * filt[rows, :]) * decay).astype(bf16)
        skip_out[...] += jnp.sum((grads[rows, :] * product[rows, :]).reshape(64, 8, 128), axis=0)
        second_out[...] += mm(sine_turned[64 * level : 64 * level + 64, rows], shaped)
        inner = (mm_nt(shaped, second) * cosine[rows, 64 * level : 64 * level + 64]).astype(bf16)
        first_out[...] += mm(feats_turned[:, rows], inner)


def filter_back_kernel(s, *refs):
    filter_back(1, s, *refs)


def token_back_kernel(
    s, spec_grad, spec_in, grads, product, filt, cosine, sine_turned, mine, rates, feats_turned, dft, twiddle,
    freq_filt, onehot, turned, conv_table, second_out, first_out, skip_out, by_token, stage, work, line,
):
    length = grads.shape[0]
    skip_row = mine[PACK_SKIP : PACK_SKIP + 1, :]
    times(freq_filt, spec_grad, stage, True)

    def store(p, row, value):
        line[pl.ds(BLOCK * p + row, 16), :] = value + skip_row * grads[pl.ds(BLOCK * p + row, 16), :]

    from_freq(dft, twiddle, stage, work, store)
    by_token[...] = jnp.zeros_like(by_token)
    width = turned.shape[2]
    for i in range(length // width):
        rows = slice(width * i, width * (i + 1))
        pair = mm(onehot[HALO + width * i : HALO + width * (i + 1), :], conv_table[...])
        back = line[rows, :]
        gate_grads = jnp.concatenate([back * pair[:, 128:256], back * pair[:, 0:128]], axis=1).astype(bf16)
        by_token[...] += mm(turned[i], gate_grads)[0:48, :]
    filter_back(
        0, s, spec_grad, spec_in, grads, product, filt, cosine, sine_turned, mine, rates, feats_turned, dft, twiddle,
        second_out, first_out, skip_out, stage, work, line,
    )


def back_gates_kernel(
    s, prod_mine, prod_other, grad_x0, gates, mixed, grad_mid, stream, gain, mine, other, w_in,
    grad_stream, normed_out, mixed_low, short_out, gain_out, line,
):
    span = stream.shape[0]
    half = span - 2 * HALO
    taps = [
        jnp.concatenate([pack[PACK_SHORT + 9 + 3 * t + g : PACK_SHORT + 10 + 3 * t + g, :] for g in range(3) for pack in (mine, other)], axis=1)
        for t in range(3)
    ]
    step = 128
    for start in list(range(HALO, HALO + half, step)) + [HALO + half]:
        stop = start + (step if start < HALO + half else HALO)
        for lanes, prod in ((slice(0, 128), prod_mine), (slice(128, 256), prod_other)):
            first, second = slice(256 + lanes.start, 256 + lanes.stop), slice(512 + lanes.start, 512 + lanes.stop)
            product = prod[start:stop, :]
            line[start:stop, lanes] = product * gates[start:stop, second]
            line[start:stop, first] = product * gates[start:stop, first]
    short_out[...] = jnp.zeros_like(short_out)
    gain_out[...] = jnp.zeros_like(gain_out)
    for start in range(HALO, HALO + half, step):
        stop = start + step
        for g in range(3):
            lanes = slice(256 * g, 256 * g + 256)
            values = mixed[start:stop, lanes]
            total = None
            for t in range(3):
                shifted = grad_x0[start + t : stop + t, :] if g == 0 else line[start + t : stop + t, 256 * g - 256 : 256 * g]
                part = taps[t][:, lanes] * shifted
                total = part if total is None else total + part
                short_out[t, :, lanes] += jnp.sum((shifted * values).reshape(step // 8, 8, 256), axis=0)
            mixed_low[start - HALO : stop - HALO, lanes] = total.astype(bf16)

    def chunk(i, carry):
        rows = at(512 * i, 512)
        wide = at(512 * i + HALO, 512)
        normal, scale = unit(stream[wide, :])
        gain_row = gain[1, 0:1, :]
        normed_out[rows, :] = (normal * gain_row).astype(bf16)
        grad_normed = mm_nt(mixed_low[rows, :], w_in[...])
        gain_out[0:1, :] += jnp.sum(grad_normed * normal, axis=0, keepdims=True)
        grad_stream[rows, :] = grad_mid[wide, :] + unit_back(grad_normed * gain_row, normal, scale)
        return carry

    every(half // 512, chunk)


def back_first_kernel(
    s, grad_stream, mid, onehot, turned, gate_table, conv_mine, conv_other, gain, w_out, w_up, w_down,
    keep, send, hidden_out, low_out, normed_out, pre_out, gated_out, mid_low_out, by_token, gain_out,
):
    half = grad_stream.shape[0]
    k = s[CORE]
    by_token[...] = jnp.zeros_like(by_token)
    gain_out[...] = jnp.zeros_like(gain_out)

    def chunk(i, carry):
        rows = at(half * i, half)
        wide = at(half * i + HALO, half)
        hot = onehot[at(half * k + half * i + HALO, half), :]
        x0 = mm(hot, gate_table[:, 0:256])
        conv = jnp.concatenate([conv_mine[wide, :], conv_other[wide, :]], axis=1)
        gated_out[rows, :] = (conv * x0).astype(bf16)
        normal, scale = unit(mid[wide, :])
        gain_row = gain[0, 1:2, :]
        low = (normal * gain_row).astype(bf16)
        normed_out[rows, :] = low
        act, slope = gelu_parts(mm(low, w_up[...]))
        hidden_out[rows, :] = act.astype(bf16)
        grad = grad_stream[rows, :]
        grad_low = grad.astype(bf16)
        low_out[rows, :] = grad_low
        grad_pre = (slope * mm_nt(grad_low, w_down[...])).astype(bf16)
        pre_out[rows, :] = grad_pre
        grad_normed = mm_nt(grad_pre, w_up[...])
        gain_out[0:1, :] += jnp.sum(grad_normed * normal, axis=0, keepdims=True)
        mid_grad = grad + unit_back(grad_normed * gain_row, normal, scale)
        mid_low = mid_grad.astype(bf16)
        mid_low_out[rows, :] = mid_low
        grad_gated = mm_nt(mid_low, w_out[...])
        conv_grad = grad_gated * x0
        keep[rows, :] = conv_grad[:, 0:128]
        send[rows, :] = conv_grad[:, 128:256]
        flips = turned[k, :, at(half * i, half, 256)]
        rest = mid_grad - mid_low.astype(f32)
        gate_grads = jnp.concatenate([(grad_gated * conv).astype(bf16), mid_low, rest.astype(bf16)], axis=1)
        by_token[...] += mm(flips, gate_grads)[0:48, :]
        return carry

    every(1, chunk)


R_OUT, R_UP, R_DOWN, R_IN = 128, 512, 512, 384


def fill_part(s, raw_out, raw_up, raw_down, out):
    first = s[CORE] == 0
    pick = lambda a, b: jnp.where(first, a.astype(f32), b.astype(f32))
    out[0:128, :] = pick(raw_out[:, 0:128], raw_out[:, 128:256])
    for j in range(2):
        lanes = slice(128 * j, 128 * j + 128)
        out[128 + 256 * j : 384 + 256 * j, :] = pick(
            raw_up[:, 128 * j : 128 * j + 128], raw_up[:, 256 + 128 * j : 384 + 128 * j]
        )
        out[640 + 256 * j : 896 + 256 * j, :] = pick(raw_down[0:256, lanes], raw_down[256:512, lanes])


def fill_in_part(s, raw_in, out):
    first = s[CORE] == 0
    for g in range(3):
        a, b = raw_in[g, 0:128, :].astype(f32), raw_in[g, 128:256, :].astype(f32)
        out[128 * g : 128 * g + 128, :] = jnp.where(first, a, b)


def send_weights_kernel(s, w_out, w_up, w_down, out, raw_out, raw_up, raw_down, done):
    bring(((w_out.at[1], raw_out), (w_up.at[1], raw_up), (w_down.at[1], raw_down)), done)
    fill_part(s, raw_out, raw_up, raw_down, out)


def cot_split_kernel(s, blocks, keep, send):
    k = s[CORE]
    few = keep.shape[0]
    keep[...] = blocks[pl.ds(few * k, few)]
    send[...] = blocks[pl.ds(few * (1 - k), few)]


def cot_half_kernel(s, own, received, blocks, out):
    spot, width = s[CORE], own.shape[1]
    for j in range(own.shape[0]):
        out[pl.ds(width * (2 * j + spot), width), :] = own[j]
        out[pl.ds(width * (2 * j + 1 - spot), width), :] = received[j]
    out[2 * own.shape[0] * width :, :] = blocks[own.shape[0], 0:HALO, :]


def cot_whole_kernel(s, own, received, out, rim):
    spot = s[BIT1]
    rows = own.shape[0] - HALO
    two = rows // 2
    for j in range(2):
        out[pl.ds(two * (2 * j + spot), two), :] = own[two * j : two * j + two, :]
        out[pl.ds(two * (2 * j + 1 - spot), two), :] = received[two * j : two * j + two, :]
    rim[...] = jnp.where(spot == 0, own[rows:, :], received[rows:, :])


def relay_kernel(s, value, out):
    out[...] = value[...]


def join_weights_kernel(level, s, w_out, w_up, w_down, w_in, first_part, second_part, out_full, up_full, down_full, *in_full):
    first = s[CORE] == 0
    low = lambda ref, a, b: ref[a:b, :].astype(bf16)
    pick = lambda a, b: jnp.where(first, a, b)
    mine_out = w_out[level]
    a, b = first_part[0:128, :], second_part[0:128, :]
    peer_out = jnp.concatenate([pick(a, b), pick(b, a)], axis=1)
    out_full[0:128, :] = pick(mine_out.astype(f32), peer_out).astype(bf16)
    out_full[128:256, :] = pick(peer_out, mine_out.astype(f32)).astype(bf16)
    up_a, up_b = w_up[level, :, 0:256].astype(f32), w_up[level, :, 256:512].astype(f32)
    up_full[:, 0:256] = pick(up_a, up_b).astype(bf16)
    up_full[:, 256:512] = pick(up_b, up_a).astype(bf16)
    down_a, down_b = w_down[level, 0:256, :].astype(f32), w_down[level, 256:512, :].astype(f32)
    down_full[0:256, :] = pick(down_a, down_b).astype(bf16)
    down_full[256:512, :] = pick(down_b, down_a).astype(bf16)
    for n, part in enumerate((first_part, second_part)):
        for j in range(2):
            up_full[:, 512 + 256 * n + 128 * j : 640 + 256 * n + 128 * j] = low(part, 128 + 256 * j, 384 + 256 * j)
            down_full[512 + 256 * n : 768 + 256 * n, 128 * j : 128 * j + 128] = low(part, 640 + 256 * j, 896 + 256 * j)
    if in_full:
        (full,) = in_full
        for g in range(3):
            own = w_in[1 - level, g].astype(f32)
            a, b = first_part[1152 + 128 * g : 1280 + 128 * g, :], second_part[1152 + 128 * g : 1280 + 128 * g, :]
            peer = jnp.concatenate([pick(a, b), pick(b, a)], axis=0)
            full[:, 256 * g : 256 * g + 128] = pick(own, peer).astype(bf16)
            full[:, 256 * g + 128 : 256 * g + 256] = pick(peer, own).astype(bf16)


def wide_grads_kernel(pad, s, gated, mid_low, normed, grad_pre, hidden, grad_low, keep, send):
    k = s[CORE]
    first = k == 0
    stop = gated.shape[0] - pad
    own = lambda ref: ref[pad:stop, :]
    out = mm_tn(own(gated), own(mid_low))
    for m in range(2):
        a, b = out[128 * m : 128 * m + 128, 0:128], out[128 * m : 128 * m + 128, 128:256]
        half = m + k - 2 * m * k
        keep[half, 0:128, :] = jnp.where(first, a, b)
        send[half, 0:128, :] = jnp.where(first, b, a)
    for j in range(4):
        target = (keep, send)[j % 2]
        up = mm_tn(own(normed), grad_pre[pad:stop, 256 * j : 256 * j + 256])
        down = mm_tn(hidden[pad:stop, 256 * j : 256 * j + 256], own(grad_low))
        for n in range(2):
            lanes = slice(128 * n, 128 * n + 128)
            target[j // 2, 128 + 256 * n : 384 + 256 * n, :] = up[:, lanes]
            target[j // 2, 640 + 256 * n : 896 + 256 * n, :] = down[:, lanes]


def in_grads_kernel(s, normed_in, mixed_low, keep, send):
    k = s[CORE]
    first = k == 0
    for g in range(3):
        both = mm_tn(normed_in[...], mixed_low[:, 256 * g : 256 * g + 256])
        for m in range(2):
            block = both[:, 128 * m : 128 * m + 128]
            half = m + k - 2 * m * k
            keep[half, 128 * g : 128 * g + 128, :] = jnp.where(first, block[0:128], block[128:256])
            send[half, 128 * g : 128 * g + 128, :] = jnp.where(first, block[128:256], block[0:128])


def add_kernel(s, kept, received, own_out, peer_out):
    own_out[...] = kept[0] + received[0]
    peer_out[...] = kept[1] + received[1]


def add_half_kernel(s, kept, received, w_in, own_out, peer_out):
    rows = own_out.shape[0]
    part = at(rows * s[BIT1], rows, 8)
    own_out[...] = kept[0, part, :] + received[0, part, :]
    peer_out[0:rows, :] = kept[1, part, :] + received[1, part, :]
    fill_in_part(s, w_in.at[0], peer_out.at[rows : rows + 384])


def take_half_kernel(s, own, received, out, in_out):
    rows = own.shape[0]
    out[...] = own[...] + received[0:rows, :]
    in_out[...] = received[rows:, :]


def add_one_kernel(s, kept, received, out):
    out[...] = kept[...] + received[...]


def spread_wide_kernel(level, s, *refs):
    if level:
        outs, (a, b, out, up, down), done = refs[-9:-6], refs[-6:-1], refs[-1]
        rows = refs[0].shape[0]
        for whole, near, far in ((a, refs[0], refs[1]), (b, refs[2], refs[3])):
            whole[at(rows * s[BIT1], rows, 8), :] = near[...]
            whole[at(rows * (1 - s[BIT1]), rows, 8), :] = far[...]
    else:
        outs, (out, up, down), done = refs[-7:-4], refs[-4:-1], refs[-1]
        a, b = refs[:2]
    first = s[CORE] == 0
    pick = lambda x, y: jnp.where(first, x, y)

    def both(row, rows):
        x, y = a[row : row + rows, :], b[row : row + rows, :]
        return pick(x, y), pick(y, x)

    x, y = both(0, 128)
    out[:, 0:128] = x
    out[:, 128:256] = y
    for j in range(2):
        lanes = slice(128 * j, 128 * j + 128)
        x, y = both(128 + 256 * j, 256)
        up[:, 128 * j : 128 * j + 128] = x
        up[:, 256 + 128 * j : 384 + 128 * j] = y
        x, y = both(640 + 256 * j, 256)
        down[0:256, lanes] = x
        down[256:512, lanes] = y
    bring(zip((out, up, down), (whole.at[level] for whole in outs)), done)


def spread_in_kernel(s, kept, received, whole, near, done):
    first = s[CORE] == 0
    for g in range(3):
        x, y = kept[128 * g : 128 * g + 128, :], received[128 * g : 128 * g + 128, :]
        near[g, 0:128, :] = jnp.where(first, x, y)
        near[g, 128:256, :] = jnp.where(first, y, x)
    bring(((near, whole.at[1]),), done)


def pair_kernel(bit, s, own, received, out):
    spot = s[(CORE, BIT1, BIT2, BIT3)[bit]]
    for j in range(own.shape[0]):
        out[2 * j + spot] = own[j]
        out[2 * j + 1 - spot] = received[j]


E_GAIN, E_EMBED, E_FIRST, E_SHORT, E_TOKEN, E_ROWS = 0, 8, 24, 40, 56, 104
EM_SECOND, EM_SKIP, EM_ROWS = 0, 64, 72
L_TOKEN, L_SECOND, L_SKIP, L_ROWS = 0, 96, 160, 168
FIRST_ROWS = 16


def fold_first(values):
    last = jnp.concatenate([values[32:40], jnp.zeros((8, 64), f32)], axis=0)
    return jnp.concatenate([values[0:16], values[16:32], last, jnp.zeros((16, 64), f32)], axis=1)


def unfold_first(values):
    return jnp.concatenate([values[:, 0:64], values[:, 64:128], values[0:8, 128:192]], axis=0)[0:FEAT]


def early_kernel(s, gain_mid1, gain_in1, gain_mid0, by_token0, first1, short1, second1, skip1, flat, mine):
    k = s[CORE]
    flat[...] = jnp.zeros_like(flat)
    for row, values in enumerate((gain_mid1, gain_in1, gain_mid0)):
        flat[E_GAIN + row : E_GAIN + row + 1, :] = values[0:1, :]
    flat[E_EMBED : E_EMBED + 16, :] = by_token0[0:16, 256:512] + by_token0[0:16, 512:768]
    flat[E_FIRST : E_FIRST + FIRST_ROWS, :] = fold_first(first1[...])
    swap = lambda v: jnp.where(k == 0, v, jnp.concatenate([v[:, 128:256], v[:, 0:128]], axis=1))
    for t in range(3):
        total = jnp.sum(short1[t], axis=0, keepdims=True)
        for g in range(3):
            flat[E_SHORT + 3 * t + g : E_SHORT + 3 * t + g + 1, :] = swap(total[:, 256 * g : 256 * g + 256])
    flat[E_TOKEN : E_TOKEN + 48, :] = swap(by_token0[:, 0:256])
    mine[EM_SECOND : EM_SECOND + 64, :] = second1[...]
    mine[EM_SKIP : EM_SKIP + 8, :] = jnp.broadcast_to(jnp.sum(skip1[...], axis=0, keepdims=True), (8, 128))


def late_kernel(s, by_token12, second0, skip0, first0, mine, first_out):
    mine[L_TOKEN : L_TOKEN + 48, :] = by_token12[:, 0:128]
    mine[L_TOKEN + 48 : L_TOKEN + 96, :] = by_token12[:, 128:256]
    mine[L_SECOND : L_SECOND + 64, :] = second0[...]
    mine[L_SKIP : L_SKIP + 8, :] = jnp.broadcast_to(jnp.sum(skip0[...], axis=0, keepdims=True), (8, 128))
    first_out[...] = fold_first(first0[...])


def chip_kernel(s, flat, flat_in, mine, mine_in, out):
    first = s[CORE] == 0
    rows = flat.shape[0]
    total = flat[...] + flat_in[...]
    out[0:rows, :] = total
    out[rows:, 0:128] = jnp.where(first, mine[...], mine_in[...])
    out[rows:, 128:256] = jnp.where(first, mine_in[...], mine[...])


def last_kernel(
    s, early, early_in, late, late_in, embed, gain, own, peer, w_own, w_first, w_second, in_given,
    embed_out, gain_out, in_whole, short_out, first_out, second_out, skip_out, in_out, done,
):
    pick = lambda x, y: jnp.where(s[CORE] == 0, x, y)

    def plain(pair, row, rows):
        return pair[0][row : row + rows, :] + pair[1][row : row + rows, :]

    def halves(pair, row, rows):
        here, there = pair
        left = here[row : row + rows, 0:128] + there[row : row + rows, 128:256]
        right = here[row : row + rows, 128:256] + there[row : row + rows, 0:128]
        return left, right

    early, late = (early, early_in), (late, late_in)
    gains = plain(early, E_GAIN, 8)
    gain_out[1, 0:1, :] = gains[1:2, :]
    gain_out[1, 1:2, :] = gains[0:1, :]
    gain_out[0, 1:2, :] = gains[2:3, :]
    first_out[:, 0, :] = unfold_first(plain(late, 0, FIRST_ROWS))
    first_out[:, 1, :] = unfold_first(plain(early, E_FIRST, FIRST_ROWS))
    short = halves(early, E_SHORT, 16)[0]
    for t in range(3):
        for g in range(3):
            short_out[t, g, 1:2, :] = short[3 * t + g : 3 * t + g + 1, :]
    second_out[1] = halves(early, E_ROWS + EM_SECOND, 64)[0]
    second_out[0] = halves(late, FIRST_ROWS + L_SECOND, 64)[0]
    skip_out[0:1, :] = halves(late, FIRST_ROWS + L_SKIP, 8)[0][0:1]
    skip_out[1:2, :] = halves(early, E_ROWS + EM_SKIP, 8)[0][0:1]
    tokens = [
        halves(early, E_TOKEN, 48),
        halves(late, FIRST_ROWS + L_TOKEN, 48),
        halves(late, FIRST_ROWS + L_TOKEN + 48, 48),
    ]
    normal, scale = unit(embed[...])
    gain_row = gain[0, 0:1, :]
    low = (normal * gain_row).astype(bf16)
    grad_normed = jnp.zeros((16, 256), f32)
    for g in range(3):
        for h, pack in ((0, own), (1, peer)):
            grads = tokens[g][h]
            table = pack[16 * g : 16 * g + 16, :]
            summed = jnp.zeros((16, 128), f32)
            for t in range(3):
                row = PACK_SHORT + 3 * t + g
                part = grads[16 * t : 16 * t + 16, :]
                summed += pack[row : row + 1, :] * part
                if h == 0:
                    short_out[t, g, 0:1, :] = jnp.sum(table * part, axis=0, keepdims=True)
            high, rest = split(summed)
            if h == 0:
                in_out[g] = mm_tn(low, high) + mm_tn(low, rest)
                weight = w_own[0, g]
            else:
                rows = slice(128 * g, 128 * g + 128)
                a, b = w_first[rows, :], w_second[rows, :]
                weight = jnp.concatenate([pick(a, b), pick(b, a)], axis=0).astype(bf16)
            grad_normed += mm_nt(high, weight) + mm_nt(rest, weight)
    copy = pltpu.make_async_copy(in_out, in_whole.at[0], done.at[0])
    copy.start()
    gain_out[0, 0:1, :] = jnp.sum(grad_normed * normal, axis=0, keepdims=True)
    embed_out[...] = plain(early, E_EMBED, 16) + unit_back(grad_normed * gain_row, normal, scale)
    copy.wait()


def block_send_kernel(s, block_out, mine, other):
    spot = s[SPOT]
    mine[...] = block_out[at(HALO + 128 * spot, 128), :]
    near = spot + 1 - 2 * s[CORE]
    other[...] = block_out[at(HALO + 128 * near, 128), :]


def block_pick_kernel(s, mine, received, out):
    out[...] = jnp.where(s[HOLDER] == 1, mine[...], received[...])


def block_join_kernel(s, here, there, out):
    first = s[GROUP] == 0
    out[0] = jnp.where(first, here[...], there[...])
    out[1] = jnp.where(first, there[...], here[...])


def chip_local(
    ids, live, embed, norm_gain, in_weight, short_kernel, filter_first, filter_second, skip_gain,
    out_weight, up_weight, down_weight, cotangent,
):
    CALLS.clear()
    count = lax.axis_size("seq")
    rank = lax.axis_index("seq")
    group = lax.axis_index("ch")
    width = ids.shape[1]
    length = width * count
    half = length // 2
    span = half + 2 * HALO
    core = rank % 2
    across = lambda v: lax.ppermute(v, "ch", [(0, 1), (1, 0)])
    trade = lambda v, bit: lax.ppermute(v, "seq", [(i, i ^ bit) for i in range(count)])
    beside = lambda v: trade(v, 1)
    dft = jnp.asarray(dft_table()).astype(bf16)
    feats = jnp.asarray(feature_parts(length)).astype(bf16)
    feats_turned = jnp.asarray(np.pad(feature_table(length).T, ((0, FEAT_ROWS - FEAT), (0, 0)))).astype(bf16)
    rates = jnp.asarray(rate_table())
    low = lambda *shape: arr(*shape, kind=bf16)
    line = pltpu.VMEM((length + 2 * HALO, 128), f32)
    conv_scratch = [stage_scratch(), spec_scratch(), line]
    pair = lambda bit, v, w, **kw: run(
        functools.partial(pair_kernel, bit), jax.ShapeDtypeStruct((2 * v.shape[0],) + v.shape[1:], v.dtype), s, v, w, **kw
    )

    row_shape = lambda rows: arr(rows, 8, width, kind=jnp.int32)
    in_own = jnp.swapaxes(in_weight, 1, 2)
    packed = (embed, norm_gain, in_own, filter_second, jnp.transpose(short_kernel, (1, 2, 0, 3)), skip_gain)
    wide = (out_weight, up_weight, down_weight)
    held = [(1, 2), ids.shape, embed.shape, norm_gain.shape, in_own.shape[1:], filter_second.shape, packed[4].shape, skip_gain.shape]
    held += [v.shape[1:] for v in wide] + [in_own.shape[1:]]
    kinds = [jnp.int32, jnp.int32, f32, f32, bf16, f32, f32, f32] + [bf16] * 4
    s, ids1, cot1, pack, part0 = start(
        numbers_kernel,
        [arr(NUMBER_ROWS, 128, kind=jnp.int32), row_shape(1), arr(1, width, 256), arr(PACK_ROWS, 128), arr(1536, 128)],
        live.reshape(1, 2), ids, cotangent, *packed, *wide, in_own,
        scratch=[pltpu.VMEM(shape, kind) for shape, kind in zip(held, kinds)] + [pltpu.SemaphoreType.DMA((13,))],
    )
    pack_in = across(pack)
    part0_in = across(part0)
    ids2 = pair(3, ids1, trade(ids1, 8))
    sine, cosine, sine_turned = run(
        sine_kernel, [low(length, 256), arr(length, 128), low(128, length)], s, feats, jnp.transpose(filter_first, (1, 0, 2)),
        after=(ids2,), scratch=[pltpu.VMEM((FEAT_ROWS, 128), f32)],
    )
    twiddle = run(twiddle_kernel, arr(KINDS - 1, 2, BLOCK, 128), s, jnp.asarray(twiddle_table()), after=(sine,))
    cot2 = pair(3, cot1, trade(cot1, 8), after=(twiddle,))
    ids4 = pair(2, ids2, trade(ids2, 4), after=(cot2,))
    part1 = run(
        send_weights_kernel, arr(1152, 128), s, *wide, hbm=range(3), after=(ids4,),
        scratch=[pltpu.VMEM(v.shape[1:], v.dtype) for v in wide] + [pltpu.SemaphoreType.DMA((3,))],
    )
    part1_in = across(part1)
    mine, other, conv_table, gate_table = run(
        table_kernel, [arr(PACK_ROWS, 128), arr(PACK_ROWS, 128), low(128, 256), low(128, 512)], s, pack, pack_in, embed,
        after=(part1,),
    )
    make_filter = lambda level, after: run(
        functools.partial(filter_kernel, level), [arr(length, 128), arr(*SPECTRUM)], s, sine, mine, rates, dft, twiddle,
        scratch=[stage_scratch()], after=after,
    )
    filt0, freq0 = make_filter(0, ())
    ids8 = pair(1, ids4, trade(ids4, 2), after=(filt0,))
    cot4 = pair(2, cot2, trade(cot2, 4), after=(ids8,))
    cot_keep, cot_send = run(cot_split_kernel, [arr(2, width, 256), arr(2, width, 256)], s, cot4)
    all_ids = pair(0, ids8, beside(ids8), after=(cot_send,))
    onehot, turned = run(
        onehot_kernel, [low(length + 2 * HALO, 128), low(2, 128, half)], s, all_ids,
        scratch=[pltpu.VMEM((length + 2 * HALO, 128), f32)],
    )
    conv_mine0, sent, spec0, product0 = run(
        conv_first_kernel, [arr(span, 128), arr(span, 128), arr(*SPECTRUM), arr(length, 128)],
        s, onehot, conv_table, mine, freq0, dft, twiddle, scratch=conv_scratch,
    )
    conv_other0 = beside(sent)
    first_part = run(relay_kernel, arr(1536, 128), s, part0_in, after=(sent,))
    first_beside = beside(first_part)
    filt1, freq1 = make_filter(1, (first_part,))
    cot_half = run(cot_half_kernel, arr(4 * width + HALO, 256), s, cot_keep, beside(cot_send), cot4, after=(freq1,))
    cot_half_in = trade(cot_half, 2)
    w_out0, w_up0, w_down0, w_in1 = run(
        functools.partial(join_weights_kernel, 0), [low(256, 256), low(256, 1024), low(1024, 256), low(256, 768)],
        s, out_weight, up_weight, down_weight, in_own, first_part, first_beside, after=(cot_half,),
    )
    kept, sent, mid0, stream1, gates1, mixed1 = run(
        forward_first_kernel,
        [arr(half, 128), arr(half, 128), arr(span, 256), arr(span, 256), arr(span, 768), arr(span, 768)],
        s, onehot, gate_table, conv_mine0, conv_other0, norm_gain, w_out0, w_up0, w_down0, w_in1, mine, other,
    )
    received = beside(sent)
    second_part = run(relay_kernel, arr(1152, 128), s, part1_in, after=(sent,))
    second_beside = beside(second_part)
    conv_mine1, sent, spec1, product1 = run(
        conv_second_kernel, [arr(span, 128), arr(span, 128), arr(*SPECTRUM), arr(length, 128)],
        s, kept, received, mine, freq1, dft, twiddle, scratch=conv_scratch, after=(second_part,),
    )
    conv_other1 = beside(sent)
    cot, cot_rim = run(cot_whole_kernel, [arr(half, 256), arr(HALO, 256)], s, cot_half, cot_half_in, after=(sent,))
    w_out1, w_up1, w_down1 = run(
        functools.partial(join_weights_kernel, 1), [low(256, 256), low(256, 1024), low(1024, 256)],
        s, out_weight, up_weight, down_weight, in_own, second_part, second_beside, after=(cot_rim,),
    )
    (kept, sent, grad_x0, grad_mid1, block, hidden, grad_low, normed, grad_pre, gated, mid_low, gain_mid1) = run(
        turn_back_kernel,
        [
            arr(half, 128), arr(half, 128), arr(span, 256), arr(span, 256), arr(span, 256), low(span, 1024), low(span, 256),
            low(span, 256), low(span, 1024), low(span, 256), low(span, 256), arr(8, 256),
        ],
        s, conv_mine1, conv_other1, gates1, stream1, cot, cot_rim, norm_gain, w_out1, w_up1, w_down1,
        scratch=[pltpu.VMEM((span, 256), f32), pltpu.VMEM((span, 256), f32)],
    )
    received = beside(sent)
    grads_keep1, grads_send1 = run(
        functools.partial(wide_grads_kernel, HALO), [arr(2, 1152, 128), arr(2, 1152, 128)],
        s, gated, mid_low, normed, grad_pre, hidden, grad_low,
    )
    block_mine, block_other = run(block_send_kernel, [arr(width, 256), arr(width, 256)], s, block)
    grads_in1 = beside(grads_send1)
    block_beside = beside(block_other)

    prod_mine, sent, spec_grad1, grads1 = run(
        conv_back_kernel, [arr(span, 128), arr(span, 128), arr(*SPECTRUM), arr(length, 128)],
        s, kept, received, mine, freq1, dft, twiddle, scratch=conv_scratch, after=(grads_send1, block_mine),
    )
    prod_other = beside(sent)
    own1, peer1 = run(add_half_kernel, [arr(576, 128), arr(960, 128)], s, grads_keep1, grads_in1, in_own, after=(sent,))
    across1 = across(peer1)
    filter_shapes = [arr(64, 128), arr(40, 64), arr(8, 128)]
    filter_scratch = [stage_scratch(), spec_scratch(), pltpu.VMEM((length, 128), f32)]
    second1, first1, skip1 = run(
        filter_back_kernel, filter_shapes, s, spec_grad1, spec1, grads1, product1, filt1, cosine,
        sine_turned, mine, rates, feats_turned, dft, twiddle, scratch=filter_scratch, after=(peer1,),
    )
    grad_stream1, normed_in, mixed_low, short1, gain_in1 = run(
        back_gates_kernel,
        [arr(half, 256), low(half, 256), low(half, 768), arr(3, 8, 768), arr(8, 256)],
        s, prod_mine, prod_other, grad_x0, gates1, mixed1, grad_mid1, stream1, norm_gain, mine, other, w_in1,
        scratch=[pltpu.VMEM((span, 512), f32)], after=(skip1,),
    )
    in_keep, in_send = run(in_grads_kernel, [arr(2, 384, 128), arr(2, 384, 128)], s, normed_in, mixed_low)
    in_beside = beside(in_send)
    block_here = run(block_pick_kernel, arr(width, 256), s, block_mine, block_beside, after=(in_send,))
    block_across = across(block_here)
    in_own1, in_peer1 = run(add_kernel, [arr(384, 128), arr(384, 128)], s, in_keep, in_beside, after=(block_here,))
    in_across = across(in_peer1)
    total1, in0_first = run(take_half_kernel, [arr(576, 128), arr(384, 128)], s, own1, across1, after=(block_here,))
    total1_y, in0_second = trade(total1, 2), beside(in0_first)
    (kept, sent, hidden, grad_low, normed, grad_pre, gated, mid_low, by_token0, gain_mid0) = run(
        back_first_kernel,
        [
            arr(half, 128), arr(half, 128), low(half, 1024), low(half, 256), low(half, 256), low(half, 1024), low(half, 256),
            low(half, 256), arr(48, 768), arr(8, 256),
        ],
        s, grad_stream1, mid0, onehot, turned, gate_table, conv_mine0, conv_other0, norm_gain, w_out0, w_up0, w_down0,
        after=(in_peer1,),
    )
    received = beside(sent)
    early_flat, early_mine = run(
        early_kernel, [arr(E_ROWS, 256), arr(EM_ROWS, 128)],
        s, gain_mid1, gain_in1, gain_mid0, by_token0, first1, short1, second1, skip1,
    )
    early_flat_in, early_mine_in = beside(early_flat), beside(early_mine)
    grads_keep0, grads_send0 = run(
        functools.partial(wide_grads_kernel, 0), [arr(2, 1152, 128), arr(2, 1152, 128)],
        s, gated, mid_low, normed, grad_pre, hidden, grad_low, after=(early_flat,),
    )
    grads_in0 = beside(grads_send0)
    early = run(
        chip_kernel, arr(E_ROWS + EM_ROWS, 256),
        s, early_flat, early_flat_in, early_mine, early_mine_in, after=(grads_send0,),
    )
    early_in = across(early)
    spec_grad0, grads0 = run(
        grad_freq_kernel, [arr(*SPECTRUM), arr(length, 128)], s, kept, received, dft, twiddle, scratch=[stage_scratch()],
        after=(early,),
    )
    own0, peer0 = run(add_kernel, [arr(1152, 128), arr(1152, 128)], s, grads_keep0, grads_in0, after=(spec_grad0,))
    across0 = across(peer0)
    second0, first0, skip0, by_token12 = run(
        token_back_kernel, filter_shapes + [arr(48, 256)], s, spec_grad0, spec0, grads0, product0, filt0, cosine,
        sine_turned, mine, rates, feats_turned, dft, twiddle, freq0, onehot, turned, conv_table, scratch=filter_scratch,
        after=(peer0, early, total1),
    )
    wide_shapes = [arr(2, 128, 256), arr(2, 256, 512), arr(2, 512, 256)]
    wide_scratch = [pltpu.VMEM(v.shape[1:], f32) for v in wide_shapes] + [pltpu.SemaphoreType.DMA((3,))]
    late_mine, late_first = run(
        late_kernel, [arr(L_ROWS, 128), arr(FIRST_ROWS, 256)], s, by_token12, second0, skip0, first0, flops=FEW_FLOPS
    )
    late_mine_in, late_first_in = beside(late_mine), beside(late_first)
    in_total = run(add_one_kernel, arr(384, 128), s, in_own1, in_across, after=(late_mine,), flops=FEW_FLOPS)
    block_out, joined = run(block_join_kernel, arr(2, width, 256), s, block_here, block_across, after=(late_mine,), flops=FEW_FLOPS, token=True)
    late = run(
        chip_kernel, arr(FIRST_ROWS + L_ROWS, 256), s, late_first, late_first_in, late_mine, late_mine_in, flops=FEW_FLOPS,
        after=(joined, in_total, early_in),
    )
    late_in = across(late)
    near1_y = run(relay_kernel, arr(576, 128), s, total1_y, after=(late,), flops=FEW_FLOPS)
    quarters1 = (total1, near1_y, beside(total1), beside(near1_y))
    in_total_beside = beside(in_total)
    *wide_buffers, wide_spread = run(
        functools.partial(spread_wide_kernel, 1), wide_shapes, s, *quarters1, hbm_outs=(0, 1, 2), flops=FEW_FLOPS,
        scratch=[pltpu.VMEM((1152, 128), f32)] * 2 + wide_scratch, after=(late,), token=True,
    )
    in_buffer, in_spread = run(
        spread_in_kernel, arr(2, 3, 256, 128), s, in_total, in_total_beside, hbm_outs=(0,), flops=FEW_FLOPS, token=True,
        scratch=[pltpu.VMEM((3, 256, 128), f32), pltpu.SemaphoreType.DMA((1,))],
    )
    total0 = run(add_one_kernel, arr(1152, 128), s, own0, across0, after=(late_in, wide_spread, in_spread))
    total0_beside = beside(total0)
    grad_embed, grad_gain, grad_in, grad_short, grad_first, grad_second, grad_skip = run(
        last_kernel,
        [
            arr(16, 256), arr(2, 2, 256), arr(2, 3, 256, 128), arr(3, 3, 2, 128), arr(FEAT, 2, 64), arr(2, 64, 128), arr(2, 128),
        ],
        s, early, early_in, late, late_in, embed, norm_gain, pack, pack_in, in_own, in0_first, in0_second, in_buffer,
        hbm=(11,), hbm_outs=(2,), aliases=((11, 2),), flops=FEW_FLOPS, after=(total0,),
        scratch=[pltpu.VMEM((3, 256, 128), f32), pltpu.SemaphoreType.DMA((1,))],
    )
    grad_out, grad_up, grad_down = run(
        functools.partial(spread_wide_kernel, 0), wide_shapes, s, total0, total0_beside, *wide_buffers,
        hbm=(2, 3, 4), hbm_outs=(0, 1, 2), aliases=((2, 0), (3, 1), (4, 2)), flops=FEW_FLOPS, scratch=wide_scratch,
    )
    return (
        block_out,
        grad_embed,
        grad_gain,
        jnp.swapaxes(grad_in, 1, 2),
        jnp.transpose(grad_short, (2, 0, 1, 3)),
        jnp.transpose(grad_first, (1, 0, 2)),
        grad_second,
        grad_skip,
        grad_out,
        grad_up,
        grad_down,
    )


def solution(mesh):
    in_specs = (
        P(None, "seq"),
        P(),
        P(),
        P(),
        P(None, None, None, "ch"),
        P(None, None, None, "ch"),
        P(),
        P(None, None, "ch"),
        P(None, "ch"),
        P(None, "ch", None),
        P(None, None, "ch"),
        P(None, "ch", None),
        P(None, "seq", None),
    )
    out_specs = (
        P(None, "seq", None),
        P(),
        P(),
        P(None, None, None, "ch"),
        P(None, None, None, "ch"),
        P(),
        P(None, None, "ch"),
        P(None, "ch"),
        P(None, "ch", None),
        P(None, None, "ch"),
        P(None, "ch", None),
    )

    def either(*args):
        length = args[0].shape[1] * lax.axis_size("seq")
        near = length == BLOCKS * BLOCK and lax.axis_size("seq") == 16
        return (chip_local if near else local)(*args)

    return jax.shard_map(either, mesh=mesh, in_specs=in_specs, out_specs=out_specs, check_vma=False)
```

```python
import collections
import functools
import math

import jax
import jax.numpy as jnp
import ml_dtypes
import numpy as np
from jax import lax
from jax.experimental import pallas as pl
from jax.experimental.pallas import tpu as pltpu
from jax.sharding import PartitionSpec as P

D = 256
FEAT = 33


precise = lax.Precision.HIGHEST
epsilon = 1e-05


def passed_along(value, axis, steps):
    count = lax.axis_size(axis)
    leading, last = (max(0, -steps), min(count, count - steps))
    return lax.ppermute(value, axis, [(source, source + steps) for source in range(leading, last)])


def layer_norm(inputs, gain_vec):
    center = inputs - jnp.mean(inputs, axis=-1, keepdims=True)
    spread = jnp.mean(center * center, axis=-1, keepdims=True)
    return center * lax.rsqrt(spread + epsilon) * gain_vec


def position_features(length):
    places = jnp.arange(length, dtype=jnp.int32)
    band_ids = jnp.arange(1, (FEAT - 1) // 2 + 1, dtype=jnp.int32)
    turn_counts = places[:, None] * band_ids[None, :] % length
    angles = turn_counts.astype(jnp.float32) * (2.0 * math.pi / length)
    ramp_vals = places.astype(jnp.float32)[:, None] / length
    return jnp.concatenate([ramp_vals, jnp.cos(angles), jnp.sin(angles)], axis=1)


def decay_rates(channels):
    return 0.3 * 10.0 ** (channels.astype(jnp.float32) / (D - 1))


def dft_tables(blocks, block_len):
    doubled = 2 * blocks
    span_total = doubled * block_len
    frequency = jnp.arange(doubled, dtype=jnp.int32)
    places = jnp.arange(blocks, dtype=jnp.int32)
    inner_idx = jnp.arange(block_len, dtype=jnp.int32)
    outer_angle = (frequency[:, None] * places[None, :] % doubled).astype(jnp.float32) * (
        2.0 * math.pi / doubled
    )
    twist_angle = (frequency[:, None] * inner_idx[None, :] % span_total).astype(jnp.float32) * (
        2.0 * math.pi / span_total
    )
    inner_angle = (inner_idx[:, None] * inner_idx[None, :] % block_len).astype(jnp.float32) * (
        2.0 * math.pi / block_len
    )
    return (
        jnp.cos(outer_angle),
        jnp.sin(outer_angle),
        jnp.cos(twist_angle),
        jnp.sin(twist_angle),
        jnp.cos(inner_angle),
        jnp.sin(inner_angle),
    )


def along_block(values, table):
    return jnp.einsum("...kb,bj->...kj", values, table, precision=precise)


def to_spectrum(signal, tables):
    outer_cos, outer_sin, twist_cos, twist_sin, inner_cos, inner_sin = tables
    first_re = jnp.einsum("kp,...pb->...kb", outer_cos, signal, precision=precise)
    first_im = -jnp.einsum("kp,...pb->...kb", outer_sin, signal, precision=precise)
    turned_re = first_re * twist_cos + first_im * twist_sin
    turned_im = first_im * twist_cos - first_re * twist_sin
    spec_re = along_block(turned_re, inner_cos) + along_block(turned_im, inner_sin)
    spec_im = along_block(turned_im, inner_cos) - along_block(turned_re, inner_sin)
    return (spec_re, spec_im)


def from_spectrum(spec_re, spec_im, tables):
    outer_cos, outer_sin, twist_cos, twist_sin, inner_cos, inner_sin = tables
    back_re = along_block(spec_re, inner_cos) - along_block(spec_im, inner_sin)
    back_im = along_block(spec_re, inner_sin) + along_block(spec_im, inner_cos)
    turned_re = back_re * twist_cos - back_im * twist_sin
    turned_im = back_re * twist_sin + back_im * twist_cos
    scale_back = 1.0 / (outer_cos.shape[0] * inner_cos.shape[0])
    signal = jnp.einsum("kp,...kb->...pb", outer_cos, turned_re, precision=precise) - jnp.einsum(
        "kp,...kb->...pb", outer_sin, turned_im, precision=precise
    )
    return signal * scale_back


def causal_filter(received, filt_spec, skip_part, tables):
    item_count, chan_count, length = received.shape
    blocks = tables[0].shape[1]
    spec_re, spec_im = to_spectrum(
        received.reshape(item_count, chan_count, blocks, length // blocks), tables
    )
    prod_re = spec_re * filt_spec[0] - spec_im * filt_spec[1]
    prod_im = spec_re * filt_spec[1] + spec_im * filt_spec[0]
    result_sig = from_spectrum(prod_re, prod_im, tables).reshape(item_count, chan_count, length)
    return result_sig + skip_part[:, None] * received


def filter_backward(grad_cols, moved_in, filt_spec, skip_part, tables):
    item_count, chan_count, length = grad_cols.shape
    blocks = tables[0].shape[1]
    grad_re, grad_im = to_spectrum(
        grad_cols.reshape(item_count, chan_count, blocks, length // blocks), tables
    )
    input_re, input_im = to_spectrum(
        moved_in.reshape(item_count, chan_count, blocks, length // blocks), tables
    )
    back_re = grad_re * filt_spec[0] + grad_im * filt_spec[1]
    back_im = grad_im * filt_spec[0] - grad_re * filt_spec[1]
    grad_u_cols = (
        from_spectrum(back_re, back_im, tables).reshape(item_count, chan_count, length)
        + skip_part[:, None] * grad_cols
    )
    corr_re = grad_re * input_re + grad_im * input_im
    corr_im = grad_im * input_re - grad_re * input_im
    grad_filt = jnp.sum(from_spectrum(corr_re, corr_im, tables), axis=0).reshape(chan_count, length)
    grad_skip_part = jnp.sum(grad_cols * moved_in, axis=(0, 2))
    return (grad_u_cols, grad_filt, grad_skip_part)


def local_filter(first, second, features, select, group_idx, chan_local):
    hidden_pre = jnp.dot(features, first, precision=precise)
    hidden_act = jnp.sin(hidden_pre)
    chan_width = second.shape[1]
    second_part = jnp.dot(second, select, precision=precise)
    channel_ids = group_idx * chan_width + chan_local
    length = features.shape[0]
    ramp_vals = jnp.arange(length, dtype=jnp.int32).astype(jnp.float32) / length
    decay_part = jnp.exp(-decay_rates(channel_ids)[:, None] * ramp_vals[None, :])
    filt_cols = jnp.einsum("hc,th->ct", second_part, hidden_act, precision=precise) * decay_part
    return (filt_cols, hidden_pre, hidden_act, second_part, decay_part)


def filter_mlp_backward(grad_filt, features, filter_parts):
    hidden_pre, hidden_act, second_part, decay_part = filter_parts
    grad_shaped = grad_filt * decay_part
    grad_second_part = jnp.einsum("ct,th->hc", grad_shaped, hidden_act, precision=precise)
    grad_act = jnp.einsum("ct,hc->th", grad_shaped, second_part, precision=precise)
    grad_first = jnp.einsum(
        "tf,th->fh", features, grad_act * jnp.cos(hidden_pre), precision=precise
    )
    return (grad_first, grad_second_part)


def embed_lookup(ids, live, embed, seq_rank):
    tok_rows = ids.shape[1]
    places = seq_rank * tok_rows + jnp.arange(tok_rows, dtype=jnp.int32)
    keep_mask = (places[None, :] < live[:, None]).astype(jnp.float32)
    vocab_ids = jnp.arange(embed.shape[0], dtype=jnp.int32)
    onehot = (ids[:, :, None] == vocab_ids[None, None, :]).astype(jnp.float32) * keep_mask[
        :, :, None
    ]
    stream = jnp.einsum("mtv,vd->mtd", onehot, embed, precision=precise)
    return (stream, onehot, keep_mask)


def channel_total(partial_sum):
    return lax.psum(partial_sum, "ch")


def input_total(partial_sum):
    return lax.psum(partial_sum, "ch")


def layer_forward(stream, params, filt_spec, skip_part, tables):
    norm_gains, w_in, kernel, w_out, w_up, w_down = params
    normed = layer_norm(stream, norm_gains[0]).astype(jnp.bfloat16)
    mixed_in = jnp.einsum("mtd,dgc->mtgc", normed, w_in, preferred_element_type=jnp.float32)
    rim_rows = passed_along(mixed_in[:, -2:], "seq", 1)
    padded = jnp.concatenate([rim_rows, mixed_in], axis=1)
    micro_count, tok_rows = (mixed_in.shape[0], mixed_in.shape[1])
    chan_width = mixed_in.shape[3]
    gate_vals = (
        kernel[0] * mixed_in
        + kernel[1] * padded[:, 1 : tok_rows + 1]
        + kernel[2] * padded[:, 0:tok_rows]
    )
    product_in = gate_vals[:, :, 2] * gate_vals[:, :, 1]
    flat_rows = jnp.swapaxes(product_in, 1, 2).reshape(1, micro_count * chan_width, tok_rows)
    received = lax.all_to_all(flat_rows, "seq", split_axis=1, concat_axis=2, tiled=True)
    result_sig = causal_filter(received, filt_spec, skip_part, tables)
    conv_flat = lax.all_to_all(result_sig, "seq", split_axis=2, concat_axis=1, tiled=True)
    conv_out = jnp.swapaxes(conv_flat.reshape(micro_count, chan_width, tok_rows), 1, 2)
    gated_out = (conv_out * gate_vals[:, :, 0]).astype(jnp.bfloat16)
    mid_state = stream + channel_total(
        jnp.einsum("mtc,cd->mtd", gated_out, w_out, preferred_element_type=jnp.float32)
    )
    normed_mid = layer_norm(mid_state, norm_gains[1]).astype(jnp.bfloat16)
    pre_act = jnp.einsum("mtd,df->mtf", normed_mid, w_up, preferred_element_type=jnp.float32)
    hidden = jax.nn.gelu(pre_act).astype(jnp.bfloat16)
    new_stream = mid_state + channel_total(
        jnp.einsum("mtf,fd->mtd", hidden, w_down, preferred_element_type=jnp.float32)
    )
    kept_vals = (
        stream,
        normed,
        mixed_in,
        padded,
        gate_vals,
        received,
        conv_out,
        gated_out,
        mid_state,
        normed_mid,
        pre_act,
        hidden,
    )
    return (new_stream, kept_vals)


def layer_backward(grad_stream, kept_vals, params, filt_spec, skip_part, tables):
    norm_gains, w_in, kernel, w_out, w_up, w_down = params
    (
        stream,
        normed,
        mixed_in,
        padded,
        gate_vals,
        moved_in,
        conv_out,
        gated_out,
        mid_state,
        normed_mid,
        pre_act,
        hidden,
    ) = kept_vals
    micro_count, tok_rows = (mixed_in.shape[0], mixed_in.shape[1])
    chan_width = mixed_in.shape[3]
    grad_low = grad_stream.astype(jnp.bfloat16)
    grad_down = jnp.einsum("mtf,mtd->fd", hidden, grad_low, preferred_element_type=jnp.float32)
    grad_hidden = jnp.einsum("mtd,fd->mtf", grad_low, w_down, preferred_element_type=jnp.float32)
    _, gelu_back = jax.vjp(jax.nn.gelu, pre_act)
    grad_pre = gelu_back(grad_hidden)[0].astype(jnp.bfloat16)
    grad_up = jnp.einsum("mtd,mtf->df", normed_mid, grad_pre, preferred_element_type=jnp.float32)
    grad_normed_mid = input_total(
        jnp.einsum("mtf,df->mtd", grad_pre, w_up, preferred_element_type=jnp.float32)
    )
    _, norm_back_mid = jax.vjp(layer_norm, mid_state, norm_gains[1])
    grad_mid_norm, grad_gain_mid = norm_back_mid(grad_normed_mid)
    grad_mid = grad_stream + grad_mid_norm
    grad_mid_low = grad_mid.astype(jnp.bfloat16)
    grad_out = jnp.einsum(
        "mtc,mtd->cd", gated_out, grad_mid_low, preferred_element_type=jnp.float32
    )
    grad_gated = jnp.einsum("mtd,cd->mtc", grad_mid_low, w_out, preferred_element_type=jnp.float32)
    grad_conv = grad_gated * gate_vals[:, :, 0]
    grad_first_gate = grad_gated * conv_out
    grad_flat = jnp.swapaxes(grad_conv, 1, 2).reshape(1, micro_count * chan_width, tok_rows)
    grad_cols = lax.all_to_all(grad_flat, "seq", split_axis=1, concat_axis=2, tiled=True)
    grad_u_cols, grad_filt, grad_skip_part = filter_backward(
        grad_cols, moved_in, filt_spec, skip_part, tables
    )
    grad_back_flat = lax.all_to_all(grad_u_cols, "seq", split_axis=2, concat_axis=1, tiled=True)
    grad_product = jnp.swapaxes(grad_back_flat.reshape(micro_count, chan_width, tok_rows), 1, 2)
    grad_gates = jnp.stack(
        [grad_first_gate, grad_product * gate_vals[:, :, 2], grad_product * gate_vals[:, :, 1]],
        axis=2,
    )
    rim_back = passed_along(grad_gates[:, :2], "seq", -1)
    extended = jnp.concatenate([grad_gates, rim_back], axis=1)
    grad_mixed = (
        kernel[0] * grad_gates
        + kernel[1] * extended[:, 1 : tok_rows + 1]
        + kernel[2] * extended[:, 2 : tok_rows + 2]
    )
    grad_kernel = jnp.stack(
        [
            jnp.sum(grad_gates * mixed_in, axis=(0, 1)),
            jnp.sum(grad_gates * padded[:, 1 : tok_rows + 1], axis=(0, 1)),
            jnp.sum(grad_gates * padded[:, 0:tok_rows], axis=(0, 1)),
        ]
    )
    grad_mixed_low = grad_mixed.astype(jnp.bfloat16)
    grad_in = jnp.einsum(
        "mtd,mtgc->dgc", normed, grad_mixed_low, preferred_element_type=jnp.float32
    )
    grad_normed = input_total(
        jnp.einsum("mtgc,dgc->mtd", grad_mixed_low, w_in, preferred_element_type=jnp.float32)
    )
    _, norm_back_in = jax.vjp(layer_norm, stream, norm_gains[0])
    grad_stream_norm, grad_gain_in = norm_back_in(grad_normed)
    grad_before = grad_mid + grad_stream_norm
    layer_grads = (
        jnp.stack([grad_gain_in, grad_gain_mid]),
        grad_in,
        grad_kernel,
        grad_skip_part,
        grad_out,
        grad_up,
        grad_down,
    )
    return (grad_before, layer_grads, grad_filt)


def local(
    ids,
    live,
    embed,
    norm_gain,
    in_weight,
    short_kernel,
    filter_first,
    filter_second,
    skip_gain,
    out_weight,
    up_weight,
    down_weight,
    cotangent,
):
    seq_count = lax.axis_size("seq")
    seq_rank = lax.axis_index("seq")
    group_idx = lax.axis_index("ch")
    micro_count = ids.shape[0]
    tok_rows = ids.shape[1]
    length = tok_rows * seq_count
    chan_width = in_weight.shape[3]
    own_rows = micro_count * chan_width // seq_count
    layer_count = in_weight.shape[0]
    row_start = seq_rank * own_rows
    row_ids = row_start + jnp.arange(own_rows, dtype=jnp.int32)
    chan_local = row_ids % chan_width
    first_rows = (row_ids < chan_width).astype(jnp.float32)
    select = (jnp.arange(chan_width, dtype=jnp.int32)[:, None] == chan_local[None, :]).astype(
        jnp.float32
    )
    tables = dft_tables(seq_count, tok_rows)
    features = position_features(length)
    ramp_row = jnp.arange(length, dtype=jnp.int32).astype(jnp.float32) / length
    stream, onehot, keep_mask = embed_lookup(ids, live, embed, seq_rank)
    filters = []
    for level_idx in range(layer_count):
        filt_cols, hidden_pre, hidden_act, second_part, decay_part = local_filter(
            filter_first[level_idx],
            filter_second[level_idx],
            features,
            select,
            group_idx,
            chan_local,
        )
        filt_spec = to_spectrum(filt_cols.reshape(own_rows, seq_count, tok_rows), tables)
        skip_part = jnp.dot(skip_gain[level_idx], select, precision=precise)
        penalty_grad = 0.5 * length * ramp_row[None, :] * filt_cols * first_rows[:, None]
        params = (
            norm_gain[level_idx],
            in_weight[level_idx],
            short_kernel[level_idx],
            out_weight[level_idx],
            up_weight[level_idx],
            down_weight[level_idx],
        )
        filters.append(
            (
                params,
                filt_spec,
                skip_part,
                (hidden_pre, hidden_act, second_part, decay_part),
                penalty_grad,
            )
        )
    stored = []
    for level_idx in range(layer_count):
        params, filt_spec, skip_part, _, _ = filters[level_idx]
        layer_input = stream
        stream, kept_vals = layer_forward(stream, params, filt_spec, skip_part, tables)
        stored.append(layer_input)
    block_out = stream * keep_mask[:, :, None]
    grad_stream = cotangent * keep_mask[:, :, None]
    collected = [None] * layer_count
    first_grads = [None] * layer_count
    grad_embed = None
    for level_idx in reversed(range(layer_count)):
        params, filt_spec, skip_part, filter_parts, penalty_grad = filters[level_idx]
        _, kept_vals = layer_forward(stored[level_idx], params, filt_spec, skip_part, tables)
        grad_stream, layer_grads, grad_filt = layer_backward(
            grad_stream, kept_vals, params, filt_spec, skip_part, tables
        )
        grad_first, grad_second_part = filter_mlp_backward(
            grad_filt + penalty_grad, features, filter_parts
        )
        first_grads[level_idx] = grad_first
        grad_second = jnp.dot(grad_second_part, select.T, precision=precise)
        grad_skip = jnp.dot(layer_grads[3], select.T, precision=precise)
        gain_grad, in_grad, kernel_grad, _, out_grad, up_grad, down_grad = layer_grads
        if level_idx == 0:
            embed_part = jnp.einsum("mtv,mtd->vd", onehot, grad_stream, precision=precise)
            summed = lax.psum(
                (
                    gain_grad,
                    in_grad,
                    kernel_grad,
                    grad_second,
                    grad_skip,
                    out_grad,
                    up_grad,
                    down_grad,
                    embed_part,
                ),
                "seq",
            )
            collected[level_idx] = summed[:8]
            grad_embed = summed[8]
        else:
            collected[level_idx] = lax.psum(
                (
                    gain_grad,
                    in_grad,
                    kernel_grad,
                    grad_second,
                    grad_skip,
                    out_grad,
                    up_grad,
                    down_grad,
                ),
                "seq",
            )
    stacked = [
        jnp.stack([collected[level_idx][member] for level_idx in range(layer_count)])
        for member in range(8)
    ]
    filter_grads = lax.psum(jnp.stack(first_grads), ("seq", "ch"))
    return (
        block_out,
        grad_embed,
        stacked[0],
        stacked[1],
        stacked[2],
        filter_grads,
        stacked[3],
        stacked[4],
        stacked[5],
        stacked[6],
        stacked[7],
    )


HALO = 16
FEAT_ROWS = 40
ROOT_HALF = math.sqrt(0.5)
GELU_A = math.sqrt(2.0 / math.pi)
GELU_B = 0.044715
BLOCKS = 8
BLOCK = 256
KINDS = 9
VMEM_LIMIT = 8 * 2**20
VMEM_LIMITS = dict(turn_back_kernel=20 * 2**20, back_first_kernel=16 * 2**20)
FLOPS, FEW_FLOPS, MANY_FLOPS = 10**10, 10**8, 10**12
FLOPS_OF = dict(conv_first1=100000000, pair5=10000000000, grad_freq1=30000000000, last1=1000000000, conv_second1=3000000000, join_weights2=100000000)
CALLS = collections.Counter()
f32 = jnp.float32
bf16 = jnp.bfloat16


class Numbers:
    def __init__(self, table):
        self.table = table

    def __getitem__(self, row):
        return self.table[row, 0]


CORE, GROUP, LIVE, WHICH, SPOT, HOLDER, BIT1, BIT2, BIT3 = range(9)
NUMBER_ROWS = 16


def bring(pairs, done):
    copies = [pltpu.make_async_copy(far, near, done.at[i]) for i, (far, near) in enumerate(pairs)]
    for copy in copies:
        copy.start()
    for copy in copies:
        copy.wait()


def numbers_kernel(*refs):
    far, (table, own_ids, cot, pack, part), near, done = refs[:13], refs[13:18], refs[18:30], refs[30]
    far_live, far_ids, far_cot, far_embed, far_gain, far_in, far_second, far_short, far_skip, far_out, far_up, far_down, far_in1 = far
    live, ids, embed, gain, in_own, second, short, skip, raw_out, raw_up, raw_down, in1 = near
    rank, group = lax.axis_index("seq"), lax.axis_index("ch")
    bring(
        (
            (far_live, live), (far_ids, ids), (far_cot.at[group], cot.at[0]), (far_embed, embed), (far_gain, gain),
            (far_in.at[0], in_own), (far_second, second), (far_short, short), (far_skip, skip), (far_out.at[0], raw_out),
            (far_up.at[0], raw_up), (far_down.at[0], raw_down), (far_in1.at[1], in1),
        ),
        done,
    )
    fill_pack(embed, gain, in_own, second, short, skip, pack)
    core, half = rank % 2, lax.axis_size("seq") // 2
    first = group == 0
    holder = jnp.where(rank // half == core, 1, 0)
    values = (core, group, None, group + core - 2 * group * core, rank % half, holder, rank // 2 % 2, rank // 4 % 2, rank // 8 % 2)
    for row, value in enumerate(values):
        if row != LIVE:
            table[row : row + 1, :] = jnp.full((1, 128), value, jnp.int32)
    chosen = jnp.where(first, live[0:1, 0:1], live[0:1, 1:2])
    table[LIVE : LIVE + 1, :] = jnp.broadcast_to(chosen, (1, 128))
    own_ids[0] = jnp.broadcast_to(jnp.where(first, ids[0:1, :], ids[1:2, :]), own_ids.shape[1:])
    s = Numbers(table)
    fill_part(s, raw_out, raw_up, raw_down, part)
    fill_in_part(s, in1, part.at[1152:1536])


def in_hbm(value):
    return pltpu.with_memory_space_constraint(value, pltpu.HBM)


def start(body, outs, *arrays, scratch):
    vmem, far = pl.BlockSpec(memory_space=pltpu.VMEM), pl.BlockSpec(memory_space=pltpu.HBM)
    return pl.pallas_call(
        body, out_shape=outs, in_specs=[far] * len(arrays), out_specs=[vmem] * len(outs), name=body.__name__,
        scratch_shapes=list(scratch),
        cost_estimate=pl.CostEstimate(flops=MANY_FLOPS, bytes_accessed=1, transcendentals=0),
        compiler_params=pltpu.CompilerParams(vmem_limit_bytes=VMEM_LIMIT),
    )(*(in_hbm(v) for v in arrays))


def run(body, outs, scalars, *arrays, scratch=(), after=(), hbm=(), flops=None, hbm_outs=(), aliases=(), token=False):
    vmem = pl.BlockSpec(memory_space=pltpu.VMEM)
    far, wait = pl.BlockSpec(memory_space=pltpu.HBM), pl.BlockSpec(memory_space=pl.ANY)
    single = not isinstance(outs, (list, tuple))
    shapes = [outs] if single else list(outs)
    count = len(shapes)
    shapes += [arr(8, 128)] * token
    used, waits = 1 + len(arrays), len(after)

    def call(table, *refs):
        given, rest = refs[: used - 1], refs[used - 1 + waits :]
        body(Numbers(table), *given, *rest[:count], *rest[count + token :])
        if token:
            rest[count][...] = jnp.zeros((8, 128), f32)

    inner = getattr(body, "func", body)
    CALLS[inner.__name__] += 1
    flops = flops or FLOPS_OF.get(f"{inner.__name__[:-7]}{CALLS[inner.__name__]}", FLOPS)
    result = pl.pallas_call(
        call,
        out_shape=shapes,
        in_specs=[vmem] + [far if i in hbm else vmem for i in range(len(arrays))] + [wait] * waits,
        out_specs=[far if i in hbm_outs else vmem for i in range(len(shapes))],
        input_output_aliases={1 + a: b for a, b in aliases},
        scratch_shapes=list(scratch),
        compiler_params=pltpu.CompilerParams(vmem_limit_bytes=VMEM_LIMITS.get(inner.__name__, VMEM_LIMIT)),
        cost_estimate=pl.CostEstimate(flops=flops, bytes_accessed=1, transcendentals=0),
        name=inner.__name__,
    )(scalars, *(in_hbm(v) if i in hbm else v for i, v in enumerate(arrays)), *after)
    return result[0] if len(shapes) == 1 else result


def arr(*shape, kind=f32):
    return jax.ShapeDtypeStruct(shape, kind)


def mm(a, b):
    return jnp.dot(a, b, preferred_element_type=f32)


def mm_nt(a, b):
    return lax.dot_general(a, b, (((1,), (1,)), ((), ())), preferred_element_type=f32)


def mm_tn(a, b):
    return lax.dot_general(a, b, (((0,), (0,)), ((), ())), preferred_element_type=f32)


def split(a):
    high = a.astype(bf16)
    return high, (a - high.astype(f32)).astype(bf16)


def unit(rows):
    center = rows - jnp.mean(rows, axis=-1, keepdims=True)
    scale = lax.rsqrt(jnp.mean(center * center, axis=-1, keepdims=True) + epsilon)
    return center * scale, scale


def unit_back(grad, normal, scale):
    inner = jnp.mean(grad * normal, axis=-1, keepdims=True)
    return scale * (grad - jnp.mean(grad, axis=-1, keepdims=True) - normal * inner)


def every(count, step):
    for i in range(count):
        step(i, 0)


def looped(count, step):
    def one(i, carry):
        step(i, 0)
        return carry

    lax.fori_loop(0, count, one, 0)


def at(start, size, unit_rows=16):
    return pl.ds(start if isinstance(start, int) else pl.multiple_of(start, unit_rows), size)


def dft_table():
    turns = np.outer(np.arange(BLOCK), np.arange(BLOCK)) % BLOCK
    angle = 2.0 * np.pi * turns / BLOCK
    return np.concatenate([np.cos(angle), np.sin(angle)], axis=1).astype(np.float32)


def twiddle_table():
    angle = 2.0 * np.pi * np.outer(np.arange(BLOCK), np.arange(1, KINDS)) / (2 * BLOCKS * BLOCK)
    return np.concatenate([np.cos(angle), np.sin(angle)], axis=1).astype(np.float32)


def twiddle_kernel(s, narrow, out):
    lane = lax.broadcasted_iota(jnp.int32, narrow.shape, 1)

    def one(kind, carry):
        for part in range(2):
            column = jnp.where(lane == (KINDS - 1) * part + kind, narrow[...], 0.0)
            out[kind, part] = jnp.broadcast_to(jnp.sum(column, axis=1, keepdims=True), (BLOCK, 128))
        return carry

    lax.fori_loop(0, KINDS - 1, one, 0)


def feature_table(length):
    places = np.arange(length)
    turns = np.outer(places, np.arange(1, (FEAT - 1) // 2 + 1)) % length
    angle = 2.0 * np.pi * turns / length
    ramp = places[:, None] / length
    return np.concatenate([ramp, np.cos(angle), np.sin(angle)], axis=1).astype(np.float32)


def thirds(values):
    low = lambda v: v.astype(ml_dtypes.bfloat16).astype(np.float32)
    first = low(values)
    second = low(values - first)
    return first, second, low(values - first - second)


def feature_parts(length):
    first, second, third = thirds(np.pad(feature_table(length), ((0, 0), (0, FEAT_ROWS - FEAT))))
    return np.pad(np.concatenate([first, first, second, second, first, third], axis=1), ((0, 0), (0, 256 - 6 * FEAT_ROWS)))


def rate_table():
    return (0.3 * 10.0 ** (np.arange(D) / (D - 1))).astype(np.float32).reshape(2, 1, D // 2)


def four_real(a, b, c, d):
    s, m, t, n = a + c, a - c, b + d, b - d
    hn, ht = ROOT_HALF * n, ROOT_HALF * t
    return (s + t, s - t, (a + hn, -(ht + c)), (m, -n), (a - hn, c - ht))


def turn(k):
    angle = 2.0 * math.pi * k / (2 * BLOCKS)
    return math.cos(angle), math.sin(angle)


def put_pair(stage, kind, row, re, im):
    rows = re.shape[0]
    re, im = re.astype(bf16), im.astype(bf16)
    stage[kind, pl.ds(row, rows), 0:128] = re
    stage[kind, pl.ds(row, rows), 128:256] = im
    stage[kind, pl.ds(row + BLOCK, rows), 0:128] = im
    stage[kind, pl.ds(row + BLOCK, rows), 128:256] = -re


def put_pair_back(stage, kind, row, re, im):
    rows = re.shape[0]
    re, im = re.astype(bf16), im.astype(bf16)
    stage[kind, pl.ds(row, rows), 0:128] = re
    stage[kind, pl.ds(row, rows), 128:256] = im
    stage[kind, pl.ds(row + BLOCK, rows), 0:128] = -im
    stage[kind, pl.ds(row + BLOCK, rows), 128:256] = re


def all_kinds(dft, stage, out):
    table = dft[...]
    for kind in range(KINDS):
        out[kind] = mm(table, stage[kind])


def to_freq(load, dft, twiddle, stage, out):
    def chunk(step, carry):
        row = step * 16
        u = [load(p, row) for p in range(BLOCKS)]
        e0, e4, e1, e2, e3 = four_real(u[0], u[2], u[4], u[6])
        o0, o4, o1, o2, o3 = four_real(u[1], u[3], u[5], u[7])

        def put(kind, re, im):
            c, s = twiddle[kind - 1, 0, pl.ds(row, 16), :], twiddle[kind - 1, 1, pl.ds(row, 16), :]
            put_pair(stage, kind, row, re * c + im * s, im * c - re * s)

        put_pair(stage, 0, row, e0 + o0, jnp.zeros_like(e0))
        last = e0 - o0
        c, s = twiddle[7, 0, pl.ds(row, 16), :], twiddle[7, 1, pl.ds(row, 16), :]
        put_pair(stage, 8, row, last * c, -(last * s))
        put(4, e4, -o4)
        for k, (er, ei), (orr, oi) in ((1, e1, o1), (2, e2, o2), (3, e3, o3)):
            c, s = turn(k)
            wr, wi = orr * c + oi * s, oi * c - orr * s
            put(k, er + wr, ei + wi)
            put(8 - k, er - wr, wi - ei)
        return carry

    every(BLOCK // 16, chunk)
    all_kinds(dft, stage, out)


def from_freq(dft, twiddle, stage, back, store):
    all_kinds(dft, stage, back)

    def chunk(step, carry):
        row = step * 16

        def get(kind):
            re = back[kind, pl.ds(row, 16), 0:128]
            im = back[kind, pl.ds(row, 16), 128:256]
            c, s = twiddle[kind - 1, 0, pl.ds(row, 16), :], twiddle[kind - 1, 1, pl.ds(row, 16), :]
            return re * c - im * s, re * s + im * c

        first = 0.5 * back[0, pl.ds(row, 16), 0:128]
        last = 0.5 * get(8)[0]
        mid_re, mid_im = get(4)
        even, odd = {}, {}
        for k in (1, 2, 3):
            ar, ai = get(k)
            br, bi = get(8 - k)
            even[k] = (ar + br, ai - bi)
            c, s = turn(k)
            dr, di = ar - br, ai + bi
            odd[k] = (dr * c - di * s, dr * s + di * c)
        for shift, base, extra, part in (
            (0, first + last, mid_re, even),
            (1, first - last, -mid_im, odd),
        ):
            (r1, i1), (r2, i2), (r3, i3) = part[1], part[2], part[3]
            plus, minus = base + extra, base - extra
            diff, both = ROOT_HALF * (r1 - r3), ROOT_HALF * (i1 + i3)
            store(shift, row, plus + (r1 + r2 + r3))
            store(shift + 2, row, minus - i2 + (diff - both))
            store(shift + 4, row, plus - r2 - (i1 - i3))
            store(shift + 6, row, minus + i2 - (diff + both))
        return carry

    every(BLOCK // 16, chunk)


def times(first, second, stage, conj):
    def chunk(step, carry):
        row = step * 16
        for kind in range(KINDS):
            fr = first[kind, pl.ds(row, 16), 0:128]
            fi = first[kind, pl.ds(row, 16), 128:256]
            ur = second[kind, pl.ds(row, 16), 0:128]
            ui = second[kind, pl.ds(row, 16), 128:256]
            if conj:
                put_pair_back(stage, kind, row, fr * ur + fi * ui, fr * ui - fi * ur)
            else:
                put_pair_back(stage, kind, row, fr * ur - fi * ui, fr * ui + fi * ur)
        return carry

    every(BLOCK // 16, chunk)


SPECTRUM = (KINDS, BLOCK, 256)


def stage_scratch():
    return pltpu.VMEM((KINDS, 2 * BLOCK, 256), bf16)


def spec_scratch():
    return pltpu.VMEM(SPECTRUM, f32)


PACK_SECOND = 48
PACK_SHORT = 176
PACK_SKIP = 194
PACK_ROWS = 200


def fill_pack(embed, gain, in_own, second, short, skip, out):
    normal, _ = unit(embed[...])
    low = (normal * gain[0, 0:1, :]).astype(bf16)
    for g in range(3):
        out[16 * g : 16 * g + 16, :] = mm(low, in_own[g])
    for l in range(2):
        out[PACK_SECOND + 64 * l : PACK_SECOND + 64 * l + 64, :] = second[l]
        for k in range(3):
            for g in range(3):
                row = PACK_SHORT + 9 * l + 3 * k + g
                out[row : row + 1, :] = short[k, g, l : l + 1, :]
    out[PACK_SKIP : PACK_SKIP + 2, :] = skip[...]
    out[PACK_SKIP + 2 : PACK_ROWS, :] = jnp.zeros((PACK_ROWS - PACK_SKIP - 2, 128), f32)


def table_kernel(s, own, peer, embed, mine_out, other_out, conv_table, gate_table):
    first = s[CORE] == 0
    mine = jnp.where(first, own[...], peer[...])
    other = jnp.where(first, peer[...], own[...])
    mine_out[...] = mine
    other_out[...] = other

    def fill(table, lanes, parts):
        whole = jnp.concatenate(parts, axis=0)
        high, low = split(whole)
        table[0:48, lanes] = high
        table[48:96, lanes] = low
        table[96:128, lanes] = jnp.zeros((32, 128), bf16)

    def gate(pack, g):
        parts = []
        for k in range(3):
            row = PACK_SHORT + 3 * k + g
            parts.append(pack[16 * g : 16 * g + 16] * pack[row : row + 1])
        return parts

    fill(conv_table, slice(0, 128), gate(mine, 1))
    fill(conv_table, slice(128, 256), gate(mine, 2))
    fill(gate_table, slice(0, 128), gate(mine, 0))
    fill(gate_table, slice(128, 256), gate(other, 0))
    zero = jnp.zeros((16, 128), f32)
    fill(gate_table, slice(256, 384), [embed[:, 0:128], zero, zero])
    fill(gate_table, slice(384, 512), [embed[:, 128:256], zero, zero])


def onehot_kernel(s, ids, out, turned, work):
    live = s[LIVE]
    count, _, width = ids.shape
    work[0:HALO, :] = jnp.zeros((HALO, 128), f32)
    work[HALO + count * width : 2 * HALO + count * width, :] = jnp.zeros((HALO, 128), f32)
    vocab = lax.broadcasted_iota(jnp.int32, (128, width), 0) % 16
    place = lax.broadcasted_iota(jnp.int32, (128, width), 1)
    for i in range(count):
        token = jnp.broadcast_to(ids[i, 0:1, :], (128, width))
        hit = (token == vocab) & (place + i * width < live)
        work[HALO + width * i : HALO + width * (i + 1), :] = jnp.where(hit, 1.0, 0.0).T
    lane = lax.broadcasted_iota(jnp.int32, (width, 128), 1) % 48 // 16
    used = lax.broadcasted_iota(jnp.int32, (width, 128), 1) < 96
    half = count // 2
    for i in range(count):
        row = HALO + width * i
        now = work[row : row + width, :]
        one = work[row - 1 : row - 1 + width, :]
        two = work[row - 2 : row - 2 + width, :]
        picked = jnp.where(lane == 0, now, jnp.where(lane == 1, one, two))
        picked = jnp.where(used, picked, 0.0)
        out[row : row + width, :] = picked.astype(bf16)
        turned[i // half, :, width * (i % half) : width * (i % half + 1)] = picked.T.astype(bf16)
    out[0:HALO, :] = jnp.zeros((HALO, 128), bf16)
    out[HALO + count * width : 2 * HALO + count * width, :] = jnp.zeros((HALO, 128), bf16)


def sine_and_cosine(angle):
    turns = jnp.round(angle * (2.0 / math.pi))
    x = ((angle - turns * 1.5703125) - turns * 4.837512969970703125e-4) - turns * 7.549789948768648e-8
    z = x * x
    sin = ((-1.9515295891e-4 * z + 8.3321608736e-3) * z - 1.6666654611e-1) * z * x + x
    cos = ((2.443315711809948e-5 * z - 1.388731625493765e-3) * z + 4.166664568298827e-2) * z * z - 0.5 * z + 1.0
    quarter = turns.astype(jnp.int32) & 3
    odd = (quarter & 1) == 1
    first, second = jnp.where(odd, cos, sin), jnp.where(odd, sin, cos)
    first = jnp.where(quarter >= 2, -first, first)
    second = jnp.where((quarter == 1) | (quarter == 2), -second, second)
    return first, second


def sine_kernel(s, feats, firsts, sine, cosine, turned, padded):
    padded[...] = jnp.zeros_like(padded)
    for l in range(2):
        padded[0:FEAT, 64 * l : 64 * l + 64] = firsts[:, l, :]
    both = padded[...]
    cut = lambda v: v.astype(bf16).astype(f32)
    first = cut(both)
    second = cut(both - first)
    third = both - first - second
    fill = jnp.zeros((256 - 6 * FEAT_ROWS, 128), f32)
    weights = jnp.concatenate([first, second, first, second, third, first, fill], axis=0).astype(bf16)
    count = feats.shape[0] // 512

    def chunk(i, carry):
        rows = at(512 * i, 512)
        act, cosine[rows, :] = sine_and_cosine(mm(feats[rows, :], weights))
        sine[rows, 0:128], sine[rows, 128:256] = split(act)
        turned[:, at(512 * i, 512, 256)] = act.T.astype(bf16)
        return carry

    looped(count, chunk)


def decay_of(rates, start, rows, length):
    place = (lax.broadcasted_iota(jnp.int32, (rows, 1), 0) + start).astype(f32) / length
    return jnp.exp(-place * rates), place


def filter_kernel(level, s, sine, mine, rates, dft, twiddle, filt, freq, stage):
    length = sine.shape[0]
    rate = rates[s[WHICH]]
    zero = jnp.zeros((64, 128), f32)
    second = mine[PACK_SECOND + 64 * level : PACK_SECOND + 64 * level + 64]
    high, low = split(jnp.concatenate([zero, second] if level else [second, zero], axis=0))
    twice = jnp.concatenate([high, high], axis=0)

    def chunk(i, carry):
        rows = at(512 * i, 512)
        decay, _ = decay_of(rate, 512 * i, 512, length)
        filt[rows, :] = (mm(sine[rows, :], twice) + mm(sine[rows, 0:128], low)) * decay
        return carry

    every(length // 512, chunk)
    to_freq(lambda p, row: filt[pl.ds(BLOCK * p + row, 16), :] * (1.0 / length), dft, twiddle, stage, freq)


def causal(load, skip_row, freq_filt, dft, twiddle, spec, stage, work, line):
    to_freq(load, dft, twiddle, stage, spec)
    times(freq_filt, spec, stage, False)

    def store(p, row, value):
        line[pl.ds(HALO + BLOCK * p + row, 16), :] = value + skip_row * load(p, row)

    from_freq(dft, twiddle, stage, work, store)


def hand_out(s, line, keep, send):
    half = (line.shape[0] - 2 * HALO) // 2
    span = half + 2 * HALO
    k = s[CORE]
    line[0:HALO, :] = jnp.zeros((HALO, 128), f32)
    line[HALO + 2 * half :, :] = jnp.zeros((HALO, 128), f32)
    keep[...] = line[at(half * k, span), :]
    send[...] = line[at(half * (1 - k), span), :]


def conv_first_kernel(s, onehot, conv_table, mine, freq_filt, dft, twiddle, keep, send, spec, product, stage, work, line):
    def chunk(i, carry):
        rows = at(512 * i, 512)
        pair = mm(onehot[at(512 * i + HALO, 512), :], conv_table[...])
        product[rows, :] = pair[:, 0:128] * pair[:, 128:256]
        return carry

    every(product.shape[0] // 512, chunk)
    skip_row = mine[PACK_SKIP : PACK_SKIP + 1, :]
    causal(lambda p, row: product[pl.ds(BLOCK * p + row, 16), :], skip_row, freq_filt, dft, twiddle, spec, stage, work, line)
    hand_out(s, line, keep, send)


def join_rows(s, whole, kept, received):
    half = kept.shape[0]
    whole[at(half * s[CORE], half), :] = kept[...]
    whole[at(half * (1 - s[CORE]), half), :] = received[...]


def conv_second_kernel(s, kept, received, mine, freq_filt, dft, twiddle, keep, send, spec, product, stage, work, line):
    join_rows(s, product, kept, received)
    skip_row = mine[PACK_SKIP + 1 : PACK_SKIP + 2, :]
    causal(lambda p, row: product[pl.ds(BLOCK * p + row, 16), :], skip_row, freq_filt, dft, twiddle, spec, stage, work, line)
    hand_out(s, line, keep, send)


def gelu_parts(p):
    squared = p * p
    th = jnp.tanh(GELU_A * p * (1.0 + GELU_B * squared))
    half = 0.5 * (1.0 + th)
    slope = half + 0.5 * p * (1.0 - th * th) * (GELU_A + (3.0 * GELU_A * GELU_B) * squared)
    return p * half, slope


def gelu_only(p):
    return 0.5 * p * (1.0 + jnp.tanh(GELU_A * p * (1.0 + GELU_B * (p * p))))


def forward_first_kernel(
    s, onehot, gate_table, conv_mine, conv_other, gain, w_out, w_up, w_down, w_in, mine, other,
    keep, send, mid_out, stream_out, gates, mixed,
):
    span = mid_out.shape[0]
    half = span - 2 * HALO
    k = s[CORE]
    taps = [
        jnp.concatenate([pack[PACK_SHORT + 9 + 3 * t + g : PACK_SHORT + 10 + 3 * t + g, :] for g in range(3) for pack in (mine, other)], axis=1)
        for t in range(3)
    ]

    step = span // 2

    def chunk(i, carry):
        rows = at(step * i, step)
        looked = mm(onehot[at(half * k + step * i, step), :], gate_table[...])
        conv = jnp.concatenate([conv_mine[rows, :], conv_other[rows, :]], axis=1)
        gated = (conv * looked[:, 0:256]).astype(bf16)
        mid = looked[:, 256:512] + mm(gated, w_out[...])
        mid_out[rows, :] = mid
        normal, _ = unit(mid)
        low = (normal * gain[0, 1:2, :]).astype(bf16)
        hidden = gelu_only(mm(low, w_up[...])).astype(bf16)
        stream = mid + mm(hidden, w_down[...])
        stream_out[rows, :] = stream
        normal, _ = unit(stream)
        low = (normal * gain[1, 0:1, :]).astype(bf16)
        mixed[rows, :] = mm(low, w_in[...])
        return carry

    looped(2, chunk)
    gates[0:HALO, :] = jnp.zeros((HALO, 768), f32)
    stride = 80

    def gate_step(i, carry):
        start = stride * i + HALO
        for g in range(3):
            lanes = slice(256 * g, 256 * g + 256)
            near = mixed[at(start - 8, stride + 8, 8), lanes]
            total = None
            for t in range(3):
                part = taps[t][:, lanes] * near[8 - t : 8 - t + stride]
                total = part if total is None else total + part
            gates[at(start, stride), lanes] = total

    looped((span - HALO) // stride, gate_step)
    own = slice(HALO, HALO + half)
    keep[...] = gates[own, 256:384] * gates[own, 512:640]
    send[...] = gates[own, 384:512] * gates[own, 640:768]


def turn_back_kernel(
    s, conv_mine, conv_other, gates, stream, cot, cot_rim, gain, w_out, w_up, w_down,
    keep, send, grad_x0, grad_mid, block_out, hidden_out, low_out, normed_out, pre_out, gated_out, mid_low_out, gain_out,
    cot_rows, conv_grads,
):
    span = stream.shape[0]
    half = span - 2 * HALO
    k = s[CORE]
    live = s[LIVE]
    cot_rows[0:HALO, :] = jnp.zeros((HALO, 256), f32)
    cot_rows[HALO : HALO + half, :] = cot[...]
    cot_rows[HALO + half :, :] = jnp.where(k == 0, cot_rim[...], 0.0)
    gain_out[...] = jnp.zeros_like(gain_out)

    step = span // 2

    def chunk(i, carry):
        rows = at(step * i, step)
        local_row = lax.broadcasted_iota(jnp.int32, (step, 1), 0) + step * i
        keep_mask = (local_row + (half * k - HALO) < live).astype(f32)
        own_mask = ((local_row >= HALO) & (local_row < HALO + half)).astype(f32)
        x0 = gates[rows, 0:256]
        conv = jnp.concatenate([conv_mine[rows, :], conv_other[rows, :]], axis=1)
        gated = (conv * x0).astype(bf16)
        gated_out[rows, :] = gated
        mid = stream[rows, :] + mm(gated, w_out[...])
        normal, scale = unit(mid)
        gain_row = gain[1, 1:2, :]
        low = (normal * gain_row).astype(bf16)
        normed_out[rows, :] = low
        act, slope = gelu_parts(mm(low, w_up[...]))
        hidden = act.astype(bf16)
        hidden_out[rows, :] = hidden
        block_out[rows, :] = (mid + mm(hidden, w_down[...])) * keep_mask
        grad = cot_rows[rows, :] * keep_mask
        grad_low = grad.astype(bf16)
        low_out[rows, :] = grad_low
        grad_pre = (slope * mm_nt(grad_low, w_down[...])).astype(bf16)
        pre_out[rows, :] = grad_pre
        grad_normed = mm_nt(grad_pre, w_up[...])
        gain_out[0:1, :] += jnp.sum(grad_normed * normal * own_mask, axis=0, keepdims=True)
        mid_grad = grad + unit_back(grad_normed * gain_row, normal, scale)
        grad_mid[rows, :] = mid_grad
        mid_low = mid_grad.astype(bf16)
        mid_low_out[rows, :] = mid_low
        grad_gated = mm_nt(mid_low, w_out[...])
        conv_grads[rows, :] = grad_gated * x0
        grad_x0[rows, :] = grad_gated * conv
        return carry

    looped(2, chunk)
    own = slice(HALO, HALO + half)
    keep[...] = conv_grads[own, 0:128]
    send[...] = conv_grads[own, 128:256]


def conv_back_kernel(s, kept, received, mine, freq_filt, dft, twiddle, keep, send, spec, grads, stage, work, line):
    join_rows(s, grads, kept, received)
    skip_row = mine[PACK_SKIP + 1 : PACK_SKIP + 2, :]
    load = lambda p, row: grads[pl.ds(BLOCK * p + row, 16), :]
    to_freq(load, dft, twiddle, stage, spec)
    times(freq_filt, spec, stage, True)

    def store(p, row, value):
        line[pl.ds(HALO + BLOCK * p + row, 16), :] = value + skip_row * load(p, row)

    from_freq(dft, twiddle, stage, work, store)
    hand_out(s, line, keep, send)


def grad_freq_kernel(s, kept, received, dft, twiddle, spec, grads, stage):
    join_rows(s, grads, kept, received)
    to_freq(lambda p, row: grads[pl.ds(BLOCK * p + row, 16), :], dft, twiddle, stage, spec)


def filter_back(
    level, s, spec_grad, spec_in, grads, product, filt, cosine, sine_turned, mine, rates, feats_turned, dft, twiddle,
    second_out, first_out, skip_out, stage, work, line,
):
    length = filt.shape[0]
    times(spec_in, spec_grad, stage, True)

    def store(p, row, value):
        line[pl.ds(BLOCK * p + row, 16), :] = value

    from_freq(dft, twiddle, stage, work, store)
    rate = rates[s[WHICH]]
    second = mine[PACK_SECOND + 64 * level : PACK_SECOND + 64 * level + 64, :].astype(bf16)
    weight = jnp.where(s[GROUP] == 0, 0.5 * length, 0.0)
    skip_out[...] = jnp.zeros_like(skip_out)
    second_out[...] = jnp.zeros_like(second_out)
    first_out[...] = jnp.zeros_like(first_out)
    def chunk(i, carry):
        rows = at(512 * i, 512, 128)
        decay, place = decay_of(rate, 512 * i, 512, length)
        shaped = ((line[rows, :] * (1.0 / length) + (weight * place) * filt[rows, :]) * decay).astype(bf16)
        skip_out[...] += jnp.sum((grads[rows, :] * product[rows, :]).reshape(64, 8, 128), axis=0)
        second_out[...] += mm(sine_turned[64 * level : 64 * level + 64, rows], shaped)
        inner = (mm_nt(shaped, second) * cosine[rows, 64 * level : 64 * level + 64]).astype(bf16)
        first_out[...] += mm(feats_turned[:, rows], inner)

    looped(length // 512, chunk)


def filter_back_kernel(s, *refs):
    filter_back(1, s, *refs)


def token_back_kernel(
    s, spec_grad, spec_in, grads, product, filt, cosine, sine_turned, mine, rates, feats_turned, dft, twiddle,
    freq_filt, onehot, turned, conv_table, second_out, first_out, skip_out, by_token, stage, work, line,
):
    length = grads.shape[0]
    skip_row = mine[PACK_SKIP : PACK_SKIP + 1, :]
    times(freq_filt, spec_grad, stage, True)

    def store(p, row, value):
        line[pl.ds(BLOCK * p + row, 16), :] = value + skip_row * grads[pl.ds(BLOCK * p + row, 16), :]

    from_freq(dft, twiddle, stage, work, store)
    by_token[...] = jnp.zeros_like(by_token)
    width = turned.shape[2]
    for i in range(length // width):
        rows = slice(width * i, width * (i + 1))
        pair = mm(onehot[HALO + width * i : HALO + width * (i + 1), :], conv_table[...])
        back = line[rows, :]
        gate_grads = jnp.concatenate([back * pair[:, 128:256], back * pair[:, 0:128]], axis=1).astype(bf16)
        by_token[...] += mm(turned[i], gate_grads)[0:48, :]
    filter_back(
        0, s, spec_grad, spec_in, grads, product, filt, cosine, sine_turned, mine, rates, feats_turned, dft, twiddle,
        second_out, first_out, skip_out, stage, work, line,
    )


def back_gates_kernel(
    s, prod_mine, prod_other, grad_x0, gates, mixed, grad_mid, stream, gain, mine, other, w_in,
    grad_stream, normed_out, mixed_low, short_out, gain_out, line,
):
    span = stream.shape[0]
    half = span - 2 * HALO
    taps = [
        jnp.concatenate([pack[PACK_SHORT + 9 + 3 * t + g : PACK_SHORT + 10 + 3 * t + g, :] for g in range(3) for pack in (mine, other)], axis=1)
        for t in range(3)
    ]
    step = 128

    def products(rows):
        for lanes, prod in ((slice(0, 128), prod_mine), (slice(128, 256), prod_other)):
            first, second = slice(256 + lanes.start, 256 + lanes.stop), slice(512 + lanes.start, 512 + lanes.stop)
            product = prod[rows, :]
            line[rows, lanes] = product * gates[rows, second]
            line[rows, first] = product * gates[rows, first]

    def product_step(i, carry):
        products(at(step * i + HALO, step))

    looped(half // step, product_step)
    products(slice(HALO + half, 2 * HALO + half))
    short_out[...] = jnp.zeros_like(short_out)
    gain_out[...] = jnp.zeros_like(gain_out)

    def mixed_step(i, carry):
        start = step * i + HALO
        for g in range(3):
            lanes = slice(256 * g, 256 * g + 256)
            values = mixed[at(start, step), lanes]
            total = None
            rows = at(start, step + 8)
            near = grad_x0[rows, :] if g == 0 else line[rows, 256 * g - 256 : 256 * g]
            for t in range(3):
                shifted = near[t : t + step]
                part = taps[t][:, lanes] * shifted
                total = part if total is None else total + part
                short_out[t, :, lanes] += jnp.sum((shifted * values).reshape(step // 8, 8, 256), axis=0)
            mixed_low[at(step * i, step), lanes] = total.astype(bf16)

    looped(half // step, mixed_step)

    def chunk(i, carry):
        rows = at(512 * i, 512)
        wide = at(512 * i + HALO, 512)
        normal, scale = unit(stream[wide, :])
        gain_row = gain[1, 0:1, :]
        normed_out[rows, :] = (normal * gain_row).astype(bf16)
        grad_normed = mm_nt(mixed_low[rows, :], w_in[...])
        gain_out[0:1, :] += jnp.sum(grad_normed * normal, axis=0, keepdims=True)
        grad_stream[rows, :] = grad_mid[wide, :] + unit_back(grad_normed * gain_row, normal, scale)
        return carry

    every(half // 512, chunk)


def back_first_kernel(
    s, grad_stream, mid, onehot, turned, gate_table, conv_mine, conv_other, gain, w_out, w_up, w_down,
    keep, send, hidden_out, low_out, normed_out, pre_out, gated_out, mid_low_out, by_token, gain_out,
):
    half = grad_stream.shape[0]
    k = s[CORE]
    by_token[...] = jnp.zeros_like(by_token)
    gain_out[...] = jnp.zeros_like(gain_out)

    step = half // 2

    def chunk(i, carry):
        rows = at(step * i, step)
        wide = at(step * i + HALO, step)
        hot = onehot[at(half * k + step * i + HALO, step), :]
        x0 = mm(hot, gate_table[:, 0:256])
        conv = jnp.concatenate([conv_mine[wide, :], conv_other[wide, :]], axis=1)
        gated_out[rows, :] = (conv * x0).astype(bf16)
        normal, scale = unit(mid[wide, :])
        gain_row = gain[0, 1:2, :]
        low = (normal * gain_row).astype(bf16)
        normed_out[rows, :] = low
        act, slope = gelu_parts(mm(low, w_up[...]))
        hidden_out[rows, :] = act.astype(bf16)
        grad = grad_stream[rows, :]
        grad_low = grad.astype(bf16)
        low_out[rows, :] = grad_low
        grad_pre = (slope * mm_nt(grad_low, w_down[...])).astype(bf16)
        pre_out[rows, :] = grad_pre
        grad_normed = mm_nt(grad_pre, w_up[...])
        gain_out[0:1, :] += jnp.sum(grad_normed * normal, axis=0, keepdims=True)
        mid_grad = grad + unit_back(grad_normed * gain_row, normal, scale)
        mid_low = mid_grad.astype(bf16)
        mid_low_out[rows, :] = mid_low
        grad_gated = mm_nt(mid_low, w_out[...])
        conv_grad = grad_gated * x0
        keep[rows, :] = conv_grad[:, 0:128]
        send[rows, :] = conv_grad[:, 128:256]
        flips = turned[k, :, at(step * i, step, 256)]
        rest = mid_grad - mid_low.astype(f32)
        gate_grads = jnp.concatenate([(grad_gated * conv).astype(bf16), mid_low, rest.astype(bf16)], axis=1)
        by_token[...] += mm(flips, gate_grads)[0:48, :]
        return carry

    looped(2, chunk)


R_OUT, R_UP, R_DOWN, R_IN = 128, 512, 512, 384


def fill_part(s, raw_out, raw_up, raw_down, out):
    first = s[CORE] == 0
    pick = lambda a, b: jnp.where(first, a.astype(f32), b.astype(f32))
    out[0:128, :] = pick(raw_out[:, 0:128], raw_out[:, 128:256])
    for j in range(2):
        lanes = slice(128 * j, 128 * j + 128)
        out[128 + 256 * j : 384 + 256 * j, :] = pick(
            raw_up[:, 128 * j : 128 * j + 128], raw_up[:, 256 + 128 * j : 384 + 128 * j]
        )
        out[640 + 256 * j : 896 + 256 * j, :] = pick(raw_down[0:256, lanes], raw_down[256:512, lanes])


def fill_in_part(s, raw_in, out):
    first = s[CORE] == 0
    for g in range(3):
        a, b = raw_in[g, 0:128, :].astype(f32), raw_in[g, 128:256, :].astype(f32)
        out[128 * g : 128 * g + 128, :] = jnp.where(first, a, b)


def send_weights_kernel(s, w_out, w_up, w_down, out, raw_out, raw_up, raw_down, done):
    bring(((w_out.at[1], raw_out), (w_up.at[1], raw_up), (w_down.at[1], raw_down)), done)
    fill_part(s, raw_out, raw_up, raw_down, out)


def cot_split_kernel(s, blocks, keep, send):
    k = s[CORE]
    few = keep.shape[0]
    keep[...] = blocks[pl.ds(few * k, few)]
    send[...] = blocks[pl.ds(few * (1 - k), few)]


def cot_half_kernel(s, own, received, blocks, out):
    spot, width = s[CORE], own.shape[1]
    for j in range(own.shape[0]):
        out[pl.ds(width * (2 * j + spot), width), :] = own[j]
        out[pl.ds(width * (2 * j + 1 - spot), width), :] = received[j]
    out[2 * own.shape[0] * width :, :] = blocks[own.shape[0], 0:HALO, :]


def cot_whole_kernel(s, own, received, out, rim):
    spot = s[BIT1]
    rows = own.shape[0] - HALO
    two = rows // 2
    for j in range(2):
        out[pl.ds(two * (2 * j + spot), two), :] = own[two * j : two * j + two, :]
        out[pl.ds(two * (2 * j + 1 - spot), two), :] = received[two * j : two * j + two, :]
    rim[...] = jnp.where(spot == 0, own[rows:, :], received[rows:, :])


def relay_kernel(s, value, out):
    out[...] = value[...]


def join_weights_kernel(level, s, w_out, w_up, w_down, w_in, first_part, second_part, out_full, up_full, down_full, *in_full):
    first = s[CORE] == 0
    low = lambda ref, a, b: ref[a:b, :].astype(bf16)
    pick = lambda a, b: jnp.where(first, a, b)
    mine_out = w_out[level]
    a, b = first_part[0:128, :], second_part[0:128, :]
    peer_out = jnp.concatenate([pick(a, b), pick(b, a)], axis=1)
    out_full[0:128, :] = pick(mine_out.astype(f32), peer_out).astype(bf16)
    out_full[128:256, :] = pick(peer_out, mine_out.astype(f32)).astype(bf16)
    up_a, up_b = w_up[level, :, 0:256].astype(f32), w_up[level, :, 256:512].astype(f32)
    up_full[:, 0:256] = pick(up_a, up_b).astype(bf16)
    up_full[:, 256:512] = pick(up_b, up_a).astype(bf16)
    down_a, down_b = w_down[level, 0:256, :].astype(f32), w_down[level, 256:512, :].astype(f32)
    down_full[0:256, :] = pick(down_a, down_b).astype(bf16)
    down_full[256:512, :] = pick(down_b, down_a).astype(bf16)
    for n, part in enumerate((first_part, second_part)):
        for j in range(2):
            up_full[:, 512 + 256 * n + 128 * j : 640 + 256 * n + 128 * j] = low(part, 128 + 256 * j, 384 + 256 * j)
            down_full[512 + 256 * n : 768 + 256 * n, 128 * j : 128 * j + 128] = low(part, 640 + 256 * j, 896 + 256 * j)
    if in_full:
        (full,) = in_full
        for g in range(3):
            own = w_in[1 - level, g].astype(f32)
            a, b = first_part[1152 + 128 * g : 1280 + 128 * g, :], second_part[1152 + 128 * g : 1280 + 128 * g, :]
            peer = jnp.concatenate([pick(a, b), pick(b, a)], axis=0)
            full[:, 256 * g : 256 * g + 128] = pick(own, peer).astype(bf16)
            full[:, 256 * g + 128 : 256 * g + 256] = pick(peer, own).astype(bf16)


def wide_grads_kernel(pad, s, gated, mid_low, normed, grad_pre, hidden, grad_low, keep, send):
    k = s[CORE]
    first = k == 0
    stop = gated.shape[0] - pad
    own = lambda ref: ref[pad:stop, :]
    out = mm_tn(own(gated), own(mid_low))
    for m in range(2):
        a, b = out[128 * m : 128 * m + 128, 0:128], out[128 * m : 128 * m + 128, 128:256]
        half = m + k - 2 * m * k
        keep[half, 0:128, :] = jnp.where(first, a, b)
        send[half, 0:128, :] = jnp.where(first, b, a)
    for j in range(4):
        target = (keep, send)[j % 2]
        up = mm_tn(own(normed), grad_pre[pad:stop, 256 * j : 256 * j + 256])
        down = mm_tn(hidden[pad:stop, 256 * j : 256 * j + 256], own(grad_low))
        for n in range(2):
            lanes = slice(128 * n, 128 * n + 128)
            target[j // 2, 128 + 256 * n : 384 + 256 * n, :] = up[:, lanes]
            target[j // 2, 640 + 256 * n : 896 + 256 * n, :] = down[:, lanes]


def in_grads_kernel(s, normed_in, mixed_low, keep, send):
    k = s[CORE]
    first = k == 0
    for g in range(3):
        both = mm_tn(normed_in[...], mixed_low[:, 256 * g : 256 * g + 256])
        for m in range(2):
            block = both[:, 128 * m : 128 * m + 128]
            half = m + k - 2 * m * k
            keep[half, 128 * g : 128 * g + 128, :] = jnp.where(first, block[0:128], block[128:256])
            send[half, 128 * g : 128 * g + 128, :] = jnp.where(first, block[128:256], block[0:128])


def add_kernel(s, kept, received, own_out, peer_out):
    own_out[...] = kept[0] + received[0]
    peer_out[...] = kept[1] + received[1]


def add_half_kernel(s, kept, received, w_in, own_out, peer_out):
    rows = own_out.shape[0]
    part = at(rows * s[BIT1], rows, 8)
    own_out[...] = kept[0, part, :] + received[0, part, :]
    peer_out[0:rows, :] = kept[1, part, :] + received[1, part, :]
    fill_in_part(s, w_in.at[0], peer_out.at[rows : rows + 384])


def take_half_kernel(s, own, received, out, in_out):
    rows = own.shape[0]
    out[...] = own[...] + received[0:rows, :]
    in_out[...] = received[rows:, :]


def add_one_kernel(s, kept, received, out):
    out[...] = kept[...] + received[...]


def spread_wide_kernel(level, s, *refs):
    if level:
        outs, (a, b, out, up, down), done = refs[-9:-6], refs[-6:-1], refs[-1]
        rows = refs[0].shape[0]
        for whole, near, far in ((a, refs[0], refs[1]), (b, refs[2], refs[3])):
            whole[at(rows * s[BIT1], rows, 8), :] = near[...]
            whole[at(rows * (1 - s[BIT1]), rows, 8), :] = far[...]
    else:
        outs, (out, up, down), done = refs[-7:-4], refs[-4:-1], refs[-1]
        a, b = refs[:2]
    first = s[CORE] == 0
    pick = lambda x, y: jnp.where(first, x, y)

    def both(row, rows):
        x, y = a[row : row + rows, :], b[row : row + rows, :]
        return pick(x, y), pick(y, x)

    x, y = both(0, 128)
    out[:, 0:128] = x
    out[:, 128:256] = y
    for j in range(2):
        lanes = slice(128 * j, 128 * j + 128)
        x, y = both(128 + 256 * j, 256)
        up[:, 128 * j : 128 * j + 128] = x
        up[:, 256 + 128 * j : 384 + 128 * j] = y
        x, y = both(640 + 256 * j, 256)
        down[0:256, lanes] = x
        down[256:512, lanes] = y
    bring(zip((out, up, down), (whole.at[level] for whole in outs)), done)


def spread_in_kernel(s, kept, received, whole, near, done):
    first = s[CORE] == 0
    for g in range(3):
        x, y = kept[128 * g : 128 * g + 128, :], received[128 * g : 128 * g + 128, :]
        near[g, 0:128, :] = jnp.where(first, x, y)
        near[g, 128:256, :] = jnp.where(first, y, x)
    bring(((near, whole.at[1]),), done)


def pair_kernel(bit, s, own, received, out):
    spot = s[(CORE, BIT1, BIT2, BIT3)[bit]]
    for j in range(own.shape[0]):
        out[2 * j + spot] = own[j]
        out[2 * j + 1 - spot] = received[j]


E_GAIN, E_EMBED, E_FIRST, E_SHORT, E_TOKEN, E_ROWS = 0, 8, 24, 40, 56, 104
EM_SECOND, EM_SKIP, EM_ROWS = 0, 64, 72
L_TOKEN, L_SECOND, L_SKIP, L_ROWS = 0, 96, 160, 168
FIRST_ROWS = 16


def fold_first(values):
    last = jnp.concatenate([values[32:40], jnp.zeros((8, 64), f32)], axis=0)
    return jnp.concatenate([values[0:16], values[16:32], last, jnp.zeros((16, 64), f32)], axis=1)


def unfold_first(values):
    return jnp.concatenate([values[:, 0:64], values[:, 64:128], values[0:8, 128:192]], axis=0)[0:FEAT]


def early_kernel(s, gain_mid1, gain_in1, gain_mid0, by_token0, first1, short1, second1, skip1, flat, mine):
    k = s[CORE]
    flat[...] = jnp.zeros_like(flat)
    for row, values in enumerate((gain_mid1, gain_in1, gain_mid0)):
        flat[E_GAIN + row : E_GAIN + row + 1, :] = values[0:1, :]
    flat[E_EMBED : E_EMBED + 16, :] = by_token0[0:16, 256:512] + by_token0[0:16, 512:768]
    flat[E_FIRST : E_FIRST + FIRST_ROWS, :] = fold_first(first1[...])
    swap = lambda v: jnp.where(k == 0, v, jnp.concatenate([v[:, 128:256], v[:, 0:128]], axis=1))
    for t in range(3):
        total = jnp.sum(short1[t], axis=0, keepdims=True)
        for g in range(3):
            flat[E_SHORT + 3 * t + g : E_SHORT + 3 * t + g + 1, :] = swap(total[:, 256 * g : 256 * g + 256])
    flat[E_TOKEN : E_TOKEN + 48, :] = swap(by_token0[:, 0:256])
    mine[EM_SECOND : EM_SECOND + 64, :] = second1[...]
    mine[EM_SKIP : EM_SKIP + 8, :] = jnp.broadcast_to(jnp.sum(skip1[...], axis=0, keepdims=True), (8, 128))


def late_kernel(s, by_token12, second0, skip0, first0, mine, first_out):
    mine[L_TOKEN : L_TOKEN + 48, :] = by_token12[:, 0:128]
    mine[L_TOKEN + 48 : L_TOKEN + 96, :] = by_token12[:, 128:256]
    mine[L_SECOND : L_SECOND + 64, :] = second0[...]
    mine[L_SKIP : L_SKIP + 8, :] = jnp.broadcast_to(jnp.sum(skip0[...], axis=0, keepdims=True), (8, 128))
    first_out[...] = fold_first(first0[...])


def chip_kernel(s, flat, flat_in, mine, mine_in, out):
    first = s[CORE] == 0
    rows = flat.shape[0]
    total = flat[...] + flat_in[...]
    out[0:rows, :] = total
    out[rows:, 0:128] = jnp.where(first, mine[...], mine_in[...])
    out[rows:, 128:256] = jnp.where(first, mine_in[...], mine[...])


def last_kernel(
    s, early, early_in, late, late_in, embed, gain, own, peer, w_own, w_first, w_second, in_given,
    embed_out, gain_out, in_whole, short_out, first_out, second_out, skip_out, in_out, done,
):
    pick = lambda x, y: jnp.where(s[CORE] == 0, x, y)

    def plain(pair, row, rows):
        return pair[0][row : row + rows, :] + pair[1][row : row + rows, :]

    def halves(pair, row, rows):
        here, there = pair
        left = here[row : row + rows, 0:128] + there[row : row + rows, 128:256]
        right = here[row : row + rows, 128:256] + there[row : row + rows, 0:128]
        return left, right

    early, late = (early, early_in), (late, late_in)
    gains = plain(early, E_GAIN, 8)
    gain_out[1, 0:1, :] = gains[1:2, :]
    gain_out[1, 1:2, :] = gains[0:1, :]
    gain_out[0, 1:2, :] = gains[2:3, :]
    first_out[:, 0, :] = unfold_first(plain(late, 0, FIRST_ROWS))
    first_out[:, 1, :] = unfold_first(plain(early, E_FIRST, FIRST_ROWS))
    short = halves(early, E_SHORT, 16)[0]
    for t in range(3):
        for g in range(3):
            short_out[t, g, 1:2, :] = short[3 * t + g : 3 * t + g + 1, :]
    second_out[1] = halves(early, E_ROWS + EM_SECOND, 64)[0]
    second_out[0] = halves(late, FIRST_ROWS + L_SECOND, 64)[0]
    skip_out[0:1, :] = halves(late, FIRST_ROWS + L_SKIP, 8)[0][0:1]
    skip_out[1:2, :] = halves(early, E_ROWS + EM_SKIP, 8)[0][0:1]
    tokens = [
        halves(early, E_TOKEN, 48),
        halves(late, FIRST_ROWS + L_TOKEN, 48),
        halves(late, FIRST_ROWS + L_TOKEN + 48, 48),
    ]
    normal, scale = unit(embed[...])
    gain_row = gain[0, 0:1, :]
    low = (normal * gain_row).astype(bf16)
    grad_normed = jnp.zeros((16, 256), f32)
    for g in range(3):
        for h, pack in ((0, own), (1, peer)):
            grads = tokens[g][h]
            table = pack[16 * g : 16 * g + 16, :]
            summed = jnp.zeros((16, 128), f32)
            for t in range(3):
                row = PACK_SHORT + 3 * t + g
                part = grads[16 * t : 16 * t + 16, :]
                summed += pack[row : row + 1, :] * part
                if h == 0:
                    short_out[t, g, 0:1, :] = jnp.sum(table * part, axis=0, keepdims=True)
            high, rest = split(summed)
            if h == 0:
                in_out[g] = mm_tn(low, high) + mm_tn(low, rest)
                weight = w_own[0, g]
            else:
                rows = slice(128 * g, 128 * g + 128)
                a, b = w_first[rows, :], w_second[rows, :]
                weight = jnp.concatenate([pick(a, b), pick(b, a)], axis=0).astype(bf16)
            grad_normed += mm_nt(high, weight) + mm_nt(rest, weight)
    copy = pltpu.make_async_copy(in_out, in_whole.at[0], done.at[0])
    copy.start()
    gain_out[0, 0:1, :] = jnp.sum(grad_normed * normal, axis=0, keepdims=True)
    embed_out[...] = plain(early, E_EMBED, 16) + unit_back(grad_normed * gain_row, normal, scale)
    copy.wait()


def block_send_kernel(s, block_out, mine, other):
    spot = s[SPOT]
    mine[...] = block_out[at(HALO + 128 * spot, 128), :]
    near = spot + 1 - 2 * s[CORE]
    other[...] = block_out[at(HALO + 128 * near, 128), :]


def block_pick_kernel(s, mine, received, out):
    out[...] = jnp.where(s[HOLDER] == 1, mine[...], received[...])


def block_join_kernel(s, here, there, out):
    first = s[GROUP] == 0
    out[0] = jnp.where(first, here[...], there[...])
    out[1] = jnp.where(first, there[...], here[...])


def chip_local(
    ids, live, embed, norm_gain, in_weight, short_kernel, filter_first, filter_second, skip_gain,
    out_weight, up_weight, down_weight, cotangent,
):
    CALLS.clear()
    count = lax.axis_size("seq")
    rank = lax.axis_index("seq")
    group = lax.axis_index("ch")
    width = ids.shape[1]
    length = width * count
    half = length // 2
    span = half + 2 * HALO
    core = rank % 2
    across = lambda v: lax.ppermute(v, "ch", [(0, 1), (1, 0)])
    trade = lambda v, bit: lax.ppermute(v, "seq", [(i, i ^ bit) for i in range(count)])
    beside = lambda v: trade(v, 1)
    dft = jnp.asarray(dft_table()).astype(bf16)
    feats = jnp.asarray(feature_parts(length)).astype(bf16)
    feats_turned = jnp.asarray(np.pad(feature_table(length).T, ((0, FEAT_ROWS - FEAT), (0, 0)))).astype(bf16)
    rates = jnp.asarray(rate_table())
    low = lambda *shape: arr(*shape, kind=bf16)
    line = pltpu.VMEM((length + 2 * HALO, 128), f32)
    conv_scratch = [stage_scratch(), spec_scratch(), line]
    pair = lambda bit, v, w, **kw: run(
        functools.partial(pair_kernel, bit), jax.ShapeDtypeStruct((2 * v.shape[0],) + v.shape[1:], v.dtype), s, v, w, **kw
    )

    row_shape = lambda rows: arr(rows, 8, width, kind=jnp.int32)
    in_own = jnp.swapaxes(in_weight, 1, 2)
    packed = (embed, norm_gain, in_own, filter_second, jnp.transpose(short_kernel, (1, 2, 0, 3)), skip_gain)
    wide = (out_weight, up_weight, down_weight)
    held = [(1, 2), ids.shape, embed.shape, norm_gain.shape, in_own.shape[1:], filter_second.shape, packed[4].shape, skip_gain.shape]
    held += [v.shape[1:] for v in wide] + [in_own.shape[1:]]
    kinds = [jnp.int32, jnp.int32, f32, f32, bf16, f32, f32, f32] + [bf16] * 4
    s, ids1, cot1, pack, part0 = start(
        numbers_kernel,
        [arr(NUMBER_ROWS, 128, kind=jnp.int32), row_shape(1), arr(1, width, 256), arr(PACK_ROWS, 128), arr(1536, 128)],
        live.reshape(1, 2), ids, cotangent, *packed, *wide, in_own,
        scratch=[pltpu.VMEM(shape, kind) for shape, kind in zip(held, kinds)] + [pltpu.SemaphoreType.DMA((13,))],
    )
    pack_in = across(pack)
    part0_in = across(part0)
    ids2 = pair(3, ids1, trade(ids1, 8))
    sine, cosine, sine_turned = run(
        sine_kernel, [low(length, 256), arr(length, 128), low(128, length)], s, feats, jnp.transpose(filter_first, (1, 0, 2)),
        after=(ids2,), scratch=[pltpu.VMEM((FEAT_ROWS, 128), f32)],
    )
    twiddle = run(twiddle_kernel, arr(KINDS - 1, 2, BLOCK, 128), s, jnp.asarray(twiddle_table()), after=(sine,))
    cot2 = pair(3, cot1, trade(cot1, 8), after=(twiddle,))
    ids4 = pair(2, ids2, trade(ids2, 4), after=(cot2,))
    part1 = run(
        send_weights_kernel, arr(1152, 128), s, *wide, hbm=range(3), after=(ids4,),
        scratch=[pltpu.VMEM(v.shape[1:], v.dtype) for v in wide] + [pltpu.SemaphoreType.DMA((3,))],
    )
    part1_in = across(part1)
    mine, other, conv_table, gate_table = run(
        table_kernel, [arr(PACK_ROWS, 128), arr(PACK_ROWS, 128), low(128, 256), low(128, 512)], s, pack, pack_in, embed,
        after=(part1,),
    )
    make_filter = lambda level, after: run(
        functools.partial(filter_kernel, level), [arr(length, 128), arr(*SPECTRUM)], s, sine, mine, rates, dft, twiddle,
        scratch=[stage_scratch()], after=after,
    )
    filt0, freq0 = make_filter(0, ())
    ids8 = pair(1, ids4, trade(ids4, 2), after=(filt0,))
    cot4 = pair(2, cot2, trade(cot2, 4), after=(ids8,))
    cot_keep, cot_send = run(cot_split_kernel, [arr(2, width, 256), arr(2, width, 256)], s, cot4)
    all_ids = pair(0, ids8, beside(ids8), after=(cot_send,))
    onehot, turned = run(
        onehot_kernel, [low(length + 2 * HALO, 128), low(2, 128, half)], s, all_ids,
        scratch=[pltpu.VMEM((length + 2 * HALO, 128), f32)],
    )
    conv_mine0, sent, spec0, product0 = run(
        conv_first_kernel, [arr(span, 128), arr(span, 128), arr(*SPECTRUM), arr(length, 128)],
        s, onehot, conv_table, mine, freq0, dft, twiddle, scratch=conv_scratch,
    )
    conv_other0 = beside(sent)
    first_part = run(relay_kernel, arr(1536, 128), s, part0_in, after=(sent,))
    first_beside = beside(first_part)
    filt1, freq1 = make_filter(1, (first_part,))
    cot_half = run(cot_half_kernel, arr(4 * width + HALO, 256), s, cot_keep, beside(cot_send), cot4, after=(freq1,))
    cot_half_in = trade(cot_half, 2)
    w_out0, w_up0, w_down0, w_in1 = run(
        functools.partial(join_weights_kernel, 0), [low(256, 256), low(256, 1024), low(1024, 256), low(256, 768)],
        s, out_weight, up_weight, down_weight, in_own, first_part, first_beside, after=(cot_half,),
    )
    kept, sent, mid0, stream1, gates1, mixed1 = run(
        forward_first_kernel,
        [arr(half, 128), arr(half, 128), arr(span, 256), arr(span, 256), arr(span, 768), arr(span, 768)],
        s, onehot, gate_table, conv_mine0, conv_other0, norm_gain, w_out0, w_up0, w_down0, w_in1, mine, other,
    )
    received = beside(sent)
    second_part = run(relay_kernel, arr(1152, 128), s, part1_in, after=(sent,))
    second_beside = beside(second_part)
    conv_mine1, sent, spec1, product1 = run(
        conv_second_kernel, [arr(span, 128), arr(span, 128), arr(*SPECTRUM), arr(length, 128)],
        s, kept, received, mine, freq1, dft, twiddle, scratch=conv_scratch, after=(second_part,),
    )
    conv_other1 = beside(sent)
    cot, cot_rim = run(cot_whole_kernel, [arr(half, 256), arr(HALO, 256)], s, cot_half, cot_half_in, after=(sent,))
    w_out1, w_up1, w_down1 = run(
        functools.partial(join_weights_kernel, 1), [low(256, 256), low(256, 1024), low(1024, 256)],
        s, out_weight, up_weight, down_weight, in_own, second_part, second_beside, after=(cot_rim,),
    )
    (kept, sent, grad_x0, grad_mid1, block, hidden, grad_low, normed, grad_pre, gated, mid_low, gain_mid1) = run(
        turn_back_kernel,
        [
            arr(half, 128), arr(half, 128), arr(span, 256), arr(span, 256), arr(span, 256), low(span, 1024), low(span, 256),
            low(span, 256), low(span, 1024), low(span, 256), low(span, 256), arr(8, 256),
        ],
        s, conv_mine1, conv_other1, gates1, stream1, cot, cot_rim, norm_gain, w_out1, w_up1, w_down1,
        scratch=[pltpu.VMEM((span, 256), f32), pltpu.VMEM((span, 256), f32)],
    )
    received = beside(sent)
    grads_keep1, grads_send1 = run(
        functools.partial(wide_grads_kernel, HALO), [arr(2, 1152, 128), arr(2, 1152, 128)],
        s, gated, mid_low, normed, grad_pre, hidden, grad_low,
    )
    block_mine, block_other = run(block_send_kernel, [arr(width, 256), arr(width, 256)], s, block)
    grads_in1 = beside(grads_send1)
    block_beside = beside(block_other)

    prod_mine, sent, spec_grad1, grads1 = run(
        conv_back_kernel, [arr(span, 128), arr(span, 128), arr(*SPECTRUM), arr(length, 128)],
        s, kept, received, mine, freq1, dft, twiddle, scratch=conv_scratch, after=(grads_send1, block_mine),
    )
    prod_other = beside(sent)
    own1, peer1 = run(add_half_kernel, [arr(576, 128), arr(960, 128)], s, grads_keep1, grads_in1, in_own, after=(sent,))
    across1 = across(peer1)
    filter_shapes = [arr(64, 128), arr(40, 64), arr(8, 128)]
    filter_scratch = [stage_scratch(), spec_scratch(), pltpu.VMEM((length, 128), f32)]
    second1, first1, skip1 = run(
        filter_back_kernel, filter_shapes, s, spec_grad1, spec1, grads1, product1, filt1, cosine,
        sine_turned, mine, rates, feats_turned, dft, twiddle, scratch=filter_scratch, after=(peer1,),
    )
    grad_stream1, normed_in, mixed_low, short1, gain_in1 = run(
        back_gates_kernel,
        [arr(half, 256), low(half, 256), low(half, 768), arr(3, 8, 768), arr(8, 256)],
        s, prod_mine, prod_other, grad_x0, gates1, mixed1, grad_mid1, stream1, norm_gain, mine, other, w_in1,
        scratch=[pltpu.VMEM((span, 512), f32)], after=(skip1,),
    )
    in_keep, in_send = run(in_grads_kernel, [arr(2, 384, 128), arr(2, 384, 128)], s, normed_in, mixed_low)
    in_beside = beside(in_send)
    block_here = run(block_pick_kernel, arr(width, 256), s, block_mine, block_beside, after=(in_send,))
    block_across = across(block_here)
    in_own1, in_peer1 = run(add_kernel, [arr(384, 128), arr(384, 128)], s, in_keep, in_beside, after=(block_here,))
    in_across = across(in_peer1)
    total1, in0_first = run(take_half_kernel, [arr(576, 128), arr(384, 128)], s, own1, across1, after=(block_here,))
    total1_y, in0_second = trade(total1, 2), beside(in0_first)
    (kept, sent, hidden, grad_low, normed, grad_pre, gated, mid_low, by_token0, gain_mid0) = run(
        back_first_kernel,
        [
            arr(half, 128), arr(half, 128), low(half, 1024), low(half, 256), low(half, 256), low(half, 1024), low(half, 256),
            low(half, 256), arr(48, 768), arr(8, 256),
        ],
        s, grad_stream1, mid0, onehot, turned, gate_table, conv_mine0, conv_other0, norm_gain, w_out0, w_up0, w_down0,
        after=(in_peer1,),
    )
    received = beside(sent)
    early_flat, early_mine = run(
        early_kernel, [arr(E_ROWS, 256), arr(EM_ROWS, 128)],
        s, gain_mid1, gain_in1, gain_mid0, by_token0, first1, short1, second1, skip1,
    )
    early_flat_in, early_mine_in = beside(early_flat), beside(early_mine)
    grads_keep0, grads_send0 = run(
        functools.partial(wide_grads_kernel, 0), [arr(2, 1152, 128), arr(2, 1152, 128)],
        s, gated, mid_low, normed, grad_pre, hidden, grad_low, after=(early_flat,),
    )
    grads_in0 = beside(grads_send0)
    early = run(
        chip_kernel, arr(E_ROWS + EM_ROWS, 256),
        s, early_flat, early_flat_in, early_mine, early_mine_in, after=(grads_send0,),
    )
    early_in = across(early)
    spec_grad0, grads0 = run(
        grad_freq_kernel, [arr(*SPECTRUM), arr(length, 128)], s, kept, received, dft, twiddle, scratch=[stage_scratch()],
        after=(early,),
    )
    own0, peer0 = run(add_kernel, [arr(1152, 128), arr(1152, 128)], s, grads_keep0, grads_in0, after=(spec_grad0,))
    across0 = across(peer0)
    second0, first0, skip0, by_token12 = run(
        token_back_kernel, filter_shapes + [arr(48, 256)], s, spec_grad0, spec0, grads0, product0, filt0, cosine,
        sine_turned, mine, rates, feats_turned, dft, twiddle, freq0, onehot, turned, conv_table, scratch=filter_scratch,
        after=(peer0, early, total1),
    )
    wide_shapes = [arr(2, 128, 256), arr(2, 256, 512), arr(2, 512, 256)]
    wide_scratch = [pltpu.VMEM(v.shape[1:], f32) for v in wide_shapes] + [pltpu.SemaphoreType.DMA((3,))]
    late_mine, late_first = run(
        late_kernel, [arr(L_ROWS, 128), arr(FIRST_ROWS, 256)], s, by_token12, second0, skip0, first0, flops=FEW_FLOPS
    )
    late_mine_in, late_first_in = beside(late_mine), beside(late_first)
    in_total = run(add_one_kernel, arr(384, 128), s, in_own1, in_across, after=(late_mine,), flops=FEW_FLOPS)
    block_out, joined = run(block_join_kernel, arr(2, width, 256), s, block_here, block_across, after=(late_mine,), flops=FEW_FLOPS, token=True)
    late = run(
        chip_kernel, arr(FIRST_ROWS + L_ROWS, 256), s, late_first, late_first_in, late_mine, late_mine_in, flops=FEW_FLOPS,
        after=(joined, in_total, early_in),
    )
    late_in = across(late)
    near1_y = run(relay_kernel, arr(576, 128), s, total1_y, after=(late,), flops=FEW_FLOPS)
    quarters1 = (total1, near1_y, beside(total1), beside(near1_y))
    in_total_beside = beside(in_total)
    *wide_buffers, wide_spread = run(
        functools.partial(spread_wide_kernel, 1), wide_shapes, s, *quarters1, hbm_outs=(0, 1, 2), flops=FEW_FLOPS,
        scratch=[pltpu.VMEM((1152, 128), f32)] * 2 + wide_scratch, after=(late,), token=True,
    )
    in_buffer, in_spread = run(
        spread_in_kernel, arr(2, 3, 256, 128), s, in_total, in_total_beside, hbm_outs=(0,), flops=FEW_FLOPS, token=True,
        scratch=[pltpu.VMEM((3, 256, 128), f32), pltpu.SemaphoreType.DMA((1,))],
    )
    total0 = run(add_one_kernel, arr(1152, 128), s, own0, across0, after=(late_in, wide_spread, in_spread))
    total0_beside = beside(total0)
    grad_embed, grad_gain, grad_in, grad_short, grad_first, grad_second, grad_skip = run(
        last_kernel,
        [
            arr(16, 256), arr(2, 2, 256), arr(2, 3, 256, 128), arr(3, 3, 2, 128), arr(FEAT, 2, 64), arr(2, 64, 128), arr(2, 128),
        ],
        s, early, early_in, late, late_in, embed, norm_gain, pack, pack_in, in_own, in0_first, in0_second, in_buffer,
        hbm=(11,), hbm_outs=(2,), aliases=((11, 2),), flops=FEW_FLOPS, after=(total0,),
        scratch=[pltpu.VMEM((3, 256, 128), f32), pltpu.SemaphoreType.DMA((1,))],
    )
    grad_out, grad_up, grad_down = run(
        functools.partial(spread_wide_kernel, 0), wide_shapes, s, total0, total0_beside, *wide_buffers,
        hbm=(2, 3, 4), hbm_outs=(0, 1, 2), aliases=((2, 0), (3, 1), (4, 2)), flops=FEW_FLOPS, scratch=wide_scratch,
    )
    return (
        block_out,
        grad_embed,
        grad_gain,
        jnp.swapaxes(grad_in, 1, 2),
        jnp.transpose(grad_short, (2, 0, 1, 3)),
        jnp.transpose(grad_first, (1, 0, 2)),
        grad_second,
        grad_skip,
        grad_out,
        grad_up,
        grad_down,
    )


def solution(mesh):
    in_specs = (
        P(None, "seq"),
        P(),
        P(),
        P(),
        P(None, None, None, "ch"),
        P(None, None, None, "ch"),
        P(),
        P(None, None, "ch"),
        P(None, "ch"),
        P(None, "ch", None),
        P(None, None, "ch"),
        P(None, "ch", None),
        P(None, "seq", None),
    )
    out_specs = (
        P(None, "seq", None),
        P(),
        P(),
        P(None, None, None, "ch"),
        P(None, None, None, "ch"),
        P(),
        P(None, None, "ch"),
        P(None, "ch"),
        P(None, "ch", None),
        P(None, None, "ch"),
        P(None, "ch", None),
    )

    def either(*args):
        length = args[0].shape[1] * lax.axis_size("seq")
        near = length == BLOCKS * BLOCK and lax.axis_size("seq") == 16
        return (chip_local if near else local)(*args)

    return jax.shard_map(either, mesh=mesh, in_specs=in_specs, out_specs=out_specs, check_vma=False)
```

```python
import collections
import functools
import math

import jax
import jax.numpy as jnp
import ml_dtypes
import numpy as np
from jax import lax
from jax.experimental import pallas as pl
from jax.experimental.pallas import tpu as pltpu
from jax.sharding import PartitionSpec as P

D = 256
FEAT = 33


precise = lax.Precision.HIGHEST
epsilon = 1e-05


def passed_along(value, axis, steps):
    count = lax.axis_size(axis)
    leading, last = (max(0, -steps), min(count, count - steps))
    return lax.ppermute(value, axis, [(source, source + steps) for source in range(leading, last)])


def layer_norm(inputs, gain_vec):
    center = inputs - jnp.mean(inputs, axis=-1, keepdims=True)
    spread = jnp.mean(center * center, axis=-1, keepdims=True)
    return center * lax.rsqrt(spread + epsilon) * gain_vec


def position_features(length):
    places = jnp.arange(length, dtype=jnp.int32)
    band_ids = jnp.arange(1, (FEAT - 1) // 2 + 1, dtype=jnp.int32)
    turn_counts = places[:, None] * band_ids[None, :] % length
    angles = turn_counts.astype(jnp.float32) * (2.0 * math.pi / length)
    ramp_vals = places.astype(jnp.float32)[:, None] / length
    return jnp.concatenate([ramp_vals, jnp.cos(angles), jnp.sin(angles)], axis=1)


def decay_rates(channels):
    return 0.3 * 10.0 ** (channels.astype(jnp.float32) / (D - 1))


def dft_tables(blocks, block_len):
    doubled = 2 * blocks
    span_total = doubled * block_len
    frequency = jnp.arange(doubled, dtype=jnp.int32)
    places = jnp.arange(blocks, dtype=jnp.int32)
    inner_idx = jnp.arange(block_len, dtype=jnp.int32)
    outer_angle = (frequency[:, None] * places[None, :] % doubled).astype(jnp.float32) * (
        2.0 * math.pi / doubled
    )
    twist_angle = (frequency[:, None] * inner_idx[None, :] % span_total).astype(jnp.float32) * (
        2.0 * math.pi / span_total
    )
    inner_angle = (inner_idx[:, None] * inner_idx[None, :] % block_len).astype(jnp.float32) * (
        2.0 * math.pi / block_len
    )
    return (
        jnp.cos(outer_angle),
        jnp.sin(outer_angle),
        jnp.cos(twist_angle),
        jnp.sin(twist_angle),
        jnp.cos(inner_angle),
        jnp.sin(inner_angle),
    )


def along_block(values, table):
    return jnp.einsum("...kb,bj->...kj", values, table, precision=precise)


def to_spectrum(signal, tables):
    outer_cos, outer_sin, twist_cos, twist_sin, inner_cos, inner_sin = tables
    first_re = jnp.einsum("kp,...pb->...kb", outer_cos, signal, precision=precise)
    first_im = -jnp.einsum("kp,...pb->...kb", outer_sin, signal, precision=precise)
    turned_re = first_re * twist_cos + first_im * twist_sin
    turned_im = first_im * twist_cos - first_re * twist_sin
    spec_re = along_block(turned_re, inner_cos) + along_block(turned_im, inner_sin)
    spec_im = along_block(turned_im, inner_cos) - along_block(turned_re, inner_sin)
    return (spec_re, spec_im)


def from_spectrum(spec_re, spec_im, tables):
    outer_cos, outer_sin, twist_cos, twist_sin, inner_cos, inner_sin = tables
    back_re = along_block(spec_re, inner_cos) - along_block(spec_im, inner_sin)
    back_im = along_block(spec_re, inner_sin) + along_block(spec_im, inner_cos)
    turned_re = back_re * twist_cos - back_im * twist_sin
    turned_im = back_re * twist_sin + back_im * twist_cos
    scale_back = 1.0 / (outer_cos.shape[0] * inner_cos.shape[0])
    signal = jnp.einsum("kp,...kb->...pb", outer_cos, turned_re, precision=precise) - jnp.einsum(
        "kp,...kb->...pb", outer_sin, turned_im, precision=precise
    )
    return signal * scale_back


def causal_filter(received, filt_spec, skip_part, tables):
    item_count, chan_count, length = received.shape
    blocks = tables[0].shape[1]
    spec_re, spec_im = to_spectrum(
        received.reshape(item_count, chan_count, blocks, length // blocks), tables
    )
    prod_re = spec_re * filt_spec[0] - spec_im * filt_spec[1]
    prod_im = spec_re * filt_spec[1] + spec_im * filt_spec[0]
    result_sig = from_spectrum(prod_re, prod_im, tables).reshape(item_count, chan_count, length)
    return result_sig + skip_part[:, None] * received


def filter_backward(grad_cols, moved_in, filt_spec, skip_part, tables):
    item_count, chan_count, length = grad_cols.shape
    blocks = tables[0].shape[1]
    grad_re, grad_im = to_spectrum(
        grad_cols.reshape(item_count, chan_count, blocks, length // blocks), tables
    )
    input_re, input_im = to_spectrum(
        moved_in.reshape(item_count, chan_count, blocks, length // blocks), tables
    )
    back_re = grad_re * filt_spec[0] + grad_im * filt_spec[1]
    back_im = grad_im * filt_spec[0] - grad_re * filt_spec[1]
    grad_u_cols = (
        from_spectrum(back_re, back_im, tables).reshape(item_count, chan_count, length)
        + skip_part[:, None] * grad_cols
    )
    corr_re = grad_re * input_re + grad_im * input_im
    corr_im = grad_im * input_re - grad_re * input_im
    grad_filt = jnp.sum(from_spectrum(corr_re, corr_im, tables), axis=0).reshape(chan_count, length)
    grad_skip_part = jnp.sum(grad_cols * moved_in, axis=(0, 2))
    return (grad_u_cols, grad_filt, grad_skip_part)


def local_filter(first, second, features, select, group_idx, chan_local):
    hidden_pre = jnp.dot(features, first, precision=precise)
    hidden_act = jnp.sin(hidden_pre)
    chan_width = second.shape[1]
    second_part = jnp.dot(second, select, precision=precise)
    channel_ids = group_idx * chan_width + chan_local
    length = features.shape[0]
    ramp_vals = jnp.arange(length, dtype=jnp.int32).astype(jnp.float32) / length
    decay_part = jnp.exp(-decay_rates(channel_ids)[:, None] * ramp_vals[None, :])
    filt_cols = jnp.einsum("hc,th->ct", second_part, hidden_act, precision=precise) * decay_part
    return (filt_cols, hidden_pre, hidden_act, second_part, decay_part)


def filter_mlp_backward(grad_filt, features, filter_parts):
    hidden_pre, hidden_act, second_part, decay_part = filter_parts
    grad_shaped = grad_filt * decay_part
    grad_second_part = jnp.einsum("ct,th->hc", grad_shaped, hidden_act, precision=precise)
    grad_act = jnp.einsum("ct,hc->th", grad_shaped, second_part, precision=precise)
    grad_first = jnp.einsum(
        "tf,th->fh", features, grad_act * jnp.cos(hidden_pre), precision=precise
    )
    return (grad_first, grad_second_part)


def embed_lookup(ids, live, embed, seq_rank):
    tok_rows = ids.shape[1]
    places = seq_rank * tok_rows + jnp.arange(tok_rows, dtype=jnp.int32)
    keep_mask = (places[None, :] < live[:, None]).astype(jnp.float32)
    vocab_ids = jnp.arange(embed.shape[0], dtype=jnp.int32)
    onehot = (ids[:, :, None] == vocab_ids[None, None, :]).astype(jnp.float32) * keep_mask[
        :, :, None
    ]
    stream = jnp.einsum("mtv,vd->mtd", onehot, embed, precision=precise)
    return (stream, onehot, keep_mask)


def channel_total(partial_sum):
    return lax.psum(partial_sum, "ch")


def input_total(partial_sum):
    return lax.psum(partial_sum, "ch")


def layer_forward(stream, params, filt_spec, skip_part, tables):
    norm_gains, w_in, kernel, w_out, w_up, w_down = params
    normed = layer_norm(stream, norm_gains[0]).astype(jnp.bfloat16)
    mixed_in = jnp.einsum("mtd,dgc->mtgc", normed, w_in, preferred_element_type=jnp.float32)
    rim_rows = passed_along(mixed_in[:, -2:], "seq", 1)
    padded = jnp.concatenate([rim_rows, mixed_in], axis=1)
    micro_count, tok_rows = (mixed_in.shape[0], mixed_in.shape[1])
    chan_width = mixed_in.shape[3]
    gate_vals = (
        kernel[0] * mixed_in
        + kernel[1] * padded[:, 1 : tok_rows + 1]
        + kernel[2] * padded[:, 0:tok_rows]
    )
    product_in = gate_vals[:, :, 2] * gate_vals[:, :, 1]
    flat_rows = jnp.swapaxes(product_in, 1, 2).reshape(1, micro_count * chan_width, tok_rows)
    received = lax.all_to_all(flat_rows, "seq", split_axis=1, concat_axis=2, tiled=True)
    result_sig = causal_filter(received, filt_spec, skip_part, tables)
    conv_flat = lax.all_to_all(result_sig, "seq", split_axis=2, concat_axis=1, tiled=True)
    conv_out = jnp.swapaxes(conv_flat.reshape(micro_count, chan_width, tok_rows), 1, 2)
    gated_out = (conv_out * gate_vals[:, :, 0]).astype(jnp.bfloat16)
    mid_state = stream + channel_total(
        jnp.einsum("mtc,cd->mtd", gated_out, w_out, preferred_element_type=jnp.float32)
    )
    normed_mid = layer_norm(mid_state, norm_gains[1]).astype(jnp.bfloat16)
    pre_act = jnp.einsum("mtd,df->mtf", normed_mid, w_up, preferred_element_type=jnp.float32)
    hidden = jax.nn.gelu(pre_act).astype(jnp.bfloat16)
    new_stream = mid_state + channel_total(
        jnp.einsum("mtf,fd->mtd", hidden, w_down, preferred_element_type=jnp.float32)
    )
    kept_vals = (
        stream,
        normed,
        mixed_in,
        padded,
        gate_vals,
        received,
        conv_out,
        gated_out,
        mid_state,
        normed_mid,
        pre_act,
        hidden,
    )
    return (new_stream, kept_vals)


def layer_backward(grad_stream, kept_vals, params, filt_spec, skip_part, tables):
    norm_gains, w_in, kernel, w_out, w_up, w_down = params
    (
        stream,
        normed,
        mixed_in,
        padded,
        gate_vals,
        moved_in,
        conv_out,
        gated_out,
        mid_state,
        normed_mid,
        pre_act,
        hidden,
    ) = kept_vals
    micro_count, tok_rows = (mixed_in.shape[0], mixed_in.shape[1])
    chan_width = mixed_in.shape[3]
    grad_low = grad_stream.astype(jnp.bfloat16)
    grad_down = jnp.einsum("mtf,mtd->fd", hidden, grad_low, preferred_element_type=jnp.float32)
    grad_hidden = jnp.einsum("mtd,fd->mtf", grad_low, w_down, preferred_element_type=jnp.float32)
    _, gelu_back = jax.vjp(jax.nn.gelu, pre_act)
    grad_pre = gelu_back(grad_hidden)[0].astype(jnp.bfloat16)
    grad_up = jnp.einsum("mtd,mtf->df", normed_mid, grad_pre, preferred_element_type=jnp.float32)
    grad_normed_mid = input_total(
        jnp.einsum("mtf,df->mtd", grad_pre, w_up, preferred_element_type=jnp.float32)
    )
    _, norm_back_mid = jax.vjp(layer_norm, mid_state, norm_gains[1])
    grad_mid_norm, grad_gain_mid = norm_back_mid(grad_normed_mid)
    grad_mid = grad_stream + grad_mid_norm
    grad_mid_low = grad_mid.astype(jnp.bfloat16)
    grad_out = jnp.einsum(
        "mtc,mtd->cd", gated_out, grad_mid_low, preferred_element_type=jnp.float32
    )
    grad_gated = jnp.einsum("mtd,cd->mtc", grad_mid_low, w_out, preferred_element_type=jnp.float32)
    grad_conv = grad_gated * gate_vals[:, :, 0]
    grad_first_gate = grad_gated * conv_out
    grad_flat = jnp.swapaxes(grad_conv, 1, 2).reshape(1, micro_count * chan_width, tok_rows)
    grad_cols = lax.all_to_all(grad_flat, "seq", split_axis=1, concat_axis=2, tiled=True)
    grad_u_cols, grad_filt, grad_skip_part = filter_backward(
        grad_cols, moved_in, filt_spec, skip_part, tables
    )
    grad_back_flat = lax.all_to_all(grad_u_cols, "seq", split_axis=2, concat_axis=1, tiled=True)
    grad_product = jnp.swapaxes(grad_back_flat.reshape(micro_count, chan_width, tok_rows), 1, 2)
    grad_gates = jnp.stack(
        [grad_first_gate, grad_product * gate_vals[:, :, 2], grad_product * gate_vals[:, :, 1]],
        axis=2,
    )
    rim_back = passed_along(grad_gates[:, :2], "seq", -1)
    extended = jnp.concatenate([grad_gates, rim_back], axis=1)
    grad_mixed = (
        kernel[0] * grad_gates
        + kernel[1] * extended[:, 1 : tok_rows + 1]
        + kernel[2] * extended[:, 2 : tok_rows + 2]
    )
    grad_kernel = jnp.stack(
        [
            jnp.sum(grad_gates * mixed_in, axis=(0, 1)),
            jnp.sum(grad_gates * padded[:, 1 : tok_rows + 1], axis=(0, 1)),
            jnp.sum(grad_gates * padded[:, 0:tok_rows], axis=(0, 1)),
        ]
    )
    grad_mixed_low = grad_mixed.astype(jnp.bfloat16)
    grad_in = jnp.einsum(
        "mtd,mtgc->dgc", normed, grad_mixed_low, preferred_element_type=jnp.float32
    )
    grad_normed = input_total(
        jnp.einsum("mtgc,dgc->mtd", grad_mixed_low, w_in, preferred_element_type=jnp.float32)
    )
    _, norm_back_in = jax.vjp(layer_norm, stream, norm_gains[0])
    grad_stream_norm, grad_gain_in = norm_back_in(grad_normed)
    grad_before = grad_mid + grad_stream_norm
    layer_grads = (
        jnp.stack([grad_gain_in, grad_gain_mid]),
        grad_in,
        grad_kernel,
        grad_skip_part,
        grad_out,
        grad_up,
        grad_down,
    )
    return (grad_before, layer_grads, grad_filt)


def local(
    ids,
    live,
    embed,
    norm_gain,
    in_weight,
    short_kernel,
    filter_first,
    filter_second,
    skip_gain,
    out_weight,
    up_weight,
    down_weight,
    cotangent,
):
    seq_count = lax.axis_size("seq")
    seq_rank = lax.axis_index("seq")
    group_idx = lax.axis_index("ch")
    micro_count = ids.shape[0]
    tok_rows = ids.shape[1]
    length = tok_rows * seq_count
    chan_width = in_weight.shape[3]
    own_rows = micro_count * chan_width // seq_count
    layer_count = in_weight.shape[0]
    row_start = seq_rank * own_rows
    row_ids = row_start + jnp.arange(own_rows, dtype=jnp.int32)
    chan_local = row_ids % chan_width
    first_rows = (row_ids < chan_width).astype(jnp.float32)
    select = (jnp.arange(chan_width, dtype=jnp.int32)[:, None] == chan_local[None, :]).astype(
        jnp.float32
    )
    tables = dft_tables(seq_count, tok_rows)
    features = position_features(length)
    ramp_row = jnp.arange(length, dtype=jnp.int32).astype(jnp.float32) / length
    stream, onehot, keep_mask = embed_lookup(ids, live, embed, seq_rank)
    filters = []
    for level_idx in range(layer_count):
        filt_cols, hidden_pre, hidden_act, second_part, decay_part = local_filter(
            filter_first[level_idx],
            filter_second[level_idx],
            features,
            select,
            group_idx,
            chan_local,
        )
        filt_spec = to_spectrum(filt_cols.reshape(own_rows, seq_count, tok_rows), tables)
        skip_part = jnp.dot(skip_gain[level_idx], select, precision=precise)
        penalty_grad = 0.5 * length * ramp_row[None, :] * filt_cols * first_rows[:, None]
        params = (
            norm_gain[level_idx],
            in_weight[level_idx],
            short_kernel[level_idx],
            out_weight[level_idx],
            up_weight[level_idx],
            down_weight[level_idx],
        )
        filters.append(
            (
                params,
                filt_spec,
                skip_part,
                (hidden_pre, hidden_act, second_part, decay_part),
                penalty_grad,
            )
        )
    stored = []
    for level_idx in range(layer_count):
        params, filt_spec, skip_part, _, _ = filters[level_idx]
        layer_input = stream
        stream, kept_vals = layer_forward(stream, params, filt_spec, skip_part, tables)
        stored.append(layer_input)
    block_out = stream * keep_mask[:, :, None]
    grad_stream = cotangent * keep_mask[:, :, None]
    collected = [None] * layer_count
    first_grads = [None] * layer_count
    grad_embed = None
    for level_idx in reversed(range(layer_count)):
        params, filt_spec, skip_part, filter_parts, penalty_grad = filters[level_idx]
        _, kept_vals = layer_forward(stored[level_idx], params, filt_spec, skip_part, tables)
        grad_stream, layer_grads, grad_filt = layer_backward(
            grad_stream, kept_vals, params, filt_spec, skip_part, tables
        )
        grad_first, grad_second_part = filter_mlp_backward(
            grad_filt + penalty_grad, features, filter_parts
        )
        first_grads[level_idx] = grad_first
        grad_second = jnp.dot(grad_second_part, select.T, precision=precise)
        grad_skip = jnp.dot(layer_grads[3], select.T, precision=precise)
        gain_grad, in_grad, kernel_grad, _, out_grad, up_grad, down_grad = layer_grads
        if level_idx == 0:
            embed_part = jnp.einsum("mtv,mtd->vd", onehot, grad_stream, precision=precise)
            summed = lax.psum(
                (
                    gain_grad,
                    in_grad,
                    kernel_grad,
                    grad_second,
                    grad_skip,
                    out_grad,
                    up_grad,
                    down_grad,
                    embed_part,
                ),
                "seq",
            )
            collected[level_idx] = summed[:8]
            grad_embed = summed[8]
        else:
            collected[level_idx] = lax.psum(
                (
                    gain_grad,
                    in_grad,
                    kernel_grad,
                    grad_second,
                    grad_skip,
                    out_grad,
                    up_grad,
                    down_grad,
                ),
                "seq",
            )
    stacked = [
        jnp.stack([collected[level_idx][member] for level_idx in range(layer_count)])
        for member in range(8)
    ]
    filter_grads = lax.psum(jnp.stack(first_grads), ("seq", "ch"))
    return (
        block_out,
        grad_embed,
        stacked[0],
        stacked[1],
        stacked[2],
        filter_grads,
        stacked[3],
        stacked[4],
        stacked[5],
        stacked[6],
        stacked[7],
    )


HALO = 16
FEAT_ROWS = 40
ROOT_HALF = math.sqrt(0.5)
GELU_A = math.sqrt(2.0 / math.pi)
GELU_B = 0.044715
BLOCKS = 8
BLOCK = 256
KINDS = 9
VMEM_LIMIT = 8 * 2**20
VMEM_LIMITS = dict(turn_back_kernel=20 * 2**20, back_first_kernel=16 * 2**20)
FLOPS, FEW_FLOPS, MANY_FLOPS = 10**10, 10**8, 10**12
FLOPS_OF = dict(conv_first1=100000000, pair5=10000000000, grad_freq1=30000000000, last1=1000000000, conv_second1=3000000000, join_weights2=100000000)
CALLS = collections.Counter()
f32 = jnp.float32
bf16 = jnp.bfloat16


class Numbers:
    def __init__(self, table):
        self.table = table

    def __getitem__(self, row):
        return self.table[row, 0]


CORE, GROUP, LIVE, WHICH, SPOT, HOLDER, BIT1, BIT2, BIT3 = range(9)
NUMBER_ROWS = 16


def bring(pairs, done):
    copies = [pltpu.make_async_copy(far, near, done.at[i]) for i, (far, near) in enumerate(pairs)]
    for copy in copies:
        copy.start()
    for copy in copies:
        copy.wait()


def numbers_kernel(*refs):
    far, (table, own_ids, cot, pack, part), near, done = refs[:13], refs[13:18], refs[18:30], refs[30]
    far_live, far_ids, far_cot, far_embed, far_gain, far_in, far_second, far_short, far_skip, far_out, far_up, far_down, far_in1 = far
    live, ids, embed, gain, in_own, second, short, skip, raw_out, raw_up, raw_down, in1 = near
    rank, group = lax.axis_index("seq"), lax.axis_index("ch")
    bring(
        (
            (far_live, live), (far_ids, ids), (far_cot.at[group], cot.at[0]), (far_embed, embed), (far_gain, gain),
            (far_in.at[0], in_own), (far_second, second), (far_short, short), (far_skip, skip), (far_out.at[0], raw_out),
            (far_up.at[0], raw_up), (far_down.at[0], raw_down), (far_in1.at[1], in1),
        ),
        done,
    )
    fill_pack(embed, gain, in_own, second, short, skip, pack)
    core, half = rank % 2, lax.axis_size("seq") // 2
    first = group == 0
    holder = jnp.where(rank // half == core, 1, 0)
    values = (core, group, None, group + core - 2 * group * core, rank % half, holder, rank // 2 % 2, rank // 4 % 2, rank // 8 % 2)
    for row, value in enumerate(values):
        if row != LIVE:
            table[row : row + 1, :] = jnp.full((1, 128), value, jnp.int32)
    chosen = jnp.where(first, live[0:1, 0:1], live[0:1, 1:2])
    table[LIVE : LIVE + 1, :] = jnp.broadcast_to(chosen, (1, 128))
    own_ids[0] = jnp.broadcast_to(jnp.where(first, ids[0:1, :], ids[1:2, :]), own_ids.shape[1:])
    s = Numbers(table)
    fill_part(s, raw_out, raw_up, raw_down, part)
    fill_in_part(s, in1, part.at[1152:1536])


def in_hbm(value):
    return pltpu.with_memory_space_constraint(value, pltpu.HBM)


def start(body, outs, *arrays, scratch):
    vmem, far = pl.BlockSpec(memory_space=pltpu.VMEM), pl.BlockSpec(memory_space=pltpu.HBM)
    return pl.pallas_call(
        body, out_shape=outs, in_specs=[far] * len(arrays), out_specs=[vmem] * len(outs), name=body.__name__,
        scratch_shapes=list(scratch),
        cost_estimate=pl.CostEstimate(flops=MANY_FLOPS, bytes_accessed=1, transcendentals=0),
        compiler_params=pltpu.CompilerParams(vmem_limit_bytes=VMEM_LIMIT),
    )(*(in_hbm(v) for v in arrays))


def run(body, outs, scalars, *arrays, scratch=(), after=(), hbm=(), flops=None, hbm_outs=(), aliases=(), token=False):
    vmem = pl.BlockSpec(memory_space=pltpu.VMEM)
    far, wait = pl.BlockSpec(memory_space=pltpu.HBM), pl.BlockSpec(memory_space=pl.ANY)
    single = not isinstance(outs, (list, tuple))
    shapes = [outs] if single else list(outs)
    count = len(shapes)
    shapes += [arr(8, 128)] * token
    used, waits = 1 + len(arrays), len(after)

    def call(table, *refs):
        given, rest = refs[: used - 1], refs[used - 1 + waits :]
        body(Numbers(table), *given, *rest[:count], *rest[count + token :])
        if token:
            rest[count][...] = jnp.zeros((8, 128), f32)

    inner = getattr(body, "func", body)
    CALLS[inner.__name__] += 1
    flops = flops or FLOPS_OF.get(f"{inner.__name__[:-7]}{CALLS[inner.__name__]}", FLOPS)
    result = pl.pallas_call(
        call,
        out_shape=shapes,
        in_specs=[vmem] + [far if i in hbm else vmem for i in range(len(arrays))] + [wait] * waits,
        out_specs=[far if i in hbm_outs else vmem for i in range(len(shapes))],
        input_output_aliases={1 + a: b for a, b in aliases},
        scratch_shapes=list(scratch),
        compiler_params=pltpu.CompilerParams(vmem_limit_bytes=VMEM_LIMITS.get(inner.__name__, VMEM_LIMIT)),
        cost_estimate=pl.CostEstimate(flops=flops, bytes_accessed=1, transcendentals=0),
        name=inner.__name__,
    )(scalars, *(in_hbm(v) if i in hbm else v for i, v in enumerate(arrays)), *after)
    return result[0] if len(shapes) == 1 else result


def arr(*shape, kind=f32):
    return jax.ShapeDtypeStruct(shape, kind)


def mm(a, b):
    return jnp.dot(a, b, preferred_element_type=f32)


def mm_nt(a, b):
    return lax.dot_general(a, b, (((1,), (1,)), ((), ())), preferred_element_type=f32)


def mm_tn(a, b):
    return lax.dot_general(a, b, (((0,), (0,)), ((), ())), preferred_element_type=f32)


def split(a):
    high = a.astype(bf16)
    return high, (a - high.astype(f32)).astype(bf16)


def unit(rows):
    center = rows - jnp.mean(rows, axis=-1, keepdims=True)
    scale = lax.rsqrt(jnp.mean(center * center, axis=-1, keepdims=True) + epsilon)
    return center * scale, scale


def unit_back(grad, normal, scale):
    inner = jnp.mean(grad * normal, axis=-1, keepdims=True)
    return scale * (grad - jnp.mean(grad, axis=-1, keepdims=True) - normal * inner)


def every(count, step):
    for i in range(count):
        step(i, 0)


def at(start, size, unit_rows=16):
    return pl.ds(start if isinstance(start, int) else pl.multiple_of(start, unit_rows), size)


def dft_table():
    turns = np.outer(np.arange(BLOCK), np.arange(BLOCK)) % BLOCK
    angle = 2.0 * np.pi * turns / BLOCK
    return np.concatenate([np.cos(angle), np.sin(angle)], axis=1).astype(np.float32)


def twiddle_table():
    angle = 2.0 * np.pi * np.outer(np.arange(BLOCK), np.arange(1, KINDS)) / (2 * BLOCKS * BLOCK)
    return np.concatenate([np.cos(angle), np.sin(angle)], axis=1).astype(np.float32)


def twiddle_kernel(s, narrow, out):
    for kind in range(KINDS - 1):
        for part in range(2):
            column = (KINDS - 1) * part + kind
            out[kind, part] = jnp.broadcast_to(narrow[:, column : column + 1], (BLOCK, 128))


def feature_table(length):
    places = np.arange(length)
    turns = np.outer(places, np.arange(1, (FEAT - 1) // 2 + 1)) % length
    angle = 2.0 * np.pi * turns / length
    ramp = places[:, None] / length
    return np.concatenate([ramp, np.cos(angle), np.sin(angle)], axis=1).astype(np.float32)


def thirds(values):
    low = lambda v: v.astype(ml_dtypes.bfloat16).astype(np.float32)
    first = low(values)
    second = low(values - first)
    return first, second, low(values - first - second)


def feature_parts(length):
    first, second, third = thirds(np.pad(feature_table(length), ((0, 0), (0, FEAT_ROWS - FEAT))))
    return np.pad(np.concatenate([first, first, second, second, first, third], axis=1), ((0, 0), (0, 256 - 6 * FEAT_ROWS)))


def rate_table():
    return (0.3 * 10.0 ** (np.arange(D) / (D - 1))).astype(np.float32).reshape(2, 1, D // 2)


def four_real(a, b, c, d):
    s, m, t, n = a + c, a - c, b + d, b - d
    hn, ht = ROOT_HALF * n, ROOT_HALF * t
    return (s + t, s - t, (a + hn, -(ht + c)), (m, -n), (a - hn, c - ht))


def turn(k):
    angle = 2.0 * math.pi * k / (2 * BLOCKS)
    return math.cos(angle), math.sin(angle)


def put_pair(stage, kind, row, re, im):
    rows = re.shape[0]
    re, im = re.astype(bf16), im.astype(bf16)
    stage[kind, pl.ds(row, rows), 0:128] = re
    stage[kind, pl.ds(row, rows), 128:256] = im
    stage[kind, pl.ds(row + BLOCK, rows), 0:128] = im
    stage[kind, pl.ds(row + BLOCK, rows), 128:256] = -re


def put_pair_back(stage, kind, row, re, im):
    rows = re.shape[0]
    re, im = re.astype(bf16), im.astype(bf16)
    stage[kind, pl.ds(row, rows), 0:128] = re
    stage[kind, pl.ds(row, rows), 128:256] = im
    stage[kind, pl.ds(row + BLOCK, rows), 0:128] = -im
    stage[kind, pl.ds(row + BLOCK, rows), 128:256] = re


def all_kinds(dft, stage, out):
    table = dft[...]
    for kind in range(KINDS):
        out[kind] = mm(table, stage[kind])


def to_freq(load, dft, twiddle, stage, out):
    def chunk(step, carry):
        row = step * 16
        u = [load(p, row) for p in range(BLOCKS)]
        e0, e4, e1, e2, e3 = four_real(u[0], u[2], u[4], u[6])
        o0, o4, o1, o2, o3 = four_real(u[1], u[3], u[5], u[7])

        def put(kind, re, im):
            c, s = twiddle[kind - 1, 0, pl.ds(row, 16), :], twiddle[kind - 1, 1, pl.ds(row, 16), :]
            put_pair(stage, kind, row, re * c + im * s, im * c - re * s)

        put_pair(stage, 0, row, e0 + o0, jnp.zeros_like(e0))
        last = e0 - o0
        c, s = twiddle[7, 0, pl.ds(row, 16), :], twiddle[7, 1, pl.ds(row, 16), :]
        put_pair(stage, 8, row, last * c, -(last * s))
        put(4, e4, -o4)
        for k, (er, ei), (orr, oi) in ((1, e1, o1), (2, e2, o2), (3, e3, o3)):
            c, s = turn(k)
            wr, wi = orr * c + oi * s, oi * c - orr * s
            put(k, er + wr, ei + wi)
            put(8 - k, er - wr, wi - ei)
        return carry

    every(BLOCK // 16, chunk)
    all_kinds(dft, stage, out)


def from_freq(dft, twiddle, stage, back, store):
    all_kinds(dft, stage, back)

    def chunk(step, carry):
        row = step * 16

        def get(kind):
            re = back[kind, pl.ds(row, 16), 0:128]
            im = back[kind, pl.ds(row, 16), 128:256]
            c, s = twiddle[kind - 1, 0, pl.ds(row, 16), :], twiddle[kind - 1, 1, pl.ds(row, 16), :]
            return re * c - im * s, re * s + im * c

        first = 0.5 * back[0, pl.ds(row, 16), 0:128]
        last = 0.5 * get(8)[0]
        mid_re, mid_im = get(4)
        even, odd = {}, {}
        for k in (1, 2, 3):
            ar, ai = get(k)
            br, bi = get(8 - k)
            even[k] = (ar + br, ai - bi)
            c, s = turn(k)
            dr, di = ar - br, ai + bi
            odd[k] = (dr * c - di * s, dr * s + di * c)
        for shift, base, extra, part in (
            (0, first + last, mid_re, even),
            (1, first - last, -mid_im, odd),
        ):
            (r1, i1), (r2, i2), (r3, i3) = part[1], part[2], part[3]
            plus, minus = base + extra, base - extra
            diff, both = ROOT_HALF * (r1 - r3), ROOT_HALF * (i1 + i3)
            store(shift, row, plus + (r1 + r2 + r3))
            store(shift + 2, row, minus - i2 + (diff - both))
            store(shift + 4, row, plus - r2 - (i1 - i3))
            store(shift + 6, row, minus + i2 - (diff + both))
        return carry

    every(BLOCK // 16, chunk)


def times(first, second, stage, conj):
    def chunk(step, carry):
        row = step * 16
        for kind in range(KINDS):
            fr = first[kind, pl.ds(row, 16), 0:128]
            fi = first[kind, pl.ds(row, 16), 128:256]
            ur = second[kind, pl.ds(row, 16), 0:128]
            ui = second[kind, pl.ds(row, 16), 128:256]
            if conj:
                put_pair_back(stage, kind, row, fr * ur + fi * ui, fr * ui - fi * ur)
            else:
                put_pair_back(stage, kind, row, fr * ur - fi * ui, fr * ui + fi * ur)
        return carry

    every(BLOCK // 16, chunk)


SPECTRUM = (KINDS, BLOCK, 256)


def stage_scratch():
    return pltpu.VMEM((KINDS, 2 * BLOCK, 256), bf16)


def spec_scratch():
    return pltpu.VMEM(SPECTRUM, f32)


PACK_SECOND = 48
PACK_SHORT = 176
PACK_SKIP = 194
PACK_ROWS = 200


def fill_pack(embed, gain, in_own, second, short, skip, out):
    normal, _ = unit(embed[...])
    low = (normal * gain[0, 0:1, :]).astype(bf16)
    for g in range(3):
        out[16 * g : 16 * g + 16, :] = mm(low, in_own[g])
    for l in range(2):
        out[PACK_SECOND + 64 * l : PACK_SECOND + 64 * l + 64, :] = second[l]
        for k in range(3):
            for g in range(3):
                row = PACK_SHORT + 9 * l + 3 * k + g
                out[row : row + 1, :] = short[k, g, l : l + 1, :]
    out[PACK_SKIP : PACK_SKIP + 2, :] = skip[...]
    out[PACK_SKIP + 2 : PACK_ROWS, :] = jnp.zeros((PACK_ROWS - PACK_SKIP - 2, 128), f32)


def table_kernel(s, own, peer, embed, mine_out, other_out, conv_table, gate_table):
    first = s[CORE] == 0
    mine = jnp.where(first, own[...], peer[...])
    other = jnp.where(first, peer[...], own[...])
    mine_out[...] = mine
    other_out[...] = other

    def fill(table, lanes, parts):
        whole = jnp.concatenate(parts, axis=0)
        high, low = split(whole)
        table[0:48, lanes] = high
        table[48:96, lanes] = low
        table[96:128, lanes] = jnp.zeros((32, 128), bf16)

    def gate(pack, g):
        parts = []
        for k in range(3):
            row = PACK_SHORT + 3 * k + g
            parts.append(pack[16 * g : 16 * g + 16] * pack[row : row + 1])
        return parts

    fill(conv_table, slice(0, 128), gate(mine, 1))
    fill(conv_table, slice(128, 256), gate(mine, 2))
    fill(gate_table, slice(0, 128), gate(mine, 0))
    fill(gate_table, slice(128, 256), gate(other, 0))
    zero = jnp.zeros((16, 128), f32)
    fill(gate_table, slice(256, 384), [embed[:, 0:128], zero, zero])
    fill(gate_table, slice(384, 512), [embed[:, 128:256], zero, zero])


def onehot_kernel(s, ids, out, turned, work):
    live = s[LIVE]
    count, _, width = ids.shape
    work[0:HALO, :] = jnp.zeros((HALO, 128), f32)
    work[HALO + count * width : 2 * HALO + count * width, :] = jnp.zeros((HALO, 128), f32)
    vocab = lax.broadcasted_iota(jnp.int32, (128, width), 0) % 16
    place = lax.broadcasted_iota(jnp.int32, (128, width), 1)
    for i in range(count):
        token = jnp.broadcast_to(ids[i, 0:1, :], (128, width))
        hit = (token == vocab) & (place + i * width < live)
        work[HALO + width * i : HALO + width * (i + 1), :] = jnp.where(hit, 1.0, 0.0).T
    lane = lax.broadcasted_iota(jnp.int32, (width, 128), 1) % 48 // 16
    used = lax.broadcasted_iota(jnp.int32, (width, 128), 1) < 96
    half = count // 2
    for i in range(count):
        row = HALO + width * i
        now = work[row : row + width, :]
        one = work[row - 1 : row - 1 + width, :]
        two = work[row - 2 : row - 2 + width, :]
        picked = jnp.where(lane == 0, now, jnp.where(lane == 1, one, two))
        picked = jnp.where(used, picked, 0.0)
        out[row : row + width, :] = picked.astype(bf16)
        turned[i // half, :, width * (i % half) : width * (i % half + 1)] = picked.T.astype(bf16)
    out[0:HALO, :] = jnp.zeros((HALO, 128), bf16)
    out[HALO + count * width : 2 * HALO + count * width, :] = jnp.zeros((HALO, 128), bf16)


def sine_and_cosine(angle):
    turns = jnp.round(angle * (2.0 / math.pi))
    x = ((angle - turns * 1.5703125) - turns * 4.837512969970703125e-4) - turns * 7.549789948768648e-8
    z = x * x
    sin = ((-1.9515295891e-4 * z + 8.3321608736e-3) * z - 1.6666654611e-1) * z * x + x
    cos = ((2.443315711809948e-5 * z - 1.388731625493765e-3) * z + 4.166664568298827e-2) * z * z - 0.5 * z + 1.0
    quarter = turns.astype(jnp.int32) & 3
    odd = (quarter & 1) == 1
    first, second = jnp.where(odd, cos, sin), jnp.where(odd, sin, cos)
    first = jnp.where(quarter >= 2, -first, first)
    second = jnp.where((quarter == 1) | (quarter == 2), -second, second)
    return first, second


def sine_kernel(s, feats, firsts, sine, cosine, turned, padded):
    padded[...] = jnp.zeros_like(padded)
    for l in range(2):
        padded[0:FEAT, 64 * l : 64 * l + 64] = firsts[:, l, :]
    both = padded[...]
    cut = lambda v: v.astype(bf16).astype(f32)
    first = cut(both)
    second = cut(both - first)
    third = both - first - second
    fill = jnp.zeros((256 - 6 * FEAT_ROWS, 128), f32)
    weights = jnp.concatenate([first, second, first, second, third, first, fill], axis=0).astype(bf16)
    count = feats.shape[0] // 512

    def chunk(i, carry):
        rows = at(512 * i, 512)
        act, cosine[rows, :] = sine_and_cosine(mm(feats[rows, :], weights))
        sine[rows, 0:128], sine[rows, 128:256] = split(act)
        turned[:, at(512 * i, 512, 256)] = act.T.astype(bf16)
        return carry

    every(count, chunk)


def decay_of(rates, start, rows, length):
    place = (lax.broadcasted_iota(jnp.int32, (rows, 1), 0) + start).astype(f32) / length
    return jnp.exp(-place * rates), place


def filter_kernel(level, s, sine, mine, rates, dft, twiddle, filt, freq, stage):
    length = sine.shape[0]
    rate = rates[s[WHICH]]
    zero = jnp.zeros((64, 128), f32)
    second = mine[PACK_SECOND + 64 * level : PACK_SECOND + 64 * level + 64]
    high, low = split(jnp.concatenate([zero, second] if level else [second, zero], axis=0))
    twice = jnp.concatenate([high, high], axis=0)

    def chunk(i, carry):
        rows = at(512 * i, 512)
        decay, _ = decay_of(rate, 512 * i, 512, length)
        filt[rows, :] = (mm(sine[rows, :], twice) + mm(sine[rows, 0:128], low)) * decay
        return carry

    every(length // 512, chunk)
    to_freq(lambda p, row: filt[pl.ds(BLOCK * p + row, 16), :] * (1.0 / length), dft, twiddle, stage, freq)


def causal(load, skip_row, freq_filt, dft, twiddle, spec, stage, work, line):
    to_freq(load, dft, twiddle, stage, spec)
    times(freq_filt, spec, stage, False)

    def store(p, row, value):
        line[pl.ds(HALO + BLOCK * p + row, 16), :] = value + skip_row * load(p, row)

    from_freq(dft, twiddle, stage, work, store)


def hand_out(s, line, keep, send):
    half = (line.shape[0] - 2 * HALO) // 2
    span = half + 2 * HALO
    k = s[CORE]
    line[0:HALO, :] = jnp.zeros((HALO, 128), f32)
    line[HALO + 2 * half :, :] = jnp.zeros((HALO, 128), f32)
    keep[...] = line[at(half * k, span), :]
    send[...] = line[at(half * (1 - k), span), :]


def conv_first_kernel(s, onehot, conv_table, mine, freq_filt, dft, twiddle, keep, send, spec, product, stage, work, line):
    def chunk(i, carry):
        rows = at(512 * i, 512)
        pair = mm(onehot[at(512 * i + HALO, 512), :], conv_table[...])
        product[rows, :] = pair[:, 0:128] * pair[:, 128:256]
        return carry

    every(product.shape[0] // 512, chunk)
    skip_row = mine[PACK_SKIP : PACK_SKIP + 1, :]
    causal(lambda p, row: product[pl.ds(BLOCK * p + row, 16), :], skip_row, freq_filt, dft, twiddle, spec, stage, work, line)
    hand_out(s, line, keep, send)


def join_rows(s, whole, kept, received):
    half = kept.shape[0]
    whole[at(half * s[CORE], half), :] = kept[...]
    whole[at(half * (1 - s[CORE]), half), :] = received[...]


def conv_second_kernel(s, kept, received, mine, freq_filt, dft, twiddle, keep, send, spec, product, stage, work, line):
    join_rows(s, product, kept, received)
    skip_row = mine[PACK_SKIP + 1 : PACK_SKIP + 2, :]
    causal(lambda p, row: product[pl.ds(BLOCK * p + row, 16), :], skip_row, freq_filt, dft, twiddle, spec, stage, work, line)
    hand_out(s, line, keep, send)


def gelu_parts(p):
    squared = p * p
    th = jnp.tanh(GELU_A * p * (1.0 + GELU_B * squared))
    half = 0.5 * (1.0 + th)
    slope = half + 0.5 * p * (1.0 - th * th) * (GELU_A + (3.0 * GELU_A * GELU_B) * squared)
    return p * half, slope


def gelu_only(p):
    return 0.5 * p * (1.0 + jnp.tanh(GELU_A * p * (1.0 + GELU_B * (p * p))))


def forward_first_kernel(
    s, onehot, gate_table, conv_mine, conv_other, gain, w_out, w_up, w_down, w_in, mine, other,
    keep, send, mid_out, stream_out, gates, mixed,
):
    span = mid_out.shape[0]
    half = span - 2 * HALO
    k = s[CORE]
    taps = [
        jnp.concatenate([pack[PACK_SHORT + 9 + 3 * t + g : PACK_SHORT + 10 + 3 * t + g, :] for g in range(3) for pack in (mine, other)], axis=1)
        for t in range(3)
    ]

    def chunk(i, carry):
        rows = at(span * i, span)
        looked = mm(onehot[at(half * k + span * i, span), :], gate_table[...])
        conv = jnp.concatenate([conv_mine[rows, :], conv_other[rows, :]], axis=1)
        gated = (conv * looked[:, 0:256]).astype(bf16)
        mid = looked[:, 256:512] + mm(gated, w_out[...])
        mid_out[rows, :] = mid
        normal, _ = unit(mid)
        low = (normal * gain[0, 1:2, :]).astype(bf16)
        hidden = gelu_only(mm(low, w_up[...])).astype(bf16)
        stream = mid + mm(hidden, w_down[...])
        stream_out[rows, :] = stream
        normal, _ = unit(stream)
        low = (normal * gain[1, 0:1, :]).astype(bf16)
        mixed[rows, :] = mm(low, w_in[...])
        return carry

    every(1, chunk)
    gates[0:HALO, :] = jnp.zeros((HALO, 768), f32)
    step = 80
    for start in range(HALO, span, step):
        stop = start + step
        gates[start:stop, :] = (
            taps[0] * mixed[start:stop, :]
            + taps[1] * mixed[start - 1 : stop - 1, :]
            + taps[2] * mixed[start - 2 : stop - 2, :]
        )
    own = slice(HALO, HALO + half)
    keep[...] = gates[own, 256:384] * gates[own, 512:640]
    send[...] = gates[own, 384:512] * gates[own, 640:768]


def turn_back_kernel(
    s, conv_mine, conv_other, gates, stream, cot, cot_rim, gain, w_out, w_up, w_down,
    keep, send, grad_x0, grad_mid, block_out, hidden_out, low_out, normed_out, pre_out, gated_out, mid_low_out, gain_out,
    cot_rows, conv_grads,
):
    span = stream.shape[0]
    half = span - 2 * HALO
    k = s[CORE]
    live = s[LIVE]
    cot_rows[0:HALO, :] = jnp.zeros((HALO, 256), f32)
    cot_rows[HALO : HALO + half, :] = cot[...]
    cot_rows[HALO + half :, :] = jnp.where(k == 0, cot_rim[...], 0.0)
    gain_out[...] = jnp.zeros_like(gain_out)

    def chunk(i, carry):
        rows = at(span * i, span)
        local_row = lax.broadcasted_iota(jnp.int32, (span, 1), 0) + span * i
        keep_mask = (local_row + (half * k - HALO) < live).astype(f32)
        own_mask = ((local_row >= HALO) & (local_row < HALO + half)).astype(f32)
        x0 = gates[rows, 0:256]
        conv = jnp.concatenate([conv_mine[rows, :], conv_other[rows, :]], axis=1)
        gated = (conv * x0).astype(bf16)
        gated_out[rows, :] = gated
        mid = stream[rows, :] + mm(gated, w_out[...])
        normal, scale = unit(mid)
        gain_row = gain[1, 1:2, :]
        low = (normal * gain_row).astype(bf16)
        normed_out[rows, :] = low
        act, slope = gelu_parts(mm(low, w_up[...]))
        hidden = act.astype(bf16)
        hidden_out[rows, :] = hidden
        block_out[rows, :] = (mid + mm(hidden, w_down[...])) * keep_mask
        grad = cot_rows[rows, :] * keep_mask
        grad_low = grad.astype(bf16)
        low_out[rows, :] = grad_low
        grad_pre = (slope * mm_nt(grad_low, w_down[...])).astype(bf16)
        pre_out[rows, :] = grad_pre
        grad_normed = mm_nt(grad_pre, w_up[...])
        gain_out[0:1, :] += jnp.sum(grad_normed * normal * own_mask, axis=0, keepdims=True)
        mid_grad = grad + unit_back(grad_normed * gain_row, normal, scale)
        grad_mid[rows, :] = mid_grad
        mid_low = mid_grad.astype(bf16)
        mid_low_out[rows, :] = mid_low
        grad_gated = mm_nt(mid_low, w_out[...])
        conv_grads[rows, :] = grad_gated * x0
        grad_x0[rows, :] = grad_gated * conv
        return carry

    every(1, chunk)
    own = slice(HALO, HALO + half)
    keep[...] = conv_grads[own, 0:128]
    send[...] = conv_grads[own, 128:256]


def conv_back_kernel(s, kept, received, mine, freq_filt, dft, twiddle, keep, send, spec, grads, stage, work, line):
    join_rows(s, grads, kept, received)
    skip_row = mine[PACK_SKIP + 1 : PACK_SKIP + 2, :]
    load = lambda p, row: grads[pl.ds(BLOCK * p + row, 16), :]
    to_freq(load, dft, twiddle, stage, spec)
    times(freq_filt, spec, stage, True)

    def store(p, row, value):
        line[pl.ds(HALO + BLOCK * p + row, 16), :] = value + skip_row * load(p, row)

    from_freq(dft, twiddle, stage, work, store)
    hand_out(s, line, keep, send)


def grad_freq_kernel(s, kept, received, dft, twiddle, spec, grads, stage):
    join_rows(s, grads, kept, received)
    to_freq(lambda p, row: grads[pl.ds(BLOCK * p + row, 16), :], dft, twiddle, stage, spec)


def filter_back(
    level, s, spec_grad, spec_in, grads, product, filt, cosine, sine_turned, mine, rates, feats_turned, dft, twiddle,
    second_out, first_out, skip_out, stage, work, line,
):
    length = filt.shape[0]
    times(spec_in, spec_grad, stage, True)

    def store(p, row, value):
        line[pl.ds(BLOCK * p + row, 16), :] = value

    from_freq(dft, twiddle, stage, work, store)
    rate = rates[s[WHICH]]
    second = mine[PACK_SECOND + 64 * level : PACK_SECOND + 64 * level + 64, :].astype(bf16)
    weight = jnp.where(s[GROUP] == 0, 0.5 * length, 0.0)
    skip_out[...] = jnp.zeros_like(skip_out)
    second_out[...] = jnp.zeros_like(second_out)
    first_out[...] = jnp.zeros_like(first_out)
    for i in range(length // 512):
        rows = slice(512 * i, 512 * (i + 1))
        decay, place = decay_of(rate, 512 * i, 512, length)
        shaped = ((line[rows, :] * (1.0 / length) + (weight * place) * filt[rows, :]) * decay).astype(bf16)
        skip_out[...] += jnp.sum((grads[rows, :] * product[rows, :]).reshape(64, 8, 128), axis=0)
        second_out[...] += mm(sine_turned[64 * level : 64 * level + 64, rows], shaped)
        inner = (mm_nt(shaped, second) * cosine[rows, 64 * level : 64 * level + 64]).astype(bf16)
        first_out[...] += mm(feats_turned[:, rows], inner)


def filter_back_kernel(s, *refs):
    filter_back(1, s, *refs)


def token_back_kernel(
    s, spec_grad, spec_in, grads, product, filt, cosine, sine_turned, mine, rates, feats_turned, dft, twiddle,
    freq_filt, onehot, turned, conv_table, second_out, first_out, skip_out, by_token, stage, work, line,
):
    length = grads.shape[0]
    skip_row = mine[PACK_SKIP : PACK_SKIP + 1, :]
    times(freq_filt, spec_grad, stage, True)

    def store(p, row, value):
        line[pl.ds(BLOCK * p + row, 16), :] = value + skip_row * grads[pl.ds(BLOCK * p + row, 16), :]

    from_freq(dft, twiddle, stage, work, store)
    by_token[...] = jnp.zeros_like(by_token)
    width = turned.shape[2]
    for i in range(length // width):
        rows = slice(width * i, width * (i + 1))
        pair = mm(onehot[HALO + width * i : HALO + width * (i + 1), :], conv_table[...])
        back = line[rows, :]
        gate_grads = jnp.concatenate([back * pair[:, 128:256], back * pair[:, 0:128]], axis=1).astype(bf16)
        by_token[...] += mm(turned[i], gate_grads)[0:48, :]
    filter_back(
        0, s, spec_grad, spec_in, grads, product, filt, cosine, sine_turned, mine, rates, feats_turned, dft, twiddle,
        second_out, first_out, skip_out, stage, work, line,
    )


def back_gates_kernel(
    s, prod_mine, prod_other, grad_x0, gates, mixed, grad_mid, stream, gain, mine, other, w_in,
    grad_stream, normed_out, mixed_low, short_out, gain_out, line,
):
    span = stream.shape[0]
    half = span - 2 * HALO
    taps = [
        jnp.concatenate([pack[PACK_SHORT + 9 + 3 * t + g : PACK_SHORT + 10 + 3 * t + g, :] for g in range(3) for pack in (mine, other)], axis=1)
        for t in range(3)
    ]
    step = 128
    for start in list(range(HALO, HALO + half, step)) + [HALO + half]:
        stop = start + (step if start < HALO + half else HALO)
        for lanes, prod in ((slice(0, 128), prod_mine), (slice(128, 256), prod_other)):
            first, second = slice(256 + lanes.start, 256 + lanes.stop), slice(512 + lanes.start, 512 + lanes.stop)
            product = prod[start:stop, :]
            line[start:stop, lanes] = product * gates[start:stop, second]
            line[start:stop, first] = product * gates[start:stop, first]
    short_out[...] = jnp.zeros_like(short_out)
    gain_out[...] = jnp.zeros_like(gain_out)
    for start in range(HALO, HALO + half, step):
        stop = start + step
        for g in range(3):
            lanes = slice(256 * g, 256 * g + 256)
            values = mixed[start:stop, lanes]
            total = None
            for t in range(3):
                shifted = grad_x0[start + t : stop + t, :] if g == 0 else line[start + t : stop + t, 256 * g - 256 : 256 * g]
                part = taps[t][:, lanes] * shifted
                total = part if total is None else total + part
                short_out[t, :, lanes] += jnp.sum((shifted * values).reshape(step // 8, 8, 256), axis=0)
            mixed_low[start - HALO : stop - HALO, lanes] = total.astype(bf16)

    def chunk(i, carry):
        rows = at(512 * i, 512)
        wide = at(512 * i + HALO, 512)
        normal, scale = unit(stream[wide, :])
        gain_row = gain[1, 0:1, :]
        normed_out[rows, :] = (normal * gain_row).astype(bf16)
        grad_normed = mm_nt(mixed_low[rows, :], w_in[...])
        gain_out[0:1, :] += jnp.sum(grad_normed * normal, axis=0, keepdims=True)
        grad_stream[rows, :] = grad_mid[wide, :] + unit_back(grad_normed * gain_row, normal, scale)
        return carry

    every(half // 512, chunk)


def back_first_kernel(
    s, grad_stream, mid, onehot, turned, gate_table, conv_mine, conv_other, gain, w_out, w_up, w_down,
    keep, send, hidden_out, low_out, normed_out, pre_out, gated_out, mid_low_out, by_token, gain_out,
):
    half = grad_stream.shape[0]
    k = s[CORE]
    by_token[...] = jnp.zeros_like(by_token)
    gain_out[...] = jnp.zeros_like(gain_out)

    def chunk(i, carry):
        rows = at(half * i, half)
        wide = at(half * i + HALO, half)
        hot = onehot[at(half * k + half * i + HALO, half), :]
        x0 = mm(hot, gate_table[:, 0:256])
        conv = jnp.concatenate([conv_mine[wide, :], conv_other[wide, :]], axis=1)
        gated_out[rows, :] = (conv * x0).astype(bf16)
        normal, scale = unit(mid[wide, :])
        gain_row = gain[0, 1:2, :]
        low = (normal * gain_row).astype(bf16)
        normed_out[rows, :] = low
        act, slope = gelu_parts(mm(low, w_up[...]))
        hidden_out[rows, :] = act.astype(bf16)
        grad = grad_stream[rows, :]
        grad_low = grad.astype(bf16)
        low_out[rows, :] = grad_low
        grad_pre = (slope * mm_nt(grad_low, w_down[...])).astype(bf16)
        pre_out[rows, :] = grad_pre
        grad_normed = mm_nt(grad_pre, w_up[...])
        gain_out[0:1, :] += jnp.sum(grad_normed * normal, axis=0, keepdims=True)
        mid_grad = grad + unit_back(grad_normed * gain_row, normal, scale)
        mid_low = mid_grad.astype(bf16)
        mid_low_out[rows, :] = mid_low
        grad_gated = mm_nt(mid_low, w_out[...])
        conv_grad = grad_gated * x0
        keep[rows, :] = conv_grad[:, 0:128]
        send[rows, :] = conv_grad[:, 128:256]
        flips = turned[k, :, at(half * i, half, 256)]
        rest = mid_grad - mid_low.astype(f32)
        gate_grads = jnp.concatenate([(grad_gated * conv).astype(bf16), mid_low, rest.astype(bf16)], axis=1)
        by_token[...] += mm(flips, gate_grads)[0:48, :]
        return carry

    every(1, chunk)


R_OUT, R_UP, R_DOWN, R_IN = 128, 512, 512, 384


def fill_part(s, raw_out, raw_up, raw_down, out):
    first = s[CORE] == 0
    pick = lambda a, b: jnp.where(first, a.astype(f32), b.astype(f32))
    out[0:128, :] = pick(raw_out[:, 0:128], raw_out[:, 128:256])
    for j in range(2):
        lanes = slice(128 * j, 128 * j + 128)
        out[128 + 256 * j : 384 + 256 * j, :] = pick(
            raw_up[:, 128 * j : 128 * j + 128], raw_up[:, 256 + 128 * j : 384 + 128 * j]
        )
        out[640 + 256 * j : 896 + 256 * j, :] = pick(raw_down[0:256, lanes], raw_down[256:512, lanes])


def fill_in_part(s, raw_in, out):
    first = s[CORE] == 0
    for g in range(3):
        a, b = raw_in[g, 0:128, :].astype(f32), raw_in[g, 128:256, :].astype(f32)
        out[128 * g : 128 * g + 128, :] = jnp.where(first, a, b)


def send_weights_kernel(s, w_out, w_up, w_down, out, raw_out, raw_up, raw_down, done):
    bring(((w_out.at[1], raw_out), (w_up.at[1], raw_up), (w_down.at[1], raw_down)), done)
    fill_part(s, raw_out, raw_up, raw_down, out)


def cot_split_kernel(s, blocks, keep, send):
    k = s[CORE]
    few = keep.shape[0]
    keep[...] = blocks[pl.ds(few * k, few)]
    send[...] = blocks[pl.ds(few * (1 - k), few)]


def cot_half_kernel(s, own, received, blocks, out):
    spot, width = s[CORE], own.shape[1]
    for j in range(own.shape[0]):
        out[pl.ds(width * (2 * j + spot), width), :] = own[j]
        out[pl.ds(width * (2 * j + 1 - spot), width), :] = received[j]
    out[2 * own.shape[0] * width :, :] = blocks[own.shape[0], 0:HALO, :]


def cot_whole_kernel(s, own, received, out, rim):
    spot = s[BIT1]
    rows = own.shape[0] - HALO
    two = rows // 2
    for j in range(2):
        out[pl.ds(two * (2 * j + spot), two), :] = own[two * j : two * j + two, :]
        out[pl.ds(two * (2 * j + 1 - spot), two), :] = received[two * j : two * j + two, :]
    rim[...] = jnp.where(spot == 0, own[rows:, :], received[rows:, :])


def relay_kernel(s, value, out):
    out[...] = value[...]


def join_weights_kernel(level, s, w_out, w_up, w_down, w_in, first_part, second_part, out_full, up_full, down_full, *in_full):
    first = s[CORE] == 0
    low = lambda ref, a, b: ref[a:b, :].astype(bf16)
    pick = lambda a, b: jnp.where(first, a, b)
    mine_out = w_out[level]
    a, b = first_part[0:128, :], second_part[0:128, :]
    peer_out = jnp.concatenate([pick(a, b), pick(b, a)], axis=1)
    out_full[0:128, :] = pick(mine_out.astype(f32), peer_out).astype(bf16)
    out_full[128:256, :] = pick(peer_out, mine_out.astype(f32)).astype(bf16)
    up_a, up_b = w_up[level, :, 0:256].astype(f32), w_up[level, :, 256:512].astype(f32)
    up_full[:, 0:256] = pick(up_a, up_b).astype(bf16)
    up_full[:, 256:512] = pick(up_b, up_a).astype(bf16)
    down_a, down_b = w_down[level, 0:256, :].astype(f32), w_down[level, 256:512, :].astype(f32)
    down_full[0:256, :] = pick(down_a, down_b).astype(bf16)
    down_full[256:512, :] = pick(down_b, down_a).astype(bf16)
    for n, part in enumerate((first_part, second_part)):
        for j in range(2):
            up_full[:, 512 + 256 * n + 128 * j : 640 + 256 * n + 128 * j] = low(part, 128 + 256 * j, 384 + 256 * j)
            down_full[512 + 256 * n : 768 + 256 * n, 128 * j : 128 * j + 128] = low(part, 640 + 256 * j, 896 + 256 * j)
    if in_full:
        (full,) = in_full
        for g in range(3):
            own = w_in[1 - level, g].astype(f32)
            a, b = first_part[1152 + 128 * g : 1280 + 128 * g, :], second_part[1152 + 128 * g : 1280 + 128 * g, :]
            peer = jnp.concatenate([pick(a, b), pick(b, a)], axis=0)
            full[:, 256 * g : 256 * g + 128] = pick(own, peer).astype(bf16)
            full[:, 256 * g + 128 : 256 * g + 256] = pick(peer, own).astype(bf16)


def wide_grads_kernel(pad, s, gated, mid_low, normed, grad_pre, hidden, grad_low, keep, send):
    k = s[CORE]
    first = k == 0
    stop = gated.shape[0] - pad
    own = lambda ref: ref[pad:stop, :]
    out = mm_tn(own(gated), own(mid_low))
    for m in range(2):
        a, b = out[128 * m : 128 * m + 128, 0:128], out[128 * m : 128 * m + 128, 128:256]
        half = m + k - 2 * m * k
        keep[half, 0:128, :] = jnp.where(first, a, b)
        send[half, 0:128, :] = jnp.where(first, b, a)
    for j in range(4):
        target = (keep, send)[j % 2]
        up = mm_tn(own(normed), grad_pre[pad:stop, 256 * j : 256 * j + 256])
        down = mm_tn(hidden[pad:stop, 256 * j : 256 * j + 256], own(grad_low))
        for n in range(2):
            lanes = slice(128 * n, 128 * n + 128)
            target[j // 2, 128 + 256 * n : 384 + 256 * n, :] = up[:, lanes]
            target[j // 2, 640 + 256 * n : 896 + 256 * n, :] = down[:, lanes]


def in_grads_kernel(s, normed_in, mixed_low, keep, send):
    k = s[CORE]
    first = k == 0
    for g in range(3):
        both = mm_tn(normed_in[...], mixed_low[:, 256 * g : 256 * g + 256])
        for m in range(2):
            block = both[:, 128 * m : 128 * m + 128]
            half = m + k - 2 * m * k
            keep[half, 128 * g : 128 * g + 128, :] = jnp.where(first, block[0:128], block[128:256])
            send[half, 128 * g : 128 * g + 128, :] = jnp.where(first, block[128:256], block[0:128])


def add_kernel(s, kept, received, own_out, peer_out):
    own_out[...] = kept[0] + received[0]
    peer_out[...] = kept[1] + received[1]


def add_half_kernel(s, kept, received, w_in, own_out, peer_out):
    rows = own_out.shape[0]
    part = at(rows * s[BIT1], rows, 8)
    own_out[...] = kept[0, part, :] + received[0, part, :]
    peer_out[0:rows, :] = kept[1, part, :] + received[1, part, :]
    fill_in_part(s, w_in.at[0], peer_out.at[rows : rows + 384])


def take_half_kernel(s, own, received, out, in_out):
    rows = own.shape[0]
    out[...] = own[...] + received[0:rows, :]
    in_out[...] = received[rows:, :]


def add_one_kernel(s, kept, received, out):
    out[...] = kept[...] + received[...]


def spread_wide_kernel(level, s, *refs):
    if level:
        outs, (a, b, out, up, down), done = refs[-9:-6], refs[-6:-1], refs[-1]
        rows = refs[0].shape[0]
        for whole, near, far in ((a, refs[0], refs[1]), (b, refs[2], refs[3])):
            whole[at(rows * s[BIT1], rows, 8), :] = near[...]
            whole[at(rows * (1 - s[BIT1]), rows, 8), :] = far[...]
    else:
        outs, (out, up, down), done = refs[-7:-4], refs[-4:-1], refs[-1]
        a, b = refs[:2]
    first = s[CORE] == 0
    pick = lambda x, y: jnp.where(first, x, y)

    def both(row, rows):
        x, y = a[row : row + rows, :], b[row : row + rows, :]
        return pick(x, y), pick(y, x)

    x, y = both(0, 128)
    out[:, 0:128] = x
    out[:, 128:256] = y
    for j in range(2):
        lanes = slice(128 * j, 128 * j + 128)
        x, y = both(128 + 256 * j, 256)
        up[:, 128 * j : 128 * j + 128] = x
        up[:, 256 + 128 * j : 384 + 128 * j] = y
        x, y = both(640 + 256 * j, 256)
        down[0:256, lanes] = x
        down[256:512, lanes] = y
    bring(zip((out, up, down), (whole.at[level] for whole in outs)), done)


def spread_in_kernel(s, kept, received, whole, near, done):
    first = s[CORE] == 0
    for g in range(3):
        x, y = kept[128 * g : 128 * g + 128, :], received[128 * g : 128 * g + 128, :]
        near[g, 0:128, :] = jnp.where(first, x, y)
        near[g, 128:256, :] = jnp.where(first, y, x)
    bring(((near, whole.at[1]),), done)


def pair_kernel(bit, s, own, received, out):
    spot = s[(CORE, BIT1, BIT2, BIT3)[bit]]
    for j in range(own.shape[0]):
        out[2 * j + spot] = own[j]
        out[2 * j + 1 - spot] = received[j]


E_GAIN, E_EMBED, E_FIRST, E_SHORT, E_TOKEN, E_ROWS = 0, 8, 24, 40, 56, 104
EM_SECOND, EM_SKIP, EM_ROWS = 0, 64, 72
L_TOKEN, L_SECOND, L_SKIP, L_ROWS = 0, 96, 160, 168
FIRST_ROWS = 16


def fold_first(values):
    last = jnp.concatenate([values[32:40], jnp.zeros((8, 64), f32)], axis=0)
    return jnp.concatenate([values[0:16], values[16:32], last, jnp.zeros((16, 64), f32)], axis=1)


def unfold_first(values):
    return jnp.concatenate([values[:, 0:64], values[:, 64:128], values[0:8, 128:192]], axis=0)[0:FEAT]


def early_kernel(s, gain_mid1, gain_in1, gain_mid0, by_token0, first1, short1, second1, skip1, flat, mine):
    k = s[CORE]
    flat[...] = jnp.zeros_like(flat)
    for row, values in enumerate((gain_mid1, gain_in1, gain_mid0)):
        flat[E_GAIN + row : E_GAIN + row + 1, :] = values[0:1, :]
    flat[E_EMBED : E_EMBED + 16, :] = by_token0[0:16, 256:512] + by_token0[0:16, 512:768]
    flat[E_FIRST : E_FIRST + FIRST_ROWS, :] = fold_first(first1[...])
    swap = lambda v: jnp.where(k == 0, v, jnp.concatenate([v[:, 128:256], v[:, 0:128]], axis=1))
    for t in range(3):
        total = jnp.sum(short1[t], axis=0, keepdims=True)
        for g in range(3):
            flat[E_SHORT + 3 * t + g : E_SHORT + 3 * t + g + 1, :] = swap(total[:, 256 * g : 256 * g + 256])
    flat[E_TOKEN : E_TOKEN + 48, :] = swap(by_token0[:, 0:256])
    mine[EM_SECOND : EM_SECOND + 64, :] = second1[...]
    mine[EM_SKIP : EM_SKIP + 8, :] = jnp.broadcast_to(jnp.sum(skip1[...], axis=0, keepdims=True), (8, 128))


def late_kernel(s, by_token12, second0, skip0, first0, mine, first_out):
    mine[L_TOKEN : L_TOKEN + 48, :] = by_token12[:, 0:128]
    mine[L_TOKEN + 48 : L_TOKEN + 96, :] = by_token12[:, 128:256]
    mine[L_SECOND : L_SECOND + 64, :] = second0[...]
    mine[L_SKIP : L_SKIP + 8, :] = jnp.broadcast_to(jnp.sum(skip0[...], axis=0, keepdims=True), (8, 128))
    first_out[...] = fold_first(first0[...])


FOLDED, HALF_ROWS = 40, 72


def chip_kernel(s, flat, flat_in, mine, mine_in, out, send):
    first = s[CORE] == 0
    rows = flat.shape[0]
    out[0:rows, :] = flat[...] + flat_in[...]
    out[rows:, 0:128] = jnp.where(first, mine[...], mine_in[...])
    out[rows:, 128:256] = jnp.where(first, mine_in[...], mine[...])
    whole = send.shape[0] - FOLDED
    rest = HALF_ROWS - FOLDED
    send[0:whole, :] = out[0:whole, :]
    send[whole:, 0:128] = out[whole : whole + FOLDED, 128:256]
    send[whole : whole + rest, 128:256] = out[whole + FOLDED : whole + HALF_ROWS, 128:256]
    send[whole + rest :, 128:256] = jnp.zeros((FOLDED - rest, 128), f32)


def last_kernel(
    s, early, early_in, late, late_in, embed, gain, own, peer, w_own, w_first, w_second, in_given,
    embed_out, gain_out, in_whole, short_out, first_out, second_out, skip_out, in_out, done,
):
    pick = lambda x, y: jnp.where(s[CORE] == 0, x, y)

    def plain(pair, row, rows):
        return pair[0][row : row + rows, :] + pair[1][row : row + rows, :]

    def halves(pair, row, rows):
        here, there = pair
        left = here[row : row + rows, 0:128] + there[row : row + rows, 128:256]
        right = here[row : row + rows, 128:256] + there[row : row + rows, 0:128]
        return left, right

    def own_half(pair, row, rows):
        here, there = pair
        whole, rest = there.shape[0] - FOLDED, HALF_ROWS - FOLDED
        folded = jnp.concatenate([there[whole:, 0:128], there[whole : whole + rest, 128:256]], axis=0)
        return here[whole + row : whole + row + rows, 0:128] + folded[row : row + rows]

    early, late = (early, early_in), (late, late_in)
    gains = plain(early, E_GAIN, 8)
    gain_out[1, 0:1, :] = gains[1:2, :]
    gain_out[1, 1:2, :] = gains[0:1, :]
    gain_out[0, 1:2, :] = gains[2:3, :]
    first_out[:, 0, :] = unfold_first(plain(late, 0, FIRST_ROWS))
    first_out[:, 1, :] = unfold_first(plain(early, E_FIRST, FIRST_ROWS))
    short = halves(early, E_SHORT, 16)[0]
    for t in range(3):
        for g in range(3):
            short_out[t, g, 1:2, :] = short[3 * t + g : 3 * t + g + 1, :]
    second_out[1] = own_half(early, 0, 64)
    second_out[0] = own_half(late, 0, 64)
    skip_out[0:1, :] = own_half(late, 64, 8)[0:1]
    skip_out[1:2, :] = own_half(early, 64, 8)[0:1]
    tokens = [
        halves(early, E_TOKEN, 48),
        halves(late, FIRST_ROWS + L_TOKEN, 48),
        halves(late, FIRST_ROWS + L_TOKEN + 48, 48),
    ]
    normal, scale = unit(embed[...])
    gain_row = gain[0, 0:1, :]
    low = (normal * gain_row).astype(bf16)
    grad_normed = jnp.zeros((16, 256), f32)
    for g in range(3):
        for h, pack in ((0, own), (1, peer)):
            grads = tokens[g][h]
            table = pack[16 * g : 16 * g + 16, :]
            summed = jnp.zeros((16, 128), f32)
            for t in range(3):
                row = PACK_SHORT + 3 * t + g
                part = grads[16 * t : 16 * t + 16, :]
                summed += pack[row : row + 1, :] * part
                if h == 0:
                    short_out[t, g, 0:1, :] = jnp.sum(table * part, axis=0, keepdims=True)
            high, rest = split(summed)
            if h == 0:
                in_out[g] = mm_tn(low, high) + mm_tn(low, rest)
                weight = w_own[0, g]
            else:
                rows = slice(128 * g, 128 * g + 128)
                a, b = w_first[rows, :], w_second[rows, :]
                weight = jnp.concatenate([pick(a, b), pick(b, a)], axis=0).astype(bf16)
            grad_normed += mm_nt(high, weight) + mm_nt(rest, weight)
    copy = pltpu.make_async_copy(in_out, in_whole.at[0], done.at[0])
    copy.start()
    gain_out[0, 0:1, :] = jnp.sum(grad_normed * normal, axis=0, keepdims=True)
    embed_out[...] = plain(early, E_EMBED, 16) + unit_back(grad_normed * gain_row, normal, scale)
    copy.wait()


def block_send_kernel(s, block_out, mine, other):
    spot = s[SPOT]
    mine[...] = block_out[at(HALO + 128 * spot, 128), :]
    near = spot + 1 - 2 * s[CORE]
    other[...] = block_out[at(HALO + 128 * near, 128), :]


def block_pick_kernel(s, mine, received, out):
    out[...] = jnp.where(s[HOLDER] == 1, mine[...], received[...])


def block_join_kernel(s, here, there, out):
    first = s[GROUP] == 0
    out[0] = jnp.where(first, here[...], there[...])
    out[1] = jnp.where(first, there[...], here[...])


def chip_local(
    ids, live, embed, norm_gain, in_weight, short_kernel, filter_first, filter_second, skip_gain,
    out_weight, up_weight, down_weight, cotangent,
):
    CALLS.clear()
    count = lax.axis_size("seq")
    rank = lax.axis_index("seq")
    group = lax.axis_index("ch")
    width = ids.shape[1]
    length = width * count
    half = length // 2
    span = half + 2 * HALO
    core = rank % 2
    across = lambda v: lax.ppermute(v, "ch", [(0, 1), (1, 0)])
    trade = lambda v, bit: lax.ppermute(v, "seq", [(i, i ^ bit) for i in range(count)])
    beside = lambda v: trade(v, 1)
    dft = jnp.asarray(dft_table()).astype(bf16)
    feats = jnp.asarray(feature_parts(length)).astype(bf16)
    feats_turned = jnp.asarray(np.pad(feature_table(length).T, ((0, FEAT_ROWS - FEAT), (0, 0)))).astype(bf16)
    rates = jnp.asarray(rate_table())
    low = lambda *shape: arr(*shape, kind=bf16)
    line = pltpu.VMEM((length + 2 * HALO, 128), f32)
    conv_scratch = [stage_scratch(), spec_scratch(), line]
    pair = lambda bit, v, w, **kw: run(
        functools.partial(pair_kernel, bit), jax.ShapeDtypeStruct((2 * v.shape[0],) + v.shape[1:], v.dtype), s, v, w, **kw
    )

    row_shape = lambda rows: arr(rows, 8, width, kind=jnp.int32)
    in_own = jnp.swapaxes(in_weight, 1, 2)
    packed = (embed, norm_gain, in_own, filter_second, jnp.transpose(short_kernel, (1, 2, 0, 3)), skip_gain)
    wide = (out_weight, up_weight, down_weight)
    held = [(1, 2), ids.shape, embed.shape, norm_gain.shape, in_own.shape[1:], filter_second.shape, packed[4].shape, skip_gain.shape]
    held += [v.shape[1:] for v in wide] + [in_own.shape[1:]]
    kinds = [jnp.int32, jnp.int32, f32, f32, bf16, f32, f32, f32] + [bf16] * 4
    s, ids1, cot1, pack, part0 = start(
        numbers_kernel,
        [arr(NUMBER_ROWS, 128, kind=jnp.int32), row_shape(1), arr(1, width, 256), arr(PACK_ROWS, 128), arr(1536, 128)],
        live.reshape(1, 2), ids, cotangent, *packed, *wide, in_own,
        scratch=[pltpu.VMEM(shape, kind) for shape, kind in zip(held, kinds)] + [pltpu.SemaphoreType.DMA((13,))],
    )
    pack_in = across(pack)
    part0_in = across(part0)
    ids2 = pair(3, ids1, trade(ids1, 8))
    sine, cosine, sine_turned = run(
        sine_kernel, [low(length, 256), arr(length, 128), low(128, length)], s, feats, jnp.transpose(filter_first, (1, 0, 2)),
        after=(ids2,), scratch=[pltpu.VMEM((FEAT_ROWS, 128), f32)],
    )
    twiddle = run(twiddle_kernel, arr(KINDS - 1, 2, BLOCK, 128), s, jnp.asarray(twiddle_table()), after=(sine,))
    cot2 = pair(3, cot1, trade(cot1, 8), after=(twiddle,))
    ids4 = pair(2, ids2, trade(ids2, 4), after=(cot2,))
    part1 = run(
        send_weights_kernel, arr(1152, 128), s, *wide, hbm=range(3), after=(ids4,),
        scratch=[pltpu.VMEM(v.shape[1:], v.dtype) for v in wide] + [pltpu.SemaphoreType.DMA((3,))],
    )
    part1_in = across(part1)
    mine, other, conv_table, gate_table = run(
        table_kernel, [arr(PACK_ROWS, 128), arr(PACK_ROWS, 128), low(128, 256), low(128, 512)], s, pack, pack_in, embed,
        after=(part1,),
    )
    make_filter = lambda level, after: run(
        functools.partial(filter_kernel, level), [arr(length, 128), arr(*SPECTRUM)], s, sine, mine, rates, dft, twiddle,
        scratch=[stage_scratch()], after=after,
    )
    filt0, freq0 = make_filter(0, ())
    ids8 = pair(1, ids4, trade(ids4, 2), after=(filt0,))
    cot4 = pair(2, cot2, trade(cot2, 4), after=(ids8,))
    cot_keep, cot_send = run(cot_split_kernel, [arr(2, width, 256), arr(2, width, 256)], s, cot4)
    all_ids = pair(0, ids8, beside(ids8), after=(cot_send,))
    onehot, turned = run(
        onehot_kernel, [low(length + 2 * HALO, 128), low(2, 128, half)], s, all_ids,
        scratch=[pltpu.VMEM((length + 2 * HALO, 128), f32)],
    )
    conv_mine0, sent, spec0, product0 = run(
        conv_first_kernel, [arr(span, 128), arr(span, 128), arr(*SPECTRUM), arr(length, 128)],
        s, onehot, conv_table, mine, freq0, dft, twiddle, scratch=conv_scratch,
    )
    conv_other0 = beside(sent)
    first_part = run(relay_kernel, arr(1536, 128), s, part0_in, after=(sent,))
    first_beside = beside(first_part)
    cot_half = run(cot_half_kernel, arr(4 * width + HALO, 256), s, cot_keep, beside(cot_send), cot4, after=(first_part,))
    cot_half_in = trade(cot_half, 2)
    filt1, freq1 = make_filter(1, (first_part, cot_half))
    w_out0, w_up0, w_down0, w_in1 = run(
        functools.partial(join_weights_kernel, 0), [low(256, 256), low(256, 1024), low(1024, 256), low(256, 768)],
        s, out_weight, up_weight, down_weight, in_own, first_part, first_beside, after=(cot_half,),
    )
    kept, sent, mid0, stream1, gates1, mixed1 = run(
        forward_first_kernel,
        [arr(half, 128), arr(half, 128), arr(span, 256), arr(span, 256), arr(span, 768), arr(span, 768)],
        s, onehot, gate_table, conv_mine0, conv_other0, norm_gain, w_out0, w_up0, w_down0, w_in1, mine, other,
    )
    received = beside(sent)
    second_part = run(relay_kernel, arr(1152, 128), s, part1_in, after=(sent,))
    second_beside = beside(second_part)
    conv_mine1, sent, spec1, product1 = run(
        conv_second_kernel, [arr(span, 128), arr(span, 128), arr(*SPECTRUM), arr(length, 128)],
        s, kept, received, mine, freq1, dft, twiddle, scratch=conv_scratch, after=(second_part,),
    )
    conv_other1 = beside(sent)
    cot, cot_rim = run(cot_whole_kernel, [arr(half, 256), arr(HALO, 256)], s, cot_half, cot_half_in, after=(sent,))
    w_out1, w_up1, w_down1 = run(
        functools.partial(join_weights_kernel, 1), [low(256, 256), low(256, 1024), low(1024, 256)],
        s, out_weight, up_weight, down_weight, in_own, second_part, second_beside, after=(cot_rim,),
    )
    (kept, sent, grad_x0, grad_mid1, block, hidden, grad_low, normed, grad_pre, gated, mid_low, gain_mid1) = run(
        turn_back_kernel,
        [
            arr(half, 128), arr(half, 128), arr(span, 256), arr(span, 256), arr(span, 256), low(span, 1024), low(span, 256),
            low(span, 256), low(span, 1024), low(span, 256), low(span, 256), arr(8, 256),
        ],
        s, conv_mine1, conv_other1, gates1, stream1, cot, cot_rim, norm_gain, w_out1, w_up1, w_down1,
        scratch=[pltpu.VMEM((span, 256), f32), pltpu.VMEM((span, 256), f32)],
    )
    received = beside(sent)
    grads_keep1, grads_send1 = run(
        functools.partial(wide_grads_kernel, HALO), [arr(2, 1152, 128), arr(2, 1152, 128)],
        s, gated, mid_low, normed, grad_pre, hidden, grad_low,
    )
    block_mine, block_other = run(block_send_kernel, [arr(width, 256), arr(width, 256)], s, block)
    grads_in1 = beside(grads_send1)
    block_beside = beside(block_other)

    prod_mine, sent, spec_grad1, grads1 = run(
        conv_back_kernel, [arr(span, 128), arr(span, 128), arr(*SPECTRUM), arr(length, 128)],
        s, kept, received, mine, freq1, dft, twiddle, scratch=conv_scratch, after=(grads_send1, block_mine),
    )
    prod_other = beside(sent)
    own1, peer1 = run(add_half_kernel, [arr(576, 128), arr(960, 128)], s, grads_keep1, grads_in1, in_own, after=(sent,))
    across1 = across(peer1)
    filter_shapes = [arr(64, 128), arr(40, 64), arr(8, 128)]
    filter_scratch = [stage_scratch(), spec_scratch(), pltpu.VMEM((length, 128), f32)]
    second1, first1, skip1 = run(
        filter_back_kernel, filter_shapes, s, spec_grad1, spec1, grads1, product1, filt1, cosine,
        sine_turned, mine, rates, feats_turned, dft, twiddle, scratch=filter_scratch, after=(peer1,),
    )
    grad_stream1, normed_in, mixed_low, short1, gain_in1 = run(
        back_gates_kernel,
        [arr(half, 256), low(half, 256), low(half, 768), arr(3, 8, 768), arr(8, 256)],
        s, prod_mine, prod_other, grad_x0, gates1, mixed1, grad_mid1, stream1, norm_gain, mine, other, w_in1,
        scratch=[pltpu.VMEM((span, 512), f32)], after=(skip1,),
    )
    in_keep, in_send = run(in_grads_kernel, [arr(2, 384, 128), arr(2, 384, 128)], s, normed_in, mixed_low)
    in_beside = beside(in_send)
    block_here = run(block_pick_kernel, arr(width, 256), s, block_mine, block_beside, after=(in_send,))
    block_across = across(block_here)
    in_own1, in_peer1 = run(add_kernel, [arr(384, 128), arr(384, 128)], s, in_keep, in_beside, after=(block_here,))
    in_across = across(in_peer1)
    (kept, sent, hidden, grad_low, normed, grad_pre, gated, mid_low, by_token0, gain_mid0) = run(
        back_first_kernel,
        [
            arr(half, 128), arr(half, 128), low(half, 1024), low(half, 256), low(half, 256), low(half, 1024), low(half, 256),
            low(half, 256), arr(48, 768), arr(8, 256),
        ],
        s, grad_stream1, mid0, onehot, turned, gate_table, conv_mine0, conv_other0, norm_gain, w_out0, w_up0, w_down0,
        after=(in_peer1,),
    )
    received = beside(sent)
    early_flat, early_mine = run(
        early_kernel, [arr(E_ROWS, 256), arr(EM_ROWS, 128)],
        s, gain_mid1, gain_in1, gain_mid0, by_token0, first1, short1, second1, skip1,
    )
    early_flat_in, early_mine_in = beside(early_flat), beside(early_mine)
    grads_keep0, grads_send0 = run(
        functools.partial(wide_grads_kernel, 0), [arr(2, 1152, 128), arr(2, 1152, 128)],
        s, gated, mid_low, normed, grad_pre, hidden, grad_low, after=(early_flat,),
    )
    grads_in0 = beside(grads_send0)
    early, early_send = run(
        chip_kernel, [arr(E_ROWS + EM_ROWS, 256), arr(E_ROWS + FOLDED, 256)],
        s, early_flat, early_flat_in, early_mine, early_mine_in, after=(grads_send0,),
    )
    early_in = across(early_send)
    spec_grad0, grads0 = run(
        grad_freq_kernel, [arr(*SPECTRUM), arr(length, 128)], s, kept, received, dft, twiddle, scratch=[stage_scratch()],
        after=(early,),
    )
    own0, peer0 = run(add_kernel, [arr(1152, 128), arr(1152, 128)], s, grads_keep0, grads_in0, after=(spec_grad0,))
    across0 = across(peer0)
    total1, in0_first = run(take_half_kernel, [arr(576, 128), arr(384, 128)], s, own1, across1, after=(peer0,))
    total1_y, in0_second = trade(total1, 2), beside(in0_first)
    second0, first0, skip0, by_token12 = run(
        token_back_kernel, filter_shapes + [arr(48, 256)], s, spec_grad0, spec0, grads0, product0, filt0, cosine,
        sine_turned, mine, rates, feats_turned, dft, twiddle, freq0, onehot, turned, conv_table, scratch=filter_scratch,
        after=(peer0, early),
    )
    wide_shapes = [arr(2, 128, 256), arr(2, 256, 512), arr(2, 512, 256)]
    wide_scratch = [pltpu.VMEM(v.shape[1:], f32) for v in wide_shapes] + [pltpu.SemaphoreType.DMA((3,))]
    late_mine, late_first = run(
        late_kernel, [arr(L_ROWS, 128), arr(FIRST_ROWS, 256)], s, by_token12, second0, skip0, first0, flops=FEW_FLOPS
    )
    late_mine_in, late_first_in = beside(late_mine), beside(late_first)
    in_total = run(add_one_kernel, arr(384, 128), s, in_own1, in_across, after=(late_mine,), flops=FEW_FLOPS)
    block_out, joined = run(block_join_kernel, arr(2, width, 256), s, block_here, block_across, after=(late_mine,), flops=FEW_FLOPS, token=True)
    late, late_send = run(
        chip_kernel, [arr(FIRST_ROWS + L_ROWS, 256), arr(FIRST_ROWS + L_SECOND + FOLDED, 256)], s, late_first, late_first_in, late_mine, late_mine_in, flops=FEW_FLOPS,
        after=(joined, in_total, early_in),
    )
    late_in = across(late_send)
    near1_y = run(relay_kernel, arr(576, 128), s, total1_y, after=(late,), flops=FEW_FLOPS)
    quarters1 = (total1, near1_y, beside(total1), beside(near1_y))
    in_total_beside = beside(in_total)
    *wide_buffers, wide_spread = run(
        functools.partial(spread_wide_kernel, 1), wide_shapes, s, *quarters1, hbm_outs=(0, 1, 2), flops=FEW_FLOPS,
        scratch=[pltpu.VMEM((1152, 128), f32)] * 2 + wide_scratch, after=(late, in0_second), token=True,
    )
    in_buffer, in_spread = run(
        spread_in_kernel, arr(2, 3, 256, 128), s, in_total, in_total_beside, hbm_outs=(0,), flops=FEW_FLOPS, token=True,
        scratch=[pltpu.VMEM((3, 256, 128), f32), pltpu.SemaphoreType.DMA((1,))],
    )
    total0 = run(add_one_kernel, arr(1152, 128), s, own0, across0, after=(late_in, wide_spread, in_spread))
    total0_beside = beside(total0)
    grad_embed, grad_gain, grad_in, grad_short, grad_first, grad_second, grad_skip = run(
        last_kernel,
        [
            arr(16, 256), arr(2, 2, 256), arr(2, 3, 256, 128), arr(3, 3, 2, 128), arr(FEAT, 2, 64), arr(2, 64, 128), arr(2, 128),
        ],
        s, early, early_in, late, late_in, embed, norm_gain, pack, pack_in, in_own, in0_first, in0_second, in_buffer,
        hbm=(11,), hbm_outs=(2,), aliases=((11, 2),), flops=FEW_FLOPS, after=(total0,),
        scratch=[pltpu.VMEM((3, 256, 128), f32), pltpu.SemaphoreType.DMA((1,))],
    )
    grad_out, grad_up, grad_down = run(
        functools.partial(spread_wide_kernel, 0), wide_shapes, s, total0, total0_beside, *wide_buffers,
        hbm=(2, 3, 4), hbm_outs=(0, 1, 2), aliases=((2, 0), (3, 1), (4, 2)), flops=FEW_FLOPS, scratch=wide_scratch,
    )
    return (
        block_out,
        grad_embed,
        grad_gain,
        jnp.swapaxes(grad_in, 1, 2),
        jnp.transpose(grad_short, (2, 0, 1, 3)),
        jnp.transpose(grad_first, (1, 0, 2)),
        grad_second,
        grad_skip,
        grad_out,
        grad_up,
        grad_down,
    )


def solution(mesh):
    in_specs = (
        P(None, "seq"),
        P(),
        P(),
        P(),
        P(None, None, None, "ch"),
        P(None, None, None, "ch"),
        P(),
        P(None, None, "ch"),
        P(None, "ch"),
        P(None, "ch", None),
        P(None, None, "ch"),
        P(None, "ch", None),
        P(None, "seq", None),
    )
    out_specs = (
        P(None, "seq", None),
        P(),
        P(),
        P(None, None, None, "ch"),
        P(None, None, None, "ch"),
        P(),
        P(None, None, "ch"),
        P(None, "ch"),
        P(None, "ch", None),
        P(None, None, "ch"),
        P(None, "ch", None),
    )

    def either(*args):
        length = args[0].shape[1] * lax.axis_size("seq")
        near = length == BLOCKS * BLOCK and lax.axis_size("seq") == 16
        return (chip_local if near else local)(*args)

    return jax.shard_map(either, mesh=mesh, in_specs=in_specs, out_specs=out_specs, check_vma=False)
```

```python
import collections
import functools
import math

import jax
import jax.numpy as jnp
import ml_dtypes
import numpy as np
from jax import lax
from jax.experimental import pallas as pl
from jax.experimental.pallas import tpu as pltpu
from jax.sharding import PartitionSpec as P

D = 256
FEAT = 33


precise = lax.Precision.HIGHEST
epsilon = 1e-05


def passed_along(value, axis, steps):
    count = lax.axis_size(axis)
    leading, last = (max(0, -steps), min(count, count - steps))
    return lax.ppermute(value, axis, [(source, source + steps) for source in range(leading, last)])


def layer_norm(inputs, gain_vec):
    center = inputs - jnp.mean(inputs, axis=-1, keepdims=True)
    spread = jnp.mean(center * center, axis=-1, keepdims=True)
    return center * lax.rsqrt(spread + epsilon) * gain_vec


def position_features(length):
    places = jnp.arange(length, dtype=jnp.int32)
    band_ids = jnp.arange(1, (FEAT - 1) // 2 + 1, dtype=jnp.int32)
    turn_counts = places[:, None] * band_ids[None, :] % length
    angles = turn_counts.astype(jnp.float32) * (2.0 * math.pi / length)
    ramp_vals = places.astype(jnp.float32)[:, None] / length
    return jnp.concatenate([ramp_vals, jnp.cos(angles), jnp.sin(angles)], axis=1)


def decay_rates(channels):
    return 0.3 * 10.0 ** (channels.astype(jnp.float32) / (D - 1))


def dft_tables(blocks, block_len):
    doubled = 2 * blocks
    span_total = doubled * block_len
    frequency = jnp.arange(doubled, dtype=jnp.int32)
    places = jnp.arange(blocks, dtype=jnp.int32)
    inner_idx = jnp.arange(block_len, dtype=jnp.int32)
    outer_angle = (frequency[:, None] * places[None, :] % doubled).astype(jnp.float32) * (
        2.0 * math.pi / doubled
    )
    twist_angle = (frequency[:, None] * inner_idx[None, :] % span_total).astype(jnp.float32) * (
        2.0 * math.pi / span_total
    )
    inner_angle = (inner_idx[:, None] * inner_idx[None, :] % block_len).astype(jnp.float32) * (
        2.0 * math.pi / block_len
    )
    return (
        jnp.cos(outer_angle),
        jnp.sin(outer_angle),
        jnp.cos(twist_angle),
        jnp.sin(twist_angle),
        jnp.cos(inner_angle),
        jnp.sin(inner_angle),
    )


def along_block(values, table):
    return jnp.einsum("...kb,bj->...kj", values, table, precision=precise)


def to_spectrum(signal, tables):
    outer_cos, outer_sin, twist_cos, twist_sin, inner_cos, inner_sin = tables
    first_re = jnp.einsum("kp,...pb->...kb", outer_cos, signal, precision=precise)
    first_im = -jnp.einsum("kp,...pb->...kb", outer_sin, signal, precision=precise)
    turned_re = first_re * twist_cos + first_im * twist_sin
    turned_im = first_im * twist_cos - first_re * twist_sin
    spec_re = along_block(turned_re, inner_cos) + along_block(turned_im, inner_sin)
    spec_im = along_block(turned_im, inner_cos) - along_block(turned_re, inner_sin)
    return (spec_re, spec_im)


def from_spectrum(spec_re, spec_im, tables):
    outer_cos, outer_sin, twist_cos, twist_sin, inner_cos, inner_sin = tables
    back_re = along_block(spec_re, inner_cos) - along_block(spec_im, inner_sin)
    back_im = along_block(spec_re, inner_sin) + along_block(spec_im, inner_cos)
    turned_re = back_re * twist_cos - back_im * twist_sin
    turned_im = back_re * twist_sin + back_im * twist_cos
    scale_back = 1.0 / (outer_cos.shape[0] * inner_cos.shape[0])
    signal = jnp.einsum("kp,...kb->...pb", outer_cos, turned_re, precision=precise) - jnp.einsum(
        "kp,...kb->...pb", outer_sin, turned_im, precision=precise
    )
    return signal * scale_back


def causal_filter(received, filt_spec, skip_part, tables):
    item_count, chan_count, length = received.shape
    blocks = tables[0].shape[1]
    spec_re, spec_im = to_spectrum(
        received.reshape(item_count, chan_count, blocks, length // blocks), tables
    )
    prod_re = spec_re * filt_spec[0] - spec_im * filt_spec[1]
    prod_im = spec_re * filt_spec[1] + spec_im * filt_spec[0]
    result_sig = from_spectrum(prod_re, prod_im, tables).reshape(item_count, chan_count, length)
    return result_sig + skip_part[:, None] * received


def filter_backward(grad_cols, moved_in, filt_spec, skip_part, tables):
    item_count, chan_count, length = grad_cols.shape
    blocks = tables[0].shape[1]
    grad_re, grad_im = to_spectrum(
        grad_cols.reshape(item_count, chan_count, blocks, length // blocks), tables
    )
    input_re, input_im = to_spectrum(
        moved_in.reshape(item_count, chan_count, blocks, length // blocks), tables
    )
    back_re = grad_re * filt_spec[0] + grad_im * filt_spec[1]
    back_im = grad_im * filt_spec[0] - grad_re * filt_spec[1]
    grad_u_cols = (
        from_spectrum(back_re, back_im, tables).reshape(item_count, chan_count, length)
        + skip_part[:, None] * grad_cols
    )
    corr_re = grad_re * input_re + grad_im * input_im
    corr_im = grad_im * input_re - grad_re * input_im
    grad_filt = jnp.sum(from_spectrum(corr_re, corr_im, tables), axis=0).reshape(chan_count, length)
    grad_skip_part = jnp.sum(grad_cols * moved_in, axis=(0, 2))
    return (grad_u_cols, grad_filt, grad_skip_part)


def local_filter(first, second, features, select, group_idx, chan_local):
    hidden_pre = jnp.dot(features, first, precision=precise)
    hidden_act = jnp.sin(hidden_pre)
    chan_width = second.shape[1]
    second_part = jnp.dot(second, select, precision=precise)
    channel_ids = group_idx * chan_width + chan_local
    length = features.shape[0]
    ramp_vals = jnp.arange(length, dtype=jnp.int32).astype(jnp.float32) / length
    decay_part = jnp.exp(-decay_rates(channel_ids)[:, None] * ramp_vals[None, :])
    filt_cols = jnp.einsum("hc,th->ct", second_part, hidden_act, precision=precise) * decay_part
    return (filt_cols, hidden_pre, hidden_act, second_part, decay_part)


def filter_mlp_backward(grad_filt, features, filter_parts):
    hidden_pre, hidden_act, second_part, decay_part = filter_parts
    grad_shaped = grad_filt * decay_part
    grad_second_part = jnp.einsum("ct,th->hc", grad_shaped, hidden_act, precision=precise)
    grad_act = jnp.einsum("ct,hc->th", grad_shaped, second_part, precision=precise)
    grad_first = jnp.einsum(
        "tf,th->fh", features, grad_act * jnp.cos(hidden_pre), precision=precise
    )
    return (grad_first, grad_second_part)


def embed_lookup(ids, live, embed, seq_rank):
    tok_rows = ids.shape[1]
    places = seq_rank * tok_rows + jnp.arange(tok_rows, dtype=jnp.int32)
    keep_mask = (places[None, :] < live[:, None]).astype(jnp.float32)
    vocab_ids = jnp.arange(embed.shape[0], dtype=jnp.int32)
    onehot = (ids[:, :, None] == vocab_ids[None, None, :]).astype(jnp.float32) * keep_mask[
        :, :, None
    ]
    stream = jnp.einsum("mtv,vd->mtd", onehot, embed, precision=precise)
    return (stream, onehot, keep_mask)


def channel_total(partial_sum):
    return lax.psum(partial_sum, "ch")


def input_total(partial_sum):
    return lax.psum(partial_sum, "ch")


def layer_forward(stream, params, filt_spec, skip_part, tables):
    norm_gains, w_in, kernel, w_out, w_up, w_down = params
    normed = layer_norm(stream, norm_gains[0]).astype(jnp.bfloat16)
    mixed_in = jnp.einsum("mtd,dgc->mtgc", normed, w_in, preferred_element_type=jnp.float32)
    rim_rows = passed_along(mixed_in[:, -2:], "seq", 1)
    padded = jnp.concatenate([rim_rows, mixed_in], axis=1)
    micro_count, tok_rows = (mixed_in.shape[0], mixed_in.shape[1])
    chan_width = mixed_in.shape[3]
    gate_vals = (
        kernel[0] * mixed_in
        + kernel[1] * padded[:, 1 : tok_rows + 1]
        + kernel[2] * padded[:, 0:tok_rows]
    )
    product_in = gate_vals[:, :, 2] * gate_vals[:, :, 1]
    flat_rows = jnp.swapaxes(product_in, 1, 2).reshape(1, micro_count * chan_width, tok_rows)
    received = lax.all_to_all(flat_rows, "seq", split_axis=1, concat_axis=2, tiled=True)
    result_sig = causal_filter(received, filt_spec, skip_part, tables)
    conv_flat = lax.all_to_all(result_sig, "seq", split_axis=2, concat_axis=1, tiled=True)
    conv_out = jnp.swapaxes(conv_flat.reshape(micro_count, chan_width, tok_rows), 1, 2)
    gated_out = (conv_out * gate_vals[:, :, 0]).astype(jnp.bfloat16)
    mid_state = stream + channel_total(
        jnp.einsum("mtc,cd->mtd", gated_out, w_out, preferred_element_type=jnp.float32)
    )
    normed_mid = layer_norm(mid_state, norm_gains[1]).astype(jnp.bfloat16)
    pre_act = jnp.einsum("mtd,df->mtf", normed_mid, w_up, preferred_element_type=jnp.float32)
    hidden = jax.nn.gelu(pre_act).astype(jnp.bfloat16)
    new_stream = mid_state + channel_total(
        jnp.einsum("mtf,fd->mtd", hidden, w_down, preferred_element_type=jnp.float32)
    )
    kept_vals = (
        stream,
        normed,
        mixed_in,
        padded,
        gate_vals,
        received,
        conv_out,
        gated_out,
        mid_state,
        normed_mid,
        pre_act,
        hidden,
    )
    return (new_stream, kept_vals)


def layer_backward(grad_stream, kept_vals, params, filt_spec, skip_part, tables):
    norm_gains, w_in, kernel, w_out, w_up, w_down = params
    (
        stream,
        normed,
        mixed_in,
        padded,
        gate_vals,
        moved_in,
        conv_out,
        gated_out,
        mid_state,
        normed_mid,
        pre_act,
        hidden,
    ) = kept_vals
    micro_count, tok_rows = (mixed_in.shape[0], mixed_in.shape[1])
    chan_width = mixed_in.shape[3]
    grad_low = grad_stream.astype(jnp.bfloat16)
    grad_down = jnp.einsum("mtf,mtd->fd", hidden, grad_low, preferred_element_type=jnp.float32)
    grad_hidden = jnp.einsum("mtd,fd->mtf", grad_low, w_down, preferred_element_type=jnp.float32)
    _, gelu_back = jax.vjp(jax.nn.gelu, pre_act)
    grad_pre = gelu_back(grad_hidden)[0].astype(jnp.bfloat16)
    grad_up = jnp.einsum("mtd,mtf->df", normed_mid, grad_pre, preferred_element_type=jnp.float32)
    grad_normed_mid = input_total(
        jnp.einsum("mtf,df->mtd", grad_pre, w_up, preferred_element_type=jnp.float32)
    )
    _, norm_back_mid = jax.vjp(layer_norm, mid_state, norm_gains[1])
    grad_mid_norm, grad_gain_mid = norm_back_mid(grad_normed_mid)
    grad_mid = grad_stream + grad_mid_norm
    grad_mid_low = grad_mid.astype(jnp.bfloat16)
    grad_out = jnp.einsum(
        "mtc,mtd->cd", gated_out, grad_mid_low, preferred_element_type=jnp.float32
    )
    grad_gated = jnp.einsum("mtd,cd->mtc", grad_mid_low, w_out, preferred_element_type=jnp.float32)
    grad_conv = grad_gated * gate_vals[:, :, 0]
    grad_first_gate = grad_gated * conv_out
    grad_flat = jnp.swapaxes(grad_conv, 1, 2).reshape(1, micro_count * chan_width, tok_rows)
    grad_cols = lax.all_to_all(grad_flat, "seq", split_axis=1, concat_axis=2, tiled=True)
    grad_u_cols, grad_filt, grad_skip_part = filter_backward(
        grad_cols, moved_in, filt_spec, skip_part, tables
    )
    grad_back_flat = lax.all_to_all(grad_u_cols, "seq", split_axis=2, concat_axis=1, tiled=True)
    grad_product = jnp.swapaxes(grad_back_flat.reshape(micro_count, chan_width, tok_rows), 1, 2)
    grad_gates = jnp.stack(
        [grad_first_gate, grad_product * gate_vals[:, :, 2], grad_product * gate_vals[:, :, 1]],
        axis=2,
    )
    rim_back = passed_along(grad_gates[:, :2], "seq", -1)
    extended = jnp.concatenate([grad_gates, rim_back], axis=1)
    grad_mixed = (
        kernel[0] * grad_gates
        + kernel[1] * extended[:, 1 : tok_rows + 1]
        + kernel[2] * extended[:, 2 : tok_rows + 2]
    )
    grad_kernel = jnp.stack(
        [
            jnp.sum(grad_gates * mixed_in, axis=(0, 1)),
            jnp.sum(grad_gates * padded[:, 1 : tok_rows + 1], axis=(0, 1)),
            jnp.sum(grad_gates * padded[:, 0:tok_rows], axis=(0, 1)),
        ]
    )
    grad_mixed_low = grad_mixed.astype(jnp.bfloat16)
    grad_in = jnp.einsum(
        "mtd,mtgc->dgc", normed, grad_mixed_low, preferred_element_type=jnp.float32
    )
    grad_normed = input_total(
        jnp.einsum("mtgc,dgc->mtd", grad_mixed_low, w_in, preferred_element_type=jnp.float32)
    )
    _, norm_back_in = jax.vjp(layer_norm, stream, norm_gains[0])
    grad_stream_norm, grad_gain_in = norm_back_in(grad_normed)
    grad_before = grad_mid + grad_stream_norm
    layer_grads = (
        jnp.stack([grad_gain_in, grad_gain_mid]),
        grad_in,
        grad_kernel,
        grad_skip_part,
        grad_out,
        grad_up,
        grad_down,
    )
    return (grad_before, layer_grads, grad_filt)


def local(
    ids,
    live,
    embed,
    norm_gain,
    in_weight,
    short_kernel,
    filter_first,
    filter_second,
    skip_gain,
    out_weight,
    up_weight,
    down_weight,
    cotangent,
):
    seq_count = lax.axis_size("seq")
    seq_rank = lax.axis_index("seq")
    group_idx = lax.axis_index("ch")
    micro_count = ids.shape[0]
    tok_rows = ids.shape[1]
    length = tok_rows * seq_count
    chan_width = in_weight.shape[3]
    own_rows = micro_count * chan_width // seq_count
    layer_count = in_weight.shape[0]
    row_start = seq_rank * own_rows
    row_ids = row_start + jnp.arange(own_rows, dtype=jnp.int32)
    chan_local = row_ids % chan_width
    first_rows = (row_ids < chan_width).astype(jnp.float32)
    select = (jnp.arange(chan_width, dtype=jnp.int32)[:, None] == chan_local[None, :]).astype(
        jnp.float32
    )
    tables = dft_tables(seq_count, tok_rows)
    features = position_features(length)
    ramp_row = jnp.arange(length, dtype=jnp.int32).astype(jnp.float32) / length
    stream, onehot, keep_mask = embed_lookup(ids, live, embed, seq_rank)
    filters = []
    for level_idx in range(layer_count):
        filt_cols, hidden_pre, hidden_act, second_part, decay_part = local_filter(
            filter_first[level_idx],
            filter_second[level_idx],
            features,
            select,
            group_idx,
            chan_local,
        )
        filt_spec = to_spectrum(filt_cols.reshape(own_rows, seq_count, tok_rows), tables)
        skip_part = jnp.dot(skip_gain[level_idx], select, precision=precise)
        penalty_grad = 0.5 * length * ramp_row[None, :] * filt_cols * first_rows[:, None]
        params = (
            norm_gain[level_idx],
            in_weight[level_idx],
            short_kernel[level_idx],
            out_weight[level_idx],
            up_weight[level_idx],
            down_weight[level_idx],
        )
        filters.append(
            (
                params,
                filt_spec,
                skip_part,
                (hidden_pre, hidden_act, second_part, decay_part),
                penalty_grad,
            )
        )
    stored = []
    for level_idx in range(layer_count):
        params, filt_spec, skip_part, _, _ = filters[level_idx]
        layer_input = stream
        stream, kept_vals = layer_forward(stream, params, filt_spec, skip_part, tables)
        stored.append(layer_input)
    block_out = stream * keep_mask[:, :, None]
    grad_stream = cotangent * keep_mask[:, :, None]
    collected = [None] * layer_count
    first_grads = [None] * layer_count
    grad_embed = None
    for level_idx in reversed(range(layer_count)):
        params, filt_spec, skip_part, filter_parts, penalty_grad = filters[level_idx]
        _, kept_vals = layer_forward(stored[level_idx], params, filt_spec, skip_part, tables)
        grad_stream, layer_grads, grad_filt = layer_backward(
            grad_stream, kept_vals, params, filt_spec, skip_part, tables
        )
        grad_first, grad_second_part = filter_mlp_backward(
            grad_filt + penalty_grad, features, filter_parts
        )
        first_grads[level_idx] = grad_first
        grad_second = jnp.dot(grad_second_part, select.T, precision=precise)
        grad_skip = jnp.dot(layer_grads[3], select.T, precision=precise)
        gain_grad, in_grad, kernel_grad, _, out_grad, up_grad, down_grad = layer_grads
        if level_idx == 0:
            embed_part = jnp.einsum("mtv,mtd->vd", onehot, grad_stream, precision=precise)
            summed = lax.psum(
                (
                    gain_grad,
                    in_grad,
                    kernel_grad,
                    grad_second,
                    grad_skip,
                    out_grad,
                    up_grad,
                    down_grad,
                    embed_part,
                ),
                "seq",
            )
            collected[level_idx] = summed[:8]
            grad_embed = summed[8]
        else:
            collected[level_idx] = lax.psum(
                (
                    gain_grad,
                    in_grad,
                    kernel_grad,
                    grad_second,
                    grad_skip,
                    out_grad,
                    up_grad,
                    down_grad,
                ),
                "seq",
            )
    stacked = [
        jnp.stack([collected[level_idx][member] for level_idx in range(layer_count)])
        for member in range(8)
    ]
    filter_grads = lax.psum(jnp.stack(first_grads), ("seq", "ch"))
    return (
        block_out,
        grad_embed,
        stacked[0],
        stacked[1],
        stacked[2],
        filter_grads,
        stacked[3],
        stacked[4],
        stacked[5],
        stacked[6],
        stacked[7],
    )


HALO = 16
FEAT_ROWS = 40
ROOT_HALF = math.sqrt(0.5)
GELU_A = math.sqrt(2.0 / math.pi)
GELU_B = 0.044715
BLOCKS = 8
BLOCK = 256
KINDS = 9
VMEM_LIMIT = 8 * 2**20
VMEM_LIMITS = dict(turn_back_kernel=20 * 2**20, back_first_kernel=16 * 2**20)
FLOPS, FEW_FLOPS, MANY_FLOPS = 10**10, 10**8, 10**12
FLOPS_OF = dict(conv_first1=100000000, pair5=10000000000, grad_freq1=30000000000, last1=1000000000, conv_second1=3000000000, join_weights2=100000000)
CALLS = collections.Counter()
f32 = jnp.float32
bf16 = jnp.bfloat16


class Numbers:
    def __init__(self, table):
        self.table = table

    def __getitem__(self, row):
        return self.table[row, 0]


CORE, GROUP, LIVE, WHICH, SPOT, HOLDER, BIT1, BIT2, BIT3 = range(9)
NUMBER_ROWS = 16


def bring(pairs, done):
    copies = [pltpu.make_async_copy(far, near, done.at[i]) for i, (far, near) in enumerate(pairs)]
    for copy in copies:
        copy.start()
    for copy in copies:
        copy.wait()


def numbers_kernel(*refs):
    far, (table, own_ids, cot, pack, part), near, done = refs[:13], refs[13:18], refs[18:30], refs[30]
    far_live, far_ids, far_cot, far_embed, far_gain, far_in, far_second, far_short, far_skip, far_out, far_up, far_down, far_in1 = far
    live, ids, embed, gain, in_own, second, short, skip, raw_out, raw_up, raw_down, in1 = near
    rank, group = lax.axis_index("seq"), lax.axis_index("ch")
    bring(
        (
            (far_live, live), (far_ids, ids), (far_cot.at[group], cot.at[0]), (far_embed, embed), (far_gain, gain),
            (far_in.at[0], in_own), (far_second, second), (far_short, short), (far_skip, skip), (far_out.at[0], raw_out),
            (far_up.at[0], raw_up), (far_down.at[0], raw_down), (far_in1.at[1], in1),
        ),
        done,
    )
    fill_pack(embed, gain, in_own, second, short, skip, pack)
    core, half = rank % 2, lax.axis_size("seq") // 2
    first = group == 0
    holder = jnp.where(rank // half == core, 1, 0)
    values = (core, group, None, group + core - 2 * group * core, rank % half, holder, rank // 2 % 2, rank // 4 % 2, rank // 8 % 2)
    for row, value in enumerate(values):
        if row != LIVE:
            table[row : row + 1, :] = jnp.full((1, 128), value, jnp.int32)
    chosen = jnp.where(first, live[0:1, 0:1], live[0:1, 1:2])
    table[LIVE : LIVE + 1, :] = jnp.broadcast_to(chosen, (1, 128))
    own_ids[0] = jnp.broadcast_to(jnp.where(first, ids[0:1, :], ids[1:2, :]), own_ids.shape[1:])
    s = Numbers(table)
    fill_part(s, raw_out, raw_up, raw_down, part)
    fill_in_part(s, in1, part.at[1152:1536])


def in_hbm(value):
    return pltpu.with_memory_space_constraint(value, pltpu.HBM)


def start(body, outs, *arrays, scratch):
    vmem, far = pl.BlockSpec(memory_space=pltpu.VMEM), pl.BlockSpec(memory_space=pltpu.HBM)
    return pl.pallas_call(
        body, out_shape=outs, in_specs=[far] * len(arrays), out_specs=[vmem] * len(outs), name=body.__name__,
        scratch_shapes=list(scratch),
        cost_estimate=pl.CostEstimate(flops=MANY_FLOPS, bytes_accessed=1, transcendentals=0),
        compiler_params=pltpu.CompilerParams(vmem_limit_bytes=VMEM_LIMIT),
    )(*(in_hbm(v) for v in arrays))


def run(body, outs, scalars, *arrays, scratch=(), after=(), hbm=(), flops=None, hbm_outs=(), aliases=(), token=False):
    vmem = pl.BlockSpec(memory_space=pltpu.VMEM)
    far, wait = pl.BlockSpec(memory_space=pltpu.HBM), pl.BlockSpec(memory_space=pl.ANY)
    single = not isinstance(outs, (list, tuple))
    shapes = [outs] if single else list(outs)
    count = len(shapes)
    shapes += [arr(8, 128)] * token
    used, waits = 1 + len(arrays), len(after)

    def call(table, *refs):
        given, rest = refs[: used - 1], refs[used - 1 + waits :]
        body(Numbers(table), *given, *rest[:count], *rest[count + token :])
        if token:
            rest[count][...] = jnp.zeros((8, 128), f32)

    inner = getattr(body, "func", body)
    CALLS[inner.__name__] += 1
    flops = flops or FLOPS_OF.get(f"{inner.__name__[:-7]}{CALLS[inner.__name__]}", FLOPS)
    result = pl.pallas_call(
        call,
        out_shape=shapes,
        in_specs=[vmem] + [far if i in hbm else vmem for i in range(len(arrays))] + [wait] * waits,
        out_specs=[far if i in hbm_outs else vmem for i in range(len(shapes))],
        input_output_aliases={1 + a: b for a, b in aliases},
        scratch_shapes=list(scratch),
        compiler_params=pltpu.CompilerParams(vmem_limit_bytes=VMEM_LIMITS.get(inner.__name__, VMEM_LIMIT)),
        cost_estimate=pl.CostEstimate(flops=flops, bytes_accessed=1, transcendentals=0),
        name=inner.__name__,
    )(scalars, *(in_hbm(v) if i in hbm else v for i, v in enumerate(arrays)), *after)
    return result[0] if len(shapes) == 1 else result


def arr(*shape, kind=f32):
    return jax.ShapeDtypeStruct(shape, kind)


def mm(a, b):
    return jnp.dot(a, b, preferred_element_type=f32)


def mm_nt(a, b):
    return lax.dot_general(a, b, (((1,), (1,)), ((), ())), preferred_element_type=f32)


def mm_tn(a, b):
    return lax.dot_general(a, b, (((0,), (0,)), ((), ())), preferred_element_type=f32)


def split(a):
    high = a.astype(bf16)
    return high, (a - high.astype(f32)).astype(bf16)


def unit(rows):
    center = rows - jnp.mean(rows, axis=-1, keepdims=True)
    scale = lax.rsqrt(jnp.mean(center * center, axis=-1, keepdims=True) + epsilon)
    return center * scale, scale


def unit_back(grad, normal, scale):
    inner = jnp.mean(grad * normal, axis=-1, keepdims=True)
    return scale * (grad - jnp.mean(grad, axis=-1, keepdims=True) - normal * inner)


def every(count, step):
    for i in range(count):
        step(i, 0)


def at(start, size, unit_rows=16):
    return pl.ds(start if isinstance(start, int) else pl.multiple_of(start, unit_rows), size)


def dft_table():
    turns = np.outer(np.arange(BLOCK), np.arange(BLOCK)) % BLOCK
    angle = 2.0 * np.pi * turns / BLOCK
    return np.concatenate([np.cos(angle), np.sin(angle)], axis=1).astype(np.float32)


def twiddle_table():
    angle = 2.0 * np.pi * np.outer(np.arange(BLOCK), np.arange(1, KINDS)) / (2 * BLOCKS * BLOCK)
    return np.concatenate([np.cos(angle), np.sin(angle)], axis=1).astype(np.float32)


def twiddle_kernel(s, narrow, out):
    for kind in range(KINDS - 1):
        for part in range(2):
            column = (KINDS - 1) * part + kind
            out[kind, part] = jnp.broadcast_to(narrow[:, column : column + 1], (BLOCK, 128))


def feature_table(length):
    places = np.arange(length)
    turns = np.outer(places, np.arange(1, (FEAT - 1) // 2 + 1)) % length
    angle = 2.0 * np.pi * turns / length
    ramp = places[:, None] / length
    return np.concatenate([ramp, np.cos(angle), np.sin(angle)], axis=1).astype(np.float32)


def thirds(values):
    low = lambda v: v.astype(ml_dtypes.bfloat16).astype(np.float32)
    first = low(values)
    second = low(values - first)
    return first, second, low(values - first - second)


def feature_parts(length):
    first, second, third = thirds(np.pad(feature_table(length), ((0, 0), (0, FEAT_ROWS - FEAT))))
    return np.pad(np.concatenate([first, first, second, second, first, third], axis=1), ((0, 0), (0, 256 - 6 * FEAT_ROWS)))


def rate_table():
    return (0.3 * 10.0 ** (np.arange(D) / (D - 1))).astype(np.float32).reshape(2, 1, D // 2)


def four_real(a, b, c, d):
    s, m, t, n = a + c, a - c, b + d, b - d
    hn, ht = ROOT_HALF * n, ROOT_HALF * t
    return (s + t, s - t, (a + hn, -(ht + c)), (m, -n), (a - hn, c - ht))


def turn(k):
    angle = 2.0 * math.pi * k / (2 * BLOCKS)
    return math.cos(angle), math.sin(angle)


def put_pair(stage, kind, row, re, im):
    rows = re.shape[0]
    re, im = re.astype(bf16), im.astype(bf16)
    stage[kind, pl.ds(row, rows), 0:128] = re
    stage[kind, pl.ds(row, rows), 128:256] = im
    stage[kind, pl.ds(row + BLOCK, rows), 0:128] = im
    stage[kind, pl.ds(row + BLOCK, rows), 128:256] = -re


def put_pair_back(stage, kind, row, re, im):
    rows = re.shape[0]
    re, im = re.astype(bf16), im.astype(bf16)
    stage[kind, pl.ds(row, rows), 0:128] = re
    stage[kind, pl.ds(row, rows), 128:256] = im
    stage[kind, pl.ds(row + BLOCK, rows), 0:128] = -im
    stage[kind, pl.ds(row + BLOCK, rows), 128:256] = re


def all_kinds(dft, stage, out):
    table = dft[...]
    for kind in range(KINDS):
        out[kind] = mm(table, stage[kind])


def to_freq(load, dft, twiddle, stage, out):
    def chunk(step, carry):
        row = step * 16
        u = [load(p, row) for p in range(BLOCKS)]
        e0, e4, e1, e2, e3 = four_real(u[0], u[2], u[4], u[6])
        o0, o4, o1, o2, o3 = four_real(u[1], u[3], u[5], u[7])

        def put(kind, re, im):
            c, s = twiddle[kind - 1, 0, pl.ds(row, 16), :], twiddle[kind - 1, 1, pl.ds(row, 16), :]
            put_pair(stage, kind, row, re * c + im * s, im * c - re * s)

        put_pair(stage, 0, row, e0 + o0, jnp.zeros_like(e0))
        last = e0 - o0
        c, s = twiddle[7, 0, pl.ds(row, 16), :], twiddle[7, 1, pl.ds(row, 16), :]
        put_pair(stage, 8, row, last * c, -(last * s))
        put(4, e4, -o4)
        for k, (er, ei), (orr, oi) in ((1, e1, o1), (2, e2, o2), (3, e3, o3)):
            c, s = turn(k)
            wr, wi = orr * c + oi * s, oi * c - orr * s
            put(k, er + wr, ei + wi)
            put(8 - k, er - wr, wi - ei)
        return carry

    every(BLOCK // 16, chunk)
    all_kinds(dft, stage, out)


def from_freq(dft, twiddle, stage, back, store):
    all_kinds(dft, stage, back)

    def chunk(step, carry):
        row = step * 16

        def get(kind):
            re = back[kind, pl.ds(row, 16), 0:128]
            im = back[kind, pl.ds(row, 16), 128:256]
            c, s = twiddle[kind - 1, 0, pl.ds(row, 16), :], twiddle[kind - 1, 1, pl.ds(row, 16), :]
            return re * c - im * s, re * s + im * c

        first = 0.5 * back[0, pl.ds(row, 16), 0:128]
        last = 0.5 * get(8)[0]
        mid_re, mid_im = get(4)
        even, odd = {}, {}
        for k in (1, 2, 3):
            ar, ai = get(k)
            br, bi = get(8 - k)
            even[k] = (ar + br, ai - bi)
            c, s = turn(k)
            dr, di = ar - br, ai + bi
            odd[k] = (dr * c - di * s, dr * s + di * c)
        for shift, base, extra, part in (
            (0, first + last, mid_re, even),
            (1, first - last, -mid_im, odd),
        ):
            (r1, i1), (r2, i2), (r3, i3) = part[1], part[2], part[3]
            plus, minus = base + extra, base - extra
            diff, both = ROOT_HALF * (r1 - r3), ROOT_HALF * (i1 + i3)
            store(shift, row, plus + (r1 + r2 + r3))
            store(shift + 2, row, minus - i2 + (diff - both))
            store(shift + 4, row, plus - r2 - (i1 - i3))
            store(shift + 6, row, minus + i2 - (diff + both))
        return carry

    every(BLOCK // 16, chunk)


def times(first, second, stage, conj):
    def chunk(step, carry):
        row = step * 16
        for kind in range(KINDS):
            fr = first[kind, pl.ds(row, 16), 0:128]
            fi = first[kind, pl.ds(row, 16), 128:256]
            ur = second[kind, pl.ds(row, 16), 0:128]
            ui = second[kind, pl.ds(row, 16), 128:256]
            if conj:
                put_pair_back(stage, kind, row, fr * ur + fi * ui, fr * ui - fi * ur)
            else:
                put_pair_back(stage, kind, row, fr * ur - fi * ui, fr * ui + fi * ur)
        return carry

    every(BLOCK // 16, chunk)


SPECTRUM = (KINDS, BLOCK, 256)


def stage_scratch():
    return pltpu.VMEM((KINDS, 2 * BLOCK, 256), bf16)


def spec_scratch():
    return pltpu.VMEM(SPECTRUM, f32)


PACK_SECOND = 48
PACK_SHORT = 176
PACK_SKIP = 194
PACK_ROWS = 200


def fill_pack(embed, gain, in_own, second, short, skip, out):
    normal, _ = unit(embed[...])
    low = (normal * gain[0, 0:1, :]).astype(bf16)
    for g in range(3):
        out[16 * g : 16 * g + 16, :] = mm(low, in_own[g])
    for l in range(2):
        out[PACK_SECOND + 64 * l : PACK_SECOND + 64 * l + 64, :] = second[l]
        for k in range(3):
            for g in range(3):
                row = PACK_SHORT + 9 * l + 3 * k + g
                out[row : row + 1, :] = short[k, g, l : l + 1, :]
    out[PACK_SKIP : PACK_SKIP + 2, :] = skip[...]
    out[PACK_SKIP + 2 : PACK_ROWS, :] = jnp.zeros((PACK_ROWS - PACK_SKIP - 2, 128), f32)


def table_kernel(s, own, peer, embed, mine_out, other_out, conv_table, gate_table):
    first = s[CORE] == 0
    mine = jnp.where(first, own[...], peer[...])
    other = jnp.where(first, peer[...], own[...])
    mine_out[...] = mine
    other_out[...] = other

    def fill(table, lanes, parts):
        whole = jnp.concatenate(parts, axis=0)
        high, low = split(whole)
        table[0:48, lanes] = high
        table[48:96, lanes] = low
        table[96:128, lanes] = jnp.zeros((32, 128), bf16)

    def gate(pack, g):
        parts = []
        for k in range(3):
            row = PACK_SHORT + 3 * k + g
            parts.append(pack[16 * g : 16 * g + 16] * pack[row : row + 1])
        return parts

    fill(conv_table, slice(0, 128), gate(mine, 1))
    fill(conv_table, slice(128, 256), gate(mine, 2))
    fill(gate_table, slice(0, 128), gate(mine, 0))
    fill(gate_table, slice(128, 256), gate(other, 0))
    zero = jnp.zeros((16, 128), f32)
    fill(gate_table, slice(256, 384), [embed[:, 0:128], zero, zero])
    fill(gate_table, slice(384, 512), [embed[:, 128:256], zero, zero])


def onehot_kernel(s, ids, out, turned, work):
    live = s[LIVE]
    count, _, width = ids.shape
    work[0:HALO, :] = jnp.zeros((HALO, 128), f32)
    work[HALO + count * width : 2 * HALO + count * width, :] = jnp.zeros((HALO, 128), f32)
    vocab = lax.broadcasted_iota(jnp.int32, (128, width), 0) % 16
    place = lax.broadcasted_iota(jnp.int32, (128, width), 1)
    for i in range(count):
        token = jnp.broadcast_to(ids[i, 0:1, :], (128, width))
        hit = (token == vocab) & (place + i * width < live)
        work[HALO + width * i : HALO + width * (i + 1), :] = jnp.where(hit, 1.0, 0.0).T
    lane = lax.broadcasted_iota(jnp.int32, (width, 128), 1) % 48 // 16
    used = lax.broadcasted_iota(jnp.int32, (width, 128), 1) < 96
    half = count // 2
    for i in range(count):
        row = HALO + width * i
        now = work[row : row + width, :]
        one = work[row - 1 : row - 1 + width, :]
        two = work[row - 2 : row - 2 + width, :]
        picked = jnp.where(lane == 0, now, jnp.where(lane == 1, one, two))
        picked = jnp.where(used, picked, 0.0)
        out[row : row + width, :] = picked.astype(bf16)
        turned[i // half, :, width * (i % half) : width * (i % half + 1)] = picked.T.astype(bf16)
    out[0:HALO, :] = jnp.zeros((HALO, 128), bf16)
    out[HALO + count * width : 2 * HALO + count * width, :] = jnp.zeros((HALO, 128), bf16)


def sine_and_cosine(angle):
    turns = jnp.round(angle * (2.0 / math.pi))
    x = ((angle - turns * 1.5703125) - turns * 4.837512969970703125e-4) - turns * 7.549789948768648e-8
    z = x * x
    sin = ((-1.9515295891e-4 * z + 8.3321608736e-3) * z - 1.6666654611e-1) * z * x + x
    cos = ((2.443315711809948e-5 * z - 1.388731625493765e-3) * z + 4.166664568298827e-2) * z * z - 0.5 * z + 1.0
    quarter = turns.astype(jnp.int32) & 3
    odd = (quarter & 1) == 1
    first, second = jnp.where(odd, cos, sin), jnp.where(odd, sin, cos)
    first = jnp.where(quarter >= 2, -first, first)
    second = jnp.where((quarter == 1) | (quarter == 2), -second, second)
    return first, second


def sine_kernel(s, feats, firsts, sine, cosine, turned, padded):
    padded[...] = jnp.zeros_like(padded)
    for l in range(2):
        padded[0:FEAT, 64 * l : 64 * l + 64] = firsts[:, l, :]
    both = padded[...]
    cut = lambda v: v.astype(bf16).astype(f32)
    first = cut(both)
    second = cut(both - first)
    third = both - first - second
    fill = jnp.zeros((256 - 6 * FEAT_ROWS, 128), f32)
    weights = jnp.concatenate([first, second, first, second, third, first, fill], axis=0).astype(bf16)
    count = feats.shape[0] // 512

    def chunk(i, carry):
        rows = at(512 * i, 512)
        act, cosine[rows, :] = sine_and_cosine(mm(feats[rows, :], weights))
        sine[rows, 0:128], sine[rows, 128:256] = split(act)
        turned[:, at(512 * i, 512, 256)] = act.T.astype(bf16)
        return carry

    every(count, chunk)


def decay_of(rates, start, rows, length):
    place = (lax.broadcasted_iota(jnp.int32, (rows, 1), 0) + start).astype(f32) / length
    return jnp.exp(-place * rates), place


def filter_kernel(level, s, sine, mine, rates, dft, twiddle, filt, freq, stage):
    length = sine.shape[0]
    rate = rates[s[WHICH]]
    zero = jnp.zeros((64, 128), f32)
    second = mine[PACK_SECOND + 64 * level : PACK_SECOND + 64 * level + 64]
    high, low = split(jnp.concatenate([zero, second] if level else [second, zero], axis=0))
    twice = jnp.concatenate([high, high], axis=0)

    def chunk(i, carry):
        rows = at(512 * i, 512)
        decay, _ = decay_of(rate, 512 * i, 512, length)
        filt[rows, :] = (mm(sine[rows, :], twice) + mm(sine[rows, 0:128], low)) * decay
        return carry

    every(length // 512, chunk)
    to_freq(lambda p, row: filt[pl.ds(BLOCK * p + row, 16), :] * (1.0 / length), dft, twiddle, stage, freq)


def causal(load, skip_row, freq_filt, dft, twiddle, spec, stage, work, line):
    to_freq(load, dft, twiddle, stage, spec)
    times(freq_filt, spec, stage, False)

    def store(p, row, value):
        line[pl.ds(HALO + BLOCK * p + row, 16), :] = value + skip_row * load(p, row)

    from_freq(dft, twiddle, stage, work, store)


def hand_out(s, line, keep, send):
    half = (line.shape[0] - 2 * HALO) // 2
    span = half + 2 * HALO
    k = s[CORE]
    line[0:HALO, :] = jnp.zeros((HALO, 128), f32)
    line[HALO + 2 * half :, :] = jnp.zeros((HALO, 128), f32)
    keep[...] = line[at(half * k, span), :]
    send[...] = line[at(half * (1 - k), span), :]


def conv_first_kernel(s, onehot, conv_table, mine, freq_filt, dft, twiddle, keep, send, spec, product, stage, work, line):
    def chunk(i, carry):
        rows = at(512 * i, 512)
        pair = mm(onehot[at(512 * i + HALO, 512), :], conv_table[...])
        product[rows, :] = pair[:, 0:128] * pair[:, 128:256]
        return carry

    every(product.shape[0] // 512, chunk)
    skip_row = mine[PACK_SKIP : PACK_SKIP + 1, :]
    causal(lambda p, row: product[pl.ds(BLOCK * p + row, 16), :], skip_row, freq_filt, dft, twiddle, spec, stage, work, line)
    hand_out(s, line, keep, send)


def join_rows(s, whole, kept, received):
    half = kept.shape[0]
    whole[at(half * s[CORE], half), :] = kept[...]
    whole[at(half * (1 - s[CORE]), half), :] = received[...]


def conv_second_kernel(s, kept, received, mine, freq_filt, dft, twiddle, keep, send, spec, product, stage, work, line):
    join_rows(s, product, kept, received)
    skip_row = mine[PACK_SKIP + 1 : PACK_SKIP + 2, :]
    causal(lambda p, row: product[pl.ds(BLOCK * p + row, 16), :], skip_row, freq_filt, dft, twiddle, spec, stage, work, line)
    hand_out(s, line, keep, send)


def gelu_parts(p):
    squared = p * p
    th = jnp.tanh(GELU_A * p * (1.0 + GELU_B * squared))
    half = 0.5 * (1.0 + th)
    slope = half + 0.5 * p * (1.0 - th * th) * (GELU_A + (3.0 * GELU_A * GELU_B) * squared)
    return p * half, slope


def gelu_only(p):
    return 0.5 * p * (1.0 + jnp.tanh(GELU_A * p * (1.0 + GELU_B * (p * p))))


def forward_first_kernel(
    s, onehot, gate_table, conv_mine, conv_other, gain, w_out, w_up, w_down, w_in, mine, other,
    keep, send, mid_out, stream_out, gates, mixed,
):
    span = mid_out.shape[0]
    half = span - 2 * HALO
    k = s[CORE]
    taps = [
        jnp.concatenate([pack[PACK_SHORT + 9 + 3 * t + g : PACK_SHORT + 10 + 3 * t + g, :] for g in range(3) for pack in (mine, other)], axis=1)
        for t in range(3)
    ]

    def chunk(i, carry):
        rows = at(span * i, span)
        looked = mm(onehot[at(half * k + span * i, span), :], gate_table[...])
        conv = jnp.concatenate([conv_mine[rows, :], conv_other[rows, :]], axis=1)
        gated = (conv * looked[:, 0:256]).astype(bf16)
        mid = looked[:, 256:512] + mm(gated, w_out[...])
        mid_out[rows, :] = mid
        normal, _ = unit(mid)
        low = (normal * gain[0, 1:2, :]).astype(bf16)
        hidden = gelu_only(mm(low, w_up[...])).astype(bf16)
        stream = mid + mm(hidden, w_down[...])
        stream_out[rows, :] = stream
        normal, _ = unit(stream)
        low = (normal * gain[1, 0:1, :]).astype(bf16)
        mixed[rows, :] = mm(low, w_in[...])
        return carry

    every(1, chunk)
    gates[0:HALO, :] = jnp.zeros((HALO, 768), f32)
    step = 80
    for start in range(HALO, span, step):
        stop = start + step
        gates[start:stop, :] = (
            taps[0] * mixed[start:stop, :]
            + taps[1] * mixed[start - 1 : stop - 1, :]
            + taps[2] * mixed[start - 2 : stop - 2, :]
        )
    own = slice(HALO, HALO + half)
    keep[...] = gates[own, 256:384] * gates[own, 512:640]
    send[...] = gates[own, 384:512] * gates[own, 640:768]


def turn_back_kernel(
    s, conv_mine, conv_other, gates, stream, cot, cot_rim, gain, w_out, w_up, w_down,
    keep, send, grad_x0, grad_mid, block_out, hidden_out, low_out, normed_out, pre_out, gated_out, mid_low_out, gain_out,
    cot_rows, conv_grads,
):
    span = stream.shape[0]
    half = span - 2 * HALO
    k = s[CORE]
    live = s[LIVE]
    cot_rows[0:HALO, :] = jnp.zeros((HALO, 256), f32)
    cot_rows[HALO : HALO + half, :] = cot[...]
    cot_rows[HALO + half :, :] = jnp.where(k == 0, cot_rim[...], 0.0)
    gain_out[...] = jnp.zeros_like(gain_out)

    def chunk(i, carry):
        rows = at(span * i, span)
        local_row = lax.broadcasted_iota(jnp.int32, (span, 1), 0) + span * i
        keep_mask = (local_row + (half * k - HALO) < live).astype(f32)
        own_mask = ((local_row >= HALO) & (local_row < HALO + half)).astype(f32)
        x0 = gates[rows, 0:256]
        conv = jnp.concatenate([conv_mine[rows, :], conv_other[rows, :]], axis=1)
        gated = (conv * x0).astype(bf16)
        gated_out[rows, :] = gated
        mid = stream[rows, :] + mm(gated, w_out[...])
        normal, scale = unit(mid)
        gain_row = gain[1, 1:2, :]
        low = (normal * gain_row).astype(bf16)
        normed_out[rows, :] = low
        act, slope = gelu_parts(mm(low, w_up[...]))
        hidden = act.astype(bf16)
        hidden_out[rows, :] = hidden
        block_out[rows, :] = (mid + mm(hidden, w_down[...])) * keep_mask
        grad = cot_rows[rows, :] * keep_mask
        grad_low = grad.astype(bf16)
        low_out[rows, :] = grad_low
        grad_pre = (slope * mm_nt(grad_low, w_down[...])).astype(bf16)
        pre_out[rows, :] = grad_pre
        grad_normed = mm_nt(grad_pre, w_up[...])
        gain_out[0:1, :] += jnp.sum(grad_normed * normal * own_mask, axis=0, keepdims=True)
        mid_grad = grad + unit_back(grad_normed * gain_row, normal, scale)
        grad_mid[rows, :] = mid_grad
        mid_low = mid_grad.astype(bf16)
        mid_low_out[rows, :] = mid_low
        grad_gated = mm_nt(mid_low, w_out[...])
        conv_grads[rows, :] = grad_gated * x0
        grad_x0[rows, :] = grad_gated * conv
        return carry

    every(1, chunk)
    own = slice(HALO, HALO + half)
    keep[...] = conv_grads[own, 0:128]
    send[...] = conv_grads[own, 128:256]


def conv_back_kernel(s, kept, received, mine, freq_filt, dft, twiddle, keep, send, spec, grads, stage, work, line):
    join_rows(s, grads, kept, received)
    skip_row = mine[PACK_SKIP + 1 : PACK_SKIP + 2, :]
    load = lambda p, row: grads[pl.ds(BLOCK * p + row, 16), :]
    to_freq(load, dft, twiddle, stage, spec)
    times(freq_filt, spec, stage, True)

    def store(p, row, value):
        line[pl.ds(HALO + BLOCK * p + row, 16), :] = value + skip_row * load(p, row)

    from_freq(dft, twiddle, stage, work, store)
    hand_out(s, line, keep, send)


def grad_freq_kernel(s, kept, received, dft, twiddle, spec, grads, stage):
    join_rows(s, grads, kept, received)
    to_freq(lambda p, row: grads[pl.ds(BLOCK * p + row, 16), :], dft, twiddle, stage, spec)


def filter_back(
    level, s, spec_grad, spec_in, grads, product, filt, cosine, sine_turned, mine, rates, feats_turned, dft, twiddle,
    second_out, first_out, skip_out, stage, work, line,
):
    length = filt.shape[0]
    times(spec_in, spec_grad, stage, True)

    def store(p, row, value):
        line[pl.ds(BLOCK * p + row, 16), :] = value

    from_freq(dft, twiddle, stage, work, store)
    rate = rates[s[WHICH]]
    second = mine[PACK_SECOND + 64 * level : PACK_SECOND + 64 * level + 64, :].astype(bf16)
    weight = jnp.where(s[GROUP] == 0, 0.5 * length, 0.0)
    skip_out[...] = jnp.zeros_like(skip_out)
    second_out[...] = jnp.zeros_like(second_out)
    first_out[...] = jnp.zeros_like(first_out)
    for i in range(length // 512):
        rows = slice(512 * i, 512 * (i + 1))
        decay, place = decay_of(rate, 512 * i, 512, length)
        shaped = ((line[rows, :] * (1.0 / length) + (weight * place) * filt[rows, :]) * decay).astype(bf16)
        skip_out[...] += jnp.sum((grads[rows, :] * product[rows, :]).reshape(64, 8, 128), axis=0)
        second_out[...] += mm(sine_turned[64 * level : 64 * level + 64, rows], shaped)
        inner = (mm_nt(shaped, second) * cosine[rows, 64 * level : 64 * level + 64]).astype(bf16)
        first_out[...] += mm(feats_turned[:, rows], inner)


def filter_back_kernel(s, *refs):
    filter_back(1, s, *refs)


def token_back_kernel(
    s, spec_grad, spec_in, grads, product, filt, cosine, sine_turned, mine, rates, feats_turned, dft, twiddle,
    freq_filt, onehot, turned, conv_table, second_out, first_out, skip_out, by_token, stage, work, line,
):
    length = grads.shape[0]
    skip_row = mine[PACK_SKIP : PACK_SKIP + 1, :]
    times(freq_filt, spec_grad, stage, True)

    def store(p, row, value):
        line[pl.ds(BLOCK * p + row, 16), :] = value + skip_row * grads[pl.ds(BLOCK * p + row, 16), :]

    from_freq(dft, twiddle, stage, work, store)
    by_token[...] = jnp.zeros_like(by_token)
    width = turned.shape[2]
    for i in range(length // width):
        rows = slice(width * i, width * (i + 1))
        pair = mm(onehot[HALO + width * i : HALO + width * (i + 1), :], conv_table[...])
        back = line[rows, :]
        gate_grads = jnp.concatenate([back * pair[:, 128:256], back * pair[:, 0:128]], axis=1).astype(bf16)
        by_token[...] += mm(turned[i], gate_grads)[0:48, :]
    filter_back(
        0, s, spec_grad, spec_in, grads, product, filt, cosine, sine_turned, mine, rates, feats_turned, dft, twiddle,
        second_out, first_out, skip_out, stage, work, line,
    )


def back_gates_kernel(
    s, prod_mine, prod_other, grad_x0, gates, mixed, grad_mid, stream, gain, mine, other, w_in,
    grad_stream, normed_out, mixed_low, short_out, gain_out, line,
):
    span = stream.shape[0]
    half = span - 2 * HALO
    taps = [
        jnp.concatenate([pack[PACK_SHORT + 9 + 3 * t + g : PACK_SHORT + 10 + 3 * t + g, :] for g in range(3) for pack in (mine, other)], axis=1)
        for t in range(3)
    ]
    step = 128
    for start in list(range(HALO, HALO + half, step)) + [HALO + half]:
        stop = start + (step if start < HALO + half else HALO)
        for lanes, prod in ((slice(0, 128), prod_mine), (slice(128, 256), prod_other)):
            first, second = slice(256 + lanes.start, 256 + lanes.stop), slice(512 + lanes.start, 512 + lanes.stop)
            product = prod[start:stop, :]
            line[start:stop, lanes] = product * gates[start:stop, second]
            line[start:stop, first] = product * gates[start:stop, first]
    short_out[...] = jnp.zeros_like(short_out)
    gain_out[...] = jnp.zeros_like(gain_out)
    for start in range(HALO, HALO + half, step):
        stop = start + step
        for g in range(3):
            lanes = slice(256 * g, 256 * g + 256)
            values = mixed[start:stop, lanes]
            total = None
            for t in range(3):
                shifted = grad_x0[start + t : stop + t, :] if g == 0 else line[start + t : stop + t, 256 * g - 256 : 256 * g]
                part = taps[t][:, lanes] * shifted
                total = part if total is None else total + part
                short_out[t, :, lanes] += jnp.sum((shifted * values).reshape(step // 8, 8, 256), axis=0)
            mixed_low[start - HALO : stop - HALO, lanes] = total.astype(bf16)

    def chunk(i, carry):
        rows = at(512 * i, 512)
        wide = at(512 * i + HALO, 512)
        normal, scale = unit(stream[wide, :])
        gain_row = gain[1, 0:1, :]
        normed_out[rows, :] = (normal * gain_row).astype(bf16)
        grad_normed = mm_nt(mixed_low[rows, :], w_in[...])
        gain_out[0:1, :] += jnp.sum(grad_normed * normal, axis=0, keepdims=True)
        grad_stream[rows, :] = grad_mid[wide, :] + unit_back(grad_normed * gain_row, normal, scale)
        return carry

    every(half // 512, chunk)


def back_first_kernel(
    s, grad_stream, mid, onehot, turned, gate_table, conv_mine, conv_other, gain, w_out, w_up, w_down,
    keep, send, hidden_out, low_out, normed_out, pre_out, gated_out, mid_low_out, by_token, gain_out,
):
    half = grad_stream.shape[0]
    k = s[CORE]
    by_token[...] = jnp.zeros_like(by_token)
    gain_out[...] = jnp.zeros_like(gain_out)

    def chunk(i, carry):
        rows = at(half * i, half)
        wide = at(half * i + HALO, half)
        hot = onehot[at(half * k + half * i + HALO, half), :]
        x0 = mm(hot, gate_table[:, 0:256])
        conv = jnp.concatenate([conv_mine[wide, :], conv_other[wide, :]], axis=1)
        gated_out[rows, :] = (conv * x0).astype(bf16)
        normal, scale = unit(mid[wide, :])
        gain_row = gain[0, 1:2, :]
        low = (normal * gain_row).astype(bf16)
        normed_out[rows, :] = low
        act, slope = gelu_parts(mm(low, w_up[...]))
        hidden_out[rows, :] = act.astype(bf16)
        grad = grad_stream[rows, :]
        grad_low = grad.astype(bf16)
        low_out[rows, :] = grad_low
        grad_pre = (slope * mm_nt(grad_low, w_down[...])).astype(bf16)
        pre_out[rows, :] = grad_pre
        grad_normed = mm_nt(grad_pre, w_up[...])
        gain_out[0:1, :] += jnp.sum(grad_normed * normal, axis=0, keepdims=True)
        mid_grad = grad + unit_back(grad_normed * gain_row, normal, scale)
        mid_low = mid_grad.astype(bf16)
        mid_low_out[rows, :] = mid_low
        grad_gated = mm_nt(mid_low, w_out[...])
        conv_grad = grad_gated * x0
        keep[rows, :] = conv_grad[:, 0:128]
        send[rows, :] = conv_grad[:, 128:256]
        flips = turned[k, :, at(half * i, half, 256)]
        rest = mid_grad - mid_low.astype(f32)
        gate_grads = jnp.concatenate([(grad_gated * conv).astype(bf16), mid_low, rest.astype(bf16)], axis=1)
        by_token[...] += mm(flips, gate_grads)[0:48, :]
        return carry

    every(1, chunk)


R_OUT, R_UP, R_DOWN, R_IN = 128, 512, 512, 384


def fill_part(s, raw_out, raw_up, raw_down, out):
    first = s[CORE] == 0
    pick = lambda a, b: jnp.where(first, a.astype(f32), b.astype(f32))
    out[0:128, :] = pick(raw_out[:, 0:128], raw_out[:, 128:256])
    for j in range(2):
        lanes = slice(128 * j, 128 * j + 128)
        out[128 + 256 * j : 384 + 256 * j, :] = pick(
            raw_up[:, 128 * j : 128 * j + 128], raw_up[:, 256 + 128 * j : 384 + 128 * j]
        )
        out[640 + 256 * j : 896 + 256 * j, :] = pick(raw_down[0:256, lanes], raw_down[256:512, lanes])


def fill_in_part(s, raw_in, out):
    first = s[CORE] == 0
    for g in range(3):
        a, b = raw_in[g, 0:128, :].astype(f32), raw_in[g, 128:256, :].astype(f32)
        out[128 * g : 128 * g + 128, :] = jnp.where(first, a, b)


def send_weights_kernel(s, w_out, w_up, w_down, out, raw_out, raw_up, raw_down, done):
    bring(((w_out.at[1], raw_out), (w_up.at[1], raw_up), (w_down.at[1], raw_down)), done)
    fill_part(s, raw_out, raw_up, raw_down, out)


def cot_split_kernel(s, blocks, keep, send):
    k = s[CORE]
    few = keep.shape[0]
    keep[...] = blocks[pl.ds(few * k, few)]
    send[...] = blocks[pl.ds(few * (1 - k), few)]


def cot_half_kernel(s, own, received, blocks, out):
    spot, width = s[CORE], own.shape[1]
    for j in range(own.shape[0]):
        out[pl.ds(width * (2 * j + spot), width), :] = own[j]
        out[pl.ds(width * (2 * j + 1 - spot), width), :] = received[j]
    out[2 * own.shape[0] * width :, :] = blocks[own.shape[0], 0:HALO, :]


def cot_whole_kernel(s, own, received, out, rim):
    spot = s[BIT1]
    rows = own.shape[0] - HALO
    two = rows // 2
    for j in range(2):
        out[pl.ds(two * (2 * j + spot), two), :] = own[two * j : two * j + two, :]
        out[pl.ds(two * (2 * j + 1 - spot), two), :] = received[two * j : two * j + two, :]
    rim[...] = jnp.where(spot == 0, own[rows:, :], received[rows:, :])


def relay_kernel(s, value, out):
    out[...] = value[...]


def join_weights_kernel(level, s, w_out, w_up, w_down, w_in, first_part, second_part, out_full, up_full, down_full, *in_full):
    first = s[CORE] == 0
    low = lambda ref, a, b: ref[a:b, :].astype(bf16)
    pick = lambda a, b: jnp.where(first, a, b)
    mine_out = w_out[level]
    a, b = first_part[0:128, :], second_part[0:128, :]
    peer_out = jnp.concatenate([pick(a, b), pick(b, a)], axis=1)
    out_full[0:128, :] = pick(mine_out.astype(f32), peer_out).astype(bf16)
    out_full[128:256, :] = pick(peer_out, mine_out.astype(f32)).astype(bf16)
    up_a, up_b = w_up[level, :, 0:256].astype(f32), w_up[level, :, 256:512].astype(f32)
    up_full[:, 0:256] = pick(up_a, up_b).astype(bf16)
    up_full[:, 256:512] = pick(up_b, up_a).astype(bf16)
    down_a, down_b = w_down[level, 0:256, :].astype(f32), w_down[level, 256:512, :].astype(f32)
    down_full[0:256, :] = pick(down_a, down_b).astype(bf16)
    down_full[256:512, :] = pick(down_b, down_a).astype(bf16)
    for n, part in enumerate((first_part, second_part)):
        for j in range(2):
            up_full[:, 512 + 256 * n + 128 * j : 640 + 256 * n + 128 * j] = low(part, 128 + 256 * j, 384 + 256 * j)
            down_full[512 + 256 * n : 768 + 256 * n, 128 * j : 128 * j + 128] = low(part, 640 + 256 * j, 896 + 256 * j)
    if in_full:
        (full,) = in_full
        for g in range(3):
            own = w_in[1 - level, g].astype(f32)
            a, b = first_part[1152 + 128 * g : 1280 + 128 * g, :], second_part[1152 + 128 * g : 1280 + 128 * g, :]
            peer = jnp.concatenate([pick(a, b), pick(b, a)], axis=0)
            full[:, 256 * g : 256 * g + 128] = pick(own, peer).astype(bf16)
            full[:, 256 * g + 128 : 256 * g + 256] = pick(peer, own).astype(bf16)


def wide_grads_kernel(pad, s, gated, mid_low, normed, grad_pre, hidden, grad_low, keep, send):
    k = s[CORE]
    first = k == 0
    stop = gated.shape[0] - pad
    own = lambda ref: ref[pad:stop, :]
    out = mm_tn(own(gated), own(mid_low))
    for m in range(2):
        a, b = out[128 * m : 128 * m + 128, 0:128], out[128 * m : 128 * m + 128, 128:256]
        half = m + k - 2 * m * k
        keep[half, 0:128, :] = jnp.where(first, a, b)
        send[half, 0:128, :] = jnp.where(first, b, a)
    for j in range(4):
        target = (keep, send)[j % 2]
        up = mm_tn(own(normed), grad_pre[pad:stop, 256 * j : 256 * j + 256])
        down = mm_tn(hidden[pad:stop, 256 * j : 256 * j + 256], own(grad_low))
        for n in range(2):
            lanes = slice(128 * n, 128 * n + 128)
            target[j // 2, 128 + 256 * n : 384 + 256 * n, :] = up[:, lanes]
            target[j // 2, 640 + 256 * n : 896 + 256 * n, :] = down[:, lanes]


def in_grads_kernel(s, normed_in, mixed_low, keep, send):
    k = s[CORE]
    first = k == 0
    for g in range(3):
        both = mm_tn(normed_in[...], mixed_low[:, 256 * g : 256 * g + 256])
        for m in range(2):
            block = both[:, 128 * m : 128 * m + 128]
            half = m + k - 2 * m * k
            keep[half, 128 * g : 128 * g + 128, :] = jnp.where(first, block[0:128], block[128:256])
            send[half, 128 * g : 128 * g + 128, :] = jnp.where(first, block[128:256], block[0:128])


def add_kernel(s, kept, received, own_out, peer_out):
    own_out[...] = kept[0] + received[0]
    peer_out[...] = kept[1] + received[1]


def add_half_kernel(s, kept, received, w_in, own_out, peer_out):
    rows = own_out.shape[0]
    part = at(rows * s[BIT1], rows, 8)
    own_out[...] = kept[0, part, :] + received[0, part, :]
    peer_out[0:rows, :] = kept[1, part, :] + received[1, part, :]
    fill_in_part(s, w_in.at[0], peer_out.at[rows : rows + 384])


def take_half_kernel(s, own, received, out, in_out):
    rows = own.shape[0]
    out[...] = own[...] + received[0:rows, :]
    in_out[...] = received[rows:, :]


def add_one_kernel(s, kept, received, out):
    out[...] = kept[...] + received[...]


def spread_wide_kernel(level, s, *refs):
    if level:
        outs, (a, b, out, up, down), done = refs[-9:-6], refs[-6:-1], refs[-1]
        rows = refs[0].shape[0]
        for whole, near, far in ((a, refs[0], refs[1]), (b, refs[2], refs[3])):
            whole[at(rows * s[BIT1], rows, 8), :] = near[...]
            whole[at(rows * (1 - s[BIT1]), rows, 8), :] = far[...]
    else:
        outs, (out, up, down), done = refs[-7:-4], refs[-4:-1], refs[-1]
        a, b = refs[:2]
    first = s[CORE] == 0
    pick = lambda x, y: jnp.where(first, x, y)

    def both(row, rows):
        x, y = a[row : row + rows, :], b[row : row + rows, :]
        return pick(x, y), pick(y, x)

    copies = [pltpu.make_async_copy(v, w.at[level], done.at[n]) for n, (v, w) in enumerate(zip((out, up, down), outs))]
    x, y = both(0, 128)
    out[:, 0:128] = x
    out[:, 128:256] = y
    copies[0].start()
    for j in range(2):
        x, y = both(128 + 256 * j, 256)
        up[:, 128 * j : 128 * j + 128] = x
        up[:, 256 + 128 * j : 384 + 128 * j] = y
    copies[1].start()
    for j in range(2):
        lanes = slice(128 * j, 128 * j + 128)
        x, y = both(640 + 256 * j, 256)
        down[0:256, lanes] = x
        down[256:512, lanes] = y
    copies[2].start()
    for copy in copies:
        copy.wait()


def spread_in_kernel(s, kept, received, whole, near, done):
    first = s[CORE] == 0
    for g in range(3):
        x, y = kept[128 * g : 128 * g + 128, :], received[128 * g : 128 * g + 128, :]
        near[g, 0:128, :] = jnp.where(first, x, y)
        near[g, 128:256, :] = jnp.where(first, y, x)
    bring(((near, whole.at[1]),), done)


def pair_kernel(bit, s, own, received, out):
    spot = s[(CORE, BIT1, BIT2, BIT3)[bit]]
    for j in range(own.shape[0]):
        out[2 * j + spot] = own[j]
        out[2 * j + 1 - spot] = received[j]


E_GAIN, E_EMBED, E_FIRST, E_SHORT, E_TOKEN, E_ROWS = 0, 8, 24, 40, 56, 104
EM_SECOND, EM_SKIP, EM_ROWS = 0, 64, 72
L_TOKEN, L_SECOND, L_SKIP, L_ROWS = 0, 96, 160, 168
FIRST_ROWS = 16


def fold_first(values):
    last = jnp.concatenate([values[32:40], jnp.zeros((8, 64), f32)], axis=0)
    return jnp.concatenate([values[0:16], values[16:32], last, jnp.zeros((16, 64), f32)], axis=1)


def unfold_first(values):
    return jnp.concatenate([values[:, 0:64], values[:, 64:128], values[0:8, 128:192]], axis=0)[0:FEAT]


def early_kernel(s, gain_mid1, gain_in1, gain_mid0, by_token0, first1, short1, second1, skip1, flat, mine):
    k = s[CORE]
    flat[...] = jnp.zeros_like(flat)
    for row, values in enumerate((gain_mid1, gain_in1, gain_mid0)):
        flat[E_GAIN + row : E_GAIN + row + 1, :] = values[0:1, :]
    flat[E_EMBED : E_EMBED + 16, :] = by_token0[0:16, 256:512] + by_token0[0:16, 512:768]
    flat[E_FIRST : E_FIRST + FIRST_ROWS, :] = fold_first(first1[...])
    swap = lambda v: jnp.where(k == 0, v, jnp.concatenate([v[:, 128:256], v[:, 0:128]], axis=1))
    for t in range(3):
        total = jnp.sum(short1[t], axis=0, keepdims=True)
        for g in range(3):
            flat[E_SHORT + 3 * t + g : E_SHORT + 3 * t + g + 1, :] = swap(total[:, 256 * g : 256 * g + 256])
    flat[E_TOKEN : E_TOKEN + 48, :] = swap(by_token0[:, 0:256])
    mine[EM_SECOND : EM_SECOND + 64, :] = second1[...]
    mine[EM_SKIP : EM_SKIP + 8, :] = jnp.broadcast_to(jnp.sum(skip1[...], axis=0, keepdims=True), (8, 128))


def late_kernel(s, by_token12, second0, skip0, first0, mine, first_out):
    mine[L_TOKEN : L_TOKEN + 48, :] = by_token12[:, 0:128]
    mine[L_TOKEN + 48 : L_TOKEN + 96, :] = by_token12[:, 128:256]
    mine[L_SECOND : L_SECOND + 64, :] = second0[...]
    mine[L_SKIP : L_SKIP + 8, :] = jnp.broadcast_to(jnp.sum(skip0[...], axis=0, keepdims=True), (8, 128))
    first_out[...] = fold_first(first0[...])


FOLDED, HALF_ROWS = 40, 72


def chip_kernel(s, flat, flat_in, mine, mine_in, out, send):
    first = s[CORE] == 0
    rows = flat.shape[0]
    out[0:rows, :] = flat[...] + flat_in[...]
    out[rows:, 0:128] = jnp.where(first, mine[...], mine_in[...])
    out[rows:, 128:256] = jnp.where(first, mine_in[...], mine[...])
    whole = send.shape[0] - FOLDED
    rest = HALF_ROWS - FOLDED
    send[0:whole, :] = out[0:whole, :]
    send[whole:, 0:128] = out[whole : whole + FOLDED, 128:256]
    send[whole : whole + rest, 128:256] = out[whole + FOLDED : whole + HALF_ROWS, 128:256]
    send[whole + rest :, 128:256] = jnp.zeros((FOLDED - rest, 128), f32)


def last_kernel(
    s, early, early_in, late, late_in, embed, gain, own, peer, w_own, w_first, w_second, in_given,
    embed_out, gain_out, in_whole, short_out, first_out, second_out, skip_out, in_out, done,
):
    pick = lambda x, y: jnp.where(s[CORE] == 0, x, y)

    def plain(pair, row, rows):
        return pair[0][row : row + rows, :] + pair[1][row : row + rows, :]

    def halves(pair, row, rows):
        here, there = pair
        left = here[row : row + rows, 0:128] + there[row : row + rows, 128:256]
        right = here[row : row + rows, 128:256] + there[row : row + rows, 0:128]
        return left, right

    def own_half(pair, row, rows):
        here, there = pair
        whole, rest = there.shape[0] - FOLDED, HALF_ROWS - FOLDED
        folded = jnp.concatenate([there[whole:, 0:128], there[whole : whole + rest, 128:256]], axis=0)
        return here[whole + row : whole + row + rows, 0:128] + folded[row : row + rows]

    early, late = (early, early_in), (late, late_in)
    gains = plain(early, E_GAIN, 8)
    gain_out[1, 0:1, :] = gains[1:2, :]
    gain_out[1, 1:2, :] = gains[0:1, :]
    gain_out[0, 1:2, :] = gains[2:3, :]
    first_out[:, 0, :] = unfold_first(plain(late, 0, FIRST_ROWS))
    first_out[:, 1, :] = unfold_first(plain(early, E_FIRST, FIRST_ROWS))
    short = halves(early, E_SHORT, 16)[0]
    for t in range(3):
        for g in range(3):
            short_out[t, g, 1:2, :] = short[3 * t + g : 3 * t + g + 1, :]
    second_out[1] = own_half(early, 0, 64)
    second_out[0] = own_half(late, 0, 64)
    skip_out[0:1, :] = own_half(late, 64, 8)[0:1]
    skip_out[1:2, :] = own_half(early, 64, 8)[0:1]
    tokens = [
        halves(early, E_TOKEN, 48),
        halves(late, FIRST_ROWS + L_TOKEN, 48),
        halves(late, FIRST_ROWS + L_TOKEN + 48, 48),
    ]
    normal, scale = unit(embed[...])
    gain_row = gain[0, 0:1, :]
    low = (normal * gain_row).astype(bf16)
    grad_normed = jnp.zeros((16, 256), f32)
    copies = []
    for g in range(3):
        for h, pack in ((0, own), (1, peer)):
            grads = tokens[g][h]
            table = pack[16 * g : 16 * g + 16, :]
            summed = jnp.zeros((16, 128), f32)
            for t in range(3):
                row = PACK_SHORT + 3 * t + g
                part = grads[16 * t : 16 * t + 16, :]
                summed += pack[row : row + 1, :] * part
                if h == 0:
                    short_out[t, g, 0:1, :] = jnp.sum(table * part, axis=0, keepdims=True)
            high, rest = split(summed)
            if h == 0:
                in_out[g] = mm_tn(low, high) + mm_tn(low, rest)
                copies.append(pltpu.make_async_copy(in_out.at[g], in_whole.at[0, g], done.at[g]))
                copies[-1].start()
                weight = w_own[0, g]
            else:
                rows = slice(128 * g, 128 * g + 128)
                a, b = w_first[rows, :], w_second[rows, :]
                weight = jnp.concatenate([pick(a, b), pick(b, a)], axis=0).astype(bf16)
            grad_normed += mm_nt(high, weight) + mm_nt(rest, weight)
    gain_out[0, 0:1, :] = jnp.sum(grad_normed * normal, axis=0, keepdims=True)
    embed_out[...] = plain(early, E_EMBED, 16) + unit_back(grad_normed * gain_row, normal, scale)
    for copy in copies:
        copy.wait()


def block_send_kernel(s, block_out, mine, other):
    spot = s[SPOT]
    mine[...] = block_out[at(HALO + 128 * spot, 128), :]
    near = spot + 1 - 2 * s[CORE]
    other[...] = block_out[at(HALO + 128 * near, 128), :]


def block_pick_kernel(s, mine, received, out):
    out[...] = jnp.where(s[HOLDER] == 1, mine[...], received[...])


def block_join_kernel(s, here, there, out):
    first = s[GROUP] == 0
    out[0] = jnp.where(first, here[...], there[...])
    out[1] = jnp.where(first, there[...], here[...])


def chip_local(
    ids, live, embed, norm_gain, in_weight, short_kernel, filter_first, filter_second, skip_gain,
    out_weight, up_weight, down_weight, cotangent,
):
    CALLS.clear()
    count = lax.axis_size("seq")
    rank = lax.axis_index("seq")
    group = lax.axis_index("ch")
    width = ids.shape[1]
    length = width * count
    half = length // 2
    span = half + 2 * HALO
    core = rank % 2
    across = lambda v: lax.ppermute(v, "ch", [(0, 1), (1, 0)])
    trade = lambda v, bit: lax.ppermute(v, "seq", [(i, i ^ bit) for i in range(count)])
    beside = lambda v: trade(v, 1)
    dft = jnp.asarray(dft_table()).astype(bf16)
    feats = jnp.asarray(feature_parts(length)).astype(bf16)
    feats_turned = jnp.asarray(np.pad(feature_table(length).T, ((0, FEAT_ROWS - FEAT), (0, 0)))).astype(bf16)
    rates = jnp.asarray(rate_table())
    low = lambda *shape: arr(*shape, kind=bf16)
    line = pltpu.VMEM((length + 2 * HALO, 128), f32)
    conv_scratch = [stage_scratch(), spec_scratch(), line]
    pair = lambda bit, v, w, **kw: run(
        functools.partial(pair_kernel, bit), jax.ShapeDtypeStruct((2 * v.shape[0],) + v.shape[1:], v.dtype), s, v, w, **kw
    )

    row_shape = lambda rows: arr(rows, 8, width, kind=jnp.int32)
    in_own = jnp.swapaxes(in_weight, 1, 2)
    packed = (embed, norm_gain, in_own, filter_second, jnp.transpose(short_kernel, (1, 2, 0, 3)), skip_gain)
    wide = (out_weight, up_weight, down_weight)
    held = [(1, 2), ids.shape, embed.shape, norm_gain.shape, in_own.shape[1:], filter_second.shape, packed[4].shape, skip_gain.shape]
    held += [v.shape[1:] for v in wide] + [in_own.shape[1:]]
    kinds = [jnp.int32, jnp.int32, f32, f32, bf16, f32, f32, f32] + [bf16] * 4
    s, ids1, cot1, pack, part0 = start(
        numbers_kernel,
        [arr(NUMBER_ROWS, 128, kind=jnp.int32), row_shape(1), arr(1, width, 256), arr(PACK_ROWS, 128), arr(1536, 128)],
        live.reshape(1, 2), ids, cotangent, *packed, *wide, in_own,
        scratch=[pltpu.VMEM(shape, kind) for shape, kind in zip(held, kinds)] + [pltpu.SemaphoreType.DMA((13,))],
    )
    pack_in = across(pack)
    part0_in = across(part0)
    ids2 = pair(3, ids1, trade(ids1, 8))
    sine, cosine, sine_turned = run(
        sine_kernel, [low(length, 256), arr(length, 128), low(128, length)], s, feats, jnp.transpose(filter_first, (1, 0, 2)),
        after=(ids2,), scratch=[pltpu.VMEM((FEAT_ROWS, 128), f32)],
    )
    twiddle = run(twiddle_kernel, arr(KINDS - 1, 2, BLOCK, 128), s, jnp.asarray(twiddle_table()), after=(sine,))
    cot2 = pair(3, cot1, trade(cot1, 8), after=(twiddle,))
    ids4 = pair(2, ids2, trade(ids2, 4), after=(cot2,))
    part1 = run(
        send_weights_kernel, arr(1152, 128), s, *wide, hbm=range(3), after=(ids4,),
        scratch=[pltpu.VMEM(v.shape[1:], v.dtype) for v in wide] + [pltpu.SemaphoreType.DMA((3,))],
    )
    part1_in = across(part1)
    mine, other, conv_table, gate_table = run(
        table_kernel, [arr(PACK_ROWS, 128), arr(PACK_ROWS, 128), low(128, 256), low(128, 512)], s, pack, pack_in, embed,
        after=(part1,),
    )
    make_filter = lambda level, after: run(
        functools.partial(filter_kernel, level), [arr(length, 128), arr(*SPECTRUM)], s, sine, mine, rates, dft, twiddle,
        scratch=[stage_scratch()], after=after,
    )
    filt0, freq0 = make_filter(0, ())
    ids8 = pair(1, ids4, trade(ids4, 2), after=(filt0,))
    cot4 = pair(2, cot2, trade(cot2, 4), after=(ids8,))
    cot_keep, cot_send = run(cot_split_kernel, [arr(2, width, 256), arr(2, width, 256)], s, cot4)
    all_ids = pair(0, ids8, beside(ids8), after=(cot_send,))
    onehot, turned = run(
        onehot_kernel, [low(length + 2 * HALO, 128), low(2, 128, half)], s, all_ids,
        scratch=[pltpu.VMEM((length + 2 * HALO, 128), f32)],
    )
    conv_mine0, sent, spec0, product0 = run(
        conv_first_kernel, [arr(span, 128), arr(span, 128), arr(*SPECTRUM), arr(length, 128)],
        s, onehot, conv_table, mine, freq0, dft, twiddle, scratch=conv_scratch,
    )
    conv_other0 = beside(sent)
    first_part = run(relay_kernel, arr(1536, 128), s, part0_in, after=(sent,))
    first_beside = beside(first_part)
    cot_half = run(cot_half_kernel, arr(4 * width + HALO, 256), s, cot_keep, beside(cot_send), cot4, after=(first_part,))
    cot_half_in = trade(cot_half, 2)
    filt1, freq1 = make_filter(1, (first_part, cot_half))
    w_out0, w_up0, w_down0, w_in1 = run(
        functools.partial(join_weights_kernel, 0), [low(256, 256), low(256, 1024), low(1024, 256), low(256, 768)],
        s, out_weight, up_weight, down_weight, in_own, first_part, first_beside, after=(cot_half,),
    )
    kept, sent, mid0, stream1, gates1, mixed1 = run(
        forward_first_kernel,
        [arr(half, 128), arr(half, 128), arr(span, 256), arr(span, 256), arr(span, 768), arr(span, 768)],
        s, onehot, gate_table, conv_mine0, conv_other0, norm_gain, w_out0, w_up0, w_down0, w_in1, mine, other,
    )
    received = beside(sent)
    second_part = run(relay_kernel, arr(1152, 128), s, part1_in, after=(sent,))
    second_beside = beside(second_part)
    conv_mine1, sent, spec1, product1 = run(
        conv_second_kernel, [arr(span, 128), arr(span, 128), arr(*SPECTRUM), arr(length, 128)],
        s, kept, received, mine, freq1, dft, twiddle, scratch=conv_scratch, after=(second_part,),
    )
    conv_other1 = beside(sent)
    cot, cot_rim = run(cot_whole_kernel, [arr(half, 256), arr(HALO, 256)], s, cot_half, cot_half_in, after=(sent,))
    w_out1, w_up1, w_down1 = run(
        functools.partial(join_weights_kernel, 1), [low(256, 256), low(256, 1024), low(1024, 256)],
        s, out_weight, up_weight, down_weight, in_own, second_part, second_beside, after=(cot_rim,),
    )
    (kept, sent, grad_x0, grad_mid1, block, hidden, grad_low, normed, grad_pre, gated, mid_low, gain_mid1) = run(
        turn_back_kernel,
        [
            arr(half, 128), arr(half, 128), arr(span, 256), arr(span, 256), arr(span, 256), low(span, 1024), low(span, 256),
            low(span, 256), low(span, 1024), low(span, 256), low(span, 256), arr(8, 256),
        ],
        s, conv_mine1, conv_other1, gates1, stream1, cot, cot_rim, norm_gain, w_out1, w_up1, w_down1,
        scratch=[pltpu.VMEM((span, 256), f32), pltpu.VMEM((span, 256), f32)],
    )
    received = beside(sent)
    grads_keep1, grads_send1 = run(
        functools.partial(wide_grads_kernel, HALO), [arr(2, 1152, 128), arr(2, 1152, 128)],
        s, gated, mid_low, normed, grad_pre, hidden, grad_low,
    )
    block_mine, block_other = run(block_send_kernel, [arr(width, 256), arr(width, 256)], s, block)
    grads_in1 = beside(grads_send1)
    block_beside = beside(block_other)

    prod_mine, sent, spec_grad1, grads1 = run(
        conv_back_kernel, [arr(span, 128), arr(span, 128), arr(*SPECTRUM), arr(length, 128)],
        s, kept, received, mine, freq1, dft, twiddle, scratch=conv_scratch, after=(grads_send1, block_mine),
    )
    prod_other = beside(sent)
    own1, peer1 = run(add_half_kernel, [arr(576, 128), arr(960, 128)], s, grads_keep1, grads_in1, in_own, after=(sent,))
    across1 = across(peer1)
    filter_shapes = [arr(64, 128), arr(40, 64), arr(8, 128)]
    filter_scratch = [stage_scratch(), spec_scratch(), pltpu.VMEM((length, 128), f32)]
    second1, first1, skip1 = run(
        filter_back_kernel, filter_shapes, s, spec_grad1, spec1, grads1, product1, filt1, cosine,
        sine_turned, mine, rates, feats_turned, dft, twiddle, scratch=filter_scratch, after=(peer1,),
    )
    grad_stream1, normed_in, mixed_low, short1, gain_in1 = run(
        back_gates_kernel,
        [arr(half, 256), low(half, 256), low(half, 768), arr(3, 8, 768), arr(8, 256)],
        s, prod_mine, prod_other, grad_x0, gates1, mixed1, grad_mid1, stream1, norm_gain, mine, other, w_in1,
        scratch=[pltpu.VMEM((span, 512), f32)], after=(skip1,),
    )
    in_keep, in_send = run(in_grads_kernel, [arr(2, 384, 128), arr(2, 384, 128)], s, normed_in, mixed_low)
    in_beside = beside(in_send)
    block_here = run(block_pick_kernel, arr(width, 256), s, block_mine, block_beside, after=(in_send,))
    block_across = across(block_here)
    in_own1, in_peer1 = run(add_kernel, [arr(384, 128), arr(384, 128)], s, in_keep, in_beside, after=(block_here,))
    in_across = across(in_peer1)
    (kept, sent, hidden, grad_low, normed, grad_pre, gated, mid_low, by_token0, gain_mid0) = run(
        back_first_kernel,
        [
            arr(half, 128), arr(half, 128), low(half, 1024), low(half, 256), low(half, 256), low(half, 1024), low(half, 256),
            low(half, 256), arr(48, 768), arr(8, 256),
        ],
        s, grad_stream1, mid0, onehot, turned, gate_table, conv_mine0, conv_other0, norm_gain, w_out0, w_up0, w_down0,
        after=(in_peer1,),
    )
    received = beside(sent)
    early_flat, early_mine = run(
        early_kernel, [arr(E_ROWS, 256), arr(EM_ROWS, 128)],
        s, gain_mid1, gain_in1, gain_mid0, by_token0, first1, short1, second1, skip1,
    )
    early_flat_in, early_mine_in = beside(early_flat), beside(early_mine)
    grads_keep0, grads_send0 = run(
        functools.partial(wide_grads_kernel, 0), [arr(2, 1152, 128), arr(2, 1152, 128)],
        s, gated, mid_low, normed, grad_pre, hidden, grad_low, after=(early_flat,),
    )
    grads_in0 = beside(grads_send0)
    early, early_send = run(
        chip_kernel, [arr(E_ROWS + EM_ROWS, 256), arr(E_ROWS + FOLDED, 256)],
        s, early_flat, early_flat_in, early_mine, early_mine_in, after=(grads_send0,),
    )
    early_in = across(early_send)
    spec_grad0, grads0 = run(
        grad_freq_kernel, [arr(*SPECTRUM), arr(length, 128)], s, kept, received, dft, twiddle, scratch=[stage_scratch()],
        after=(early,),
    )
    own0, peer0 = run(add_kernel, [arr(1152, 128), arr(1152, 128)], s, grads_keep0, grads_in0, after=(spec_grad0,))
    across0 = across(peer0)
    total1, in0_first = run(take_half_kernel, [arr(576, 128), arr(384, 128)], s, own1, across1, after=(peer0,))
    total1_y, in0_second = trade(total1, 2), beside(in0_first)
    second0, first0, skip0, by_token12 = run(
        token_back_kernel, filter_shapes + [arr(48, 256)], s, spec_grad0, spec0, grads0, product0, filt0, cosine,
        sine_turned, mine, rates, feats_turned, dft, twiddle, freq0, onehot, turned, conv_table, scratch=filter_scratch,
        after=(peer0, early),
    )
    wide_shapes = [arr(2, 128, 256), arr(2, 256, 512), arr(2, 512, 256)]
    wide_scratch = [pltpu.VMEM(v.shape[1:], f32) for v in wide_shapes] + [pltpu.SemaphoreType.DMA((3,))]
    late_mine, late_first = run(
        late_kernel, [arr(L_ROWS, 128), arr(FIRST_ROWS, 256)], s, by_token12, second0, skip0, first0, flops=FEW_FLOPS
    )
    late_mine_in, late_first_in = beside(late_mine), beside(late_first)
    in_total = run(add_one_kernel, arr(384, 128), s, in_own1, in_across, after=(late_mine,), flops=FEW_FLOPS)
    block_out, joined = run(block_join_kernel, arr(2, width, 256), s, block_here, block_across, after=(late_mine,), flops=FEW_FLOPS, token=True)
    late, late_send = run(
        chip_kernel, [arr(FIRST_ROWS + L_ROWS, 256), arr(FIRST_ROWS + L_SECOND + FOLDED, 256)], s, late_first, late_first_in, late_mine, late_mine_in, flops=FEW_FLOPS,
        after=(joined, in_total, early_in),
    )
    late_in = across(late_send)
    near1_y = run(relay_kernel, arr(576, 128), s, total1_y, after=(late,), flops=FEW_FLOPS)
    quarters1 = (total1, near1_y, beside(total1), beside(near1_y))
    in_total_beside = beside(in_total)
    *wide_buffers, wide_spread = run(
        functools.partial(spread_wide_kernel, 1), wide_shapes, s, *quarters1, hbm_outs=(0, 1, 2), flops=FEW_FLOPS,
        scratch=[pltpu.VMEM((1152, 128), f32)] * 2 + wide_scratch, after=(late, in0_second), token=True,
    )
    in_buffer, in_spread = run(
        spread_in_kernel, arr(2, 3, 256, 128), s, in_total, in_total_beside, hbm_outs=(0,), flops=FEW_FLOPS, token=True,
        scratch=[pltpu.VMEM((3, 256, 128), f32), pltpu.SemaphoreType.DMA((1,))],
    )
    total0 = run(add_one_kernel, arr(1152, 128), s, own0, across0, after=(late_in, wide_spread, in_spread))
    total0_beside = beside(total0)
    grad_embed, grad_gain, grad_in, grad_short, grad_first, grad_second, grad_skip = run(
        last_kernel,
        [
            arr(16, 256), arr(2, 2, 256), arr(2, 3, 256, 128), arr(3, 3, 2, 128), arr(FEAT, 2, 64), arr(2, 64, 128), arr(2, 128),
        ],
        s, early, early_in, late, late_in, embed, norm_gain, pack, pack_in, in_own, in0_first, in0_second, in_buffer,
        hbm=(11,), hbm_outs=(2,), aliases=((11, 2),), flops=FEW_FLOPS, after=(total0,),
        scratch=[pltpu.VMEM((3, 256, 128), f32), pltpu.SemaphoreType.DMA((3,))],
    )
    grad_out, grad_up, grad_down = run(
        functools.partial(spread_wide_kernel, 0), wide_shapes, s, total0, total0_beside, *wide_buffers,
        hbm=(2, 3, 4), hbm_outs=(0, 1, 2), aliases=((2, 0), (3, 1), (4, 2)), flops=FEW_FLOPS, scratch=wide_scratch,
    )
    return (
        block_out,
        grad_embed,
        grad_gain,
        jnp.swapaxes(grad_in, 1, 2),
        jnp.transpose(grad_short, (2, 0, 1, 3)),
        jnp.transpose(grad_first, (1, 0, 2)),
        grad_second,
        grad_skip,
        grad_out,
        grad_up,
        grad_down,
    )


def solution(mesh):
    in_specs = (
        P(None, "seq"),
        P(),
        P(),
        P(),
        P(None, None, None, "ch"),
        P(None, None, None, "ch"),
        P(),
        P(None, None, "ch"),
        P(None, "ch"),
        P(None, "ch", None),
        P(None, None, "ch"),
        P(None, "ch", None),
        P(None, "seq", None),
    )
    out_specs = (
        P(None, "seq", None),
        P(),
        P(),
        P(None, None, None, "ch"),
        P(None, None, None, "ch"),
        P(),
        P(None, None, "ch"),
        P(None, "ch"),
        P(None, "ch", None),
        P(None, None, "ch"),
        P(None, "ch", None),
    )

    def either(*args):
        length = args[0].shape[1] * lax.axis_size("seq")
        near = length == BLOCKS * BLOCK and lax.axis_size("seq") == 16
        return (chip_local if near else local)(*args)

    return jax.shard_map(either, mesh=mesh, in_specs=in_specs, out_specs=out_specs, check_vma=False)
```
